32 devices in a mesh: role: 4 (over y, x), pairs: 8 (over z, core).
Axes of the slice: x: 2, y: 2, z: 4, core: 2. Of those that a mesh axis runs over, the one named last changes fastest.
Arguments:
- three_index: bfloat16 [16, 1024, 512], P('pairs'), may hold values from -6 to 6
- coeff: bfloat16 [32, 512, 256], P('pairs'), may hold values from -6 to 6
- amps: bfloat16 [32, 256, 256], P('pairs'), may hold values from -4 to 4
- eps_virt: float32 [32, 256], P('pairs'), may hold values from 0.3 to 3
- eps_occ: float32 [16], replicated, may hold values from -1.5 to -0.3
- nvirt: int32 [32], P('pairs'), may hold values from 64 to 256, as said below
- pair_occ: int32 [32, 2], P('pairs'), may hold values from 0 to 15, as said below
- partners: int32 [32, 8], P('pairs'), may hold values from 0 to 31, as said below
- coupling: float32 [32, 8], P('pairs'), may hold values from -1 to 1
- pair_owner: int32 [32], P('pairs'), may hold values from 1 to 3, as said below
Outputs:
- amps_out: bfloat16 [64, 256, 256], P(('role', 'pairs'))
- dressed_out: bfloat16 [64, 512, 256], P(('role', 'pairs'))
The draws below stay inside these ranges and needn't reach their ends.
Inputs may be any that keep to these rules, and one draw needn't show every extreme that they name: `nvirt`: each block of 4 consecutive pairs has one pair with all 256 virtuals. `pair_occ`: for pair k in block c = k // 4, the first orbital is one of the 2 orbitals numbered from 2 * c, and the second is one of the 6 orbitals numbered cyclically from 2 * (c - 1) modulo 16. Pair k's partners are distinct pairs of its own block of 4 pairs and the blocks just before and after it, cyclically modulo 32. `pair_owner`: in each block of 4 consecutive pairs, each of the roles 1 to 3 holds one or two pairs and exactly one role holds two.
All inputs are finite; a program needn't handle non-finite values.
Results may differ from the reference program's by a relative error of at most 0.012.
Values may be sent and summed in bfloat16 or wider, within the bound.
No kernel may reach another device: no remote copies, remote signals or barrier semaphores. Data moves between devices by JAX's collectives and lax.ppermute only.
A program may use at most 64 MiB of HBM per device.

```python
import math
import jax
import jax.numpy as jnp
from jax import lax

NAUX = 1024
NPAO = 512
NV = 256
PARTNERS = 8
ITERS = 2
O_COL = 2
P_COL = 4
SLOTS = 2
NOCC = 16
PAIRS = 32
SLOT_ALL = 64
N_PAIRS = 8


def draw_nvirt(key, part):
    column_count = PAIRS // P_COL
    counts = jax.random.randint(jax.random.fold_in(key, 101), (column_count, P_COL), NV // 4, NV + 1, dtype=jnp.int32)
    full_at = jax.random.randint(jax.random.fold_in(key, 102), (column_count, 1), 0, P_COL, dtype=jnp.int32)
    places = jnp.arange(P_COL, dtype=jnp.int32)[None, :]
    counts = jnp.where(places == full_at, NV, counts)
    return counts.reshape(PAIRS).astype(jnp.int32)


def draw_pair_occ(key, part):
    column_count = PAIRS // P_COL
    own = O_COL * jnp.arange(column_count, dtype=jnp.int32)
    picks = jax.random.randint(jax.random.fold_in(key, 201), (column_count, 6), 0, O_COL, dtype=jnp.int32)
    side_pick = picks[:, 5] % 2
    first_a = own + picks[:, 0]
    second_a = own - O_COL + picks[:, 1]
    first_b = own + picks[:, 2]
    second_b = own + O_COL + picks[:, 3]
    first_c = own + 1 - jnp.where(side_pick == 0, picks[:, 0], picks[:, 2])
    second_c = own + jnp.where(side_pick == 0, -O_COL, O_COL) + picks[:, 4]
    firsts = jnp.stack([own, first_a, first_b, first_c], axis=1)
    seconds = jnp.stack([own + 1, second_a, second_b, second_c], axis=1)
    seconds = jnp.mod(seconds, NOCC)
    return jnp.stack([firsts, seconds], axis=2).reshape(PAIRS, 2).astype(jnp.int32)


def draw_partners(key, part):
    column_count = PAIRS // P_COL
    pair_ids = jnp.arange(PAIRS, dtype=jnp.int32)
    columns = pair_ids // P_COL
    nearby = jnp.arange(3 * P_COL, dtype=jnp.int32)
    scores = jax.random.randint(jax.random.fold_in(key, 301), (PAIRS, 3 * P_COL), 0, 1 << 20, dtype=jnp.int32) * (3 * P_COL) + nearby[None, :]
    chosen = jnp.argsort(scores, axis=1)[:, :PARTNERS].astype(jnp.int32)
    block_ids = jnp.mod(columns[:, None] - 1 + chosen // P_COL, column_count)
    return (block_ids * P_COL + chosen % P_COL).astype(jnp.int32)


def draw_pair_owner(key, part):
    column_count = PAIRS // P_COL
    extra = jax.random.randint(jax.random.fold_in(key, 401), (column_count, 1), 1, 4, dtype=jnp.int32)
    basic = jnp.broadcast_to(jnp.array([1, 2, 3], jnp.int32)[None, :], (column_count, 3))
    owners = jnp.concatenate([basic, extra], axis=1)
    scores = jax.random.randint(jax.random.fold_in(key, 402), (column_count, 4), 0, 1 << 20, dtype=jnp.int32) * 4 + jnp.arange(4, dtype=jnp.int32)[None, :]
    order = jnp.argsort(scores, axis=1)
    owners = jnp.take_along_axis(owners, order, axis=1)
    return owners.reshape(PAIRS).astype(jnp.int32)


def levels(stream_key, shape, shards, low, top_value):
    loudness, own = 1.0, jax.random.fold_in(stream_key, 6)
    for axis_at, parts in shards:
        draws = jnp.exp(jax.random.uniform(jax.random.fold_in(own, axis_at), (parts,), jnp.float32, low / len(shards), top_value / len(shards)))
        loudness = loudness * jnp.repeat(draws, shape[axis_at] // parts).reshape([-1 if axis == axis_at else 1 for axis in range(len(shape))])
    return loudness


def noise(rng, dims, width, limit, split=(), held_as=jnp.bfloat16):
    values = width * jax.random.normal(rng, dims, jnp.float32)
    if split:
        values = values * levels(rng, dims, split, -0.22, 0.18)
    return jnp.clip(values, -limit, limit).astype(held_as)


def setup_inputs(seed: int = 0) -> dict:
    key_of = jax.random.split(jax.random.key(seed), 11)
    three_index = noise(key_of[0], (NOCC, NAUX, NPAO), 1.0, 6.0, ((0, 8),))
    coeff = noise(key_of[1], (PAIRS, NPAO, NV), 1.0, 6.0, ((0, 8),))
    amps = noise(key_of[2], (PAIRS, NV, NV), 0.5, 4.0, ((0, 8),))
    eps_virt = jnp.clip(jnp.exp(math.log(3.0) - 2.3025851 * jax.random.uniform(key_of[3], (PAIRS, NV), jnp.float32) ** levels(key_of[3], (PAIRS, NV), ((0, 8),), -0.2, 0.2)), 0.3, 3.0)
    eps_occ = jnp.clip(jax.random.uniform(key_of[4], (NOCC,), jnp.float32, -1.5, -0.3), -1.5, -0.3)
    nvirt = draw_nvirt(jax.random.fold_in(key_of[10], 71), 0)
    pair_occ = draw_pair_occ(jax.random.fold_in(key_of[10], 71), 0)
    partners = draw_partners(jax.random.fold_in(key_of[10], 71), 0)
    coupling = jnp.clip(jax.random.uniform(key_of[8], (PAIRS, PARTNERS), jnp.float32, -1.0, 1.0) * levels(key_of[8], (PAIRS, PARTNERS), ((0, 8),), -0.4, 0.0), -1.0, 1.0)
    pair_owner = draw_pair_owner(jax.random.fold_in(key_of[10], 71), 0)
    return dict(three_index=three_index, coeff=coeff, amps=amps, eps_virt=eps_virt, eps_occ=eps_occ, nvirt=nvirt, pair_occ=pair_occ, partners=partners, coupling=coupling, pair_owner=pair_owner)


def slot_numbers(pair_owner):
    owners = pair_owner.reshape(-1, P_COL)
    same_owner = (owners[:, :, None] == owners[:, None, :]).astype(jnp.int32)
    earlier = jnp.tril(jnp.ones((P_COL, P_COL), jnp.int32), -1)
    pair_ranks = lax.optimization_barrier(jnp.sum(same_owner * earlier[None, :, :], axis=2))
    columns = jnp.arange(owners.shape[0], dtype=jnp.int32)[:, None]
    return ((owners * N_PAIRS + columns) * SLOTS + pair_ranks).reshape(-1).astype(jnp.int32)

def reference(three_index, coeff, amps, eps_virt, eps_occ, nvirt, pair_occ, partners, coupling, pair_owner):
    pao_scale = 1.0 / math.sqrt(NPAO)
    aux_scale = 1.0 / math.sqrt(NAUX)
    virt_scale = 1.0 / math.sqrt(NV)
    virtuals = jnp.arange(NV, dtype=jnp.int32)
    pair_ids = jnp.arange(PAIRS, dtype=jnp.int32)

    def integral(packed):
        pair_at, orbitals = packed
        first_half = (jnp.dot(three_index[pair_occ[pair_at, 0]], orbitals, preferred_element_type=jnp.float32) * pao_scale).astype(jnp.bfloat16)
        second_half = (jnp.dot(three_index[pair_occ[pair_at, 1]], orbitals, preferred_element_type=jnp.float32) * pao_scale).astype(jnp.bfloat16)
        return (jnp.dot(first_half.T, second_half, preferred_element_type=jnp.float32) * aux_scale).astype(jnp.bfloat16)

    def update(packed, current):
        pair_at, pair_int = packed
        partner_ids = partners[pair_at]
        own_orb = coeff[pair_at].astype(jnp.float32)
        partner_orb = coeff[partner_ids].astype(jnp.float32)
        intersection = (jnp.einsum('mb,kmc->kbc', own_orb, partner_orb) * (1.0 / NPAO)).astype(jnp.bfloat16)
        partner_amp = current[partner_ids].astype(jnp.float32)
        middle = jnp.einsum('kbc,kcd->kbd', intersection.astype(jnp.float32), partner_amp).astype(jnp.bfloat16)
        partner_terms = jnp.einsum('kbd,ked->kbe', middle.astype(jnp.float32), intersection.astype(jnp.float32))
        coupled = lax.optimization_barrier(jnp.sum(coupling[pair_at][:, None, None] * partner_terms, axis=0))
        occ_shift = eps_occ[pair_occ[pair_at, 0]] + eps_occ[pair_occ[pair_at, 1]]
        energy = eps_virt[pair_at][:, None] + eps_virt[pair_at][None, :] - occ_shift
        own_amp = current[pair_at].astype(jnp.float32)
        fresh_amp = own_amp - (pair_int.astype(jnp.float32) + energy * own_amp + coupled) / (energy + 1.0)
        keep_rows = (virtuals < nvirt[pair_at]).astype(jnp.float32)
        fresh_amp = (fresh_amp * keep_rows[:, None] * keep_rows[None, :]).astype(jnp.bfloat16)
        dressed = (coeff[pair_at].astype(jnp.float32) + jnp.dot(coeff[pair_at], fresh_amp, preferred_element_type=jnp.float32) * virt_scale).astype(jnp.bfloat16)
        return (fresh_amp, dressed)
    current_amp = amps
    current_orb = coeff
    for iteration in range(ITERS):
        pair_ints = lax.map(integral, (pair_ids, current_orb))
        held_amp = current_amp
        current_amp, current_orb = lax.map(lambda packed: update(packed, held_amp), (pair_ids, pair_ints))
    slot_ids = slot_numbers(pair_owner)
    amps_out = jnp.zeros((SLOT_ALL, NV, NV), jnp.bfloat16).at[slot_ids].set(current_amp)
    dressed_out = jnp.zeros((SLOT_ALL, NPAO, NV), jnp.bfloat16).at[slot_ids].set(current_orb)
    return (amps_out, dressed_out)
```

```python
import math

import jax
import jax.numpy as jnp
from jax import lax
from jax.experimental import pallas as pl
from jax.experimental.pallas import tpu as pltpu
from jax.sharding import PartitionSpec as P

F32 = jnp.float32
BF16 = jnp.bfloat16
NN = ((1,), (0,))
NT = ((1,), (1,))

VMEM = pl.BlockSpec(memory_space=pltpu.VMEM)
SMEM = pl.BlockSpec(memory_space=pltpu.SMEM)
ANY = pl.BlockSpec(memory_space=pl.ANY)

MINE, EXTRA, OWNER, FIRST, SECOND, NV_MINE, NV_EXTRA, ROLE_PAIR = 0, 1, 2, 3, 4, 5, 6, 7


def mxu(a, b, dims):
    return lax.dot_general(a, b, (dims, ((), ())), preferred_element_type=F32)


def call(body, ins, outs, args, scratch=(), flops=0):
    moved = sum(a.size * a.dtype.itemsize for a in args)
    return pl.pallas_call(
        body,
        in_specs=ins,
        out_specs=[spec for spec, _, _ in outs],
        out_shape=[jax.ShapeDtypeStruct(shape, dtype) for _, shape, dtype in outs],
        scratch_shapes=list(scratch),
        cost_estimate=pl.CostEstimate(flops=flops, bytes_accessed=moved, transcendentals=0),
        compiler_params=pltpu.CompilerParams(vmem_limit_bytes=48 * 1024 * 1024),
    )(*args)


def pair_of_role(owner_ref, role, pairs):
    chosen = jnp.int32(0)
    for p in range(pairs):
        earlier = jnp.int32(0)
        for o in range(p):
            earlier += (owner_ref[o] == owner_ref[p]).astype(jnp.int32)
        hit = jnp.where(role > 0, (owner_ref[p] == role) & (earlier == 0), earlier == 1)
        chosen = jnp.where(hit, p, chosen)
    return chosen


def local(
    three_index, coeff, amps, eps_virt, eps_occ, nvirt, pair_occ, partners, coupling, pair_owner
):
    columns = lax.axis_size("pairs")
    roles = lax.axis_size("role")
    occ_block, aux, pao = three_index.shape
    pairs, _, virt = coeff.shape
    partner_count = partners.shape[1]
    slots = 2
    assert roles == pairs
    tile = min(256, aux)
    pao_scale = 1.0 / math.sqrt(pao)
    aux_scale = 1.0 / math.sqrt(aux)
    virt_scale = 1.0 / math.sqrt(virt)
    square = (virt, virt)

    def shift(x, by):
        return lax.ppermute(x, "pairs", [(i, (i + by) % columns) for i in range(columns)])

    def swap(x, by, skip=()):
        return lax.ppermute(
            x, "role", [(i, i ^ by) for i in range(roles) if i ^ by not in skip]
        )

    def pick_body(owner_ref, coeff_ref, out_ref, sem):
        mine = pair_of_role(owner_ref, lax.axis_index("role"), pairs)
        copy = pltpu.make_async_copy(coeff_ref.at[mine], out_ref, sem)
        copy.start()
        copy.wait()

    (x_mine,) = call(
        pick_body,
        [SMEM, ANY],
        [(ANY, (pao, virt), BF16)],
        (pair_owner, coeff),
        scratch=[pltpu.SemaphoreType.DMA],
    )
    x_left = shift(x_mine, 1)
    x_right = shift(x_mine, -1)

    def plan_body(
        owner_ref, occ_ref, partner_ref, coupling_ref, eps_ref, nvirt_ref,
        to_left, to_right, ints, floats, extra_w,
    ):
        role = lax.axis_index("role")
        column = lax.axis_index("pairs")
        mine = pair_of_role(owner_ref, role, pairs)
        extra = pair_of_role(owner_ref, jnp.int32(0), pairs)
        ints[MINE] = mine
        ints[EXTRA] = extra
        ints[OWNER] = owner_ref[extra]
        for s in range(roles):
            ints[ROLE_PAIR + s] = pair_of_role(owner_ref, jnp.int32(s), pairs)
        ints[NV_MINE] = nvirt_ref[mine]
        ints[NV_EXTRA] = nvirt_ref[extra]
        ints[FIRST] = occ_ref[mine, 0] - column * occ_block
        occ_all = occ_block * columns
        second = lax.rem(occ_ref[mine, 1] - (column - 1) * occ_block + occ_all, occ_all)
        ints[SECOND] = second
        floats[pairs] = eps_ref[occ_ref[mine, 0]] + eps_ref[occ_ref[mine, 1]]
        floats[pairs + 1] = eps_ref[occ_ref[extra, 0]] + eps_ref[occ_ref[extra, 1]]
        for q in range(pairs):
            to_left[q] = jnp.float32(0)
            to_right[q] = jnp.float32(0)
            floats[q] = jnp.float32(0)
        for q in range(3 * pairs):
            extra_w[q] = jnp.float32(0)
        pair_all = pairs * columns

        def near(p, k):
            return lax.rem(partner_ref[p, k] - (column - 1) * pairs + pair_all, pair_all)

        for k in range(partner_count):
            at, weight = near(mine, k), coupling_ref[mine, k]

            @pl.when(at < pairs)
            def _():
                to_left[at] += weight

            @pl.when((at >= pairs) & (at < 2 * pairs))
            def _():
                floats[at - pairs] += weight

            @pl.when(at >= 2 * pairs)
            def _():
                to_right[at - 2 * pairs] += weight

            extra_w[near(extra, k)] += coupling_ref[extra, k]
        to_left[pairs] = jnp.minimum(second, occ_block - 1).astype(F32)
        to_right[pairs] = jnp.maximum(second - 2 * occ_block, 0).astype(F32)
        to_left[pairs + 1] = mine.astype(F32)
        to_right[pairs + 1] = mine.astype(F32)

    meta = (SMEM, (pairs + 2,), F32)
    to_left, to_right, ints, floats, extra_w = call(
        plan_body,
        [SMEM] * 6,
        [
            meta,
            meta,
            (SMEM, (ROLE_PAIR + roles,), jnp.int32),
            (SMEM, (pairs + 2,), F32),
            (SMEM, (3 * pairs,), F32),
        ],
        (pair_owner, pair_occ, partners, coupling, eps_occ, nvirt),
    )
    of_left = shift(to_right, 1)
    of_right = shift(to_left, -1)

    def overlaps(x, coeff_ref, out_ref):
        turned = x.T
        for q in range(pairs):
            s = mxu(turned, coeff_ref[q], NN) * (1.0 / pao)
            out_ref[q] = s.astype(BF16)

    def coupled(s_ref, parts):
        total = None
        for at, weight, amp in parts:
            s = s_ref[at]
            middle = mxu(s, amp, NN).astype(BF16)
            term = weight * mxu(middle, s, NT)
            total = term if total is None else total + term
        return total

    def own_body(
        ints, floats, three_ref, coeff_ref, amps_ref, eps_ref,
        first_ref, second_ref, s_ref, c_ref, gain_ref, gain_extra_ref,
    ):
        mine = ints[MINE]
        x = coeff_ref[mine]
        turned = x.T
        first = ints[FIRST]
        second = jnp.clip(ints[SECOND] - occ_block, 0, occ_block - 1)
        for at in range(0, aux, tile):
            rows = pl.ds(at, tile)
            first_ref[:, rows] = (mxu(turned, three_ref[first, rows, :], NT) * pao_scale).astype(BF16)
            second_ref[rows, :] = (mxu(three_ref[second, rows, :], x, NN) * pao_scale).astype(BF16)
        overlaps(x, coeff_ref, s_ref)
        c_ref[...] = coupled(s_ref, [(q, floats[q], amps_ref[q]) for q in range(pairs)])

        def gain(pair, count, shift_at):
            row = jnp.broadcast_to(eps_ref[pl.ds(pair, 1), :], square)
            energy = row + row.T - floats[shift_at]
            inside = (lax.broadcasted_iota(jnp.int32, square, 0) < count) & (
                lax.broadcasted_iota(jnp.int32, square, 1) < count
            )
            return jnp.where(inside, 1.0 / (energy + 1.0), 0.0)

        gain_ref[...] = gain(mine, ints[NV_MINE], pairs)
        gain_extra_ref[...] = gain(ints[EXTRA], ints[NV_EXTRA], pairs + 1)

    all_s = (VMEM, (pairs, virt, virt), BF16)
    first_t, second_own, s_own, c_own, gain, gain_extra = call(
        own_body,
        [SMEM, SMEM, VMEM, VMEM, VMEM, VMEM],
        [
            (VMEM, (virt, aux), BF16),
            (VMEM, (aux, virt), BF16),
            all_s,
            (VMEM, square, F32),
            (VMEM, square, F32),
            (VMEM, square, F32),
        ],
        (ints, floats, three_index, coeff, amps, eps_virt),
        flops=2 * virt * (2 * aux * pao + pairs * virt * (pao + 2 * virt)),
    )

    def half_body(of_left, of_right, three_ref, xl_ref, xr_ref, yl_ref, yr_ref):
        for of, x_ref, y_ref in ((of_left, xl_ref, yl_ref), (of_right, xr_ref, yr_ref)):
            at_occ = of[pairs].astype(jnp.int32)
            for at in range(0, aux, tile):
                rows = pl.ds(at, tile)
                y_ref[rows, :] = (mxu(three_ref[at_occ, rows, :], x_ref[...], NN) * pao_scale).astype(BF16)

    half = (VMEM, (aux, virt), BF16)
    y_left, y_right = call(
        half_body,
        [SMEM, SMEM, VMEM, VMEM, VMEM],
        [half, half],
        (of_left, of_right, three_index, x_left, x_right),
        flops=4 * aux * pao * virt,
    )
    y_from_right = shift(y_left, -1)
    y_from_left = shift(y_right, 1)

    def near_body(of_left, of_right, coeff_ref, amps_ref, xl_ref, xr_ref, sl_ref, sr_ref, cl_ref, cr_ref):
        for of, x_ref, s_ref, c_ref in (
            (of_left, xl_ref, sl_ref, cl_ref),
            (of_right, xr_ref, sr_ref, cr_ref),
        ):
            overlaps(x_ref[...], coeff_ref, s_ref)
            c_ref[...] = coupled(
                s_ref, [(q, of[q], amps_ref[q]) for q in range(pairs)]
            ).astype(BF16)

    sq_b = (VMEM, square, BF16)
    sq_f = (VMEM, square, F32)
    s_left, s_right, c_left, c_right = call(
        near_body,
        [SMEM, SMEM, VMEM, VMEM, VMEM, VMEM],
        [all_s, all_s, sq_b, sq_b],
        (of_left, of_right, coeff, amps, x_left, x_right),
        flops=4 * pairs * virt * virt * (pao + 2 * virt),
    )
    c_from_right = shift(c_left, -1)
    c_from_left = shift(c_right, 1)

    def first_body(
        ints, first_ref, own_ref, left_ref, right_ref, amps_ref, c_ref, cl_ref, cr_ref, gain_ref,
        amp_ref, k_ref, held, sem,
    ):
        second = ints[SECOND]

        def take(source):
            copy = pltpu.make_async_copy(source, held, sem)
            copy.start()
            copy.wait()

        @pl.when(second < occ_block)
        def _():
            take(left_ref)

        @pl.when((second >= occ_block) & (second < 2 * occ_block))
        def _():
            take(own_ref)

        @pl.when(second >= 2 * occ_block)
        def _():
            take(right_ref)

        k = mxu(first_ref[...], held[...], NN) * aux_scale
        k_ref[...] = k
        c = c_ref[...] + cl_ref[...].astype(F32) + cr_ref[...].astype(F32)
        old = amps_ref[ints[MINE]].astype(F32)
        amp_ref[...] = (gain_ref[...] * (old - k - c)).astype(BF16)

    amp, k_first = call(
        first_body,
        [SMEM, VMEM, ANY, ANY, ANY, VMEM, VMEM, VMEM, VMEM, VMEM],
        [sq_b, sq_f],
        (
            ints, first_t, second_own, y_from_left, y_from_right,
            amps, c_own, c_from_left, c_from_right, gain,
        ),
        scratch=[pltpu.VMEM((aux, virt), BF16), pltpu.SemaphoreType.DMA],
        flops=2 * aux * virt * virt,
    )

    amp_roles = [amp] + [swap(amp, m) for m in range(1, roles)]
    amp_left = shift(amp, 1)
    amp_right = shift(amp, -1)

    def second_body(amp_ref, k_ref, out_ref):
        amp = amp_ref[...]
        k = k_ref[...]
        right = k + mxu(k.astype(BF16), amp, NN) * virt_scale
        both = right + mxu(amp.T, right.astype(BF16), NN) * virt_scale
        out_ref[...] = amp.astype(F32) - both

    (rest,) = call(
        second_body, [VMEM, VMEM], [sq_f], (amp, k_first), flops=4 * virt * virt * virt
    )

    def extra_body(
        ints, extra_w, of_left, of_right, so_ref, sl_ref, sr_ref, ao_ref, al_ref, ar_ref, rest_ref, out_ref
    ):
        extra = ints[EXTRA]
        left = of_left[pairs + 1].astype(jnp.int32)
        right = of_right[pairs + 1].astype(jnp.int32)
        total = jnp.where(lax.axis_index("role") == 0, rest_ref[...], 0.0)
        for s_ref, amp_ref, at in (
            (sl_ref, al_ref, left),
            (so_ref, ao_ref, pairs + ints[MINE]),
            (sr_ref, ar_ref, 2 * pairs + right),
        ):
            s = s_ref[extra]
            middle = mxu(amp_ref[...], s, NN).astype(BF16)
            total -= extra_w[at] * mxu(s.T, middle, NN)
        out_ref[...] = total.astype(BF16)

    (extra_part,) = call(
        extra_body,
        [SMEM] * 4 + [VMEM] * 7,
        [sq_b],
        (
            ints, extra_w, of_left, of_right, s_own, s_left, s_right,
            amp, amp_left, amp_right, rest,
        ),
        flops=12 * virt * virt * virt,
    )
    extra_parts = [extra_part] + [swap(extra_part, m, skip=(0,)) for m in range(1, roles)]

    def column_parts(ints, weight, amp_refs):
        role = lax.axis_index("role")
        parts = []
        for m in range(roles):
            at = ints[ROLE_PAIR + (role ^ m)]
            parts.append((at, weight[at], amp_refs[m][...]))
        return parts

    def again_body(ints, of_left, of_right, sl_ref, sr_ref, a0, a1, a2, a3, cl_ref, cr_ref):
        amp_refs = (a0, a1, a2, a3)
        for of, s_ref, c_ref in ((of_left, sl_ref, cl_ref), (of_right, sr_ref, cr_ref)):
            c_ref[...] = coupled(s_ref, column_parts(ints, of, amp_refs)).astype(BF16)

    c_left, c_right = call(
        again_body,
        [SMEM] * 3 + [VMEM] * 6,
        [sq_b, sq_b],
        (ints, of_left, of_right, s_left, s_right, *amp_roles),
        flops=8 * pairs * virt * virt * virt,
    )
    c_from_right = shift(c_left, -1)
    c_from_left = shift(c_right, 1)

    def own_again_body(ints, floats, s_ref, a0, a1, a2, a3, rest_ref, out_ref):
        c = coupled(s_ref, column_parts(ints, floats, (a0, a1, a2, a3)))
        out_ref[...] = rest_ref[...] - c

    (rest,) = call(
        own_again_body,
        [SMEM] * 2 + [VMEM] * 6,
        [sq_f],
        (ints, floats, s_own, *amp_roles, rest),
        flops=4 * pairs * virt * virt * virt,
    )

    def last_body(
        ints, coeff_ref, gain_ref, gain_extra_ref, rest_ref, cl_ref, cr_ref, e0, e1, e2, e3,
        amp_ref, orb_ref,
    ):
        role = lax.axis_index("role")

        def store(slot, amp, pair):
            amp = amp.astype(BF16)
            amp_ref[slot] = amp
            x = coeff_ref[pair]
            orb_ref[slot] = (x.astype(F32) + mxu(x, amp, NN) * virt_scale).astype(BF16)

        def clear(slot):
            amp_ref[slot] = jnp.zeros(square, BF16)
            orb_ref[slot] = jnp.zeros((pao, virt), BF16)

        has_extra = role == ints[OWNER]

        @pl.when(has_extra)
        def _():
            total = sum(e[...].astype(F32) for e in (e0, e1, e2, e3))
            store(1, gain_extra_ref[...] * total, ints[EXTRA])

        @pl.when(jnp.logical_not(has_extra))
        def _():
            clear(1)

        @pl.when(role > 0)
        def _():
            total = rest_ref[...] - cl_ref[...].astype(F32) - cr_ref[...].astype(F32)
            store(0, gain_ref[...] * total, ints[MINE])

        @pl.when(role == 0)
        def _():
            clear(0)

    amps_out, dressed_out = call(
        last_body,
        [SMEM] + [VMEM] * 10,
        [(VMEM, (slots, virt, virt), BF16), (VMEM, (slots, pao, virt), BF16)],
        (ints, coeff, gain, gain_extra, rest, c_from_left, c_from_right, *extra_parts),
        flops=4 * pao * virt * virt,
    )
    return amps_out, dressed_out


def solution(mesh):
    in_specs = (
        P("pairs", None, None),
        P("pairs", None, None),
        P("pairs", None, None),
        P("pairs", None),
        P(),
        P("pairs"),
        P("pairs", None),
        P("pairs", None),
        P("pairs", None),
        P("pairs"),
    )
    out_specs = (P(("role", "pairs"), None, None), P(("role", "pairs"), None, None))
    return jax.shard_map(local, mesh=mesh, in_specs=in_specs, out_specs=out_specs, check_vma=False)
```

```python
import math

import jax
import jax.numpy as jnp
from jax import lax
from jax.experimental import pallas as pl
from jax.experimental.pallas import tpu as pltpu
from jax.sharding import PartitionSpec as P

F32 = jnp.float32
BF16 = jnp.bfloat16
I32 = jnp.int32
NN = ((1,), (0,))
NT = ((1,), (1,))

VMEM = pl.BlockSpec(memory_space=pltpu.VMEM)
SMEM = pl.BlockSpec(memory_space=pltpu.SMEM)
ANY = pl.BlockSpec(memory_space=pl.ANY)
HBM = pl.BlockSpec(memory_space=pltpu.HBM)

MINE, EXTRA, OWNER, FIRST, SECOND, WHOSE, NV_MINE, NV_EXTRA, ROLE_PAIR = range(9)


def mxu(a, b, dims):
    return lax.dot_general(a, b, (dims, ((), ())), preferred_element_type=F32)


def call(body, ins, outs, args, scratch=(), flops=0, vmem=48):
    moved = sum(a.size * a.dtype.itemsize for a in args)
    return pl.pallas_call(
        body,
        in_specs=ins,
        out_specs=[spec for spec, _, _ in outs],
        out_shape=[jax.ShapeDtypeStruct(shape, dtype) for _, shape, dtype in outs],
        scratch_shapes=list(scratch),
        cost_estimate=pl.CostEstimate(flops=flops, bytes_accessed=moved, transcendentals=0),
        compiler_params=pltpu.CompilerParams(vmem_limit_bytes=vmem * 1024 * 1024),
    )(*args)


def local(
    three_index, coeff, amps, eps_virt, eps_occ, nvirt, pair_occ, partners, coupling, pair_owner
):
    columns = lax.axis_size("pairs")
    roles = lax.axis_size("role")
    occ_block, aux, pao = three_index.shape
    pairs, _, virt = coeff.shape
    partner_count = partners.shape[1]
    slots = 2
    assert roles == pairs and columns % 2 == 0
    tile = min(256, aux)
    pao_scale = 1.0 / math.sqrt(pao)
    aux_scale = 1.0 / math.sqrt(aux)
    virt_scale = 1.0 / math.sqrt(virt)
    square = (virt, virt)
    sq_b = (VMEM, square, BF16)
    sq_f = (VMEM, square, F32)
    two_b = (VMEM, (2, virt, virt), BF16)
    all_s = (VMEM, (pairs, virt, virt), BF16)
    orb = (VMEM, (pao, virt), BF16)

    def inner(x):
        return lax.ppermute(x, "pairs", [(i, i ^ 1) for i in range(columns)])

    def outer(x):
        return lax.ppermute(
            x, "pairs", [(i, (i + (1 if i % 2 else -1)) % columns) for i in range(columns)]
        )

    def swap(x, by):
        return lax.ppermute(x, "role", [(i, i ^ by) for i in range(roles)])

    weights = 2 * pairs

    def plan_body(
        owner_hbm, occ_hbm, partner_hbm, coupling_hbm, eps_hbm, nvirt_hbm, coeff_hbm,
        mine_ref, extra_ref, to_inner, to_outer, ints, floats,
        owner_ref, occ_ref, partner_ref, coupling_ref, eps_ref, nvirt_ref, near_w, sems,
    ):
        small = [
            pltpu.make_async_copy(source, target, sems.at[at])
            for at, (source, target) in enumerate(
                (
                    (owner_hbm, owner_ref),
                    (occ_hbm, occ_ref),
                    (partner_hbm, partner_ref),
                    (coupling_hbm, coupling_ref),
                    (eps_hbm, eps_ref),
                    (nvirt_hbm, nvirt_ref),
                )
            )
        ]
        for copy in small:
            copy.start()
        role = lax.axis_index("role")
        column = lax.axis_index("pairs")
        small[0].wait()
        of_role = [jnp.int32(0)] * roles
        for p in range(pairs):
            earlier = jnp.int32(0)
            for o in range(p):
                earlier += (owner_ref[o] == owner_ref[p]).astype(I32)
            for s in range(roles):
                hit = (earlier == 0) & (owner_ref[p] == s) if s else earlier == 1
                of_role[s] = jnp.where(hit, p, of_role[s])
        extra = of_role[0]
        mine = extra
        for s in range(1, roles):
            mine = jnp.where(role == s, of_role[s], mine)
        large = [
            pltpu.make_async_copy(coeff_hbm.at[mine], mine_ref, sems.at[6]),
            pltpu.make_async_copy(coeff_hbm.at[extra], extra_ref, sems.at[7]),
        ]
        for copy in large:
            copy.start()
        for copy in small[1:]:
            copy.wait()
        ints[MINE] = mine
        ints[EXTRA] = extra
        ints[OWNER] = owner_ref[extra]
        for s in range(roles):
            ints[ROLE_PAIR + s] = of_role[s]
        ints[NV_MINE] = nvirt_ref[mine]
        ints[NV_EXTRA] = nvirt_ref[extra]
        ints[FIRST] = occ_ref[0, mine] - column * occ_block
        odd = lax.rem(column, 2) == 1
        inner_at = jnp.where(odd, 0, 2)
        outer_at = 2 - inner_at
        occ_all = occ_block * columns
        second = lax.rem(occ_ref[1, mine] - (column - 1) * occ_block + occ_all, occ_all)
        block = (second >= occ_block).astype(I32) + (second >= 2 * occ_block).astype(I32)
        ints[SECOND] = second - block * occ_block
        ints[WHOSE] = jnp.where(block == 1, 0, jnp.where(block == inner_at, 1, 2))
        floats[weights] = eps_ref[occ_ref[0, mine]] + eps_ref[occ_ref[1, mine]]
        floats[weights + 1] = eps_ref[occ_ref[0, extra]] + eps_ref[occ_ref[1, extra]]
        pair_all = pairs * columns
        for which, pair in enumerate((mine, extra)):
            for q in range(3 * pairs):
                near_w[q] = jnp.float32(0)
            for k in range(partner_count):
                at = lax.rem(partner_ref[pair, k] - (column - 1) * pairs + pair_all, pair_all)
                near_w[at] += coupling_ref[pair, k]
            for q in range(pairs):
                to = which * pairs + q
                to_inner[to] = near_w[inner_at * pairs + q]
                floats[to] = near_w[pairs + q]
                to_outer[to] = near_w[outer_at * pairs + q]
        to_inner[weights] = ints[SECOND].astype(F32)
        to_outer[weights] = ints[SECOND].astype(F32)
        for copy in large:
            copy.wait()

    meta = (SMEM, (weights + 1,), F32)
    x_mine, x_extra, to_inner, to_outer, ints, floats = call(
        plan_body,
        [HBM] * 7,
        [
            (ANY, (pao, virt), BF16),
            (ANY, (pao, virt), BF16),
            meta,
            meta,
            (SMEM, (ROLE_PAIR + roles,), I32),
            (SMEM, (weights + 2,), F32),
        ],
        (pair_owner, pair_occ.T, partners, coupling, eps_occ, nvirt, coeff),
        scratch=[
            pltpu.SMEM(pair_owner.shape, I32),
            pltpu.SMEM(pair_occ.shape[::-1], I32),
            pltpu.SMEM(partners.shape, I32),
            pltpu.SMEM(coupling.shape, F32),
            pltpu.SMEM(eps_occ.shape, F32),
            pltpu.SMEM(nvirt.shape, I32),
            pltpu.SMEM((3 * pairs,), F32),
            pltpu.SemaphoreType.DMA((8,)),
        ],
        vmem=60,
    )
    x_out = outer(x_mine)
    of_out = outer(to_outer)
    x_in = inner(x_mine)
    of_in = inner(to_inner)
    x_extra_in = inner(x_extra)

    def overlaps(x, coeff_ref, out_ref):
        turned = x.T
        for q in range(pairs):
            s = mxu(turned, coeff_ref[q], NN) * (1.0 / pao)
            out_ref[q] = s.astype(BF16)

    def coupled(s_ref, parts):
        total = None
        for at, weight, amp in parts:
            s = s_ref[at]
            middle = mxu(s, amp, NN).astype(BF16)
            term = weight * mxu(middle, s, NT)
            total = term if total is None else total + term
        return total

    def half_into(y_ref, three_ref, at_occ, x):
        for at in range(0, aux, tile):
            rows = pl.ds(at, tile)
            y_ref[rows, :] = (mxu(three_ref[at_occ, rows, :], x, NN) * pao_scale).astype(BF16)

    def own_body(
        ints, floats, three_ref, coeff_ref, amps_ref, eps_ref,
        first_ref, second_ref, s_ref, se_ref, c_ref, gain_ref, gain_extra_ref,
    ):
        mine = ints[MINE]
        x = coeff_ref[mine]
        turned = x.T
        first = ints[FIRST]
        for at in range(0, aux, tile):
            rows = pl.ds(at, tile)
            first_ref[:, rows] = (mxu(turned, three_ref[first, rows, :], NT) * pao_scale).astype(BF16)
        half_into(second_ref, three_ref, ints[SECOND], x)
        overlaps(x, coeff_ref, s_ref)
        overlaps(coeff_ref[ints[EXTRA]], coeff_ref, se_ref)
        c_ref[...] = coupled(s_ref, [(q, floats[q], amps_ref[q]) for q in range(pairs)])

        def gain(pair, count, shift_at):
            row = jnp.broadcast_to(eps_ref[pl.ds(pair, 1), :], square)
            energy = row + row.T - floats[shift_at]
            inside = (lax.broadcasted_iota(I32, square, 0) < count) & (
                lax.broadcasted_iota(I32, square, 1) < count
            )
            return jnp.where(inside, 1.0 / (energy + 1.0), 0.0)

        gain_ref[...] = gain(mine, ints[NV_MINE], weights)
        gain_extra_ref[...] = gain(ints[EXTRA], ints[NV_EXTRA], weights + 1)

    half = (VMEM, (aux, virt), BF16)
    first_t, second_own, s_own, se_own, c_own, gain, gain_extra = call(
        own_body,
        [SMEM, SMEM, VMEM, VMEM, VMEM, VMEM],
        [(VMEM, (virt, aux), BF16), half, all_s, all_s, sq_f, sq_f, sq_f],
        (ints, floats, three_index, coeff, amps, eps_virt),
        flops=2 * virt * (2 * aux * pao + pairs * virt * (2 * pao + 2 * virt)),
    )

    def inner_body(of, three_ref, coeff_ref, amps_ref, x_ref, xe_ref, y_ref, s_ref, se_ref, c_ref):
        half_into(y_ref, three_ref, of[weights].astype(I32), x_ref[...])
        overlaps(x_ref[...], coeff_ref, s_ref)
        overlaps(xe_ref[...], coeff_ref, se_ref)
        c = coupled(s_ref, [(q, of[q], amps_ref[q]) for q in range(pairs)])
        c_ref[...] = c.astype(BF16)

    y_in, s_in, se_in, c_in = call(
        inner_body,
        [SMEM] + [VMEM] * 5,
        [half, all_s, all_s, sq_b],
        (of_in, three_index, coeff, amps, x_in, x_extra_in),
        flops=2 * virt * (aux * pao + pairs * virt * (2 * pao + 2 * virt)),
    )
    y_from_in = inner(y_in)
    c_from_in = inner(c_in)

    def outer_half_body(of, three_ref, x_ref, own_ref, in_ref, y_ref):
        half_into(y_ref, three_ref, of[weights].astype(I32), x_ref[...])

    (y_out,) = call(
        outer_half_body,
        [SMEM, VMEM, VMEM, ANY, ANY],
        [half],
        (of_out, three_index, x_out, first_t, y_in),
        flops=2 * aux * pao * virt,
    )
    y_from_out = outer(y_out)

    def outer_body(of, coeff_ref, amps_ref, x_ref, s_ref, c_ref):
        overlaps(x_ref[...], coeff_ref, s_ref)
        c = coupled(s_ref, [(q, of[q], amps_ref[q]) for q in range(pairs)])
        c_ref[...] = c.astype(BF16)

    s_out, c_out = call(
        outer_body,
        [SMEM, VMEM, VMEM, VMEM],
        [all_s, sq_b],
        (of_out, coeff, amps, x_out),
        flops=2 * pairs * virt * virt * (pao + 2 * virt),
    )
    c_from_out = outer(c_out)

    x_sent, _ = lax.optimization_barrier((x_out, y_out))
    x_extras = [lax.ppermute(x_sent, "role", [(0, s)]) for s in range(1, roles)]

    def first_body(
        ints, first_ref, own_ref, in_ref, out_ref, amps_ref, c_ref, ci_ref, co_ref, gain_ref,
        amp_ref, k_ref, held, sem,
    ):
        for whose, source in enumerate((own_ref, in_ref, out_ref)):

            @pl.when(ints[WHOSE] == whose)
            def _():
                copy = pltpu.make_async_copy(source, held, sem)
                copy.start()
                copy.wait()

        k = mxu(first_ref[...], held[...], NN) * aux_scale
        k_ref[...] = k
        c = c_ref[...] + ci_ref[...].astype(F32) + co_ref[...].astype(F32)
        old = amps_ref[ints[MINE]].astype(F32)
        amp_ref[...] = (gain_ref[...] * (old - k - c)).astype(BF16)

    amp, k_first = call(
        first_body,
        [SMEM, VMEM, ANY, ANY, ANY, VMEM, VMEM, VMEM, VMEM, VMEM],
        [sq_b, sq_f],
        (
            ints, first_t, second_own, y_from_in, y_from_out,
            amps, c_own, c_from_in, c_from_out, gain,
        ),
        scratch=[pltpu.VMEM((aux, virt), BF16), pltpu.SemaphoreType.DMA],
        flops=2 * aux * virt * virt,
    )
    amp_roles = [amp] + [swap(amp, m) for m in range(1, roles)]

    def second_body(amp_ref, k_ref, out_ref, out_b_ref):
        amp = amp_ref[...]
        k = k_ref[...]
        right = k + mxu(k.astype(BF16), amp, NN) * virt_scale
        both = right + mxu(amp.T, right.astype(BF16), NN) * virt_scale
        rest = amp.astype(F32) - both
        out_ref[...] = rest
        out_b_ref[...] = rest.astype(BF16)

    rest, rest_b = call(
        second_body, [VMEM, VMEM], [sq_f, sq_b], (amp, k_first), flops=4 * virt * virt * virt
    )
    rests = [lax.ppermute(rest_b, "role", [(0, s)]) for s in range(1, roles)]

    def outer_extra_body(s_near_ref, coeff_ref, after_ref, *refs):
        x_refs, s_ref = refs[:-1], refs[-1]
        role = lax.axis_index("role")

        @pl.when(role == 0)
        def _():
            s_ref[...] = s_near_ref[...]

        for s in range(1, roles):

            @pl.when(role == s)
            def _():
                overlaps(x_refs[s - 1][...], coeff_ref, s_ref)

    (se_out,) = call(
        outer_extra_body,
        [VMEM, VMEM, ANY] + [VMEM] * (roles - 1),
        [all_s],
        (s_out, coeff, rest, *x_extras),
        flops=2 * pairs * virt * virt * pao,
    )

    def parts_of(ints, weight_ref, first_weight, amp_refs):
        role = lax.axis_index("role")
        parts = []
        for m in range(roles):
            at = ints[ROLE_PAIR + (role ^ m)]
            parts.append((at, weight_ref[first_weight + at], amp_refs[m][...]))
        return parts

    def near_again_body(ints, of, s_ref, se_ref, *refs):
        amp_refs, c_ref = refs[:roles], refs[roles]
        c_ref[0] = coupled(s_ref, parts_of(ints, of, 0, amp_refs)).astype(BF16)
        c_ref[1] = coupled(se_ref, parts_of(ints, of, pairs, amp_refs)).astype(BF16)

    def near_again(of, s, se):
        (c,) = call(
            near_again_body,
            [SMEM, SMEM] + [VMEM] * (2 + roles),
            [two_b],
            (ints, of, s, se, *amp_roles),
            flops=8 * pairs * virt * virt * virt,
        )
        return c

    cc_from_out = outer(near_again(of_out, s_out, se_out))
    cc_from_in = inner(near_again(of_in, s_in, se_in))

    def own_again_body(ints, floats, s_ref, se_ref, rest_ref, *refs):
        amp_refs, rest_refs, (out_ref, out_extra_ref) = (
            refs[:roles], refs[roles : 2 * roles - 1], refs[2 * roles - 1 :],
        )
        out_ref[...] = rest_ref[...] - coupled(s_ref, parts_of(ints, floats, 0, amp_refs))
        role = lax.axis_index("role")
        total = -coupled(se_ref, parts_of(ints, floats, pairs, amp_refs))
        for s in range(1, roles):
            total += jnp.where(role == s, rest_refs[s - 1][...].astype(F32), 0.0)
        out_extra_ref[...] = total

    rest, rest_extra = call(
        own_again_body,
        [SMEM] * 2 + [VMEM] * (3 + 2 * roles - 1),
        [sq_f, sq_f],
        (ints, floats, s_own, se_own, rest, *amp_roles, *rests),
        flops=8 * pairs * virt * virt * virt,
    )

    def last_body(
        ints, coeff_ref, gain_ref, gain_extra_ref, rest_ref, rest_extra_ref, ci_ref, co_ref, amp_ref, orb_ref
    ):
        role = lax.axis_index("role")

        def store(slot, here, gain, rest, pair):
            @pl.when(here)
            def _():
                c = ci_ref[slot].astype(F32) + co_ref[slot].astype(F32)
                amp = (gain[...] * (rest[...] - c)).astype(BF16)
                amp_ref[slot] = amp
                x = coeff_ref[pair]
                orb_ref[slot] = (x.astype(F32) + mxu(x, amp, NN) * virt_scale).astype(BF16)

            @pl.when(jnp.logical_not(here))
            def _():
                amp_ref[slot] = jnp.zeros(square, BF16)
                orb_ref[slot] = jnp.zeros((pao, virt), BF16)

        store(0, role > 0, gain_ref, rest_ref, ints[MINE])
        store(1, role == ints[OWNER], gain_extra_ref, rest_extra_ref, ints[EXTRA])

    amps_out, dressed_out = call(
        last_body,
        [SMEM] + [VMEM] * 7,
        [(VMEM, (slots, virt, virt), BF16), (VMEM, (slots, pao, virt), BF16)],
        (ints, coeff, gain, gain_extra, rest, rest_extra, cc_from_in, cc_from_out),
        flops=4 * pao * virt * virt,
    )
    return amps_out, dressed_out


def solution(mesh):
    in_specs = (
        P("pairs", None, None),
        P("pairs", None, None),
        P("pairs", None, None),
        P("pairs", None),
        P(),
        P("pairs"),
        P("pairs", None),
        P("pairs", None),
        P("pairs", None),
        P("pairs"),
    )
    out_specs = (P(("role", "pairs"), None, None), P(("role", "pairs"), None, None))
    return jax.shard_map(local, mesh=mesh, in_specs=in_specs, out_specs=out_specs, check_vma=False)
```

```python
import math

import jax
import jax.numpy as jnp
from jax import lax
from jax.experimental import pallas as pl
from jax.experimental.pallas import tpu as pltpu
from jax.sharding import PartitionSpec as P

F32 = jnp.float32
BF16 = jnp.bfloat16
I32 = jnp.int32
NN = ((1,), (0,))
NT = ((1,), (1,))

VMEM = pl.BlockSpec(memory_space=pltpu.VMEM)
SMEM = pl.BlockSpec(memory_space=pltpu.SMEM)
ANY = pl.BlockSpec(memory_space=pl.ANY)
HBM = pl.BlockSpec(memory_space=pltpu.HBM)

MINE, EXTRA, OWNER, FIRST, SECOND, WHOSE, NV_MINE, NV_EXTRA, OCC_MINE, OCC_EXTRA, ROLE_PAIR = range(11)


def whole(number):
    return number.astype(jnp.int32)


def mxu(a, b, dims):
    return lax.dot_general(a, b, (dims, ((), ())), preferred_element_type=F32)


def call(body, ins, outs, args, scratch=(), flops=0, vmem=48):
    moved = sum(a.size * a.dtype.itemsize for a in args)
    return pl.pallas_call(
        body,
        in_specs=ins,
        out_specs=[spec for spec, _, _ in outs],
        out_shape=[jax.ShapeDtypeStruct(shape, dtype) for _, shape, dtype in outs],
        scratch_shapes=list(scratch),
        cost_estimate=pl.CostEstimate(flops=flops, bytes_accessed=moved, transcendentals=0),
        compiler_params=pltpu.CompilerParams(vmem_limit_bytes=vmem * 1024 * 1024),
    )(*args)


def local(
    three_index, coeff, amps, eps_virt, eps_occ, nvirt, pair_occ, partners, coupling, pair_owner
):
    columns = lax.axis_size("pairs")
    roles = lax.axis_size("role")
    occ_block, aux, pao = three_index.shape
    pairs, _, virt = coeff.shape
    partner_count = partners.shape[1]
    slots = 2
    assert roles == pairs and columns % 2 == 0
    tile = min(256, aux)
    pao_scale = 1.0 / math.sqrt(pao)
    aux_scale = 1.0 / math.sqrt(aux)
    virt_scale = 1.0 / math.sqrt(virt)
    square = (virt, virt)
    wide = (virt, pairs * virt)
    sq_b = (VMEM, square, BF16)
    sq_f = (VMEM, square, F32)
    two_b = (VMEM, (2, virt, virt), BF16)
    all_s = (VMEM, wide, BF16)
    half = (VMEM, (aux, virt), BF16)
    orb = (VMEM, (pao, virt), BF16)
    middle = pltpu.VMEM(wide, BF16)

    def inner(x):
        return lax.ppermute(x, "pairs", [(i, i ^ 1) for i in range(columns)])

    def outer(x):
        return lax.ppermute(
            x, "pairs", [(i, (i + (1 if i % 2 else -1)) % columns) for i in range(columns)]
        )

    def swap(x, by):
        return lax.ppermute(x, "role", [(i, i ^ by) for i in range(roles)])

    weights = 2 * pairs
    own_weights = ROLE_PAIR + roles

    def plan_body(
        owner_hbm, occ_hbm, partner_hbm, coupling_hbm, eps_hbm, nvirt_hbm, coeff_hbm,
        mine_ref, extra_ref, to_inner, to_outer, nums,
        owner_ref, occ_ref, partner_ref, coupling_ref, eps_ref, nvirt_ref, near_w, sems,
    ):
        small = [
            pltpu.make_async_copy(source, target, sems.at[at])
            for at, (source, target) in enumerate(
                (
                    (owner_hbm, owner_ref),
                    (occ_hbm, occ_ref),
                    (partner_hbm, partner_ref),
                    (coupling_hbm, coupling_ref),
                    (eps_hbm, eps_ref),
                    (nvirt_hbm, nvirt_ref),
                )
            )
        ]
        for copy in small:
            copy.start()
        role = lax.axis_index("role")
        column = lax.axis_index("pairs")
        small[0].wait()
        of_role = [jnp.int32(0)] * roles
        for p in range(pairs):
            earlier = jnp.int32(0)
            for o in range(p):
                earlier += (owner_ref[o] == owner_ref[p]).astype(I32)
            for s in range(roles):
                hit = (earlier == 0) & (owner_ref[p] == s) if s else earlier == 1
                of_role[s] = jnp.where(hit, p, of_role[s])
        extra = of_role[0]
        mine = extra
        for s in range(1, roles):
            mine = jnp.where(role == s, of_role[s], mine)
        large = [
            pltpu.make_async_copy(coeff_hbm.at[mine], mine_ref, sems.at[6]),
            pltpu.make_async_copy(coeff_hbm.at[extra], extra_ref, sems.at[7]),
        ]
        for copy in large:
            copy.start()
        for copy in small[1:]:
            copy.wait()
        nums[MINE] = mine.astype(F32)
        nums[EXTRA] = extra.astype(F32)
        nums[OWNER] = owner_ref[extra].astype(F32)
        for s in range(roles):
            nums[ROLE_PAIR + s] = of_role[s].astype(F32)
        nums[NV_MINE] = nvirt_ref[mine].astype(F32)
        nums[NV_EXTRA] = nvirt_ref[extra].astype(F32)
        nums[FIRST] = (occ_ref[0, mine] - column * occ_block).astype(F32)
        odd = lax.rem(column, 2) == 1
        inner_at = jnp.where(odd, 0, 2)
        outer_at = 2 - inner_at
        occ_all = occ_block * columns
        second = lax.rem(occ_ref[1, mine] - (column - 1) * occ_block + occ_all, occ_all)
        block = (second >= occ_block).astype(I32) + (second >= 2 * occ_block).astype(I32)
        place = (second - block * occ_block).astype(F32)
        nums[SECOND] = place
        to_inner[weights] = place
        to_outer[weights] = place
        nums[WHOSE] = jnp.where(block == 1, 0, jnp.where(block == inner_at, 1, 2)).astype(F32)
        nums[OCC_MINE] = eps_ref[occ_ref[0, mine]] + eps_ref[occ_ref[1, mine]]
        nums[OCC_EXTRA] = eps_ref[occ_ref[0, extra]] + eps_ref[occ_ref[1, extra]]
        pair_all = pairs * columns
        for which, pair in enumerate((mine, extra)):
            for q in range(3 * pairs):
                near_w[q] = jnp.float32(0)
            for k in range(partner_count):
                at = lax.rem(partner_ref[pair, k] - (column - 1) * pairs + pair_all, pair_all)
                near_w[at] += coupling_ref[pair, k]
            for q in range(pairs):
                to = which * pairs + q
                to_inner[to] = near_w[inner_at * pairs + q]
                nums[own_weights + to] = near_w[pairs + q]
                to_outer[to] = near_w[outer_at * pairs + q]
        for copy in large:
            copy.wait()

    meta = (SMEM, (weights + 1,), F32)
    x_mine, x_extra, to_inner, to_outer, nums = call(
        plan_body,
        [HBM] * 7,
        [orb, orb, meta, meta, (SMEM, (own_weights + weights,), F32)],
        (pair_owner, pair_occ.T, partners, coupling, eps_occ, nvirt, coeff),
        scratch=[
            pltpu.SMEM(pair_owner.shape, I32),
            pltpu.SMEM(pair_occ.shape[::-1], I32),
            pltpu.SMEM(partners.shape, I32),
            pltpu.SMEM(coupling.shape, F32),
            pltpu.SMEM(eps_occ.shape, F32),
            pltpu.SMEM(nvirt.shape, I32),
            pltpu.SMEM((3 * pairs,), F32),
            pltpu.SemaphoreType.DMA((8,)),
        ],
        vmem=60,
    )
    x_out = outer(x_mine)
    of_out = outer(to_outer)

    def place_of(at):
        return pl.ds(at * virt if isinstance(at, int) else pl.multiple_of(at * virt, virt), virt)

    def overlaps(x, coeff_ref, out_ref):
        turned = x.T
        for q in range(pairs):
            s = mxu(turned, coeff_ref[q], NN) * (1.0 / pao)
            out_ref[:, place_of(q)] = s.astype(BF16)

    def coupled(s_ref, middle_ref, parts):
        for at, weight, amp in parts:
            u = weight * mxu(s_ref[:, place_of(at)], amp, NN)
            middle_ref[:, place_of(at)] = u.astype(BF16)
        return mxu(middle_ref[...], s_ref[...], NT)

    def half_into(y_ref, three_ref, at_occ, x):
        for at in range(0, aux, tile):
            rows = pl.ds(at, tile)
            y_ref[rows, :] = (mxu(three_ref[at_occ, rows, :], x, NN) * pao_scale).astype(BF16)

    def own_half_body(
        nums, to_inner, three_ref, mine_ref, extra_ref, first_ref, second_ref, both_ref, inner_ref
    ):
        x = mine_ref[...]
        both_ref[0] = x
        both_ref[1] = extra_ref[...]
        for at in range(weights + 1):
            inner_ref[at] = to_inner[at]
        turned = x.T
        first = whole(nums[FIRST])
        for at in range(0, aux, tile):
            rows = pl.ds(at, tile)
            first_ref[:, rows] = (mxu(turned, three_ref[first, rows, :], NT) * pao_scale).astype(BF16)
        half_into(second_ref, three_ref, whole(nums[SECOND]), x)

    first_t, second_own, x_both, to_inner = call(
        own_half_body,
        [SMEM, SMEM, VMEM, VMEM, VMEM],
        [(VMEM, (virt, aux), BF16), half, (VMEM, (2, pao, virt), BF16), meta],
        (nums, to_inner, three_index, x_mine, x_extra),
        flops=4 * virt * aux * pao,
    )
    def outer_half_body(of, three_ref, x_ref, own_ref, y_ref):
        half_into(y_ref, three_ref, whole(of[weights]), x_ref[...])

    (y_out,) = call(
        outer_half_body,
        [SMEM, VMEM, VMEM, ANY],
        [half],
        (of_out, three_index, x_out, first_t),
        flops=2 * aux * pao * virt,
    )
    y_from_out = outer(y_out)
    def outer_body(of, coeff_ref, amps_ref, x_ref, after_ref, s_ref, c_ref, middle_ref):
        overlaps(x_ref[...], coeff_ref, s_ref)
        c = coupled(s_ref, middle_ref, [(q, of[q], amps_ref[q]) for q in range(pairs)])
        c_ref[...] = c.astype(BF16)

    s_out, c_out = call(
        outer_body,
        [SMEM, VMEM, VMEM, VMEM, ANY],
        [all_s, sq_b],
        (of_out, coeff, amps, x_out, y_out),
        scratch=[middle],
        flops=2 * pairs * virt * virt * (pao + 2 * virt),
    )
    c_from_out = outer(c_out)
    x_later, x_both, to_inner, _ = lax.optimization_barrier((x_extra, x_both, to_inner, c_out))
    x_extra_out = outer(x_later)
    x_in = inner(x_both)
    of_in = inner(to_inner)

    def inner_body(
        of, three_ref, coeff_ref, amps_ref, x_ref, after_ref, y_ref, s_ref, se_ref, c_ref, middle_ref
    ):
        half_into(y_ref, three_ref, whole(of[weights]), x_ref[0])
        overlaps(x_ref[0], coeff_ref, s_ref)
        c = coupled(s_ref, middle_ref, [(q, of[q], amps_ref[q]) for q in range(pairs)])
        c_ref[...] = c.astype(BF16)
        overlaps(x_ref[1], coeff_ref, se_ref)

    y_in, s_in, se_in, c_in = call(
        inner_body,
        [SMEM] + [VMEM] * 4 + [ANY],
        [half, all_s, all_s, sq_b],
        (of_in, three_index, coeff, amps, x_in, c_out),
        scratch=[middle],
        flops=2 * virt * (aux * pao + pairs * virt * (2 * pao + 2 * virt)),
    )
    y_from_in = inner(y_in)
    c_from_in = inner(c_in)

    def own_body(
        nums, coeff_ref, amps_ref, eps_ref, after_ref,
        s_ref, se_ref, c_ref, gain_ref, gain_extra_ref, middle_ref,
    ):
        mine, extra = whole(nums[MINE]), whole(nums[EXTRA])
        overlaps(coeff_ref[mine], coeff_ref, s_ref)
        c_ref[...] = coupled(
            s_ref, middle_ref, [(q, nums[own_weights + q], amps_ref[q]) for q in range(pairs)]
        )
        overlaps(coeff_ref[extra], coeff_ref, se_ref)

        def gain(pair, count, occupied):
            row = jnp.broadcast_to(eps_ref[pl.ds(pair, 1), :], square)
            energy = row + row.T - occupied
            inside = (lax.broadcasted_iota(I32, square, 0) < count) & (
                lax.broadcasted_iota(I32, square, 1) < count
            )
            return jnp.where(inside, 1.0 / (energy + 1.0), 0.0)

        gain_ref[...] = gain(mine, whole(nums[NV_MINE]), nums[OCC_MINE])
        gain_extra_ref[...] = gain(extra, whole(nums[NV_EXTRA]), nums[OCC_EXTRA])

    s_own, se_own, c_own, gain, gain_extra = call(
        own_body,
        [SMEM, VMEM, VMEM, VMEM, ANY],
        [all_s, all_s, sq_f, sq_f, sq_f],
        (nums, coeff, amps, eps_virt, c_out),
        scratch=[middle],
        flops=2 * pairs * virt * virt * (2 * pao + 2 * virt),
    )

    def first_body(
        nums, first_ref, own_ref, in_ref, out_ref, amps_ref, c_ref, ci_ref, co_ref, gain_ref,
        amp_ref, k_ref, held, sem,
    ):
        for whose, source in enumerate((own_ref, in_ref, out_ref)):

            @pl.when(whole(nums[WHOSE]) == whose)
            def _():
                copy = pltpu.make_async_copy(source, held, sem)
                copy.start()
                copy.wait()

        k = mxu(first_ref[...], held[...], NN) * aux_scale
        k_ref[...] = k
        c = c_ref[...] + ci_ref[...].astype(F32) + co_ref[...].astype(F32)
        old = amps_ref[whole(nums[MINE])].astype(F32)
        amp_ref[...] = (gain_ref[...] * (old - k - c)).astype(BF16)

    amp, k_first = call(
        first_body,
        [SMEM, VMEM, ANY, ANY, ANY, VMEM, VMEM, VMEM, VMEM, VMEM],
        [sq_b, sq_f],
        (
            nums, first_t, second_own, y_from_in, y_from_out,
            amps, c_own, c_from_in, c_from_out, gain,
        ),
        scratch=[pltpu.VMEM((aux, virt), BF16), pltpu.SemaphoreType.DMA],
        flops=2 * aux * virt * virt,
    )
    amp_roles = [amp] + [swap(amp, m) for m in range(1, roles)]

    def second_body(amp_ref, k_ref, out_ref, out_b_ref):
        amp = amp_ref[...]
        k = k_ref[...]
        right = k + mxu(k.astype(BF16), amp, NN) * virt_scale
        both = right + mxu(amp.T, right.astype(BF16), NN) * virt_scale
        rest = amp.astype(F32) - both
        out_ref[...] = rest
        out_b_ref[...] = rest.astype(BF16)

    rest, rest_b = call(
        second_body, [VMEM, VMEM], [sq_f, sq_b], (amp, k_first), flops=4 * virt * virt * virt
    )
    rests = [lax.ppermute(rest_b, "role", [(0, s)]) for s in range(1, roles)]

    def outer_extra_body(coeff_ref, x_ref, after_ref, s_ref):
        overlaps(x_ref[...], coeff_ref, s_ref)

    (se_out,) = call(
        outer_extra_body,
        [VMEM, VMEM, ANY],
        [all_s],
        (coeff, x_extra_out, rest),
        flops=2 * pairs * virt * virt * pao,
    )

    def parts_of(nums, weight_ref, first_weight, amp_refs):
        role = lax.axis_index("role")
        parts = []
        for m in range(roles):
            at = whole(nums[ROLE_PAIR + (role ^ m)])
            parts.append((at, weight_ref[first_weight + at], amp_refs[m][...]))
        return parts

    def near_again_body(nums, of, s_ref, se_ref, *refs):
        amp_refs, (c_ref, middle_ref, middle_e_ref) = refs[:roles], refs[-3:]
        c = coupled(s_ref, middle_ref, parts_of(nums, of, 0, amp_refs))
        c_ref[0] = c.astype(BF16)
        c = coupled(se_ref, middle_e_ref, parts_of(nums, of, pairs, amp_refs))
        c_ref[1] = c.astype(BF16)

    def near_again(of, s, se, after=()):
        (c,) = call(
            near_again_body,
            [SMEM, SMEM] + [VMEM] * (2 + roles) + [ANY] * len(after),
            [two_b],
            (nums, of, s, se, *amp_roles, *after),
            scratch=[middle, middle],
            flops=8 * pairs * virt * virt * virt,
        )
        return c

    cc_from_out = outer(near_again(of_out, s_out, se_out))
    cc_from_in = inner(near_again(of_in, s_in, se_in, rests))

    def own_again_body(nums, s_ref, se_ref, rest_ref, *refs):
        amp_refs, rest_refs = refs[:roles], refs[roles : 2 * roles - 1]
        out_ref, out_extra_ref, middle_ref, middle_e_ref = refs[2 * roles - 1 :]
        parts = parts_of(nums, nums, own_weights, amp_refs)
        out_ref[...] = rest_ref[...] - coupled(s_ref, middle_ref, parts)
        role = lax.axis_index("role")
        parts = parts_of(nums, nums, own_weights + pairs, amp_refs)
        total = -coupled(se_ref, middle_e_ref, parts)
        for s in range(1, roles):
            total += jnp.where(role == s, rest_refs[s - 1][...].astype(F32), 0.0)
        out_extra_ref[...] = total

    rest, rest_extra = call(
        own_again_body,
        [SMEM] + [VMEM] * (3 + 2 * roles - 1),
        [sq_f, sq_f],
        (nums, s_own, se_own, rest, *amp_roles, *rests),
        scratch=[middle, middle],
        flops=8 * pairs * virt * virt * virt,
    )

    def last_body(
        nums, coeff_ref, gain_ref, gain_extra_ref, rest_ref, rest_extra_ref, ci_ref, co_ref, amp_ref, orb_ref
    ):
        role = lax.axis_index("role")

        def store(slot, here, gain, rest, pair):
            @pl.when(here)
            def _():
                c = ci_ref[slot].astype(F32) + co_ref[slot].astype(F32)
                amp = (gain[...] * (rest[...] - c)).astype(BF16)
                amp_ref[slot] = amp
                x = coeff_ref[pair]
                orb_ref[slot] = (x.astype(F32) + mxu(x, amp, NN) * virt_scale).astype(BF16)

            @pl.when(jnp.logical_not(here))
            def _():
                amp_ref[slot] = jnp.zeros(square, BF16)
                orb_ref[slot] = jnp.zeros((pao, virt), BF16)

        store(0, role > 0, gain_ref, rest_ref, whole(nums[MINE]))
        store(1, role == whole(nums[OWNER]), gain_extra_ref, rest_extra_ref, whole(nums[EXTRA]))

    amps_out, dressed_out = call(
        last_body,
        [SMEM] + [VMEM] * 7,
        [(VMEM, (slots, virt, virt), BF16), (VMEM, (slots, pao, virt), BF16)],
        (nums, coeff, gain, gain_extra, rest, rest_extra, cc_from_in, cc_from_out),
        flops=4 * pao * virt * virt,
    )
    return amps_out, dressed_out


def solution(mesh):
    in_specs = (
        P("pairs", None, None),
        P("pairs", None, None),
        P("pairs", None, None),
        P("pairs", None),
        P(),
        P("pairs"),
        P("pairs", None),
        P("pairs", None),
        P("pairs", None),
        P("pairs"),
    )
    out_specs = (P(("role", "pairs"), None, None), P(("role", "pairs"), None, None))
    return jax.shard_map(local, mesh=mesh, in_specs=in_specs, out_specs=out_specs, check_vma=False)
```

```python
import math

import jax
import jax.numpy as jnp
from jax import lax
from jax.experimental import pallas as pl
from jax.experimental.pallas import tpu as pltpu
from jax.sharding import PartitionSpec as P

F32 = jnp.float32
BF16 = jnp.bfloat16
I32 = jnp.int32
NN = ((1,), (0,))
NT = ((1,), (1,))

VMEM = pl.BlockSpec(memory_space=pltpu.VMEM)
SMEM = pl.BlockSpec(memory_space=pltpu.SMEM)
ANY = pl.BlockSpec(memory_space=pl.ANY)
HBM = pl.BlockSpec(memory_space=pltpu.HBM)

MINE, EXTRA, OWNER, FIRST, SECOND, WHOSE, NV_MINE, NV_EXTRA, OCC_MINE, OCC_EXTRA, ROLE_PAIR = range(11)


def whole(number):
    return number.astype(jnp.int32)


def mxu(a, b, dims):
    return lax.dot_general(a, b, (dims, ((), ())), preferred_element_type=F32)


def call(body, ins, outs, args, scratch=(), vmem=48):
    return pl.pallas_call(
        body,
        in_specs=ins,
        out_specs=[spec for spec, _, _ in outs],
        out_shape=[jax.ShapeDtypeStruct(shape, dtype) for _, shape, dtype in outs],
        scratch_shapes=list(scratch),
        cost_estimate=pl.CostEstimate(flops=1, bytes_accessed=1, transcendentals=0),
        compiler_params=pltpu.CompilerParams(vmem_limit_bytes=vmem * 1024 * 1024),
    )(*args)


def local(
    three_index, coeff, amps, eps_virt, eps_occ, nvirt, pair_occ, partners, coupling, pair_owner
):
    columns = lax.axis_size("pairs")
    roles = lax.axis_size("role")
    occ_block, aux, pao = three_index.shape
    pairs, _, virt = coeff.shape
    partner_count = partners.shape[1]
    slots = 2
    assert roles == pairs and columns % 2 == 0 and virt % 2 == 0
    tile = min(256, aux)
    pao_scale = 1.0 / math.sqrt(pao)
    aux_scale = 1.0 / math.sqrt(aux)
    virt_scale = 1.0 / math.sqrt(virt)
    square = (virt, virt)
    part = virt // 2
    sq_b = (VMEM, square, BF16)
    sq_f = (VMEM, square, F32)
    two_b = (VMEM, (2, virt, virt), BF16)
    all_s = (VMEM, (pairs, virt, virt), BF16)
    half = (VMEM, (aux, virt), BF16)

    inner_of = [i ^ 1 for i in range(columns)]
    outer_of = [(i + (1 if i % 2 else -1)) % columns for i in range(columns)]

    def inner(x):
        return lax.ppermute(x, "pairs", list(enumerate(inner_of)))

    def outer(x):
        return lax.ppermute(x, "pairs", list(enumerate(outer_of)))

    def owners(x, other):
        pairings = [
            (s * columns + i, s * columns + j) for s in range(1, roles) for i, j in enumerate(other)
        ]
        return lax.ppermute(x, ("role", "pairs"), pairings)

    def swap(x, by):
        return lax.ppermute(x, "role", [(i, i ^ by) for i in range(roles) if i ^ by])

    def pairs_of_roles(owner_ref):
        of_role = [jnp.int32(0)] * roles
        for p in range(pairs):
            earlier = jnp.int32(0)
            for o in range(p):
                earlier += (owner_ref[o] == owner_ref[p]).astype(I32)
            for s in range(roles):
                hit = (earlier == 0) & (owner_ref[p] == s) if s else earlier == 1
                of_role[s] = jnp.where(hit, p, of_role[s])
        return of_role

    def pick(numbers, at):
        chosen = numbers[0]
        for s in range(1, len(numbers)):
            chosen = jnp.where(at == s, numbers[s], chosen)
        return chosen

    weights = 2 * pairs
    riders = 16
    own_weights = ROLE_PAIR + roles

    def plan_body(
        owner_hbm, occ_hbm, partner_hbm, coupling_hbm, eps_hbm, nvirt_hbm, coeff_hbm,
        low_ref, high_ref, nums,
        owner_ref, occ_ref, partner_ref, coupling_ref, eps_ref, nvirt_ref, near_w, sems,
    ):
        small = [
            pltpu.make_async_copy(source, target, sems.at[at])
            for at, (source, target) in enumerate(
                (
                    (owner_hbm, owner_ref),
                    (occ_hbm, occ_ref),
                    (partner_hbm, partner_ref),
                    (coupling_hbm, coupling_ref),
                    (eps_hbm, eps_ref),
                    (nvirt_hbm, nvirt_ref),
                )
            )
        ]
        for copy in small:
            copy.start()
        role = lax.axis_index("role")
        column = lax.axis_index("pairs")
        small[0].wait()
        of_role = pairs_of_roles(owner_ref)
        extra = of_role[0]
        mine = pick(of_role, role)
        large = [
            pltpu.make_async_copy(coeff_hbm.at[mine, :, pl.ds(0, part)], low_ref.at[pl.ds(0, pao)], sems.at[6]),
            pltpu.make_async_copy(coeff_hbm.at[mine, :, pl.ds(part, part)], high_ref, sems.at[7]),
        ]
        for copy in large:
            copy.start()
        for copy in small[1:]:
            copy.wait()
        nums[MINE] = mine.astype(F32)
        nums[EXTRA] = extra.astype(F32)
        nums[OWNER] = owner_ref[extra].astype(F32)
        for s in range(roles):
            nums[ROLE_PAIR + s] = of_role[s].astype(F32)
        nums[NV_MINE] = nvirt_ref[mine].astype(F32)
        nums[NV_EXTRA] = nvirt_ref[extra].astype(F32)
        nums[FIRST] = (occ_ref[0, mine] - column * occ_block).astype(F32)
        odd = lax.rem(column, 2) == 1
        inner_at = jnp.where(odd, 0, 2)
        outer_at = 2 - inner_at
        occ_all = occ_block * columns
        second = lax.rem(occ_ref[1, mine] - (column - 1) * occ_block + occ_all, occ_all)
        block = (second >= occ_block).astype(I32) + (second >= 2 * occ_block).astype(I32)
        place = (second - block * occ_block).astype(F32)
        nums[SECOND] = place
        lane = lax.broadcasted_iota(I32, (riders, part), 1)
        row = lax.broadcasted_iota(I32, (riders, part), 0)
        told = jnp.where(lane == weights, place, 0.0)
        nums[WHOSE] = jnp.where(block == 1, 0, jnp.where(block == inner_at, 1, 2)).astype(F32)
        nums[OCC_MINE] = eps_ref[occ_ref[0, mine]] + eps_ref[occ_ref[1, mine]]
        nums[OCC_EXTRA] = eps_ref[occ_ref[0, extra]] + eps_ref[occ_ref[1, extra]]
        pair_all = pairs * columns
        for which, pair in enumerate((mine, extra)):
            for q in range(3 * pairs):
                near_w[q] = jnp.float32(0)
            for k in range(partner_count):
                at = lax.rem(partner_ref[pair, k] - (column - 1) * pairs + pair_all, pair_all)
                near_w[at] += coupling_ref[pair, k]
            for q in range(pairs):
                to = which * pairs + q
                nums[own_weights + 2 * which * pairs + q] = near_w[pairs + q]
                nums[own_weights + (2 * which + 1) * pairs + q] = near_w[inner_at * pairs + q]
                told = jnp.where(lane == to, near_w[outer_at * pairs + q], told)
        coarse = told.astype(BF16).astype(F32)
        middle = (told - coarse).astype(BF16).astype(F32)
        fine = told - coarse - middle
        told = jnp.where(row == 0, coarse, jnp.where(row == 1, middle, jnp.where(row == 2, fine, 0.0)))
        low_ref[pao:, :] = told.astype(BF16)
        for copy in large:
            copy.wait()

    rode = (VMEM, (pao + riders, part), BF16)
    x_low, x_high, nums = call(
        plan_body,
        [HBM] * 7,
        [rode, (VMEM, (pao, part), BF16), (SMEM, (own_weights + 2 * weights,), F32)],
        (pair_owner, pair_occ.T, partners, coupling, eps_occ, nvirt, coeff),
        scratch=[
            pltpu.SMEM(pair_owner.shape, I32),
            pltpu.SMEM(pair_occ.shape[::-1], I32),
            pltpu.SMEM(partners.shape, I32),
            pltpu.SMEM(coupling.shape, F32),
            pltpu.SMEM(eps_occ.shape, F32),
            pltpu.SMEM(nvirt.shape, I32),
            pltpu.SMEM((3 * pairs,), F32),
            pltpu.SemaphoreType.DMA((8,)),
        ],
        vmem=60,
    )
    low_out, high_out = outer(x_low), outer(x_high)

    def told_of(low_ref):
        rows = low_ref[pao:, :].astype(F32)
        return rows[0:1] + rows[1:2] + rows[2:3]

    def overlaps(x, coeff_ref, out_ref):
        turned = x.T
        for q in range(pairs):
            s = mxu(turned, coeff_ref[q], NN) * (1.0 / pao)
            out_ref[q] = s.astype(BF16)

    def coupled(s_ref, parts):
        total = None
        for at, weight, amp in parts:
            s = s_ref[at]
            u = mxu(s, amp, NN).astype(BF16)
            term = weight * mxu(u, s, NT)
            total = term if total is None else total + term
        return total

    def half_into(y_ref, three_ref, at_occ, x):
        for at in range(0, aux, tile):
            rows = pl.ds(at, tile)
            y_ref[rows, :] = (mxu(three_ref[at_occ, rows, :], x, NN) * pao_scale).astype(BF16)

    def outer_low_body(three_ref, x_ref, y_ref):
        half_into(y_ref, three_ref, whole(told_of(x_ref)[0, weights]), x_ref[:pao, :])
        y_ref[aux:, :] = jnp.zeros((2 * riders, part), BF16)

    (y_low,) = call(
        outer_low_body,
        [VMEM, VMEM],
        [(VMEM, (aux + 2 * riders, part), BF16)],
        (three_index, low_out),
    )
    y_low_from_out = outer(y_low)

    def outer_high_body(three_ref, low_ref, x_ref, after_ref, y_ref):
        half_into(y_ref, three_ref, whole(told_of(low_ref)[0, weights]), x_ref[...])
        y_ref[aux:, :] = jnp.zeros((riders, part), BF16)

    (y_high,) = call(
        outer_high_body,
        [VMEM, VMEM, VMEM, ANY],
        [(VMEM, (aux + riders, part), BF16)],
        (three_index, low_out, high_out, y_low),
    )
    y_high_from_out = outer(y_high)

    *sent, _ = lax.optimization_barrier((three_index, coeff, amps, pair_owner, y_high))
    three_in, coeff_in, amps_in, owner_in = [inner(x) for x in sent]

    def outer_body(coeff_ref, amps_ref, low_ref, high_ref, after_ref, s_ref, c_ref, x_ref):
        x_ref[:, :part] = low_ref[:pao, :]
        x_ref[:, part:] = high_ref[...]
        overlaps(x_ref[...], coeff_ref, s_ref)
        told = told_of(low_ref)
        c = coupled(s_ref, [(q, told[0, q], amps_ref[q]) for q in range(pairs)])
        c_ref[...] = c.astype(BF16)

    s_out, c_out = call(
        outer_body,
        [VMEM, VMEM, VMEM, VMEM, ANY],
        [all_s, sq_b],
        (coeff, amps, low_out, high_out, y_high),
        scratch=[pltpu.VMEM((pao, virt), BF16)],
    )
    c_from_out = outer(c_out)

    def own_half_body(
        nums, three_ref, three_in_ref, coeff_ref, after_ref, first_ref, second_ref, extra_ref
    ):
        x = coeff_ref[whole(nums[MINE])]
        extra_ref[...] = coeff_ref[whole(nums[EXTRA])]
        turned = x.T
        first = whole(nums[FIRST])
        for at in range(0, aux, tile):
            rows = pl.ds(at, tile)
            first_ref[:, rows] = (mxu(turned, three_ref[first, rows, :], NT) * pao_scale).astype(BF16)
        for whose, source in enumerate((three_ref, three_in_ref)):

            @pl.when(whole(nums[WHOSE]) == whose)
            def _():
                half_into(second_ref, source, whole(nums[SECOND]), x)

    first_t, second, x_extra = call(
        own_half_body,
        [SMEM, VMEM, VMEM, VMEM, ANY],
        [(VMEM, (virt, aux), BF16), (VMEM, (aux, virt), BF16), (VMEM, (pao, virt), BF16)],
        (nums, three_index, three_in, coeff, c_out),
    )
    x_extra_out = outer(x_extra)

    def own_body(
        nums, coeff_ref, coeff_in_ref, amps_ref, amps_in_ref, eps_ref, after_ref,
        s_ref, s_in_ref, c_ref, gain_ref, gain_extra_ref,
    ):
        mine, extra = whole(nums[MINE]), whole(nums[EXTRA])
        x = coeff_ref[mine]
        total = None
        for at, of_s, of_coeff, of_amps in (
            (own_weights, s_ref, coeff_ref, amps_ref),
            (own_weights + pairs, s_in_ref, coeff_in_ref, amps_in_ref),
        ):
            overlaps(x, of_coeff, of_s)
            c = coupled(of_s, [(q, nums[at + q], of_amps[q]) for q in range(pairs)])
            total = c if total is None else total + c
        c_ref[...] = total

        def gain(pair, count, occupied):
            row = jnp.broadcast_to(eps_ref[pl.ds(pair, 1), :], square)
            energy = row + row.T - occupied
            inside = (lax.broadcasted_iota(I32, square, 0) < count) & (
                lax.broadcasted_iota(I32, square, 1) < count
            )
            return jnp.where(inside, 1.0 / (energy + 1.0), 0.0)

        gain_ref[...] = gain(mine, whole(nums[NV_MINE]), nums[OCC_MINE])
        gain_extra_ref[...] = gain(extra, whole(nums[NV_EXTRA]), nums[OCC_EXTRA])

    s_own, s_in, c_own, gain, gain_extra = call(
        own_body,
        [SMEM] + [VMEM] * 5 + [ANY],
        [all_s, all_s, sq_f, sq_f, sq_f],
        (nums, coeff, coeff_in, amps, amps_in, eps_virt, first_t),
    )

    def first_body(
        nums, first_ref, second_ref, low_ref, high_ref, amps_ref, c_ref, co_ref, gain_ref, amp_ref, k_ref
    ):
        first = first_ref[...]
        outside = whole(nums[WHOSE]) == 2

        @pl.when(outside)
        def _():
            k_ref[:, :part] = mxu(first, low_ref[:aux, :], NN) * aux_scale
            k_ref[:, part:] = mxu(first, high_ref[:aux, :], NN) * aux_scale

        @pl.when(jnp.logical_not(outside))
        def _():
            k_ref[...] = mxu(first, second_ref[...], NN) * aux_scale

        old = amps_ref[whole(nums[MINE])].astype(F32)
        c = c_ref[...] + co_ref[...].astype(F32)
        amp_ref[...] = (gain_ref[...] * (old - k_ref[...] - c)).astype(BF16)

    amp, k_first = call(
        first_body,
        [SMEM] + [VMEM] * 8,
        [sq_b, sq_f],
        (nums, first_t, second, y_low_from_out, y_high_from_out, amps, c_own, c_from_out, gain),
    )
    amp_roles = [amp] + [swap(amp, m) for m in range(1, roles)]

    def second_body(amp_ref, k_ref, out_ref, out_b_ref):
        amp = amp_ref[...]
        k = k_ref[...]
        right = k + mxu(k.astype(BF16), amp, NN) * virt_scale
        both = right + mxu(amp.T, right.astype(BF16), NN) * virt_scale
        rest = amp.astype(F32) - both
        out_ref[...] = rest
        out_b_ref[...] = rest.astype(BF16)

    rest, rest_b = call(
        second_body, [VMEM, VMEM], [sq_f, sq_b], (amp, k_first)
    )
    rests = [lax.ppermute(rest_b, "role", [(0, s)]) for s in range(1, roles)]

    def extra_body(nums, coeff_ref, in_ref, out_ref, after_ref, own_s_ref, in_s_ref, out_s_ref):
        overlaps(out_ref[...], coeff_ref, out_s_ref)
        x = coeff_ref[whole(nums[EXTRA])]
        overlaps(x, coeff_ref, own_s_ref)
        overlaps(x, in_ref, in_s_ref)

    se_own, se_in, se_out = call(
        extra_body,
        [SMEM, VMEM, VMEM, VMEM, ANY],
        [all_s, all_s, all_s],
        (nums, coeff, coeff_in, x_extra_out, rest),
    )

    def outer_again_body(nums, low_ref, s_ref, se_ref, *refs):
        amp_refs, c_ref = refs[:roles], refs[-1]
        role = lax.axis_index("role")

        @pl.when(role > 0)
        def _():
            told = told_of(low_ref)
            for slot, of_s in enumerate((s_ref, se_ref)):
                parts = []
                for m in range(roles):
                    at = whole(nums[ROLE_PAIR + (role ^ m)])
                    weight = pick([told[:, slot * pairs + q : slot * pairs + q + 1] for q in range(pairs)], at)
                    parts.append((at, weight, amp_refs[m][...]))
                c_ref[slot] = coupled(of_s, parts).astype(BF16)

    (cc_out,) = call(
        outer_again_body,
        [SMEM] + [VMEM] * (3 + roles),
        [two_b],
        (nums, low_out, s_out, se_out, *amp_roles),
    )
    cc_from_out = owners(cc_out, outer_of)

    later = lax.optimization_barrier((*amp_roles, cc_out))[:roles]
    amp_roles_in = [owners(x, inner_of) for x in later]

    def own_again_body(nums, owner_in, rest_ref, s_ref, s_in_ref, se_ref, se_in_ref, *refs):
        amp_refs, amp_in_refs, rest_refs = refs[:roles], refs[roles : 2 * roles], refs[2 * roles : -2]
        out_ref, out_extra_ref = refs[-2:]
        role = lax.axis_index("role")

        @pl.when(role > 0)
        def _():
            of_role = [whole(nums[ROLE_PAIR + s]) for s in range(roles)]
            of_role_in = pairs_of_roles(owner_in)
            totals = []
            for slot, of_s, of_s_in in ((0, s_ref, s_in_ref), (1, se_ref, se_in_ref)):
                total = None
                for at_w, of, pair_of, amp_of in (
                    (own_weights + 2 * slot * pairs, of_s, of_role, amp_refs),
                    (own_weights + (2 * slot + 1) * pairs, of_s_in, of_role_in, amp_in_refs),
                ):
                    parts = []
                    for m in range(roles):
                        at = pick(pair_of, role ^ m)
                        parts.append((at, nums[at_w + at], amp_of[m][...]))
                    c = coupled(of, parts)
                    total = c if total is None else total + c
                totals.append(total)
            out_ref[...] = rest_ref[...] - totals[0]
            total = -totals[1]
            for s in range(1, roles):
                total += jnp.where(role == s, rest_refs[s - 1][...].astype(F32), 0.0)
            out_extra_ref[...] = total

    rest, rest_extra = call(
        own_again_body,
        [SMEM] * 2 + [VMEM] * (5 + 3 * roles - 1),
        [sq_f, sq_f],
        (nums, owner_in, rest, s_own, s_in, se_own, se_in, *amp_roles, *amp_roles_in, *rests),
    )

    def last_body(
        nums, coeff_ref, gain_ref, gain_extra_ref, rest_ref, rest_extra_ref, c_ref, amp_ref, orb_ref
    ):
        role = lax.axis_index("role")

        def store(slot, here, gain, rest, pair):
            @pl.when(here)
            def _():
                amp = (gain[...] * (rest[...] - c_ref[slot].astype(F32))).astype(BF16)
                amp_ref[slot] = amp
                x = coeff_ref[pair]
                orb_ref[slot] = (x.astype(F32) + mxu(x, amp, NN) * virt_scale).astype(BF16)

            @pl.when(jnp.logical_not(here))
            def _():
                amp_ref[slot] = jnp.zeros(square, BF16)
                orb_ref[slot] = jnp.zeros((pao, virt), BF16)

        store(0, role > 0, gain_ref, rest_ref, whole(nums[MINE]))
        store(1, role == whole(nums[OWNER]), gain_extra_ref, rest_extra_ref, whole(nums[EXTRA]))

    amps_out, dressed_out = call(
        last_body,
        [SMEM] + [VMEM] * 6,
        [(VMEM, (slots, virt, virt), BF16), (VMEM, (slots, pao, virt), BF16)],
        (nums, coeff, gain, gain_extra, rest, rest_extra, cc_from_out),
    )
    return amps_out, dressed_out


def solution(mesh):
    in_specs = (
        P("pairs", None, None),
        P("pairs", None, None),
        P("pairs", None, None),
        P("pairs", None),
        P(),
        P("pairs"),
        P("pairs", None),
        P("pairs", None),
        P("pairs", None),
        P("pairs"),
    )
    out_specs = (P(("role", "pairs"), None, None), P(("role", "pairs"), None, None))
    return jax.shard_map(local, mesh=mesh, in_specs=in_specs, out_specs=out_specs, check_vma=False)
```

```python
import math

import jax
import jax.numpy as jnp
from jax import lax
from jax.experimental import pallas as pl
from jax.experimental.pallas import tpu as pltpu
from jax.sharding import PartitionSpec as P

F32 = jnp.float32
BF16 = jnp.bfloat16
I32 = jnp.int32
NN = ((1,), (0,))
NT = ((1,), (1,))

VMEM = pl.BlockSpec(memory_space=pltpu.VMEM)
SMEM = pl.BlockSpec(memory_space=pltpu.SMEM)
ANY = pl.BlockSpec(memory_space=pl.ANY)
HBM = pl.BlockSpec(memory_space=pltpu.HBM)

MINE, EXTRA, OWNER, FIRST, SECOND, WHOSE, NV_MINE, NV_EXTRA, OCC_MINE, OCC_EXTRA, ROLE_PAIR = range(11)


def whole(number):
    return number.astype(jnp.int32)


def mxu(a, b, dims):
    return lax.dot_general(a, b, (dims, ((), ())), preferred_element_type=F32)


def call(body, ins, outs, args, scratch=(), vmem=48):
    return pl.pallas_call(
        body,
        in_specs=ins,
        out_specs=[spec for spec, _, _ in outs],
        out_shape=[jax.ShapeDtypeStruct(shape, dtype) for _, shape, dtype in outs],
        scratch_shapes=list(scratch),
        cost_estimate=pl.CostEstimate(flops=1, bytes_accessed=1, transcendentals=0),
        compiler_params=pltpu.CompilerParams(vmem_limit_bytes=vmem * 1024 * 1024),
    )(*args)


def local(
    three_index, coeff, amps, eps_virt, eps_occ, nvirt, pair_occ, partners, coupling, pair_owner
):
    columns = lax.axis_size("pairs")
    roles = lax.axis_size("role")
    occ_block, aux, pao = three_index.shape
    pairs, _, virt = coeff.shape
    partner_count = partners.shape[1]
    slots = 2
    assert roles == pairs and columns % 2 == 0 and virt % 2 == 0
    tile = min(256, aux)
    pao_scale = 1.0 / math.sqrt(pao)
    aux_scale = 1.0 / math.sqrt(aux)
    virt_scale = 1.0 / math.sqrt(virt)
    square = (virt, virt)
    part = virt // 2
    sq_b = (VMEM, square, BF16)
    sq_f = (VMEM, square, F32)
    two_b = (VMEM, (2, virt, virt), BF16)
    all_s = (VMEM, (pairs, virt, virt), BF16)
    half = (VMEM, (aux, virt), BF16)

    inner_of = [i ^ 1 for i in range(columns)]
    outer_of = [(i + (1 if i % 2 else -1)) % columns for i in range(columns)]

    def inner(x):
        return lax.ppermute(x, "pairs", list(enumerate(inner_of)))

    def outer(x):
        return lax.ppermute(x, "pairs", list(enumerate(outer_of)))

    def swap(x, by):
        return lax.ppermute(x, "role", [(i, i ^ by) for i in range(roles)])

    three_in, coeff_in, amps_in = inner(three_index), inner(coeff), inner(amps)

    def pairs_of_roles(owner_ref):
        of_role = [jnp.int32(0)] * roles
        for p in range(pairs):
            earlier = jnp.int32(0)
            for o in range(p):
                earlier += (owner_ref[o] == owner_ref[p]).astype(I32)
            for s in range(roles):
                hit = (earlier == 0) & (owner_ref[p] == s) if s else earlier == 1
                of_role[s] = jnp.where(hit, p, of_role[s])
        return of_role

    def pick(numbers, at):
        chosen = numbers[0]
        for s in range(1, len(numbers)):
            chosen = jnp.where(at == s, numbers[s], chosen)
        return chosen

    weights = 2 * pairs
    riders = 16
    own_weights = ROLE_PAIR + roles

    def plan_body(
        owner_hbm, occ_hbm, partner_hbm, coupling_hbm, eps_hbm, nvirt_hbm, coeff_hbm,
        low_ref, high_ref, nums,
        owner_ref, occ_ref, partner_ref, coupling_ref, eps_ref, nvirt_ref, near_w, sems,
    ):
        small = [
            pltpu.make_async_copy(source, target, sems.at[at])
            for at, (source, target) in enumerate(
                (
                    (owner_hbm, owner_ref),
                    (occ_hbm, occ_ref),
                    (partner_hbm, partner_ref),
                    (coupling_hbm, coupling_ref),
                    (eps_hbm, eps_ref),
                    (nvirt_hbm, nvirt_ref),
                )
            )
        ]
        for copy in small:
            copy.start()
        role = lax.axis_index("role")
        column = lax.axis_index("pairs")
        small[0].wait()
        of_role = pairs_of_roles(owner_ref)
        extra = of_role[0]
        mine = pick(of_role, role)
        large = [
            pltpu.make_async_copy(coeff_hbm.at[mine, :, pl.ds(0, part)], low_ref.at[pl.ds(0, pao)], sems.at[6]),
            pltpu.make_async_copy(coeff_hbm.at[mine, :, pl.ds(part, part)], high_ref, sems.at[7]),
        ]
        for copy in large:
            copy.start()
        for copy in small[1:]:
            copy.wait()
        nums[MINE] = mine.astype(F32)
        nums[EXTRA] = extra.astype(F32)
        nums[OWNER] = owner_ref[extra].astype(F32)
        for s in range(roles):
            nums[ROLE_PAIR + s] = of_role[s].astype(F32)
        nums[NV_MINE] = nvirt_ref[mine].astype(F32)
        nums[NV_EXTRA] = nvirt_ref[extra].astype(F32)
        nums[FIRST] = (occ_ref[0, mine] - column * occ_block).astype(F32)
        odd = lax.rem(column, 2) == 1
        inner_at = jnp.where(odd, 0, 2)
        outer_at = 2 - inner_at
        occ_all = occ_block * columns
        second = lax.rem(occ_ref[1, mine] - (column - 1) * occ_block + occ_all, occ_all)
        block = (second >= occ_block).astype(I32) + (second >= 2 * occ_block).astype(I32)
        place = (second - block * occ_block).astype(F32)
        nums[SECOND] = place
        lane = lax.broadcasted_iota(I32, (riders, part), 1)
        row = lax.broadcasted_iota(I32, (riders, part), 0)
        told = jnp.where(lane == weights, place, 0.0)
        nums[WHOSE] = jnp.where(block == 1, 0, jnp.where(block == inner_at, 1, 2)).astype(F32)
        nums[OCC_MINE] = eps_ref[occ_ref[0, mine]] + eps_ref[occ_ref[1, mine]]
        nums[OCC_EXTRA] = eps_ref[occ_ref[0, extra]] + eps_ref[occ_ref[1, extra]]
        pair_all = pairs * columns
        for which, pair in enumerate((mine, extra)):
            for q in range(3 * pairs):
                near_w[q] = jnp.float32(0)
            for k in range(partner_count):
                at = lax.rem(partner_ref[pair, k] - (column - 1) * pairs + pair_all, pair_all)
                near_w[at] += coupling_ref[pair, k]
            for q in range(pairs):
                to = which * pairs + q
                nums[own_weights + 2 * which * pairs + q] = near_w[pairs + q]
                nums[own_weights + (2 * which + 1) * pairs + q] = near_w[inner_at * pairs + q]
                told = jnp.where(lane == to, near_w[outer_at * pairs + q], told)
        coarse = told.astype(BF16).astype(F32)
        middle = (told - coarse).astype(BF16).astype(F32)
        fine = told - coarse - middle
        told = jnp.where(row == 0, coarse, jnp.where(row == 1, middle, jnp.where(row == 2, fine, 0.0)))
        low_ref[pao:, :] = told.astype(BF16)
        for copy in large:
            copy.wait()

    rode = (VMEM, (pao + riders, part), BF16)
    x_low, x_high, nums = call(
        plan_body,
        [HBM] * 7,
        [rode, (VMEM, (pao, part), BF16), (SMEM, (own_weights + 2 * weights,), F32)],
        (pair_owner, pair_occ.T, partners, coupling, eps_occ, nvirt, coeff),
        scratch=[
            pltpu.SMEM(pair_owner.shape, I32),
            pltpu.SMEM(pair_occ.shape[::-1], I32),
            pltpu.SMEM(partners.shape, I32),
            pltpu.SMEM(coupling.shape, F32),
            pltpu.SMEM(eps_occ.shape, F32),
            pltpu.SMEM(nvirt.shape, I32),
            pltpu.SMEM((3 * pairs,), F32),
            pltpu.SemaphoreType.DMA((8,)),
        ],
        vmem=60,
    )
    low_out, high_out = outer(x_low), outer(x_high)

    def told_of(low_ref):
        rows = low_ref[pao:, :].astype(F32)
        return rows[0:1] + rows[1:2] + rows[2:3]

    def overlaps(x, coeff_ref, out_ref):
        turned = x.T
        for q in range(pairs):
            s = mxu(turned, coeff_ref[q], NN) * (1.0 / pao)
            out_ref[q] = s.astype(BF16)

    def coupled(s_ref, parts):
        total = None
        for at, weight, amp in parts:
            s = s_ref[at]
            u = mxu(s, amp, NN).astype(BF16)
            term = weight * mxu(u, s, NT)
            total = term if total is None else total + term
        return total

    block_scratch = [pltpu.VMEM((aux, pao), BF16), pltpu.SemaphoreType.DMA((aux // tile,))]

    def by_tiles(three_ref, at_occ, block_ref, sems, product):
        tiles = [pl.ds(at, tile) for at in range(0, aux, tile)]
        copies = [
            pltpu.make_async_copy(three_ref.at[at_occ, rows], block_ref.at[rows], sems.at[at])
            for at, rows in enumerate(tiles)
        ]
        for copy in copies:
            copy.start()
        for copy, rows in zip(copies, tiles):
            copy.wait()
            product(rows, block_ref[rows, :])

    def half_into(y_ref, x):
        def product(rows, block):
            y_ref[rows, :] = (mxu(block, x, NN) * pao_scale).astype(BF16)

        return product

    def own_first_body(nums, three_ref, coeff_ref, first_ref, extra_ref, x_ref, block_ref, sems, x_sems):
        copies = [
            pltpu.make_async_copy(coeff_ref.at[whole(nums[MINE])], x_ref, x_sems.at[0]),
            pltpu.make_async_copy(coeff_ref.at[whole(nums[EXTRA])], extra_ref, x_sems.at[1]),
        ]
        for copy in copies:
            copy.start()
        copies[0].wait()
        turned = x_ref[...].T

        def product(rows, block):
            first_ref[:, rows] = (mxu(turned, block, NT) * pao_scale).astype(BF16)

        by_tiles(three_ref, whole(nums[FIRST]), block_ref, sems, product)
        copies[1].wait()

    first_t, x_extra = call(
        own_first_body,
        [SMEM, ANY, ANY],
        [(VMEM, (virt, aux), BF16), (VMEM, (pao, virt), BF16)],
        (nums, three_index, coeff),
        scratch=[pltpu.VMEM((pao, virt), BF16), *block_scratch, pltpu.SemaphoreType.DMA((2,))],
    )

    def outer_low_body(three_ref, x_ref, after_ref, y_ref, block_ref, sems):
        at_occ = whole(told_of(x_ref)[0, weights])
        by_tiles(three_ref, at_occ, block_ref, sems, half_into(y_ref, x_ref[:pao, :]))
        y_ref[aux:, :] = jnp.zeros((2 * riders, part), BF16)

    y_low, block_out = call(
        outer_low_body,
        [ANY, VMEM, ANY],
        [(VMEM, (aux + 2 * riders, part), BF16), (VMEM, (aux, pao), BF16)],
        (three_index, low_out, first_t),
        scratch=block_scratch[1:],
    )
    y_low_from_out = outer(y_low)

    def outer_high_body(block_ref, x_ref, after_ref, y_ref):
        product = half_into(y_ref, x_ref[...])
        for at in range(0, aux, tile):
            rows = pl.ds(at, tile)
            product(rows, block_ref[rows, :])
        y_ref[aux:, :] = jnp.zeros((riders, part), BF16)

    (y_high,) = call(
        outer_high_body,
        [VMEM, VMEM, ANY],
        [(VMEM, (aux + riders, part), BF16)],
        (block_out, high_out, y_low),
    )
    y_high_from_out = outer(y_high)

    def outer_body(coeff_ref, amps_ref, low_ref, high_ref, after_ref, s_ref, c_ref, x_ref):
        x_ref[:, :part] = low_ref[:pao, :]
        x_ref[:, part:] = high_ref[...]
        overlaps(x_ref[...], coeff_ref, s_ref)
        told = told_of(low_ref)
        c = coupled(s_ref, [(q, told[0, q], amps_ref[q]) for q in range(pairs)])
        c_ref[...] = c.astype(BF16)

    s_out, c_out = call(
        outer_body,
        [VMEM, VMEM, VMEM, VMEM, ANY],
        [all_s, sq_b],
        (coeff, amps, low_out, high_out, y_high),
        scratch=[pltpu.VMEM((pao, virt), BF16)],
    )
    c_from_out = outer(c_out)

    def own_second_body(nums, three_ref, three_in_ref, coeff_ref, after_ref, second_ref, block_ref, sems):
        x = coeff_ref[whole(nums[MINE])]
        for whose, source in enumerate((three_ref, three_in_ref)):

            @pl.when(whole(nums[WHOSE]) == whose)
            def _():
                by_tiles(source, whole(nums[SECOND]), block_ref, sems, half_into(second_ref, x))

    (second,) = call(
        own_second_body,
        [SMEM, ANY, ANY, VMEM, ANY],
        [(VMEM, (aux, virt), BF16)],
        (nums, three_index, three_in, coeff, c_out),
        scratch=block_scratch,
    )
    x_extra, _ = lax.optimization_barrier((x_extra, c_out))
    x_extra_out = outer(x_extra)

    def own_body(
        nums, coeff_ref, coeff_in_ref, amps_ref, amps_in_ref, eps_ref, after_ref,
        s_ref, s_in_ref, c_ref, gain_ref, gain_extra_ref,
    ):
        mine, extra = whole(nums[MINE]), whole(nums[EXTRA])
        x = coeff_ref[mine]
        total = None
        for at, of_s, of_coeff, of_amps in (
            (own_weights, s_ref, coeff_ref, amps_ref),
            (own_weights + pairs, s_in_ref, coeff_in_ref, amps_in_ref),
        ):
            overlaps(x, of_coeff, of_s)
            c = coupled(of_s, [(q, nums[at + q], of_amps[q]) for q in range(pairs)])
            total = c if total is None else total + c
        c_ref[...] = total

        def gain(pair, count, occupied):
            row = jnp.broadcast_to(eps_ref[pl.ds(pair, 1), :], square)
            energy = row + row.T - occupied
            inside = (lax.broadcasted_iota(I32, square, 0) < count) & (
                lax.broadcasted_iota(I32, square, 1) < count
            )
            return jnp.where(inside, 1.0 / (energy + 1.0), 0.0)

        gain_ref[...] = gain(mine, whole(nums[NV_MINE]), nums[OCC_MINE])
        gain_extra_ref[...] = gain(extra, whole(nums[NV_EXTRA]), nums[OCC_EXTRA])

    s_own, s_in, c_own, gain, gain_extra = call(
        own_body,
        [SMEM] + [VMEM] * 5 + [ANY],
        [all_s, all_s, sq_f, sq_f, sq_f],
        (nums, coeff, coeff_in, amps, amps_in, eps_virt, c_out),
    )

    def first_body(
        nums, first_ref, second_ref, low_ref, high_ref, amps_ref, c_ref, co_ref, gain_ref, amp_ref, k_ref
    ):
        first = first_ref[...]
        outside = whole(nums[WHOSE]) == 2

        @pl.when(outside)
        def _():
            k_ref[:, :part] = mxu(first, low_ref[:aux, :], NN) * aux_scale
            k_ref[:, part:] = mxu(first, high_ref[:aux, :], NN) * aux_scale

        @pl.when(jnp.logical_not(outside))
        def _():
            k_ref[...] = mxu(first, second_ref[...], NN) * aux_scale

        old = amps_ref[whole(nums[MINE])].astype(F32)
        c = c_ref[...] + co_ref[...].astype(F32)
        amp_ref[...] = (gain_ref[...] * (old - k_ref[...] - c)).astype(BF16)

    amp, k_first = call(
        first_body,
        [SMEM] + [VMEM] * 8,
        [sq_b, sq_f],
        (nums, first_t, second, y_low_from_out, y_high_from_out, amps, c_own, c_from_out, gain),
    )
    amp_roles = [amp] + [swap(amp, m) for m in range(1, roles)]

    def second_body(amp_ref, k_ref, out_ref, out_b_ref):
        amp = amp_ref[...]
        k = k_ref[...]
        right = k + mxu(k.astype(BF16), amp, NN) * virt_scale
        both = right + mxu(amp.T, right.astype(BF16), NN) * virt_scale
        rest = amp.astype(F32) - both
        out_ref[...] = rest
        out_b_ref[...] = rest.astype(BF16)

    rest, rest_b = call(
        second_body, [VMEM, VMEM], [sq_f, sq_b], (amp, k_first)
    )
    rests = [lax.ppermute(rest_b, "role", [(0, s)]) for s in range(1, roles)]

    def extra_body(nums, coeff_ref, in_ref, out_ref, after_ref, own_s_ref, in_s_ref, out_s_ref):
        overlaps(out_ref[...], coeff_ref, out_s_ref)
        x = coeff_ref[whole(nums[EXTRA])]
        overlaps(x, coeff_ref, own_s_ref)
        overlaps(x, in_ref, in_s_ref)

    se_own, se_in, se_out = call(
        extra_body,
        [SMEM, VMEM, VMEM, VMEM, ANY],
        [all_s, all_s, all_s],
        (nums, coeff, coeff_in, x_extra_out, rest),
    )

    def outer_again_body(nums, low_ref, s_ref, se_ref, *refs):
        amp_refs, (c_ref, stack_ref) = refs[:roles], refs[-2:]
        role = lax.axis_index("role")

        @pl.when(role > 0)
        def _():
            told = told_of(low_ref)
            pair_at = [whole(nums[ROLE_PAIR + (role ^ m)]) for m in range(roles)]
            for slot, of_s in enumerate((s_ref, se_ref)):
                parts = []
                for m in range(roles):
                    choices = [told[:, slot * pairs + q : slot * pairs + q + 1] for q in range(pairs)]
                    parts.append((pair_at[m], pick(choices, pair_at[m]), amp_refs[m][...]))
                c_ref[slot] = coupled(of_s, parts).astype(BF16)
            for m in range(roles):
                stack_ref[pair_at[m]] = amp_refs[m][...]

    cc_out, stack = call(
        outer_again_body,
        [SMEM] + [VMEM] * (3 + roles),
        [two_b, all_s],
        (nums, low_out, s_out, se_out, *amp_roles),
    )
    cc_from_out = outer(cc_out)
    stack_in = inner(stack)

    def own_again_body(
        nums, rest_ref, s_ref, s_in_ref, se_ref, se_in_ref, stack_ref, stack_in_ref, *refs
    ):
        rest_refs, (out_ref, out_extra_ref) = refs[:-2], refs[-2:]
        role = lax.axis_index("role")

        @pl.when(role > 0)
        def _():
            totals = []
            for slot, of_s, of_s_in in ((0, s_ref, s_in_ref), (1, se_ref, se_in_ref)):
                total = None
                for at, of, amp_ref in (
                    (own_weights + 2 * slot * pairs, of_s, stack_ref),
                    (own_weights + (2 * slot + 1) * pairs, of_s_in, stack_in_ref),
                ):
                    c = coupled(of, [(q, nums[at + q], amp_ref[q]) for q in range(pairs)])
                    total = c if total is None else total + c
                totals.append(total)
            out_ref[...] = rest_ref[...] - totals[0]
            total = -totals[1]
            for s in range(1, roles):
                total += jnp.where(role == s, rest_refs[s - 1][...].astype(F32), 0.0)
            out_extra_ref[...] = total

    rest, rest_extra = call(
        own_again_body,
        [SMEM] + [VMEM] * (7 + roles - 1),
        [sq_f, sq_f],
        (nums, rest, s_own, s_in, se_own, se_in, stack, stack_in, *rests),
    )

    def last_body(
        nums, coeff_ref, gain_ref, gain_extra_ref, rest_ref, rest_extra_ref, c_ref, amp_ref, orb_ref
    ):
        role = lax.axis_index("role")

        def store(slot, here, gain, rest, pair):
            @pl.when(here)
            def _():
                amp = (gain[...] * (rest[...] - c_ref[slot].astype(F32))).astype(BF16)
                amp_ref[slot] = amp
                x = coeff_ref[pair]
                orb_ref[slot] = (x.astype(F32) + mxu(x, amp, NN) * virt_scale).astype(BF16)

            @pl.when(jnp.logical_not(here))
            def _():
                amp_ref[slot] = jnp.zeros(square, BF16)
                orb_ref[slot] = jnp.zeros((pao, virt), BF16)

        store(0, role > 0, gain_ref, rest_ref, whole(nums[MINE]))
        store(1, role == whole(nums[OWNER]), gain_extra_ref, rest_extra_ref, whole(nums[EXTRA]))

    amps_out, dressed_out = call(
        last_body,
        [SMEM] + [VMEM] * 6,
        [(VMEM, (slots, virt, virt), BF16), (VMEM, (slots, pao, virt), BF16)],
        (nums, coeff, gain, gain_extra, rest, rest_extra, cc_from_out),
    )
    return amps_out, dressed_out


def solution(mesh):
    in_specs = (
        P("pairs", None, None),
        P("pairs", None, None),
        P("pairs", None, None),
        P("pairs", None),
        P(),
        P("pairs"),
        P("pairs", None),
        P("pairs", None),
        P("pairs", None),
        P("pairs"),
    )
    out_specs = (P(("role", "pairs"), None, None), P(("role", "pairs"), None, None))
    return jax.shard_map(local, mesh=mesh, in_specs=in_specs, out_specs=out_specs, check_vma=False)
```

```python
import math

import jax
import jax.numpy as jnp
from jax import lax
from jax.experimental import pallas as pl
from jax.experimental.pallas import tpu as pltpu
from jax.sharding import PartitionSpec as P

F32 = jnp.float32
BF16 = jnp.bfloat16
I32 = jnp.int32
NN = ((1,), (0,))
NT = ((1,), (1,))

VMEM = pl.BlockSpec(memory_space=pltpu.VMEM)
SMEM = pl.BlockSpec(memory_space=pltpu.SMEM)
ANY = pl.BlockSpec(memory_space=pl.ANY)
HBM = pl.BlockSpec(memory_space=pltpu.HBM)

MINE, EXTRA, OWNER, FIRST, SECOND, WHOSE, NV_MINE, NV_EXTRA, OCC_MINE, OCC_EXTRA, ROLE_PAIR = range(11)


def whole(number):
    return number.astype(jnp.int32)


def mxu(a, b, dims):
    return lax.dot_general(a, b, (dims, ((), ())), preferred_element_type=F32)


def call(body, ins, outs, args, scratch=(), vmem=48):
    return pl.pallas_call(
        body,
        in_specs=ins,
        out_specs=[spec for spec, _, _ in outs],
        out_shape=[jax.ShapeDtypeStruct(shape, dtype) for _, shape, dtype in outs],
        scratch_shapes=list(scratch),
        cost_estimate=pl.CostEstimate(flops=1, bytes_accessed=1, transcendentals=0),
        compiler_params=pltpu.CompilerParams(vmem_limit_bytes=vmem * 1024 * 1024),
    )(*args)


def local(
    three_index, coeff, amps, eps_virt, eps_occ, nvirt, pair_occ, partners, coupling, pair_owner
):
    columns = lax.axis_size("pairs")
    roles = lax.axis_size("role")
    occ_block, aux, pao = three_index.shape
    pairs, _, virt = coeff.shape
    partner_count = partners.shape[1]
    slots = 2
    assert roles == pairs and pairs % 2 == 0 and columns % 2 == 0 and virt % 2 == 0
    tile = min(256, aux)
    pao_scale = 1.0 / math.sqrt(pao)
    aux_scale = 1.0 / math.sqrt(aux)
    virt_scale = 1.0 / math.sqrt(virt)
    square = (virt, virt)
    part = virt // 2
    sq_b = (VMEM, square, BF16)
    sq_f = (VMEM, square, F32)
    two_b = (VMEM, (2, virt, virt), BF16)
    all_s = (VMEM, (pairs, virt, virt), BF16)
    half = (VMEM, (aux, virt), BF16)

    inner_of = [i ^ 1 for i in range(columns)]
    outer_of = [(i + (1 if i % 2 else -1)) % columns for i in range(columns)]

    def inner(x):
        return lax.ppermute(x, "pairs", list(enumerate(inner_of)))

    def outer(x):
        return lax.ppermute(x, "pairs", list(enumerate(outer_of)))

    def swap(x, by):
        return lax.ppermute(x, "role", [(i, i ^ by) for i in range(roles)])

    three_in, coeff_in, amps_in = inner(three_index), inner(coeff), inner(amps)

    def pairs_of_roles(owner_ref):
        of_role = [jnp.int32(0)] * roles
        for p in range(pairs):
            earlier = jnp.int32(0)
            for o in range(p):
                earlier += (owner_ref[o] == owner_ref[p]).astype(I32)
            for s in range(roles):
                hit = (earlier == 0) & (owner_ref[p] == s) if s else earlier == 1
                of_role[s] = jnp.where(hit, p, of_role[s])
        return of_role

    def pick(numbers, at):
        chosen = numbers[0]
        for s in range(1, len(numbers)):
            chosen = jnp.where(at == s, numbers[s], chosen)
        return chosen

    weights = 2 * pairs
    riders = 16
    longer = (VMEM, (virt + riders, virt), BF16)
    own_weights = ROLE_PAIR + roles

    def plan_body(
        owner_hbm, occ_hbm, partner_hbm, coupling_hbm, eps_hbm, nvirt_hbm, coeff_hbm,
        low_ref, high_ref, nums,
        owner_ref, occ_ref, partner_ref, coupling_ref, eps_ref, nvirt_ref, near_w, sems,
    ):
        small = [
            pltpu.make_async_copy(source, target, sems.at[at])
            for at, (source, target) in enumerate(
                (
                    (owner_hbm, owner_ref),
                    (occ_hbm, occ_ref),
                    (partner_hbm, partner_ref),
                    (coupling_hbm, coupling_ref),
                    (eps_hbm, eps_ref),
                    (nvirt_hbm, nvirt_ref),
                )
            )
        ]
        for copy in small:
            copy.start()
        role = lax.axis_index("role")
        column = lax.axis_index("pairs")
        small[0].wait()
        of_role = pairs_of_roles(owner_ref)
        extra = of_role[0]
        mine = pick(of_role, role)
        large = [
            pltpu.make_async_copy(coeff_hbm.at[mine, :, pl.ds(0, part)], low_ref.at[pl.ds(0, pao)], sems.at[6]),
            pltpu.make_async_copy(coeff_hbm.at[mine, :, pl.ds(part, part)], high_ref, sems.at[7]),
        ]
        for copy in large:
            copy.start()
        for copy in small[1:]:
            copy.wait()
        nums[MINE] = mine.astype(F32)
        nums[EXTRA] = extra.astype(F32)
        nums[OWNER] = owner_ref[extra].astype(F32)
        for s in range(roles):
            nums[ROLE_PAIR + s] = of_role[s].astype(F32)
        nums[NV_MINE] = nvirt_ref[mine].astype(F32)
        nums[NV_EXTRA] = nvirt_ref[extra].astype(F32)
        nums[FIRST] = (occ_ref[0, mine] - column * occ_block).astype(F32)
        odd = lax.rem(column, 2) == 1
        inner_at = jnp.where(odd, 0, 2)
        outer_at = 2 - inner_at
        occ_all = occ_block * columns
        second = lax.rem(occ_ref[1, mine] - (column - 1) * occ_block + occ_all, occ_all)
        block = (second >= occ_block).astype(I32) + (second >= 2 * occ_block).astype(I32)
        place = (second - block * occ_block).astype(F32)
        nums[SECOND] = place
        lane = lax.broadcasted_iota(I32, (riders, part), 1)
        row = lax.broadcasted_iota(I32, (riders, part), 0)
        told = jnp.where(lane == weights, place, 0.0)
        nums[WHOSE] = jnp.where(block == 1, 0, jnp.where(block == inner_at, 1, 2)).astype(F32)
        nums[OCC_MINE] = eps_ref[occ_ref[0, mine]] + eps_ref[occ_ref[1, mine]]
        nums[OCC_EXTRA] = eps_ref[occ_ref[0, extra]] + eps_ref[occ_ref[1, extra]]
        pair_all = pairs * columns
        for which, pair in enumerate((mine, extra)):
            for q in range(3 * pairs):
                near_w[q] = jnp.float32(0)
            for k in range(partner_count):
                at = lax.rem(partner_ref[pair, k] - (column - 1) * pairs + pair_all, pair_all)
                near_w[at] += coupling_ref[pair, k]
            for q in range(pairs):
                to = which * pairs + q
                nums[own_weights + 2 * which * pairs + q] = near_w[pairs + q]
                nums[own_weights + (2 * which + 1) * pairs + q] = near_w[inner_at * pairs + q]
                told = jnp.where(lane == to, near_w[outer_at * pairs + q], told)
        coarse = told.astype(BF16).astype(F32)
        middle = (told - coarse).astype(BF16).astype(F32)
        fine = told - coarse - middle
        told = jnp.where(row == 0, coarse, jnp.where(row == 1, middle, jnp.where(row == 2, fine, 0.0)))
        low_ref[pao:, :] = told.astype(BF16)
        for copy in large:
            copy.wait()

    rode = (VMEM, (pao + riders, part), BF16)
    x_low, x_high, nums = call(
        plan_body,
        [HBM] * 7,
        [rode, (VMEM, (pao, part), BF16), (SMEM, (own_weights + 2 * weights,), F32)],
        (pair_owner, pair_occ.T, partners, coupling, eps_occ, nvirt, coeff),
        scratch=[
            pltpu.SMEM(pair_owner.shape, I32),
            pltpu.SMEM(pair_occ.shape[::-1], I32),
            pltpu.SMEM(partners.shape, I32),
            pltpu.SMEM(coupling.shape, F32),
            pltpu.SMEM(eps_occ.shape, F32),
            pltpu.SMEM(nvirt.shape, I32),
            pltpu.SMEM((3 * pairs,), F32),
            pltpu.SemaphoreType.DMA((8,)),
        ],
        vmem=60,
    )
    low_out, high_out = outer(x_low), outer(x_high)

    def told_of(low_ref):
        rows = low_ref[pao:, :].astype(F32)
        return rows[0:1] + rows[1:2] + rows[2:3]

    def overlaps(x, coeff_ref, out_ref):
        turned = x.T
        for q in range(pairs):
            s = mxu(turned, coeff_ref[q], NN) * (1.0 / pao)
            out_ref[q] = s.astype(BF16)

    def coupled(s_ref, parts):
        total = None
        for at, weight, amp in parts:
            s = s_ref[at]
            u = mxu(s, amp, NN).astype(BF16)
            term = weight * mxu(u, s, NT)
            total = term if total is None else total + term
        return total

    block_scratch = [pltpu.VMEM((aux, pao), BF16), pltpu.SemaphoreType.DMA((aux // tile,))]

    def by_tiles(three_ref, at_occ, block_ref, sems, product):
        tiles = [pl.ds(at, tile) for at in range(0, aux, tile)]
        copies = [
            pltpu.make_async_copy(three_ref.at[at_occ, rows], block_ref.at[rows], sems.at[at])
            for at, rows in enumerate(tiles)
        ]
        for copy in copies:
            copy.start()
        for copy, rows in zip(copies, tiles):
            copy.wait()
            product(rows, block_ref[rows, :])

    def half_into(y_ref, x):
        def product(rows, block):
            y_ref[rows, :] = (mxu(block, x, NN) * pao_scale).astype(BF16)

        return product

    def outer_low_body(three_ref, x_ref, y_ref, block_ref, sems):
        at_occ = whole(told_of(x_ref)[0, weights])
        by_tiles(three_ref, at_occ, block_ref, sems, half_into(y_ref, x_ref[:pao, :]))
        y_ref[aux:, :] = jnp.zeros((2 * riders, part), BF16)

    (y_low,) = call(
        outer_low_body,
        [ANY, VMEM],
        [(VMEM, (aux + 2 * riders, part), BF16)],
        (three_index, low_out),
        scratch=block_scratch,
        vmem=52,
    )
    y_low_from_out = outer(y_low)

    def outer_high_body(three_ref, low_ref, x_ref, after_ref, y_ref, block_ref, sems):
        at_occ = whole(told_of(low_ref)[0, weights])
        by_tiles(three_ref, at_occ, block_ref, sems, half_into(y_ref, x_ref[...]))
        y_ref[aux:, :] = jnp.zeros((riders, part), BF16)

    (y_high,) = call(
        outer_high_body,
        [ANY, VMEM, VMEM, ANY],
        [(VMEM, (aux + riders, part), BF16)],
        (three_index, low_out, high_out, y_low),
        scratch=block_scratch,
        vmem=52,
    )
    y_high_from_out = outer(y_high)

    def outer_body(coeff_ref, amps_ref, low_ref, high_ref, after_ref, s_ref, c_ref, x_ref):
        x_ref[:, :part] = low_ref[:pao, :]
        x_ref[:, part:] = high_ref[...]
        overlaps(x_ref[...], coeff_ref, s_ref)
        told = told_of(low_ref)
        c = coupled(s_ref, [(q, told[0, q], amps_ref[q]) for q in range(pairs)])
        c_ref[...] = c.astype(BF16)

    s_out, c_out = call(
        outer_body,
        [VMEM, VMEM, VMEM, VMEM, ANY],
        [all_s, sq_b],
        (coeff, amps, low_out, high_out, y_high),
        scratch=[pltpu.VMEM((pao, virt), BF16)],
    )
    c_from_out = outer(c_out)

    def own_half_body(
        nums, three_ref, three_in_ref, coeff_ref, after_ref, first_ref, second_ref, extra_ref, block_ref, sems
    ):
        x = coeff_ref[whole(nums[MINE])]
        extra_ref[...] = coeff_ref[whole(nums[EXTRA])]
        turned = x.T

        def product(rows, block):
            first_ref[:, rows] = (mxu(turned, block, NT) * pao_scale).astype(BF16)

        by_tiles(three_ref, whole(nums[FIRST]), block_ref, sems, product)
        for whose, source in enumerate((three_ref, three_in_ref)):

            @pl.when(whole(nums[WHOSE]) == whose)
            def _():
                by_tiles(source, whole(nums[SECOND]), block_ref, sems, half_into(second_ref, x))

    first_t, second, x_extra = call(
        own_half_body,
        [SMEM, ANY, ANY, VMEM, ANY],
        [(VMEM, (virt, aux), BF16), (VMEM, (aux, virt), BF16), (VMEM, (pao, virt), BF16)],
        (nums, three_index, three_in, coeff, c_out),
        scratch=block_scratch,
    )
    x_extra_out = outer(x_extra)

    def own_body(
        nums, coeff_ref, coeff_in_ref, amps_ref, amps_in_ref, eps_ref, after_ref,
        s_ref, s_in_ref, c_ref, gain_ref, gain_extra_ref,
    ):
        mine, extra = whole(nums[MINE]), whole(nums[EXTRA])
        x = coeff_ref[mine]
        total = None
        for at, of_s, of_coeff, of_amps in (
            (own_weights, s_ref, coeff_ref, amps_ref),
            (own_weights + pairs, s_in_ref, coeff_in_ref, amps_in_ref),
        ):
            overlaps(x, of_coeff, of_s)
            c = coupled(of_s, [(q, nums[at + q], of_amps[q]) for q in range(pairs)])
            total = c if total is None else total + c
        c_ref[...] = total

        def gain(pair, count, occupied):
            row = jnp.broadcast_to(eps_ref[pl.ds(pair, 1), :], square)
            energy = row + row.T - occupied
            inside = (lax.broadcasted_iota(I32, square, 0) < count) & (
                lax.broadcasted_iota(I32, square, 1) < count
            )
            return jnp.where(inside, 1.0 / (energy + 1.0), 0.0)

        gain_ref[...] = gain(mine, whole(nums[NV_MINE]), nums[OCC_MINE])
        gain_extra_ref[...] = gain(extra, whole(nums[NV_EXTRA]), nums[OCC_EXTRA])

    s_own, s_in, c_own, gain, gain_extra = call(
        own_body,
        [SMEM] + [VMEM] * 5 + [ANY],
        [all_s, all_s, sq_f, sq_f, sq_f],
        (nums, coeff, coeff_in, amps, amps_in, eps_virt, c_out),
    )

    def first_body(
        nums, first_ref, second_ref, low_ref, high_ref, amps_ref, c_ref, co_ref, gain_ref, amp_ref, k_ref
    ):
        first = first_ref[...]
        outside = whole(nums[WHOSE]) == 2

        @pl.when(outside)
        def _():
            k_ref[:, :part] = mxu(first, low_ref[:aux, :], NN) * aux_scale
            k_ref[:, part:] = mxu(first, high_ref[:aux, :], NN) * aux_scale

        @pl.when(jnp.logical_not(outside))
        def _():
            k_ref[...] = mxu(first, second_ref[...], NN) * aux_scale

        old = amps_ref[whole(nums[MINE])].astype(F32)
        c = c_ref[...] + co_ref[...].astype(F32)
        amp_ref[...] = (gain_ref[...] * (old - k_ref[...] - c)).astype(BF16)

    amp, k_first = call(
        first_body,
        [SMEM] + [VMEM] * 8,
        [sq_b, sq_f],
        (nums, first_t, second, y_low_from_out, y_high_from_out, amps, c_own, c_from_out, gain),
    )
    amp_roles = [amp] + [swap(amp, m) for m in range(1, roles)]

    def second_body(amp_ref, k_ref, out_ref, out_b_ref):
        amp = amp_ref[...]
        k = k_ref[...]
        right = k + mxu(k.astype(BF16), amp, NN) * virt_scale
        both = right + mxu(amp.T, right.astype(BF16), NN) * virt_scale
        rest = amp.astype(F32) - both
        out_ref[...] = rest
        out_b_ref[:virt, :] = rest.astype(BF16)
        out_b_ref[virt:, :] = jnp.zeros((riders, virt), BF16)

    rest, rest_b = call(
        second_body, [VMEM, VMEM], [sq_f, longer], (amp, k_first)
    )
    rests = [lax.ppermute(rest_b, "role", [(0, s)]) for s in range(1, roles)]

    def extra_body(nums, coeff_ref, in_ref, out_ref, after_ref, own_s_ref, in_s_ref, out_s_ref):
        overlaps(out_ref[...], coeff_ref, out_s_ref)
        x = coeff_ref[whole(nums[EXTRA])]
        overlaps(x, coeff_ref, own_s_ref)
        overlaps(x, in_ref, in_s_ref)

    se_own, se_in, se_out = call(
        extra_body,
        [SMEM, VMEM, VMEM, VMEM, ANY],
        [all_s, all_s, all_s],
        (nums, coeff, coeff_in, x_extra_out, rest),
    )

    def outer_again_body(nums, low_ref, s_ref, se_ref, *refs):
        amp_refs, c_ref = refs[:roles], refs[-1]
        role = lax.axis_index("role")

        @pl.when(role > 0)
        def _():
            told = told_of(low_ref)
            pair_at = [whole(nums[ROLE_PAIR + (role ^ m)]) for m in range(roles)]
            for slot, of_s in enumerate((s_ref, se_ref)):
                parts = []
                for m in range(roles):
                    choices = [told[:, slot * pairs + q : slot * pairs + q + 1] for q in range(pairs)]
                    parts.append((pair_at[m], pick(choices, pair_at[m]), amp_refs[m][...]))
                c_ref[slot] = coupled(of_s, parts).astype(BF16)

    (cc_out,) = call(
        outer_again_body,
        [SMEM] + [VMEM] * (3 + roles),
        [two_b],
        (nums, low_out, s_out, se_out, *amp_roles),
    )
    cc_from_out = outer(cc_out)

    def order_body(nums, *refs):
        amp_refs, ordered_refs = refs[:roles], refs[-pairs:]
        role = lax.axis_index("role")
        for m in range(roles):
            at = whole(nums[ROLE_PAIR + (role ^ m)])
            for q, ordered_ref in enumerate(ordered_refs):

                @pl.when(at == q)
                def _():
                    ordered_ref[:virt, :] = amp_refs[m][...]

        for ordered_ref in ordered_refs:
            ordered_ref[virt:, :] = jnp.zeros((riders, virt), BF16)

    ordered = call(
        order_body,
        [SMEM] + [VMEM] * roles + [ANY] * (roles - 1),
        [longer] * pairs,
        (nums, *amp_roles, *rests),
    )
    ordered_in = [inner(x) for x in ordered]

    def own_again_body(nums, rest_ref, s_ref, s_in_ref, se_ref, se_in_ref, *refs):
        amp_refs, amp_in_refs, rest_refs = refs[:pairs], refs[pairs : 2 * pairs], refs[2 * pairs : -2]
        out_ref, out_extra_ref = refs[-2:]
        role = lax.axis_index("role")

        @pl.when(role > 0)
        def _():
            totals = []
            for slot, of_s, of_s_in in ((0, s_ref, s_in_ref), (1, se_ref, se_in_ref)):
                total = None
                for at, of, of_amps in (
                    (own_weights + 2 * slot * pairs, of_s, amp_refs),
                    (own_weights + (2 * slot + 1) * pairs, of_s_in, amp_in_refs),
                ):
                    parts = [(q, nums[at + q], of_amps[q][:virt, :]) for q in range(pairs)]
                    c = coupled(of, parts)
                    total = c if total is None else total + c
                totals.append(total)
            out_ref[...] = rest_ref[...] - totals[0]
            total = -totals[1]
            for s in range(1, roles):
                total += jnp.where(role == s, rest_refs[s - 1][:virt, :].astype(F32), 0.0)
            out_extra_ref[...] = total

    rest, rest_extra = call(
        own_again_body,
        [SMEM] + [VMEM] * (5 + 2 * pairs + roles - 1),
        [sq_f, sq_f],
        (nums, rest, s_own, s_in, se_own, se_in, *ordered, *ordered_in, *rests),
    )

    def last_body(
        nums, coeff_ref, gain_ref, gain_extra_ref, rest_ref, rest_extra_ref, c_ref, amp_ref, orb_ref
    ):
        role = lax.axis_index("role")

        def store(slot, here, gain, rest, pair):
            @pl.when(here)
            def _():
                amp = (gain[...] * (rest[...] - c_ref[slot].astype(F32))).astype(BF16)
                amp_ref[slot] = amp
                x = coeff_ref[pair]
                orb_ref[slot] = (x.astype(F32) + mxu(x, amp, NN) * virt_scale).astype(BF16)

            @pl.when(jnp.logical_not(here))
            def _():
                amp_ref[slot] = jnp.zeros(square, BF16)
                orb_ref[slot] = jnp.zeros((pao, virt), BF16)

        store(0, role > 0, gain_ref, rest_ref, whole(nums[MINE]))
        store(1, role == whole(nums[OWNER]), gain_extra_ref, rest_extra_ref, whole(nums[EXTRA]))

    amps_out, dressed_out = call(
        last_body,
        [SMEM] + [VMEM] * 6,
        [(VMEM, (slots, virt, virt), BF16), (VMEM, (slots, pao, virt), BF16)],
        (nums, coeff, gain, gain_extra, rest, rest_extra, cc_from_out),
    )
    return amps_out, dressed_out


def solution(mesh):
    in_specs = (
        P("pairs", None, None),
        P("pairs", None, None),
        P("pairs", None, None),
        P("pairs", None),
        P(),
        P("pairs"),
        P("pairs", None),
        P("pairs", None),
        P("pairs", None),
        P("pairs"),
    )
    out_specs = (P(("role", "pairs"), None, None), P(("role", "pairs"), None, None))
    return jax.shard_map(local, mesh=mesh, in_specs=in_specs, out_specs=out_specs, check_vma=False)
```

```python
import math

import jax
import jax.numpy as jnp
from jax import lax
from jax.experimental import pallas as pl
from jax.experimental.pallas import tpu as pltpu
from jax.sharding import PartitionSpec as P

F32 = jnp.float32
BF16 = jnp.bfloat16
I32 = jnp.int32
NN = ((1,), (0,))
NT = ((1,), (1,))

VMEM = pl.BlockSpec(memory_space=pltpu.VMEM)
SMEM = pl.BlockSpec(memory_space=pltpu.SMEM)
ANY = pl.BlockSpec(memory_space=pl.ANY)
HBM = pl.BlockSpec(memory_space=pltpu.HBM)

MINE, EXTRA, OWNER, FIRST, SECOND, WHOSE, NV_MINE, NV_EXTRA, OCC_MINE, OCC_EXTRA, ROLE_PAIR = range(11)


def whole(number):
    return number.astype(jnp.int32)


def mxu(a, b, dims):
    return lax.dot_general(a, b, (dims, ((), ())), preferred_element_type=F32)


def call(body, ins, outs, args, scratch=(), vmem=48):
    return pl.pallas_call(
        body,
        in_specs=ins,
        out_specs=[spec for spec, _, _ in outs],
        out_shape=[jax.ShapeDtypeStruct(shape, dtype) for _, shape, dtype in outs],
        scratch_shapes=list(scratch),
        cost_estimate=pl.CostEstimate(flops=1, bytes_accessed=1, transcendentals=0),
        compiler_params=pltpu.CompilerParams(vmem_limit_bytes=vmem * 1024 * 1024),
    )(*args)


def local(
    three_index, coeff, amps, eps_virt, eps_occ, nvirt, pair_occ, partners, coupling, pair_owner
):
    columns = lax.axis_size("pairs")
    roles = lax.axis_size("role")
    occ_block, aux, pao = three_index.shape
    pairs, _, virt = coeff.shape
    partner_count = partners.shape[1]
    slots = 2
    assert roles == pairs and pairs % 2 == 0 and columns % 2 == 0 and virt % 2 == 0
    tile = min(256, aux)
    pao_scale = 1.0 / math.sqrt(pao)
    aux_scale = 1.0 / math.sqrt(aux)
    virt_scale = 1.0 / math.sqrt(virt)
    square = (virt, virt)
    part = virt // 2
    sq_b = (VMEM, square, BF16)
    sq_f = (VMEM, square, F32)
    two_b = (VMEM, (2, virt, virt), BF16)
    all_s = (VMEM, (pairs, virt, virt), BF16)
    half = (VMEM, (aux, virt), BF16)

    inner_of = [i ^ 1 for i in range(columns)]
    outer_of = [(i + (1 if i % 2 else -1)) % columns for i in range(columns)]

    def inner(x):
        return lax.ppermute(x, "pairs", list(enumerate(inner_of)))

    def outer(x):
        return lax.ppermute(x, "pairs", list(enumerate(outer_of)))

    def swap(x, by):
        return lax.ppermute(x, "role", [(i, i ^ by) for i in range(roles)])

    three_in, coeff_in, amps_in = inner(three_index), inner(coeff), inner(amps)

    def pairs_of_roles(owner_ref):
        of_role = [jnp.int32(0)] * roles
        for p in range(pairs):
            earlier = jnp.int32(0)
            for o in range(p):
                earlier += (owner_ref[o] == owner_ref[p]).astype(I32)
            for s in range(roles):
                hit = (earlier == 0) & (owner_ref[p] == s) if s else earlier == 1
                of_role[s] = jnp.where(hit, p, of_role[s])
        return of_role

    def pick(numbers, at):
        chosen = numbers[0]
        for s in range(1, len(numbers)):
            chosen = jnp.where(at == s, numbers[s], chosen)
        return chosen

    weights = 2 * pairs
    riders = 16
    longer = (VMEM, (virt + riders, virt), BF16)
    own_weights = ROLE_PAIR + roles

    def plan_body(
        owner_hbm, occ_hbm, partner_hbm, coupling_hbm, eps_hbm, nvirt_hbm, coeff_hbm,
        low_ref, high_ref, nums,
        owner_ref, occ_ref, partner_ref, coupling_ref, eps_ref, nvirt_ref, near_w, sems,
    ):
        small = [
            pltpu.make_async_copy(source, target, sems.at[at])
            for at, (source, target) in enumerate(
                (
                    (owner_hbm, owner_ref),
                    (occ_hbm, occ_ref),
                    (partner_hbm, partner_ref),
                    (coupling_hbm, coupling_ref),
                    (eps_hbm, eps_ref),
                    (nvirt_hbm, nvirt_ref),
                )
            )
        ]
        for copy in small:
            copy.start()
        role = lax.axis_index("role")
        column = lax.axis_index("pairs")
        small[0].wait()
        of_role = pairs_of_roles(owner_ref)
        extra = of_role[0]
        mine = pick(of_role, role)
        large = [
            pltpu.make_async_copy(coeff_hbm.at[mine, :, pl.ds(0, part)], low_ref.at[pl.ds(0, pao)], sems.at[6]),
            pltpu.make_async_copy(coeff_hbm.at[mine, :, pl.ds(part, part)], high_ref, sems.at[7]),
        ]
        for copy in large:
            copy.start()
        for copy in small[1:]:
            copy.wait()
        nums[MINE] = mine.astype(F32)
        nums[EXTRA] = extra.astype(F32)
        nums[OWNER] = owner_ref[extra].astype(F32)
        for s in range(roles):
            nums[ROLE_PAIR + s] = of_role[s].astype(F32)
        nums[NV_MINE] = nvirt_ref[mine].astype(F32)
        nums[NV_EXTRA] = nvirt_ref[extra].astype(F32)
        nums[FIRST] = (occ_ref[0, mine] - column * occ_block).astype(F32)
        odd = lax.rem(column, 2) == 1
        inner_at = jnp.where(odd, 0, 2)
        outer_at = 2 - inner_at
        occ_all = occ_block * columns
        second = lax.rem(occ_ref[1, mine] - (column - 1) * occ_block + occ_all, occ_all)
        block = (second >= occ_block).astype(I32) + (second >= 2 * occ_block).astype(I32)
        place = (second - block * occ_block).astype(F32)
        nums[SECOND] = place
        lane = lax.broadcasted_iota(I32, (riders, part), 1)
        row = lax.broadcasted_iota(I32, (riders, part), 0)
        told = jnp.where(lane == weights, place, 0.0)
        nums[WHOSE] = jnp.where(block == 1, 0, jnp.where(block == inner_at, 1, 2)).astype(F32)
        nums[OCC_MINE] = eps_ref[occ_ref[0, mine]] + eps_ref[occ_ref[1, mine]]
        nums[OCC_EXTRA] = eps_ref[occ_ref[0, extra]] + eps_ref[occ_ref[1, extra]]
        pair_all = pairs * columns
        for which, pair in enumerate((mine, extra)):
            for q in range(3 * pairs):
                near_w[q] = jnp.float32(0)
            for k in range(partner_count):
                at = lax.rem(partner_ref[pair, k] - (column - 1) * pairs + pair_all, pair_all)
                near_w[at] += coupling_ref[pair, k]
            for q in range(pairs):
                to = which * pairs + q
                nums[own_weights + 2 * which * pairs + q] = near_w[pairs + q]
                nums[own_weights + (2 * which + 1) * pairs + q] = near_w[inner_at * pairs + q]
                told = jnp.where(lane == to, near_w[outer_at * pairs + q], told)
        coarse = told.astype(BF16).astype(F32)
        middle = (told - coarse).astype(BF16).astype(F32)
        fine = told - coarse - middle
        told = jnp.where(row == 0, coarse, jnp.where(row == 1, middle, jnp.where(row == 2, fine, 0.0)))
        low_ref[pao:, :] = told.astype(BF16)
        for copy in large:
            copy.wait()

    rode = (VMEM, (pao + riders, part), BF16)
    x_low, x_high, nums = call(
        plan_body,
        [HBM] * 7,
        [rode, (VMEM, (pao, part), BF16), (SMEM, (own_weights + 2 * weights,), F32)],
        (pair_owner, pair_occ.T, partners, coupling, eps_occ, nvirt, coeff),
        scratch=[
            pltpu.SMEM(pair_owner.shape, I32),
            pltpu.SMEM(pair_occ.shape[::-1], I32),
            pltpu.SMEM(partners.shape, I32),
            pltpu.SMEM(coupling.shape, F32),
            pltpu.SMEM(eps_occ.shape, F32),
            pltpu.SMEM(nvirt.shape, I32),
            pltpu.SMEM((3 * pairs,), F32),
            pltpu.SemaphoreType.DMA((8,)),
        ],
        vmem=60,
    )
    low_out, high_out = outer(x_low), outer(x_high)

    def told_of(low_ref):
        rows = low_ref[pao:, :].astype(F32)
        return rows[0:1] + rows[1:2] + rows[2:3]

    def overlaps(x, coeff_ref, out_ref):
        turned = x.T
        for q in range(pairs):
            s = mxu(turned, coeff_ref[q], NN) * (1.0 / pao)
            out_ref[q] = s.astype(BF16)

    def coupled(s_ref, parts):
        total = None
        for at, weight, amp in parts:
            s = s_ref[at]
            u = mxu(s, amp, NN).astype(BF16)
            term = weight * mxu(u, s, NT)
            total = term if total is None else total + term
        return total

    tiles = [pl.ds(at, tile) for at in range(0, aux, tile)]

    def half_into(y_ref, three_ref, at_occ, x):
        for rows in tiles:
            y_ref[rows, :] = (mxu(three_ref[at_occ, rows, :], x, NN) * pao_scale).astype(BF16)

    def fetch_body(three_ref, after_ref, held_ref, sem):
        copy = pltpu.make_async_copy(three_ref, held_ref, sem)
        copy.start()
        copy.wait()

    (blocks,) = call(
        fetch_body,
        [ANY, ANY],
        [(VMEM, three_index.shape, BF16)],
        (three_index, x_high),
        scratch=[pltpu.SemaphoreType.DMA],
        vmem=50,
    )

    def outer_low_body(three_ref, x_ref, y_ref):
        half_into(y_ref, three_ref, whole(told_of(x_ref)[0, weights]), x_ref[:pao, :])
        y_ref[aux:, :] = jnp.zeros((2 * riders, part), BF16)

    (y_low,) = call(
        outer_low_body,
        [VMEM, VMEM],
        [(VMEM, (aux + 2 * riders, part), BF16)],
        (blocks, low_out),
    )
    y_low_from_out = outer(y_low)

    def outer_high_body(three_ref, low_ref, x_ref, after_ref, y_ref):
        half_into(y_ref, three_ref, whole(told_of(low_ref)[0, weights]), x_ref[...])
        y_ref[aux:, :] = jnp.zeros((riders, part), BF16)

    (y_high,) = call(
        outer_high_body,
        [VMEM, VMEM, VMEM, ANY],
        [(VMEM, (aux + riders, part), BF16)],
        (blocks, low_out, high_out, y_low),
    )
    y_high_from_out = outer(y_high)

    def outer_body(coeff_ref, amps_ref, low_ref, high_ref, after_ref, s_ref, c_ref, x_ref):
        x_ref[:, :part] = low_ref[:pao, :]
        x_ref[:, part:] = high_ref[...]
        overlaps(x_ref[...], coeff_ref, s_ref)
        told = told_of(low_ref)
        c = coupled(s_ref, [(q, told[0, q], amps_ref[q]) for q in range(pairs)])
        c_ref[:virt, :] = c.astype(BF16)
        c_ref[virt:, :] = jnp.zeros((3 * riders, virt), BF16)

    s_out, c_out = call(
        outer_body,
        [VMEM, VMEM, VMEM, VMEM, ANY],
        [all_s, (VMEM, (virt + 3 * riders, virt), BF16)],
        (coeff, amps, low_out, high_out, y_high),
        scratch=[pltpu.VMEM((pao, virt), BF16)],
    )
    c_from_out = outer(c_out)

    def own_half_body(
        nums, three_ref, three_in_ref, coeff_ref, after_ref, first_ref, second_ref, extra_ref, block_ref, sem
    ):
        x = coeff_ref[whole(nums[MINE])]
        extra_ref[:pao, :] = coeff_ref[whole(nums[EXTRA])]
        extra_ref[pao:, :] = jnp.zeros((2 * riders, virt), BF16)
        whose, second = whole(nums[WHOSE]), whole(nums[SECOND])
        copy = pltpu.make_async_copy(three_in_ref.at[second], block_ref.at[0], sem)

        @pl.when(whose == 1)
        def _():
            copy.start()

        turned = x.T
        first = whole(nums[FIRST])
        for rows in tiles:
            first_ref[:, rows] = (mxu(turned, three_ref[first, rows, :], NT) * pao_scale).astype(BF16)

        @pl.when(whose == 0)
        def _():
            half_into(second_ref, three_ref, second, x)

        @pl.when(whose == 1)
        def _():
            copy.wait()
            half_into(second_ref, block_ref, 0, x)

    first_t, second, x_extra = call(
        own_half_body,
        [SMEM, VMEM, ANY, VMEM, ANY],
        [
            (VMEM, (virt, aux), BF16),
            (VMEM, (aux, virt), BF16),
            (VMEM, (pao + 2 * riders, virt), BF16),
        ],
        (nums, blocks, three_in, coeff, c_out),
        scratch=[pltpu.VMEM((1, aux, pao), BF16), pltpu.SemaphoreType.DMA],
    )
    x_extra_out = outer(x_extra)

    def own_body(
        nums, coeff_ref, coeff_in_ref, amps_ref, amps_in_ref, eps_ref, after_ref,
        s_ref, s_in_ref, c_ref, gain_ref, gain_extra_ref,
    ):
        mine, extra = whole(nums[MINE]), whole(nums[EXTRA])
        x = coeff_ref[mine]
        total = None
        for at, of_s, of_coeff, of_amps in (
            (own_weights, s_ref, coeff_ref, amps_ref),
            (own_weights + pairs, s_in_ref, coeff_in_ref, amps_in_ref),
        ):
            overlaps(x, of_coeff, of_s)
            c = coupled(of_s, [(q, nums[at + q], of_amps[q]) for q in range(pairs)])
            total = c if total is None else total + c
        c_ref[...] = total

        def gain(pair, count, occupied):
            row = jnp.broadcast_to(eps_ref[pl.ds(pair, 1), :], square)
            energy = row + row.T - occupied
            inside = (lax.broadcasted_iota(I32, square, 0) < count) & (
                lax.broadcasted_iota(I32, square, 1) < count
            )
            return jnp.where(inside, 1.0 / (energy + 1.0), 0.0)

        gain_ref[...] = gain(mine, whole(nums[NV_MINE]), nums[OCC_MINE])
        gain_extra_ref[...] = gain(extra, whole(nums[NV_EXTRA]), nums[OCC_EXTRA])

    s_own, s_in, c_own, gain, gain_extra = call(
        own_body,
        [SMEM] + [VMEM] * 5 + [ANY],
        [all_s, all_s, sq_f, sq_f, sq_f],
        (nums, coeff, coeff_in, amps, amps_in, eps_virt, c_out),
    )

    def k_body(nums, first_ref, second_ref, low_ref, high_ref, after_ref, k_ref, k_b_ref):
        first = first_ref[...]
        outside = whole(nums[WHOSE]) == 2

        @pl.when(outside)
        def _():
            k_ref[:, :part] = mxu(first, low_ref[:aux, :], NN) * aux_scale
            k_ref[:, part:] = mxu(first, high_ref[:aux, :], NN) * aux_scale

        @pl.when(jnp.logical_not(outside))
        def _():
            k_ref[...] = mxu(first, second_ref[...], NN) * aux_scale

        k_b_ref[:virt, :] = k_ref[...].astype(BF16)
        k_b_ref[virt:, :] = jnp.zeros((riders, virt), BF16)

    k_first, k_b = call(
        k_body,
        [SMEM] + [VMEM] * 4 + [ANY],
        [sq_f, longer],
        (nums, first_t, second, y_low_from_out, y_high_from_out, c_own),
    )
    k_extras = [lax.ppermute(k_b, "role", [(0, s)]) for s in range(1, roles)]

    def first_body(nums, k_ref, amps_ref, c_ref, co_ref, gain_ref, amp_ref):
        old = amps_ref[whole(nums[MINE])].astype(F32)
        c = c_ref[...] + co_ref[:virt, :].astype(F32)
        amp_ref[...] = (gain_ref[...] * (old - k_ref[...] - c)).astype(BF16)

    (amp,) = call(
        first_body,
        [SMEM] + [VMEM] * 5,
        [sq_b],
        (nums, k_first, amps, c_own, c_from_out, gain),
    )
    amp_roles = [amp] + [swap(amp, m) for m in range(1, roles)]

    def extra_out_body(coeff_ref, x_ref, *refs):
        @pl.when(lax.axis_index("role") > 0)
        def _():
            overlaps(x_ref[:pao, :], coeff_ref, refs[-1])

    (se_out,) = call(
        extra_out_body,
        [VMEM, VMEM] + [ANY] * roles,
        [all_s],
        (coeff, x_extra_out, amp, *k_extras),
    )

    def outer_again_body(nums, low_ref, s_ref, se_ref, *refs):
        amp_refs, c_ref = refs[:roles], refs[-1]
        role = lax.axis_index("role")

        @pl.when(role > 0)
        def _():
            told = told_of(low_ref)
            pair_at = [whole(nums[ROLE_PAIR + (role ^ m)]) for m in range(roles)]
            for slot, of_s in enumerate((s_ref, se_ref)):
                parts = []
                for m in range(roles):
                    choices = [told[:, slot * pairs + q : slot * pairs + q + 1] for q in range(pairs)]
                    parts.append((pair_at[m], pick(choices, pair_at[m]), amp_refs[m][...]))
                c_ref[slot] = coupled(of_s, parts).astype(BF16)

    (cc_out,) = call(
        outer_again_body,
        [SMEM] + [VMEM] * (3 + roles),
        [two_b],
        (nums, low_out, s_out, se_out, *amp_roles),
    )
    cc_from_out = outer(cc_out)

    def order_body(nums, *refs):
        amp_refs, ordered_refs = refs[:roles], refs[-pairs:]
        role = lax.axis_index("role")
        for m in range(roles):
            at = whole(nums[ROLE_PAIR + (role ^ m)])
            for q, ordered_ref in enumerate(ordered_refs):

                @pl.when(at == q)
                def _():
                    ordered_ref[:virt, :] = amp_refs[m][...]

        for ordered_ref in ordered_refs:
            ordered_ref[virt:, :] = jnp.zeros((riders, virt), BF16)

    ordered = call(
        order_body,
        [SMEM] + [VMEM] * roles,
        [longer] * pairs,
        (nums, *amp_roles),
    )
    ordered_in = [inner(x) for x in ordered]

    def extra_body(nums, coeff_ref, in_ref, after_ref, s_ref, s_in_ref):
        @pl.when(lax.axis_index("role") > 0)
        def _():
            x = coeff_ref[whole(nums[EXTRA])]
            overlaps(x, coeff_ref, s_ref)
            overlaps(x, in_ref, s_in_ref)

    se_own, se_in = call(
        extra_body,
        [SMEM, VMEM, VMEM, ANY],
        [all_s, all_s],
        (nums, coeff, coeff_in, cc_out),
    )

    def own_again_body(nums, k_ref, s_ref, s_in_ref, se_ref, se_in_ref, *refs):
        amp_refs, amp_in_refs, k_refs = refs[:pairs], refs[pairs : 2 * pairs], refs[2 * pairs : -2]
        role = lax.axis_index("role")

        def rest(pair, k, of_s, of_s_in, at):
            amp = amp_refs[0][:virt, :]
            for q in range(1, pairs):
                amp = jnp.where(pair == q, amp_refs[q][:virt, :], amp)
            right = k + mxu(k.astype(BF16), amp, NN) * virt_scale
            total = right + mxu(amp.T, right.astype(BF16), NN) * virt_scale
            for first, of, of_amps in ((at, of_s, amp_refs), (at + pairs, of_s_in, amp_in_refs)):
                parts = [(q, nums[first + q], of_amps[q][:virt, :]) for q in range(pairs)]
                total += coupled(of, parts)
            return amp.astype(F32) - total

        @pl.when(role > 0)
        def _():
            refs[-2][...] = rest(whole(nums[MINE]), k_ref[...], s_ref, s_in_ref, own_weights)
            k = k_refs[0][:virt, :].astype(F32)
            for s in range(2, roles):
                k = jnp.where(role == s, k_refs[s - 1][:virt, :].astype(F32), k)
            refs[-1][...] = rest(whole(nums[EXTRA]), k, se_ref, se_in_ref, own_weights + 2 * pairs)

    rest, rest_extra = call(
        own_again_body,
        [SMEM] + [VMEM] * (5 + 2 * pairs + roles - 1),
        [sq_f, sq_f],
        (nums, k_first, s_own, s_in, se_own, se_in, *ordered, *ordered_in, *k_extras),
    )

    def last_body(
        nums, coeff_ref, gain_ref, gain_extra_ref, rest_ref, rest_extra_ref, c_ref, amp_ref, orb_ref
    ):
        role = lax.axis_index("role")

        def store(slot, here, gain, rest, pair):
            @pl.when(here)
            def _():
                amp = (gain[...] * (rest[...] - c_ref[slot].astype(F32))).astype(BF16)
                amp_ref[slot] = amp
                x = coeff_ref[pair]
                orb_ref[slot] = (x.astype(F32) + mxu(x, amp, NN) * virt_scale).astype(BF16)

            @pl.when(jnp.logical_not(here))
            def _():
                amp_ref[slot] = jnp.zeros(square, BF16)
                orb_ref[slot] = jnp.zeros((pao, virt), BF16)

        store(0, role > 0, gain_ref, rest_ref, whole(nums[MINE]))
        store(1, role == whole(nums[OWNER]), gain_extra_ref, rest_extra_ref, whole(nums[EXTRA]))

    amps_out, dressed_out = call(
        last_body,
        [SMEM] + [VMEM] * 6,
        [(VMEM, (slots, virt, virt), BF16), (VMEM, (slots, pao, virt), BF16)],
        (nums, coeff, gain, gain_extra, rest, rest_extra, cc_from_out),
    )
    return amps_out, dressed_out


def solution(mesh):
    in_specs = (
        P("pairs", None, None),
        P("pairs", None, None),
        P("pairs", None, None),
        P("pairs", None),
        P(),
        P("pairs"),
        P("pairs", None),
        P("pairs", None),
        P("pairs", None),
        P("pairs"),
    )
    out_specs = (P(("role", "pairs"), None, None), P(("role", "pairs"), None, None))
    return jax.shard_map(local, mesh=mesh, in_specs=in_specs, out_specs=out_specs, check_vma=False)
```

```python
import math

import jax
import jax.numpy as jnp
from jax import lax
from jax.experimental import pallas as pl
from jax.experimental.pallas import tpu as pltpu
from jax.sharding import PartitionSpec as P

F32 = jnp.float32
BF16 = jnp.bfloat16
I32 = jnp.int32
NN = ((1,), (0,))
NT = ((1,), (1,))

VMEM = pl.BlockSpec(memory_space=pltpu.VMEM)
SMEM = pl.BlockSpec(memory_space=pltpu.SMEM)
ANY = pl.BlockSpec(memory_space=pl.ANY)
HBM = pl.BlockSpec(memory_space=pltpu.HBM)

MINE, EXTRA, OWNER, FIRST, SECOND, WHOSE, NV_MINE, NV_EXTRA, OCC_MINE, OCC_EXTRA, ROLE_PAIR = range(11)


def whole(number):
    return number.astype(jnp.int32)


def mxu(a, b, dims):
    return lax.dot_general(a, b, (dims, ((), ())), preferred_element_type=F32)


def call(body, ins, outs, args, scratch=(), vmem=48):
    return pl.pallas_call(
        body,
        in_specs=ins,
        out_specs=[spec for spec, _, _ in outs],
        out_shape=[jax.ShapeDtypeStruct(shape, dtype) for _, shape, dtype in outs],
        scratch_shapes=list(scratch),
        cost_estimate=pl.CostEstimate(flops=1, bytes_accessed=1, transcendentals=0),
        compiler_params=pltpu.CompilerParams(vmem_limit_bytes=vmem * 1024 * 1024),
    )(*args)


def local(
    three_index, coeff, amps, eps_virt, eps_occ, nvirt, pair_occ, partners, coupling, pair_owner
):
    columns = lax.axis_size("pairs")
    roles = lax.axis_size("role")
    occ_block, aux, pao = three_index.shape
    pairs, _, virt = coeff.shape
    partner_count = partners.shape[1]
    slots = 2
    assert roles == pairs and pairs % 2 == 0 and columns % 2 == 0 and virt % 2 == 0
    tile = min(256, aux)
    pao_scale = 1.0 / math.sqrt(pao)
    aux_scale = 1.0 / math.sqrt(aux)
    virt_scale = 1.0 / math.sqrt(virt)
    square = (virt, virt)
    part = virt // 2
    sq_b = (VMEM, square, BF16)
    sq_f = (VMEM, square, F32)
    two_b = (VMEM, (2, virt, virt), BF16)
    all_s = (VMEM, (pairs, virt, virt), BF16)
    half = (VMEM, (aux, virt), BF16)

    inner_of = [i ^ 1 for i in range(columns)]
    outer_of = [(i + (1 if i % 2 else -1)) % columns for i in range(columns)]

    def inner(x):
        return lax.ppermute(x, "pairs", list(enumerate(inner_of)))

    def outer(x):
        return lax.ppermute(x, "pairs", list(enumerate(outer_of)))

    def swap(x, by):
        return lax.ppermute(x, "role", [(i, i ^ by) for i in range(roles)])

    three_in, coeff_in, amps_in = inner(three_index), inner(coeff), inner(amps)

    def pairs_of_roles(owner_ref):
        of_role = [jnp.int32(0)] * roles
        for p in range(pairs):
            earlier = jnp.int32(0)
            for o in range(p):
                earlier += (owner_ref[o] == owner_ref[p]).astype(I32)
            for s in range(roles):
                hit = (earlier == 0) & (owner_ref[p] == s) if s else earlier == 1
                of_role[s] = jnp.where(hit, p, of_role[s])
        return of_role

    def pick(numbers, at):
        chosen = numbers[0]
        for s in range(1, len(numbers)):
            chosen = jnp.where(at == s, numbers[s], chosen)
        return chosen

    weights = 2 * pairs
    place_at, mine_at, extra_at = 2 * weights, 2 * weights + 1, 2 * weights + 2
    riders = 16
    longer = (VMEM, (virt + riders, virt), BF16)
    own_weights = ROLE_PAIR + roles

    def plan_body(
        owner_hbm, occ_hbm, partner_hbm, coupling_hbm, eps_hbm, nvirt_hbm, coeff_hbm,
        low_ref, high_ref, nums,
        owner_ref, occ_ref, partner_ref, coupling_ref, eps_ref, nvirt_ref, near_w, sems,
    ):
        small = [
            pltpu.make_async_copy(source, target, sems.at[at])
            for at, (source, target) in enumerate(
                (
                    (owner_hbm, owner_ref),
                    (occ_hbm, occ_ref),
                    (partner_hbm, partner_ref),
                    (coupling_hbm, coupling_ref),
                    (eps_hbm, eps_ref),
                    (nvirt_hbm, nvirt_ref),
                )
            )
        ]
        for copy in small:
            copy.start()
        role = lax.axis_index("role")
        column = lax.axis_index("pairs")
        small[0].wait()
        of_role = pairs_of_roles(owner_ref)
        extra = of_role[0]
        mine = pick(of_role, role)
        large = [
            pltpu.make_async_copy(coeff_hbm.at[mine, :, pl.ds(0, part)], low_ref.at[pl.ds(0, pao)], sems.at[6]),
            pltpu.make_async_copy(coeff_hbm.at[mine, :, pl.ds(part, part)], high_ref, sems.at[7]),
        ]
        for copy in large:
            copy.start()
        for copy in small[1:]:
            copy.wait()
        nums[MINE] = mine.astype(F32)
        nums[EXTRA] = extra.astype(F32)
        nums[OWNER] = owner_ref[extra].astype(F32)
        for s in range(roles):
            nums[ROLE_PAIR + s] = of_role[s].astype(F32)
        nums[NV_MINE] = nvirt_ref[mine].astype(F32)
        nums[NV_EXTRA] = nvirt_ref[extra].astype(F32)
        nums[FIRST] = (occ_ref[0, mine] - column * occ_block).astype(F32)
        odd = lax.rem(column, 2) == 1
        inner_at = jnp.where(odd, 0, 2)
        outer_at = 2 - inner_at
        occ_all = occ_block * columns
        second = lax.rem(occ_ref[1, mine] - (column - 1) * occ_block + occ_all, occ_all)
        block = (second >= occ_block).astype(I32) + (second >= 2 * occ_block).astype(I32)
        place = (second - block * occ_block).astype(F32)
        nums[SECOND] = place
        lane = lax.broadcasted_iota(I32, (riders, part), 1)
        row = lax.broadcasted_iota(I32, (riders, part), 0)
        told = jnp.where(lane == place_at, place, 0.0)
        told = jnp.where(lane == mine_at, mine.astype(F32), told)
        told = jnp.where(lane == extra_at, extra.astype(F32), told)
        nums[WHOSE] = jnp.where(block == 1, 0, jnp.where(block == inner_at, 1, 2)).astype(F32)
        nums[OCC_MINE] = eps_ref[occ_ref[0, mine]] + eps_ref[occ_ref[1, mine]]
        nums[OCC_EXTRA] = eps_ref[occ_ref[0, extra]] + eps_ref[occ_ref[1, extra]]
        pair_all = pairs * columns
        for which, pair in enumerate((mine, extra)):
            for q in range(3 * pairs):
                near_w[q] = jnp.float32(0)
            for k in range(partner_count):
                at = lax.rem(partner_ref[pair, k] - (column - 1) * pairs + pair_all, pair_all)
                near_w[at] += coupling_ref[pair, k]
            for q in range(pairs):
                to = which * pairs + q
                nums[own_weights + to] = near_w[pairs + q]
                nums[own_weights + weights + to] = near_w[inner_at * pairs + q]
                told = jnp.where(lane == to, near_w[outer_at * pairs + q], told)
                told = jnp.where(lane == weights + to, near_w[inner_at * pairs + q], told)
        coarse = told.astype(BF16).astype(F32)
        middle = (told - coarse).astype(BF16).astype(F32)
        fine = told - coarse - middle
        told = jnp.where(row == 0, coarse, jnp.where(row == 1, middle, jnp.where(row == 2, fine, 0.0)))
        low_ref[pao:, :] = told.astype(BF16)
        for copy in large:
            copy.wait()

    rode = (VMEM, (pao + riders, part), BF16)
    x_low, x_high, nums = call(
        plan_body,
        [HBM] * 7,
        [rode, (VMEM, (pao, part), BF16), (SMEM, (own_weights + 2 * weights,), F32)],
        (pair_owner, pair_occ.T, partners, coupling, eps_occ, nvirt, coeff),
        scratch=[
            pltpu.SMEM(pair_owner.shape, I32),
            pltpu.SMEM(pair_occ.shape[::-1], I32),
            pltpu.SMEM(partners.shape, I32),
            pltpu.SMEM(coupling.shape, F32),
            pltpu.SMEM(eps_occ.shape, F32),
            pltpu.SMEM(nvirt.shape, I32),
            pltpu.SMEM((3 * pairs,), F32),
            pltpu.SemaphoreType.DMA((8,)),
        ],
        vmem=60,
    )
    low_out, high_out, low_in = outer(x_low), outer(x_high), inner(x_low)

    def told_of(low_ref):
        rows = low_ref[pao:, :].astype(F32)
        return rows[0:1] + rows[1:2] + rows[2:3]

    def overlaps(x, coeff_ref, out_ref):
        turned = x.T
        for q in range(pairs):
            s = mxu(turned, coeff_ref[q], NN) * (1.0 / pao)
            out_ref[q] = s.astype(BF16)

    def coupled(s_ref, parts):
        total = None
        for at, weight, amp in parts:
            s = s_ref[at]
            u = mxu(s, amp, NN).astype(BF16)
            term = weight * mxu(u, s, NT)
            total = term if total is None else total + term
        return total

    tiles = [pl.ds(at, tile) for at in range(0, aux, tile)]

    def half_into(y_ref, three_ref, at_occ, x):
        for rows in tiles:
            y_ref[rows, :] = (mxu(three_ref[at_occ, rows, :], x, NN) * pao_scale).astype(BF16)

    def fetch_body(three_ref, after_ref, held_ref, sem):
        copy = pltpu.make_async_copy(three_ref, held_ref, sem)
        copy.start()
        copy.wait()

    (blocks,) = call(
        fetch_body,
        [ANY, ANY],
        [(VMEM, three_index.shape, BF16)],
        (three_index, nums),
        scratch=[pltpu.SemaphoreType.DMA],
        vmem=50,
    )

    def outer_low_body(three_ref, x_ref, y_ref):
        half_into(y_ref, three_ref, whole(told_of(x_ref)[0, place_at]), x_ref[:pao, :])
        y_ref[aux:, :] = jnp.zeros((2 * riders, part), BF16)

    (y_low,) = call(
        outer_low_body,
        [VMEM, VMEM],
        [(VMEM, (aux + 2 * riders, part), BF16)],
        (blocks, low_out),
    )
    y_low_from_out = outer(y_low)

    def outer_high_body(three_ref, low_ref, x_ref, after_ref, y_ref):
        half_into(y_ref, three_ref, whole(told_of(low_ref)[0, place_at]), x_ref[...])
        y_ref[aux:, :] = jnp.zeros((riders, part), BF16)

    (y_high,) = call(
        outer_high_body,
        [VMEM, VMEM, VMEM, ANY],
        [(VMEM, (aux + riders, part), BF16)],
        (blocks, low_out, high_out, y_low),
    )
    y_high_from_out = outer(y_high)

    def outer_body(coeff_ref, amps_ref, low_ref, high_ref, after_ref, s_ref, c_ref, x_ref):
        x_ref[:, :part] = low_ref[:pao, :]
        x_ref[:, part:] = high_ref[...]
        overlaps(x_ref[...], coeff_ref, s_ref)
        told = told_of(low_ref)
        c = coupled(s_ref, [(q, told[0, q], amps_ref[q]) for q in range(pairs)])
        c_ref[:virt, :] = c.astype(BF16)
        c_ref[virt:, :] = jnp.zeros((3 * riders, virt), BF16)

    s_out, c_out = call(
        outer_body,
        [VMEM, VMEM, VMEM, VMEM, ANY],
        [all_s, (VMEM, (virt + 3 * riders, virt), BF16)],
        (coeff, amps, low_out, high_out, y_high),
        scratch=[pltpu.VMEM((pao, virt), BF16)],
    )
    c_from_out = outer(c_out)

    def own_half_body(
        nums, three_ref, three_in_ref, coeff_ref, after_ref, first_ref, second_ref, extra_ref, block_ref, sem
    ):
        x = coeff_ref[whole(nums[MINE])]
        extra_ref[:pao, :] = coeff_ref[whole(nums[EXTRA])]
        extra_ref[pao:, :] = jnp.zeros((2 * riders, virt), BF16)
        whose, second = whole(nums[WHOSE]), whole(nums[SECOND])
        copy = pltpu.make_async_copy(three_in_ref.at[second], block_ref.at[0], sem)

        @pl.when(whose == 1)
        def _():
            copy.start()

        turned = x.T
        first = whole(nums[FIRST])
        for rows in tiles:
            first_ref[:, rows] = (mxu(turned, three_ref[first, rows, :], NT) * pao_scale).astype(BF16)

        @pl.when(whose == 0)
        def _():
            half_into(second_ref, three_ref, second, x)

        @pl.when(whose == 1)
        def _():
            copy.wait()
            half_into(second_ref, block_ref, 0, x)

    first_t, second, x_extra = call(
        own_half_body,
        [SMEM, VMEM, ANY, VMEM, ANY],
        [
            (VMEM, (virt, aux), BF16),
            (VMEM, (aux, virt), BF16),
            (VMEM, (pao + 2 * riders, virt), BF16),
        ],
        (nums, blocks, three_in, coeff, c_out),
        scratch=[pltpu.VMEM((1, aux, pao), BF16), pltpu.SemaphoreType.DMA],
    )
    x_extra_out = outer(x_extra)

    def own_body(
        nums, coeff_ref, coeff_in_ref, amps_ref, amps_in_ref, eps_ref, after_ref,
        s_ref, c_ref, gain_ref, gain_extra_ref, s_in_ref,
    ):
        mine, extra = whole(nums[MINE]), whole(nums[EXTRA])
        x = coeff_ref[mine]
        total = None
        for at, of_s, of_coeff, of_amps in (
            (own_weights, s_ref, coeff_ref, amps_ref),
            (own_weights + weights, s_in_ref, coeff_in_ref, amps_in_ref),
        ):
            overlaps(x, of_coeff, of_s)
            c = coupled(of_s, [(q, nums[at + q], of_amps[q]) for q in range(pairs)])
            total = c if total is None else total + c
        c_ref[...] = total

        def gain(pair, count, occupied):
            row = jnp.broadcast_to(eps_ref[pl.ds(pair, 1), :], square)
            energy = row + row.T - occupied
            inside = (lax.broadcasted_iota(I32, square, 0) < count) & (
                lax.broadcasted_iota(I32, square, 1) < count
            )
            return jnp.where(inside, 1.0 / (energy + 1.0), 0.0)

        gain_ref[...] = gain(mine, whole(nums[NV_MINE]), nums[OCC_MINE])
        gain_extra_ref[...] = gain(extra, whole(nums[NV_EXTRA]), nums[OCC_EXTRA])

    s_own, c_own, gain, gain_extra = call(
        own_body,
        [SMEM] + [VMEM] * 5 + [ANY],
        [all_s, sq_f, sq_f, sq_f],
        (nums, coeff, coeff_in, amps, amps_in, eps_virt, c_out),
        scratch=[pltpu.VMEM((pairs, virt, virt), BF16)],
    )

    def more_body(nums, coeff_ref, in_ref, low_ref, after_ref, se_ref, s_in_ref, se_in_ref):
        @pl.when(lax.axis_index("role") > 0)
        def _():
            told = told_of(low_ref)
            overlaps(coeff_ref[whole(nums[EXTRA])], coeff_ref, se_ref)
            overlaps(in_ref[whole(told[0, mine_at])], coeff_ref, s_in_ref)
            overlaps(in_ref[whole(told[0, extra_at])], coeff_ref, se_in_ref)

    se_own, s_in, se_in = call(
        more_body,
        [SMEM, VMEM, VMEM, VMEM, ANY],
        [all_s, all_s, all_s],
        (nums, coeff, coeff_in, low_in, c_own),
    )

    def first_body(
        nums, first_ref, second_ref, low_ref, high_ref, amps_ref, c_ref, co_ref, gain_ref, after_ref,
        amp_ref, k_ref,
    ):
        first = first_ref[...]
        outside = whole(nums[WHOSE]) == 2

        @pl.when(outside)
        def _():
            k_ref[:, :part] = mxu(first, low_ref[:aux, :], NN) * aux_scale
            k_ref[:, part:] = mxu(first, high_ref[:aux, :], NN) * aux_scale

        @pl.when(jnp.logical_not(outside))
        def _():
            k_ref[...] = mxu(first, second_ref[...], NN) * aux_scale

        old = amps_ref[whole(nums[MINE])].astype(F32)
        c = c_ref[...] + co_ref[:virt, :].astype(F32)
        amp_ref[...] = (gain_ref[...] * (old - k_ref[...] - c)).astype(BF16)

    amp, k_first = call(
        first_body,
        [SMEM] + [VMEM] * 8 + [ANY],
        [sq_b, sq_f],
        (
            nums, first_t, second, y_low_from_out, y_high_from_out,
            amps, c_own, c_from_out, gain, se_own,
        ),
    )
    amp_roles = [amp] + [swap(amp, m) for m in range(1, roles)]

    def rest_body(amp_ref, k_ref, out_ref, out_b_ref):
        amp = amp_ref[...]
        k = k_ref[...]
        right = k + mxu(k.astype(BF16), amp, NN) * virt_scale
        both = right + mxu(amp.T, right.astype(BF16), NN) * virt_scale
        rest = amp.astype(F32) - both
        out_ref[...] = rest
        out_b_ref[:virt, :] = rest.astype(BF16)
        out_b_ref[virt:, :] = jnp.zeros((riders, virt), BF16)

    rest, rest_b = call(rest_body, [VMEM, VMEM], [sq_f, longer], (amp, k_first))
    rests = [lax.ppermute(rest_b, "role", [(0, s)]) for s in range(1, roles)]

    def extra_out_body(coeff_ref, x_ref, after_ref, s_ref):
        @pl.when(lax.axis_index("role") > 0)
        def _():
            overlaps(x_ref[:pao, :], coeff_ref, s_ref)

    (se_out,) = call(
        extra_out_body,
        [VMEM, VMEM, ANY],
        [all_s],
        (coeff, x_extra_out, amp),
    )

    def parts_of(nums, weight_of, amp_refs):
        role = lax.axis_index("role")
        parts = []
        for m in range(roles):
            at = whole(nums[ROLE_PAIR + (role ^ m)])
            parts.append((at, weight_of(at), amp_refs[m][...]))
        return parts

    def told_weight(told, first):
        return lambda at: pick([told[:, first + q : first + q + 1] for q in range(pairs)], at)

    def outer_again_body(nums, low_ref, s_ref, se_ref, *refs):
        amp_refs, c_ref = refs[:roles], refs[-1]

        @pl.when(lax.axis_index("role") > 0)
        def _():
            told = told_of(low_ref)
            for slot, of_s in enumerate((s_ref, se_ref)):
                parts = parts_of(nums, told_weight(told, slot * pairs), amp_refs)
                c_ref[slot] = coupled(of_s, parts).astype(BF16)

    (cc_out,) = call(
        outer_again_body,
        [SMEM] + [VMEM] * (3 + roles),
        [two_b],
        (nums, low_out, s_out, se_out, *amp_roles),
    )
    cc_from_out = outer(cc_out)

    def inner_again_body(nums, low_ref, s_ref, se_ref, *refs):
        amp_refs, c_refs = refs[:roles], refs[-2:]

        @pl.when(lax.axis_index("role") > 0)
        def _():
            told = told_of(low_ref)
            for slot, of_s, c_ref in zip(range(2), (s_ref, se_ref), c_refs):
                parts = parts_of(nums, told_weight(told, weights + slot * pairs), amp_refs)
                c_ref[:virt, :] = coupled(of_s, parts).astype(BF16)
                c_ref[virt:, :] = jnp.zeros((riders, virt), BF16)

    c_in, ce_in = call(
        inner_again_body,
        [SMEM] + [VMEM] * (3 + roles) + [ANY],
        [longer, longer],
        (nums, low_in, s_in, se_in, *amp_roles, cc_out),
    )
    c_from_in = inner(c_in)

    def own_again_body(nums, rest_ref, s_ref, se_ref, *refs):
        amp_refs, (after_ref, out_ref, out_extra_ref) = refs[:roles], refs[-3:]

        @pl.when(lax.axis_index("role") > 0)
        def _():
            parts = parts_of(nums, lambda at: nums[own_weights + at], amp_refs)
            out_ref[...] = rest_ref[...] - coupled(s_ref, parts)
            parts = parts_of(nums, lambda at: nums[own_weights + pairs + at], amp_refs)
            out_extra_ref[...] = -coupled(se_ref, parts)

    rest, rest_extra = call(
        own_again_body,
        [SMEM] + [VMEM] * (3 + roles) + [ANY],
        [sq_f, sq_f],
        (nums, rest, s_own, se_own, *amp_roles, c_in),
    )

    def tell_body(last_ref, *refs):
        refs[-1][...] = last_ref[...]

    (ce_in,) = call(tell_body, [VMEM] + [ANY] * roles, [longer], (ce_in, rest, *rests))
    ce_from_in = inner(ce_in)

    def last_body(
        nums, coeff_ref, gain_ref, gain_extra_ref, rest_ref, rest_extra_ref, co_ref, ci_ref, cei_ref, *refs
    ):
        rest_refs, (amp_out, orb_out, amp_ref, orb_ref, sems) = refs[: roles - 1], refs[roles - 1 :]
        role = lax.axis_index("role")
        copies = []

        def send(source, target):
            copies.append(pltpu.make_async_copy(source, target, sems.at[len(copies)]))
            copies[-1].start()

        def store(slot, here, gain, rest, c_in, pair):
            @pl.when(here)
            def _():
                total = rest[...] - co_ref[slot].astype(F32) - c_in[:virt, :].astype(F32)
                for s in range(1, roles):
                    if slot:
                        come = rest_refs[s - 1][:virt, :].astype(F32)
                        total += jnp.where(role == s, come, 0.0)
                amp_ref[slot] = (gain[...] * total).astype(BF16)

            @pl.when(jnp.logical_not(here))
            def _():
                amp_ref[slot] = jnp.zeros(square, BF16)

            send(amp_ref.at[slot], amp_out.at[slot])
            for at in range(0, pao, virt):
                rows = pl.ds(at, virt)

                @pl.when(here)
                def _():
                    x = coeff_ref[pair, rows, :]
                    dressed = x.astype(F32) + mxu(x, amp_ref[slot], NN) * virt_scale
                    orb_ref[slot, rows, :] = dressed.astype(BF16)

                @pl.when(jnp.logical_not(here))
                def _():
                    orb_ref[slot, rows, :] = jnp.zeros((virt, virt), BF16)

                send(orb_ref.at[slot, rows], orb_out.at[slot, rows])

        store(0, role > 0, gain_ref, rest_ref, ci_ref, whole(nums[MINE]))
        has_extra = role == whole(nums[OWNER])
        store(1, has_extra, gain_extra_ref, rest_extra_ref, cei_ref, whole(nums[EXTRA]))
        for copy in copies:
            copy.wait()

    amps_out, dressed_out = call(
        last_body,
        [SMEM] + [VMEM] * (8 + roles - 1),
        [(ANY, (slots, virt, virt), BF16), (ANY, (slots, pao, virt), BF16)],
        (
            nums, coeff, gain, gain_extra, rest, rest_extra,
            cc_from_out, c_from_in, ce_from_in, *rests,
        ),
        scratch=[
            pltpu.VMEM((slots, virt, virt), BF16),
            pltpu.VMEM((slots, pao, virt), BF16),
            pltpu.SemaphoreType.DMA((slots * (1 + pao // virt),)),
        ],
    )
    return amps_out, dressed_out


def solution(mesh):
    in_specs = (
        P("pairs", None, None),
        P("pairs", None, None),
        P("pairs", None, None),
        P("pairs", None),
        P(),
        P("pairs"),
        P("pairs", None),
        P("pairs", None),
        P("pairs", None),
        P("pairs"),
    )
    out_specs = (P(("role", "pairs"), None, None), P(("role", "pairs"), None, None))
    return jax.shard_map(local, mesh=mesh, in_specs=in_specs, out_specs=out_specs, check_vma=False)
```

```python
import math

import jax
import jax.numpy as jnp
from jax import lax
from jax.experimental import pallas as pl
from jax.experimental.pallas import tpu as pltpu
from jax.sharding import PartitionSpec as P

F32 = jnp.float32
BF16 = jnp.bfloat16
I32 = jnp.int32
NN = ((1,), (0,))
NT = ((1,), (1,))

VMEM = pl.BlockSpec(memory_space=pltpu.VMEM)
SMEM = pl.BlockSpec(memory_space=pltpu.SMEM)
ANY = pl.BlockSpec(memory_space=pl.ANY)
HBM = pl.BlockSpec(memory_space=pltpu.HBM)

MINE, EXTRA, OWNER, FIRST, SECOND, WHOSE, NV_MINE, NV_EXTRA, OCC_MINE, OCC_EXTRA, ROLE_PAIR = range(11)


def whole(number):
    return number.astype(jnp.int32)


def mxu(a, b, dims):
    return lax.dot_general(a, b, (dims, ((), ())), preferred_element_type=F32)


def call(body, ins, outs, args, scratch=(), vmem=48):
    return pl.pallas_call(
        body,
        in_specs=ins,
        out_specs=[spec for spec, _, _ in outs],
        out_shape=[jax.ShapeDtypeStruct(shape, dtype) for _, shape, dtype in outs],
        scratch_shapes=list(scratch),
        cost_estimate=pl.CostEstimate(flops=1, bytes_accessed=1, transcendentals=0),
        compiler_params=pltpu.CompilerParams(vmem_limit_bytes=vmem * 1024 * 1024),
    )(*args)


def local(
    three_index, coeff, amps, eps_virt, eps_occ, nvirt, pair_occ, partners, coupling, pair_owner
):
    columns = lax.axis_size("pairs")
    roles = lax.axis_size("role")
    occ_block, aux, pao = three_index.shape
    pairs, _, virt = coeff.shape
    partner_count = partners.shape[1]
    slots = 2
    assert roles == pairs and pairs % 2 == 0 and columns % 2 == 0 and virt % 2 == 0 and pao % roles == 0 and roles == 4
    tile = min(256, aux)
    pao_scale = 1.0 / math.sqrt(pao)
    aux_scale = 1.0 / math.sqrt(aux)
    virt_scale = 1.0 / math.sqrt(virt)
    square = (virt, virt)
    part = virt // 2
    quarter = pao // roles
    sq_b = (VMEM, square, BF16)
    sq_f = (VMEM, square, F32)
    two_b = (VMEM, (2, virt, virt), BF16)
    all_s = (VMEM, (pairs, virt, virt), BF16)
    half = (VMEM, (aux, virt), BF16)

    inner_of = [i ^ 1 for i in range(columns)]
    outer_of = [(i + (1 if i % 2 else -1)) % columns for i in range(columns)]

    def inner(x):
        return lax.ppermute(x, "pairs", list(enumerate(inner_of)))

    def outer(x):
        return lax.ppermute(x, "pairs", list(enumerate(outer_of)))

    def swap(x, by):
        return lax.ppermute(x, "role", [(i, i ^ by) for i in range(roles)])

    three_in, coeff_in, amps_in = inner(three_index), inner(coeff), inner(amps)

    def pairs_of_roles(owner_ref):
        of_role = [jnp.int32(0)] * roles
        for p in range(pairs):
            earlier = jnp.int32(0)
            for o in range(p):
                earlier += (owner_ref[o] == owner_ref[p]).astype(I32)
            for s in range(roles):
                hit = (earlier == 0) & (owner_ref[p] == s) if s else earlier == 1
                of_role[s] = jnp.where(hit, p, of_role[s])
        return of_role

    def pick(numbers, at):
        chosen = numbers[0]
        for s in range(1, len(numbers)):
            chosen = jnp.where(at == s, numbers[s], chosen)
        return chosen

    weights = 2 * pairs
    place_at, mine_at, extra_at = 2 * weights, 2 * weights + 1, 2 * weights + 2
    riders = 16
    longer = (VMEM, (virt + riders, virt), BF16)
    own_weights = ROLE_PAIR + roles

    def plan_body(
        owner_hbm, occ_hbm, partner_hbm, coupling_hbm, eps_hbm, nvirt_hbm, coeff_hbm,
        low_out, high_out, nums,
        owner_ref, occ_ref, partner_ref, coupling_ref, eps_ref, nvirt_ref, near_w,
        lows_ref, high_ref, quarter_ref, told_ref, sems,
    ):
        small = [
            pltpu.make_async_copy(source, target, sems.at[at])
            for at, (source, target) in enumerate(
                (
                    (owner_hbm, owner_ref),
                    (occ_hbm, occ_ref),
                    (partner_hbm, partner_ref),
                    (coupling_hbm, coupling_ref),
                    (eps_hbm, eps_ref),
                    (nvirt_hbm, nvirt_ref),
                )
            )
        ]
        lows = pltpu.make_async_copy(coeff_hbm.at[:, :, pl.ds(0, part)], lows_ref, sems.at[6])
        for copy in (*small, lows):
            copy.start()
        role = lax.axis_index("role")
        column = lax.axis_index("pairs")
        small[0].wait()
        of_role = pairs_of_roles(owner_ref)
        extra = of_role[0]
        mine = pick(of_role, role)
        rows = pl.ds(pl.multiple_of(role * quarter, quarter), quarter)
        large = [
            pltpu.make_async_copy(coeff_hbm.at[mine, :, pl.ds(part, part)], high_ref, sems.at[7])
        ]
        for half in range(2):
            source = coeff_hbm.at[extra, rows, pl.ds(half * part, part)]
            target = quarter_ref.at[pl.ds(half * quarter, quarter)]
            large.append(pltpu.make_async_copy(source, target, sems.at[8 + half]))
        for copy in large:
            copy.start()
        lows.wait()
        leaving = [
            pltpu.make_async_copy(lows_ref.at[mine], low_out.at[pl.ds(0, pao)], sems.at[10]),
            pltpu.make_async_copy(told_ref, low_out.at[pl.ds(pao, riders)], sems.at[11]),
            pltpu.make_async_copy(high_ref, high_out, sems.at[12]),
            pltpu.make_async_copy(quarter_ref, low_out.at[pl.ds(pao + riders, 2 * quarter)], sems.at[13]),
        ]
        leaving[0].start()
        for copy in small[1:]:
            copy.wait()
        nums[MINE] = mine.astype(F32)
        nums[EXTRA] = extra.astype(F32)
        nums[OWNER] = owner_ref[extra].astype(F32)
        for s in range(roles):
            nums[ROLE_PAIR + s] = of_role[s].astype(F32)
        nums[NV_MINE] = nvirt_ref[mine].astype(F32)
        nums[NV_EXTRA] = nvirt_ref[extra].astype(F32)
        nums[FIRST] = (occ_ref[0, mine] - column * occ_block).astype(F32)
        odd = lax.rem(column, 2) == 1
        inner_at = jnp.where(odd, 0, 2)
        outer_at = 2 - inner_at
        occ_all = occ_block * columns
        second = lax.rem(occ_ref[1, mine] - (column - 1) * occ_block + occ_all, occ_all)
        block = (second >= occ_block).astype(I32) + (second >= 2 * occ_block).astype(I32)
        place = (second - block * occ_block).astype(F32)
        nums[SECOND] = place
        lane = lax.broadcasted_iota(I32, (riders, part), 1)
        row = lax.broadcasted_iota(I32, (riders, part), 0)
        told = jnp.where(lane == place_at, place, 0.0)
        told = jnp.where(lane == mine_at, mine.astype(F32), told)
        told = jnp.where(lane == extra_at, extra.astype(F32), told)
        nums[WHOSE] = jnp.where(block == 1, 0, jnp.where(block == inner_at, 1, 2)).astype(F32)
        nums[OCC_MINE] = eps_ref[occ_ref[0, mine]] + eps_ref[occ_ref[1, mine]]
        nums[OCC_EXTRA] = eps_ref[occ_ref[0, extra]] + eps_ref[occ_ref[1, extra]]
        pair_all = pairs * columns
        for which, pair in enumerate((mine, extra)):
            for q in range(3 * pairs):
                near_w[q] = jnp.float32(0)
            for k in range(partner_count):
                at = lax.rem(partner_ref[pair, k] - (column - 1) * pairs + pair_all, pair_all)
                near_w[at] += coupling_ref[pair, k]
            for q in range(pairs):
                to = which * pairs + q
                nums[own_weights + to] = near_w[pairs + q]
                nums[own_weights + weights + to] = near_w[inner_at * pairs + q]
                told = jnp.where(lane == to, near_w[outer_at * pairs + q], told)
                told = jnp.where(lane == weights + to, near_w[inner_at * pairs + q], told)
        coarse = told.astype(BF16).astype(F32)
        middle = (told - coarse).astype(BF16).astype(F32)
        fine = told - coarse - middle
        told = jnp.where(row == 0, coarse, jnp.where(row == 1, middle, jnp.where(row == 2, fine, 0.0)))
        told_ref[...] = told.astype(BF16)
        leaving[1].start()
        for copy in large:
            copy.wait()
        for copy in leaving[2:]:
            copy.start()
        for copy in leaving:
            copy.wait()

    x_low, x_high, nums = call(
        plan_body,
        [HBM] * 7,
        [
            (ANY, (pao + riders + 2 * quarter, part), BF16),
            (ANY, (pao, part), BF16),
            (SMEM, (own_weights + 2 * weights,), F32),
        ],
        (pair_owner, pair_occ.T, partners, coupling, eps_occ, nvirt, coeff),
        scratch=[
            pltpu.SMEM(pair_owner.shape, I32),
            pltpu.SMEM(pair_occ.shape[::-1], I32),
            pltpu.SMEM(partners.shape, I32),
            pltpu.SMEM(coupling.shape, F32),
            pltpu.SMEM(eps_occ.shape, F32),
            pltpu.SMEM(nvirt.shape, I32),
            pltpu.SMEM((3 * pairs,), F32),
            pltpu.VMEM((pairs, pao, part), BF16),
            pltpu.VMEM((pao, part), BF16),
            pltpu.VMEM((2 * quarter, part), BF16),
            pltpu.VMEM((riders, part), BF16),
            pltpu.SemaphoreType.DMA((14,)),
        ],
        vmem=61,
    )
    low_out, high_out, low_in = outer(x_low), outer(x_high), inner(x_low)

    def told_of(low_ref):
        rows = low_ref[pao : pao + riders, :].astype(F32)
        return rows[0:1] + rows[1:2] + rows[2:3]

    def overlaps(x, coeff_ref, out_ref):
        turned = x.T
        for q in range(pairs):
            s = mxu(turned, coeff_ref[q], NN) * (1.0 / pao)
            out_ref[q] = s.astype(BF16)

    def coupled(s_ref, parts):
        total = None
        for at, weight, amp in parts:
            s = s_ref[at]
            u = mxu(s, amp, NN).astype(BF16)
            term = weight * mxu(u, s, NT)
            total = term if total is None else total + term
        return total

    tiles = [pl.ds(at, tile) for at in range(0, aux, tile)]

    def half_into(y_ref, three_ref, at_occ, x):
        for rows in tiles:
            y_ref[rows, :] = (mxu(three_ref[at_occ, rows, :], x, NN) * pao_scale).astype(BF16)

    def fetch_body(three_ref, *refs):
        held_ref, sem = refs[-2:]
        copy = pltpu.make_async_copy(three_ref, held_ref, sem)
        copy.start()
        copy.wait()

    (blocks,) = call(
        fetch_body,
        [ANY] * 4,
        [(VMEM, three_index.shape, BF16)],
        (three_index, nums, coeff_in, amps_in),
        scratch=[pltpu.SemaphoreType.DMA],
        vmem=50,
    )

    def outer_low_body(three_ref, x_ref, after_ref, y_ref):
        half_into(y_ref, three_ref, whole(told_of(x_ref)[0, place_at]), x_ref[:pao, :])
        y_ref[aux:, :] = jnp.zeros((2 * riders, part), BF16)

    (y_low,) = call(
        outer_low_body,
        [VMEM, VMEM, ANY],
        [(VMEM, (aux + 2 * riders, part), BF16)],
        (blocks, low_out, three_in),
    )
    y_low_from_out = outer(y_low)

    def outer_high_body(three_ref, low_ref, x_ref, after_ref, y_ref, quarter_ref):
        half_into(y_ref, three_ref, whole(told_of(low_ref)[0, place_at]), x_ref[...])
        y_ref[aux:, :] = jnp.zeros((riders, part), BF16)
        quarter_ref[...] = low_ref[pao + riders :, :]

    y_high, quarters = call(
        outer_high_body,
        [VMEM, VMEM, VMEM, ANY],
        [(VMEM, (aux + riders, part), BF16), (VMEM, (2 * quarter, part), BF16)],
        (blocks, low_out, high_out, y_low),
    )
    y_high_from_out = outer(y_high)

    def outer_body(coeff_ref, amps_ref, low_ref, high_ref, after_ref, s_ref, c_ref, x_ref):
        x_ref[:, :part] = low_ref[:pao, :]
        x_ref[:, part:] = high_ref[...]
        overlaps(x_ref[...], coeff_ref, s_ref)
        told = told_of(low_ref)
        c = coupled(s_ref, [(q, told[0, q], amps_ref[q]) for q in range(pairs)])
        c_ref[:virt, :] = c.astype(BF16)
        c_ref[virt:, :] = jnp.zeros((3 * riders, virt), BF16)

    s_out, c_out = call(
        outer_body,
        [VMEM, VMEM, VMEM, VMEM, ANY],
        [all_s, (VMEM, (virt + 3 * riders, virt), BF16)],
        (coeff, amps, low_out, high_out, y_high),
        scratch=[pltpu.VMEM((pao, virt), BF16)],
    )
    c_from_out = outer(c_out)

    def double_body(mine_ref, come_ref, out_ref):
        out_ref[0] = mine_ref[...]
        out_ref[1] = come_ref[...]

    steps = [1 << at for at in range(roles.bit_length() - 1)]
    for step in steps[:-1]:
        shape = (2, *quarters.shape)
        (quarters,) = call(
            double_body, [VMEM, VMEM], [(VMEM, shape, BF16)], (quarters, swap(quarters, step))
        )
    quarters = [quarters, swap(quarters, steps[-1])]

    def own_half_body(
        nums, three_ref, three_in_ref, coeff_ref, after_ref, first_ref, second_ref, block_ref, sem
    ):
        x = coeff_ref[whole(nums[MINE])]
        whose, second = whole(nums[WHOSE]), whole(nums[SECOND])
        copy = pltpu.make_async_copy(three_in_ref.at[second], block_ref.at[0], sem)

        @pl.when(whose == 1)
        def _():
            copy.start()

        turned = x.T
        first = whole(nums[FIRST])
        for rows in tiles:
            first_ref[:, rows] = (mxu(turned, three_ref[first, rows, :], NT) * pao_scale).astype(BF16)

        @pl.when(whose == 0)
        def _():
            half_into(second_ref, three_ref, second, x)

        @pl.when(whose == 1)
        def _():
            copy.wait()
            half_into(second_ref, block_ref, 0, x)

    first_t, second = call(
        own_half_body,
        [SMEM, VMEM, ANY, VMEM, ANY],
        [(VMEM, (virt, aux), BF16), (VMEM, (aux, virt), BF16)],
        (nums, blocks, three_in, coeff, c_out),
        scratch=[pltpu.VMEM((1, aux, pao), BF16), pltpu.SemaphoreType.DMA],
    )
    def own_body(
        nums, coeff_ref, coeff_in_ref, amps_ref, amps_in_ref, eps_ref, after_ref,
        s_ref, c_ref, gain_ref, gain_extra_ref, s_in_ref,
    ):
        mine, extra = whole(nums[MINE]), whole(nums[EXTRA])
        x = coeff_ref[mine]
        total = None
        for at, of_s, of_coeff, of_amps in (
            (own_weights, s_ref, coeff_ref, amps_ref),
            (own_weights + weights, s_in_ref, coeff_in_ref, amps_in_ref),
        ):
            overlaps(x, of_coeff, of_s)
            c = coupled(of_s, [(q, nums[at + q], of_amps[q]) for q in range(pairs)])
            total = c if total is None else total + c
        c_ref[...] = total

        def gain(pair, count, occupied):
            row = jnp.broadcast_to(eps_ref[pl.ds(pair, 1), :], square)
            energy = row + row.T - occupied
            inside = (lax.broadcasted_iota(I32, square, 0) < count) & (
                lax.broadcasted_iota(I32, square, 1) < count
            )
            return jnp.where(inside, 1.0 / (energy + 1.0), 0.0)

        gain_ref[...] = gain(mine, whole(nums[NV_MINE]), nums[OCC_MINE])
        gain_extra_ref[...] = gain(extra, whole(nums[NV_EXTRA]), nums[OCC_EXTRA])

    s_own, c_own, gain, gain_extra = call(
        own_body,
        [SMEM] + [VMEM] * 5 + [ANY],
        [all_s, sq_f, sq_f, sq_f],
        (nums, coeff, coeff_in, amps, amps_in, eps_virt, c_out),
        scratch=[pltpu.VMEM((pairs, virt, virt), BF16)],
    )

    def more_body(nums, coeff_ref, in_ref, low_ref, after_ref, se_ref, s_in_ref, se_in_ref):
        @pl.when(lax.axis_index("role") > 0)
        def _():
            told = told_of(low_ref)
            overlaps(coeff_ref[whole(nums[EXTRA])], coeff_ref, se_ref)
            overlaps(in_ref[whole(told[0, mine_at])], coeff_ref, s_in_ref)
            overlaps(in_ref[whole(told[0, extra_at])], coeff_ref, se_in_ref)

    se_own, s_in, se_in = call(
        more_body,
        [SMEM, VMEM, VMEM, VMEM, ANY],
        [all_s, all_s, all_s],
        (nums, coeff, coeff_in, low_in, c_own),
    )

    def extra_out_body(coeff_ref, after_ref, *refs):
        mine_ref, come_ref, s_ref, x_ref = refs
        role = lax.axis_index("role")

        @pl.when(role > 0)
        def _():
            for m in range(roles):
                part_ref = (mine_ref, come_ref)[m // steps[-1]].at[m % steps[-1]]
                rows = pl.ds(pl.multiple_of((role ^ m) * quarter, quarter), quarter)
                x_ref[rows, :part] = part_ref[:quarter, :]
                x_ref[rows, part:] = part_ref[quarter:, :]
            overlaps(x_ref[...], coeff_ref, s_ref)

    (se_out,) = call(
        extra_out_body,
        [VMEM, ANY, VMEM, VMEM],
        [all_s],
        (coeff, se_own, *quarters),
        scratch=[pltpu.VMEM((pao, virt), BF16)],
    )

    def first_body(
        nums, first_ref, second_ref, low_ref, high_ref, amps_ref, c_ref, co_ref, gain_ref, after_ref,
        amp_ref, k_ref,
    ):
        first = first_ref[...]
        outside = whole(nums[WHOSE]) == 2

        @pl.when(outside)
        def _():
            k_ref[:, :part] = mxu(first, low_ref[:aux, :], NN) * aux_scale
            k_ref[:, part:] = mxu(first, high_ref[:aux, :], NN) * aux_scale

        @pl.when(jnp.logical_not(outside))
        def _():
            k_ref[...] = mxu(first, second_ref[...], NN) * aux_scale

        old = amps_ref[whole(nums[MINE])].astype(F32)
        c = c_ref[...] + co_ref[:virt, :].astype(F32)
        amp_ref[...] = (gain_ref[...] * (old - k_ref[...] - c)).astype(BF16)

    amp, k_first = call(
        first_body,
        [SMEM] + [VMEM] * 8 + [ANY],
        [sq_b, sq_f],
        (
            nums, first_t, second, y_low_from_out, y_high_from_out,
            amps, c_own, c_from_out, gain, se_out,
        ),
    )
    amp_roles = [amp] + [swap(amp, m) for m in range(1, roles)]

    def rest_body(amp_ref, k_ref, out_ref, out_b_ref):
        amp = amp_ref[...]
        k = k_ref[...]
        right = k + mxu(k.astype(BF16), amp, NN) * virt_scale
        both = right + mxu(amp.T, right.astype(BF16), NN) * virt_scale
        rest = amp.astype(F32) - both
        out_ref[...] = rest
        out_b_ref[:virt, :] = rest.astype(BF16)
        out_b_ref[virt:, :] = jnp.zeros((riders, virt), BF16)

    rest, rest_b = call(rest_body, [VMEM, VMEM], [sq_f, longer], (amp, k_first))
    rests = [lax.ppermute(rest_b, "role", [(0, s)]) for s in range(1, roles)]

    def parts_of(nums, weight_of, amp_refs):
        role = lax.axis_index("role")
        parts = []
        for m in range(roles):
            at = whole(nums[ROLE_PAIR + (role ^ m)])
            parts.append((at, weight_of(at), amp_refs[m][...]))
        return parts

    def told_weight(told, first):
        return lambda at: pick([told[:, first + q : first + q + 1] for q in range(pairs)], at)

    def outer_again_body(nums, low_ref, s_ref, se_ref, *refs):
        amp_refs, c_ref = refs[:roles], refs[-1]

        @pl.when(lax.axis_index("role") > 0)
        def _():
            told = told_of(low_ref)
            for slot, of_s in enumerate((s_ref, se_ref)):
                parts = parts_of(nums, told_weight(told, slot * pairs), amp_refs)
                c_ref[slot] = coupled(of_s, parts).astype(BF16)

    (cc_out,) = call(
        outer_again_body,
        [SMEM] + [VMEM] * (3 + roles),
        [two_b],
        (nums, low_out, s_out, se_out, *amp_roles),
    )
    cc_from_out = outer(cc_out)

    def inner_again_body(nums, low_ref, s_ref, se_ref, *refs):
        amp_refs, c_refs = refs[:roles], refs[-2:]

        @pl.when(lax.axis_index("role") > 0)
        def _():
            told = told_of(low_ref)
            for slot, of_s, c_ref in zip(range(2), (s_ref, se_ref), c_refs):
                parts = parts_of(nums, told_weight(told, weights + slot * pairs), amp_refs)
                c_ref[:virt, :] = coupled(of_s, parts).astype(BF16)
                c_ref[virt:, :] = jnp.zeros((riders, virt), BF16)

    c_in, ce_in = call(
        inner_again_body,
        [SMEM] + [VMEM] * (3 + roles) + [ANY],
        [longer, longer],
        (nums, low_in, s_in, se_in, *amp_roles, cc_out),
    )
    c_from_in = inner(c_in)

    def own_again_body(nums, rest_ref, s_ref, se_ref, *refs):
        amp_refs, (after_ref, out_ref, out_extra_ref) = refs[:roles], refs[-3:]

        @pl.when(lax.axis_index("role") > 0)
        def _():
            parts = parts_of(nums, lambda at: nums[own_weights + at], amp_refs)
            out_ref[...] = rest_ref[...] - coupled(s_ref, parts)
            parts = parts_of(nums, lambda at: nums[own_weights + pairs + at], amp_refs)
            out_extra_ref[...] = -coupled(se_ref, parts)

    rest, rest_extra = call(
        own_again_body,
        [SMEM] + [VMEM] * (3 + roles) + [ANY],
        [sq_f, sq_f],
        (nums, rest, s_own, se_own, *amp_roles, c_in),
    )

    def tell_body(last_ref, *refs):
        refs[-1][...] = last_ref[...]

    (ce_in,) = call(tell_body, [VMEM] + [ANY] * roles, [longer], (ce_in, rest, *rests))
    ce_from_in = inner(ce_in)

    def last_body(
        nums, coeff_ref, gain_ref, gain_extra_ref, rest_ref, rest_extra_ref, co_ref, ci_ref, cei_ref, *refs
    ):
        rest_refs, (amp_out, orb_out, amp_ref, orb_ref, sems) = refs[: roles - 1], refs[roles - 1 :]
        role = lax.axis_index("role")
        copies = []

        def send(source, target):
            copies.append(pltpu.make_async_copy(source, target, sems.at[len(copies)]))
            copies[-1].start()

        def store(slot, here, gain, rest, c_in, pair):
            @pl.when(here)
            def _():
                total = rest[...] - co_ref[slot].astype(F32) - c_in[:virt, :].astype(F32)
                for s in range(1, roles):
                    if slot:
                        come = rest_refs[s - 1][:virt, :].astype(F32)
                        total += jnp.where(role == s, come, 0.0)
                amp_ref[slot] = (gain[...] * total).astype(BF16)

            @pl.when(jnp.logical_not(here))
            def _():
                amp_ref[slot] = jnp.zeros(square, BF16)

            send(amp_ref.at[slot], amp_out.at[slot])
            for at in range(0, pao, virt):
                rows = pl.ds(at, virt)

                @pl.when(here)
                def _():
                    x = coeff_ref[pair, rows, :]
                    dressed = x.astype(F32) + mxu(x, amp_ref[slot], NN) * virt_scale
                    orb_ref[slot, rows, :] = dressed.astype(BF16)

                @pl.when(jnp.logical_not(here))
                def _():
                    orb_ref[slot, rows, :] = jnp.zeros((virt, virt), BF16)

                send(orb_ref.at[slot, rows], orb_out.at[slot, rows])

        store(0, role > 0, gain_ref, rest_ref, ci_ref, whole(nums[MINE]))
        has_extra = role == whole(nums[OWNER])
        store(1, has_extra, gain_extra_ref, rest_extra_ref, cei_ref, whole(nums[EXTRA]))
        for copy in copies:
            copy.wait()

    amps_out, dressed_out = call(
        last_body,
        [SMEM] + [VMEM] * (8 + roles - 1),
        [(ANY, (slots, virt, virt), BF16), (ANY, (slots, pao, virt), BF16)],
        (
            nums, coeff, gain, gain_extra, rest, rest_extra,
            cc_from_out, c_from_in, ce_from_in, *rests,
        ),
        scratch=[
            pltpu.VMEM((slots, virt, virt), BF16),
            pltpu.VMEM((slots, pao, virt), BF16),
            pltpu.SemaphoreType.DMA((slots * (1 + pao // virt),)),
        ],
    )
    return amps_out, dressed_out


def solution(mesh):
    in_specs = (
        P("pairs", None, None),
        P("pairs", None, None),
        P("pairs", None, None),
        P("pairs", None),
        P(),
        P("pairs"),
        P("pairs", None),
        P("pairs", None),
        P("pairs", None),
        P("pairs"),
    )
    out_specs = (P(("role", "pairs"), None, None), P(("role", "pairs"), None, None))
    return jax.shard_map(local, mesh=mesh, in_specs=in_specs, out_specs=out_specs, check_vma=False)
```

```python
import math

import jax
import jax.numpy as jnp
from jax import lax
from jax.experimental import pallas as pl
from jax.experimental.pallas import tpu as pltpu
from jax.sharding import PartitionSpec as P

F32 = jnp.float32
BF16 = jnp.bfloat16
I32 = jnp.int32
NN = ((1,), (0,))
NT = ((1,), (1,))

VMEM = pl.BlockSpec(memory_space=pltpu.VMEM)
SMEM = pl.BlockSpec(memory_space=pltpu.SMEM)
ANY = pl.BlockSpec(memory_space=pl.ANY)
HBM = pl.BlockSpec(memory_space=pltpu.HBM)

MINE, EXTRA, OWNER, FIRST, SECOND, WHOSE, NV_MINE, NV_EXTRA, OCC_MINE, OCC_EXTRA, ROLE_PAIR = range(11)


def whole(number):
    return number.astype(jnp.int32)


def mxu(a, b, dims):
    return lax.dot_general(a, b, (dims, ((), ())), preferred_element_type=F32)


def call(body, ins, outs, args, scratch=(), vmem=48):
    return pl.pallas_call(
        body,
        in_specs=ins,
        out_specs=[spec for spec, _, _ in outs],
        out_shape=[jax.ShapeDtypeStruct(shape, dtype) for _, shape, dtype in outs],
        scratch_shapes=list(scratch),
        cost_estimate=pl.CostEstimate(flops=1, bytes_accessed=1, transcendentals=0),
        compiler_params=pltpu.CompilerParams(vmem_limit_bytes=vmem * 1024 * 1024),
    )(*args)


def local(
    three_index, coeff, amps, eps_virt, eps_occ, nvirt, pair_occ, partners, coupling, pair_owner
):
    columns = lax.axis_size("pairs")
    roles = lax.axis_size("role")
    occ_block, aux, pao = three_index.shape
    pairs, _, virt = coeff.shape
    partner_count = partners.shape[1]
    slots = 2
    assert roles == pairs and pairs % 2 == 0 and columns % 2 == 0 and virt % 2 == 0
    tile = min(256, aux)
    pao_scale = 1.0 / math.sqrt(pao)
    aux_scale = 1.0 / math.sqrt(aux)
    virt_scale = 1.0 / math.sqrt(virt)
    square = (virt, virt)
    part = virt // 2
    sq_b = (VMEM, square, BF16)
    sq_f = (VMEM, square, F32)
    two_b = (VMEM, (2, virt, virt), BF16)
    all_s = (VMEM, (pairs, virt, virt), BF16)
    half = (VMEM, (aux, virt), BF16)

    inner_of = [i ^ 1 for i in range(columns)]
    outer_of = [(i + (1 if i % 2 else -1)) % columns for i in range(columns)]

    def inner(x):
        return lax.ppermute(x, "pairs", list(enumerate(inner_of)))

    def outer(x):
        return lax.ppermute(x, "pairs", list(enumerate(outer_of)))

    def swap(x, by):
        return lax.ppermute(x, "role", [(i, i ^ by) for i in range(roles)])

    three_in, coeff_in, amps_in = inner(three_index), inner(coeff), inner(amps)

    def pairs_of_roles(owner_ref):
        of_role = [jnp.int32(0)] * roles
        for p in range(pairs):
            earlier = jnp.int32(0)
            for o in range(p):
                earlier += (owner_ref[o] == owner_ref[p]).astype(I32)
            for s in range(roles):
                hit = (earlier == 0) & (owner_ref[p] == s) if s else earlier == 1
                of_role[s] = jnp.where(hit, p, of_role[s])
        return of_role

    def pick(numbers, at):
        chosen = numbers[0]
        for s in range(1, len(numbers)):
            chosen = jnp.where(at == s, numbers[s], chosen)
        return chosen

    weights = 2 * pairs
    place_at, mine_at, extra_at = 2 * weights, 2 * weights + 1, 2 * weights + 2
    riders = 16
    longer = (VMEM, (virt + riders, virt), BF16)
    own_weights = ROLE_PAIR + roles

    def plan_body(
        owner_hbm, occ_hbm, partner_hbm, coupling_hbm, eps_hbm, nvirt_hbm, coeff_hbm,
        low_ref, high_ref, nums,
        owner_ref, occ_ref, partner_ref, coupling_ref, eps_ref, nvirt_ref, near_w, sems,
    ):
        small = [
            pltpu.make_async_copy(source, target, sems.at[at])
            for at, (source, target) in enumerate(
                (
                    (owner_hbm, owner_ref),
                    (occ_hbm, occ_ref),
                    (partner_hbm, partner_ref),
                    (coupling_hbm, coupling_ref),
                    (eps_hbm, eps_ref),
                    (nvirt_hbm, nvirt_ref),
                )
            )
        ]
        for copy in small:
            copy.start()
        role = lax.axis_index("role")
        column = lax.axis_index("pairs")
        small[0].wait()
        of_role = pairs_of_roles(owner_ref)
        extra = of_role[0]
        mine = pick(of_role, role)
        large = [
            pltpu.make_async_copy(coeff_hbm.at[mine, :, pl.ds(0, part)], low_ref.at[pl.ds(0, pao)], sems.at[6]),
            pltpu.make_async_copy(coeff_hbm.at[mine, :, pl.ds(part, part)], high_ref, sems.at[7]),
        ]
        for copy in large:
            copy.start()
        for copy in small[1:]:
            copy.wait()
        nums[MINE] = mine.astype(F32)
        nums[EXTRA] = extra.astype(F32)
        nums[OWNER] = owner_ref[extra].astype(F32)
        for s in range(roles):
            nums[ROLE_PAIR + s] = of_role[s].astype(F32)
        nums[NV_MINE] = nvirt_ref[mine].astype(F32)
        nums[NV_EXTRA] = nvirt_ref[extra].astype(F32)
        nums[FIRST] = (occ_ref[0, mine] - column * occ_block).astype(F32)
        odd = lax.rem(column, 2) == 1
        inner_at = jnp.where(odd, 0, 2)
        outer_at = 2 - inner_at
        occ_all = occ_block * columns
        second = lax.rem(occ_ref[1, mine] - (column - 1) * occ_block + occ_all, occ_all)
        block = (second >= occ_block).astype(I32) + (second >= 2 * occ_block).astype(I32)
        place = (second - block * occ_block).astype(F32)
        nums[SECOND] = place
        lane = lax.broadcasted_iota(I32, (riders, part), 1)
        row = lax.broadcasted_iota(I32, (riders, part), 0)
        told = jnp.where(lane == place_at, place, 0.0)
        told = jnp.where(lane == mine_at, mine.astype(F32), told)
        told = jnp.where(lane == extra_at, extra.astype(F32), told)
        nums[WHOSE] = jnp.where(block == 1, 0, jnp.where(block == inner_at, 1, 2)).astype(F32)
        nums[OCC_MINE] = eps_ref[occ_ref[0, mine]] + eps_ref[occ_ref[1, mine]]
        nums[OCC_EXTRA] = eps_ref[occ_ref[0, extra]] + eps_ref[occ_ref[1, extra]]
        pair_all = pairs * columns
        for which, pair in enumerate((mine, extra)):
            for q in range(3 * pairs):
                near_w[q] = jnp.float32(0)
            for k in range(partner_count):
                at = lax.rem(partner_ref[pair, k] - (column - 1) * pairs + pair_all, pair_all)
                near_w[at] += coupling_ref[pair, k]
            for q in range(pairs):
                to = which * pairs + q
                nums[own_weights + to] = near_w[pairs + q]
                nums[own_weights + weights + to] = near_w[inner_at * pairs + q]
                told = jnp.where(lane == to, near_w[outer_at * pairs + q], told)
                told = jnp.where(lane == weights + to, near_w[inner_at * pairs + q], told)
        coarse = told.astype(BF16).astype(F32)
        middle = (told - coarse).astype(BF16).astype(F32)
        fine = told - coarse - middle
        told = jnp.where(row == 0, coarse, jnp.where(row == 1, middle, jnp.where(row == 2, fine, 0.0)))
        low_ref[pao:, :] = told.astype(BF16)
        for copy in large:
            copy.wait()

    rode = (VMEM, (pao + riders, part), BF16)
    x_low, x_high, nums = call(
        plan_body,
        [HBM] * 7,
        [rode, (VMEM, (pao, part), BF16), (SMEM, (own_weights + 2 * weights,), F32)],
        (pair_owner, pair_occ.T, partners, coupling, eps_occ, nvirt, coeff),
        scratch=[
            pltpu.SMEM(pair_owner.shape, I32),
            pltpu.SMEM(pair_occ.shape[::-1], I32),
            pltpu.SMEM(partners.shape, I32),
            pltpu.SMEM(coupling.shape, F32),
            pltpu.SMEM(eps_occ.shape, F32),
            pltpu.SMEM(nvirt.shape, I32),
            pltpu.SMEM((3 * pairs,), F32),
            pltpu.SemaphoreType.DMA((8,)),
        ],
        vmem=60,
    )
    low_out, high_out, low_in = outer(x_low), outer(x_high), inner(x_low)

    def told_of(low_ref):
        rows = low_ref[pao:, :].astype(F32)
        return rows[0:1] + rows[1:2] + rows[2:3]

    def overlaps(x, coeff_ref, out_ref):
        turned = x.T
        for q in range(pairs):
            s = mxu(turned, coeff_ref[q], NN) * (1.0 / pao)
            out_ref[q] = s.astype(BF16)

    def coupled(s_ref, parts):
        total = None
        for at, weight, amp in parts:
            s = s_ref[at]
            u = mxu(s, amp, NN).astype(BF16)
            term = weight * mxu(u, s, NT)
            total = term if total is None else total + term
        return total

    tiles = [pl.ds(at, tile) for at in range(0, aux, tile)]

    def half_into(y_ref, three_ref, at_occ, x):
        for rows in tiles:
            y_ref[rows, :] = (mxu(three_ref[at_occ, rows, :], x, NN) * pao_scale).astype(BF16)

    def fetch_body(three_ref, after_ref, held_ref, sem):
        copy = pltpu.make_async_copy(three_ref, held_ref, sem)
        copy.start()
        copy.wait()

    (blocks,) = call(
        fetch_body,
        [ANY, ANY],
        [(VMEM, three_index.shape, BF16)],
        (three_index, nums),
        scratch=[pltpu.SemaphoreType.DMA],
        vmem=50,
    )

    def outer_low_body(three_ref, x_ref, y_ref):
        half_into(y_ref, three_ref, whole(told_of(x_ref)[0, place_at]), x_ref[:pao, :])
        y_ref[aux:, :] = jnp.zeros((riders, part), BF16)

    (y_low,) = call(
        outer_low_body,
        [VMEM, VMEM],
        [(VMEM, (aux + riders, part), BF16)],
        (blocks, low_out),
    )
    y_low_from_out = outer(y_low)

    def outer_high_body(three_ref, low_ref, x_ref, after_ref, y_ref):
        half_into(y_ref, three_ref, whole(told_of(low_ref)[0, place_at]), x_ref[...])

    (y_high,) = call(
        outer_high_body,
        [VMEM, VMEM, VMEM, ANY],
        [(VMEM, (aux, part), BF16)],
        (blocks, low_out, high_out, y_low),
    )
    y_high_from_out = outer(y_high)

    def outer_body(coeff_ref, amps_ref, low_ref, high_ref, after_ref, s_ref, c_ref, x_ref):
        x_ref[:, :part] = low_ref[:pao, :]
        x_ref[:, part:] = high_ref[...]
        overlaps(x_ref[...], coeff_ref, s_ref)
        told = told_of(low_ref)
        c = coupled(s_ref, [(q, told[0, q], amps_ref[q]) for q in range(pairs)])
        c_ref[:virt, :] = c.astype(BF16)
        c_ref[virt:, :] = jnp.zeros((riders, virt), BF16)

    s_out, c_out = call(
        outer_body,
        [VMEM, VMEM, VMEM, VMEM, ANY],
        [all_s, longer],
        (coeff, amps, low_out, high_out, y_high),
        scratch=[pltpu.VMEM((pao, virt), BF16)],
    )
    c_from_out = outer(c_out)

    def own_half_body(
        nums, three_ref, three_in_ref, coeff_ref, after_ref, first_ref, second_ref, extra_ref, block_ref, sem
    ):
        x = coeff_ref[whole(nums[MINE])]
        extra_ref[...] = coeff_ref[whole(nums[EXTRA])]
        whose, second = whole(nums[WHOSE]), whole(nums[SECOND])
        copy = pltpu.make_async_copy(three_in_ref.at[second], block_ref.at[0], sem)

        @pl.when(whose == 1)
        def _():
            copy.start()

        turned = x.T
        first = whole(nums[FIRST])
        for rows in tiles:
            first_ref[:, rows] = (mxu(turned, three_ref[first, rows, :], NT) * pao_scale).astype(BF16)

        @pl.when(whose == 0)
        def _():
            half_into(second_ref, three_ref, second, x)

        @pl.when(whose == 1)
        def _():
            copy.wait()
            half_into(second_ref, block_ref, 0, x)

    first_t, second, x_extra = call(
        own_half_body,
        [SMEM, VMEM, ANY, VMEM, ANY],
        [
            (VMEM, (virt, aux), BF16),
            (VMEM, (aux, virt), BF16),
            (VMEM, (pao, virt), BF16),
        ],
        (nums, blocks, three_in, coeff, c_out),
        scratch=[pltpu.VMEM((1, aux, pao), BF16), pltpu.SemaphoreType.DMA],
    )
    x_extra_out = outer(x_extra)

    def own_body(
        nums, coeff_ref, coeff_in_ref, amps_ref, amps_in_ref, eps_ref, after_ref,
        s_ref, c_ref, gain_ref, gain_extra_ref, s_in_ref,
    ):
        mine, extra = whole(nums[MINE]), whole(nums[EXTRA])
        x = coeff_ref[mine]
        total = None
        for at, of_s, of_coeff, of_amps in (
            (own_weights, s_ref, coeff_ref, amps_ref),
            (own_weights + weights, s_in_ref, coeff_in_ref, amps_in_ref),
        ):
            overlaps(x, of_coeff, of_s)
            c = coupled(of_s, [(q, nums[at + q], of_amps[q]) for q in range(pairs)])
            total = c if total is None else total + c
        c_ref[...] = total

        def gain(pair, count, occupied):
            row = jnp.broadcast_to(eps_ref[pl.ds(pair, 1), :], square)
            energy = row + row.T - occupied
            inside = (lax.broadcasted_iota(I32, square, 0) < count) & (
                lax.broadcasted_iota(I32, square, 1) < count
            )
            return jnp.where(inside, 1.0 / (energy + 1.0), 0.0)

        gain_ref[...] = gain(mine, whole(nums[NV_MINE]), nums[OCC_MINE])
        gain_extra_ref[...] = gain(extra, whole(nums[NV_EXTRA]), nums[OCC_EXTRA])

    s_own, c_own, gain, gain_extra = call(
        own_body,
        [SMEM] + [VMEM] * 5 + [ANY],
        [all_s, sq_f, sq_f, sq_f],
        (nums, coeff, coeff_in, amps, amps_in, eps_virt, c_out),
        scratch=[pltpu.VMEM((pairs, virt, virt), BF16)],
    )

    def more_body(nums, coeff_ref, in_ref, low_ref, after_ref, se_ref, s_in_ref, se_in_ref):
        @pl.when(lax.axis_index("role") > 0)
        def _():
            told = told_of(low_ref)
            overlaps(coeff_ref[whole(nums[EXTRA])], coeff_ref, se_ref)
            overlaps(in_ref[whole(told[0, mine_at])], coeff_ref, s_in_ref)
            overlaps(in_ref[whole(told[0, extra_at])], coeff_ref, se_in_ref)

    se_own, s_in, se_in = call(
        more_body,
        [SMEM, VMEM, VMEM, VMEM, ANY],
        [all_s, all_s, all_s],
        (nums, coeff, coeff_in, low_in, c_own),
    )

    def first_body(
        nums, first_ref, second_ref, low_ref, high_ref, amps_ref, c_ref, co_ref, gain_ref, after_ref,
        amp_ref, k_ref,
    ):
        first = first_ref[...]
        outside = whole(nums[WHOSE]) == 2

        @pl.when(outside)
        def _():
            k_ref[:, :part] = mxu(first, low_ref[:aux, :], NN) * aux_scale
            k_ref[:, part:] = mxu(first, high_ref[...], NN) * aux_scale

        @pl.when(jnp.logical_not(outside))
        def _():
            k_ref[...] = mxu(first, second_ref[...], NN) * aux_scale

        old = amps_ref[whole(nums[MINE])].astype(F32)
        c = c_ref[...] + co_ref[:virt, :].astype(F32)
        amp_ref[...] = (gain_ref[...] * (old - k_ref[...] - c)).astype(BF16)

    amp, k_first = call(
        first_body,
        [SMEM] + [VMEM] * 8 + [ANY],
        [sq_b, sq_f],
        (
            nums, first_t, second, y_low_from_out, y_high_from_out,
            amps, c_own, c_from_out, gain, se_own,
        ),
    )
    amp_roles = [amp] + [swap(amp, m) for m in range(1, roles)]

    def rest_body(amp_ref, k_ref, out_ref, out_b_ref):
        amp = amp_ref[...]
        k = k_ref[...]
        right = k + mxu(k.astype(BF16), amp, NN) * virt_scale
        both = right + mxu(amp.T, right.astype(BF16), NN) * virt_scale
        rest = amp.astype(F32) - both
        out_ref[...] = rest
        out_b_ref[:virt, :] = rest.astype(BF16)
        out_b_ref[virt:, :] = jnp.zeros((riders, virt), BF16)

    rest, rest_b = call(rest_body, [VMEM, VMEM], [sq_f, longer], (amp, k_first))
    rests = [lax.ppermute(rest_b, "role", [(0, s)]) for s in range(1, roles)]

    def extra_out_body(coeff_ref, x_ref, after_ref, s_ref):
        @pl.when(lax.axis_index("role") > 0)
        def _():
            overlaps(x_ref[...], coeff_ref, s_ref)

    (se_out,) = call(
        extra_out_body,
        [VMEM, VMEM, ANY],
        [all_s],
        (coeff, x_extra_out, amp),
    )

    def parts_of(nums, weight_of, amp_refs):
        role = lax.axis_index("role")
        parts = []
        for m in range(roles):
            at = whole(nums[ROLE_PAIR + (role ^ m)])
            parts.append((at, weight_of(at), amp_refs[m][...]))
        return parts

    def told_weight(told, first):
        return lambda at: pick([told[:, first + q : first + q + 1] for q in range(pairs)], at)

    def outer_again_body(nums, low_ref, s_ref, se_ref, *refs):
        amp_refs, c_ref = refs[:roles], refs[-1]

        @pl.when(lax.axis_index("role") > 0)
        def _():
            told = told_of(low_ref)
            for slot, of_s in enumerate((s_ref, se_ref)):
                parts = parts_of(nums, told_weight(told, slot * pairs), amp_refs)
                c_ref[slot] = coupled(of_s, parts).astype(BF16)

    (cc_out,) = call(
        outer_again_body,
        [SMEM] + [VMEM] * (3 + roles),
        [two_b],
        (nums, low_out, s_out, se_out, *amp_roles),
    )
    cc_from_out = outer(cc_out)

    def inner_again_body(nums, low_ref, s_ref, se_ref, *refs):
        amp_refs, c_refs = refs[:roles], refs[-2:]

        @pl.when(lax.axis_index("role") > 0)
        def _():
            told = told_of(low_ref)
            for slot, of_s, c_ref in zip(range(2), (s_ref, se_ref), c_refs):
                parts = parts_of(nums, told_weight(told, weights + slot * pairs), amp_refs)
                c_ref[:virt, :] = coupled(of_s, parts).astype(BF16)
                c_ref[virt:, :] = jnp.zeros((riders, virt), BF16)

    c_in, ce_in = call(
        inner_again_body,
        [SMEM] + [VMEM] * (3 + roles) + [ANY],
        [longer, longer],
        (nums, low_in, s_in, se_in, *amp_roles, cc_out),
    )
    c_from_in = inner(c_in)

    def own_again_body(nums, rest_ref, s_ref, se_ref, *refs):
        amp_refs, (after_ref, out_ref, out_extra_ref) = refs[:roles], refs[-3:]

        @pl.when(lax.axis_index("role") > 0)
        def _():
            parts = parts_of(nums, lambda at: nums[own_weights + at], amp_refs)
            out_ref[...] = rest_ref[...] - coupled(s_ref, parts)
            parts = parts_of(nums, lambda at: nums[own_weights + pairs + at], amp_refs)
            out_extra_ref[...] = -coupled(se_ref, parts)

    rest, rest_extra = call(
        own_again_body,
        [SMEM] + [VMEM] * (3 + roles) + [ANY],
        [sq_f, sq_f],
        (nums, rest, s_own, se_own, *amp_roles, c_in),
    )

    def tell_body(last_ref, *refs):
        refs[-1][...] = last_ref[...]

    (ce_in,) = call(tell_body, [VMEM] + [ANY] * roles, [longer], (ce_in, rest, *rests))
    ce_from_in = inner(ce_in)

    def last_body(
        nums, coeff_ref, gain_ref, gain_extra_ref, rest_ref, rest_extra_ref, co_ref, ci_ref, cei_ref, *refs
    ):
        rest_refs, (amp_out, orb_out, amp_ref, orb_ref, sems) = refs[: roles - 1], refs[roles - 1 :]
        role = lax.axis_index("role")
        copies = []

        def send(source, target):
            copies.append(pltpu.make_async_copy(source, target, sems.at[len(copies)]))
            copies[-1].start()

        def store(slot, here, gain, rest, c_in, pair):
            @pl.when(here)
            def _():
                total = rest[...] - co_ref[slot].astype(F32) - c_in[:virt, :].astype(F32)
                for s in range(1, roles):
                    if slot:
                        come = rest_refs[s - 1][:virt, :].astype(F32)
                        total += jnp.where(role == s, come, 0.0)
                amp_ref[slot] = (gain[...] * total).astype(BF16)

            @pl.when(jnp.logical_not(here))
            def _():
                amp_ref[slot] = jnp.zeros(square, BF16)

            send(amp_ref.at[slot], amp_out.at[slot])
            for at in range(0, pao, virt):
                rows = pl.ds(at, virt)

                @pl.when(here)
                def _():
                    x = coeff_ref[pair, rows, :]
                    dressed = x.astype(F32) + mxu(x, amp_ref[slot], NN) * virt_scale
                    orb_ref[slot, rows, :] = dressed.astype(BF16)

                @pl.when(jnp.logical_not(here))
                def _():
                    orb_ref[slot, rows, :] = jnp.zeros((virt, virt), BF16)

                send(orb_ref.at[slot, rows], orb_out.at[slot, rows])

        store(0, role > 0, gain_ref, rest_ref, ci_ref, whole(nums[MINE]))
        has_extra = role == whole(nums[OWNER])
        store(1, has_extra, gain_extra_ref, rest_extra_ref, cei_ref, whole(nums[EXTRA]))
        for copy in copies:
            copy.wait()

    amps_out, dressed_out = call(
        last_body,
        [SMEM] + [VMEM] * (8 + roles - 1),
        [(ANY, (slots, virt, virt), BF16), (ANY, (slots, pao, virt), BF16)],
        (
            nums, coeff, gain, gain_extra, rest, rest_extra,
            cc_from_out, c_from_in, ce_from_in, *rests,
        ),
        scratch=[
            pltpu.VMEM((slots, virt, virt), BF16),
            pltpu.VMEM((slots, pao, virt), BF16),
            pltpu.SemaphoreType.DMA((slots * (1 + pao // virt),)),
        ],
    )
    return amps_out, dressed_out


def solution(mesh):
    in_specs = (
        P("pairs", None, None),
        P("pairs", None, None),
        P("pairs", None, None),
        P("pairs", None),
        P(),
        P("pairs"),
        P("pairs", None),
        P("pairs", None),
        P("pairs", None),
        P("pairs"),
    )
    out_specs = (P(("role", "pairs"), None, None), P(("role", "pairs"), None, None))
    return jax.shard_map(local, mesh=mesh, in_specs=in_specs, out_specs=out_specs, check_vma=False)
```

```python
import math

import jax
import jax.numpy as jnp
from jax import lax
from jax.experimental import pallas as pl
from jax.experimental.pallas import tpu as pltpu
from jax.sharding import PartitionSpec as P

F32 = jnp.float32
BF16 = jnp.bfloat16
I32 = jnp.int32
NN = ((1,), (0,))
NT = ((1,), (1,))

VMEM = pl.BlockSpec(memory_space=pltpu.VMEM)
SMEM = pl.BlockSpec(memory_space=pltpu.SMEM)
ANY = pl.BlockSpec(memory_space=pl.ANY)
HBM = pl.BlockSpec(memory_space=pltpu.HBM)

MINE, EXTRA, OWNER, FIRST, SECOND, WHOSE, NV_MINE, NV_EXTRA, OCC_MINE, OCC_EXTRA, ROLE_PAIR = range(11)


def whole(number):
    return number.astype(jnp.int32)


def mxu(a, b, dims):
    return lax.dot_general(a, b, (dims, ((), ())), preferred_element_type=F32)


def call(body, ins, outs, args, scratch=(), vmem=48):
    return pl.pallas_call(
        body,
        in_specs=ins,
        out_specs=[spec for spec, _, _ in outs],
        out_shape=[jax.ShapeDtypeStruct(shape, dtype) for _, shape, dtype in outs],
        scratch_shapes=list(scratch),
        cost_estimate=pl.CostEstimate(flops=1, bytes_accessed=1, transcendentals=0),
        compiler_params=pltpu.CompilerParams(vmem_limit_bytes=vmem * 1024 * 1024),
    )(*args)


def local(
    three_index, coeff, amps, eps_virt, eps_occ, nvirt, pair_occ, partners, coupling, pair_owner
):
    columns = lax.axis_size("pairs")
    roles = lax.axis_size("role")
    occ_block, aux, pao = three_index.shape
    pairs, _, virt = coeff.shape
    partner_count = partners.shape[1]
    slots = 2
    assert roles == pairs and pairs % 2 == 0 and columns % 2 == 0 and virt % 2 == 0
    tile = min(256, aux)
    pao_scale = 1.0 / math.sqrt(pao)
    aux_scale = 1.0 / math.sqrt(aux)
    virt_scale = 1.0 / math.sqrt(virt)
    square = (virt, virt)
    part = virt // 2
    sq_b = (VMEM, square, BF16)
    sq_f = (VMEM, square, F32)
    two_b = (VMEM, (2, virt, virt), BF16)
    all_s = (VMEM, (pairs, virt, virt), BF16)
    half = (VMEM, (aux, virt), BF16)

    inner_of = [i ^ 1 for i in range(columns)]
    outer_of = [(i + (1 if i % 2 else -1)) % columns for i in range(columns)]

    def inner(x):
        return lax.ppermute(x, "pairs", list(enumerate(inner_of)))

    def outer(x):
        return lax.ppermute(x, "pairs", list(enumerate(outer_of)))

    def swap(x, by):
        return lax.ppermute(x, "role", [(i, i ^ by) for i in range(roles)])

    three_in, coeff_in, amps_in = inner(three_index), inner(coeff), inner(amps)

    def pairs_of_roles(owner_ref):
        of_role = [jnp.int32(0)] * roles
        for p in range(pairs):
            earlier = jnp.int32(0)
            for o in range(p):
                earlier += (owner_ref[o] == owner_ref[p]).astype(I32)
            for s in range(roles):
                hit = (earlier == 0) & (owner_ref[p] == s) if s else earlier == 1
                of_role[s] = jnp.where(hit, p, of_role[s])
        return of_role

    def pick(numbers, at):
        chosen = numbers[0]
        for s in range(1, len(numbers)):
            chosen = jnp.where(at == s, numbers[s], chosen)
        return chosen

    weights = 2 * pairs
    place_at, mine_at, extra_at = 2 * weights, 2 * weights + 1, 2 * weights + 2
    riders = 16
    longer = (VMEM, (virt + riders, virt), BF16)
    own_weights = ROLE_PAIR + roles

    def plan_body(
        owner_hbm, occ_hbm, partner_hbm, coupling_hbm, eps_hbm, nvirt_hbm, coeff_hbm,
        low_ref, high_ref, nums,
        owner_ref, occ_ref, partner_ref, coupling_ref, eps_ref, nvirt_ref, near_w, sems,
    ):
        small = [
            pltpu.make_async_copy(source, target, sems.at[at])
            for at, (source, target) in enumerate(
                (
                    (owner_hbm, owner_ref),
                    (occ_hbm, occ_ref),
                    (partner_hbm, partner_ref),
                    (coupling_hbm, coupling_ref),
                    (eps_hbm, eps_ref),
                    (nvirt_hbm, nvirt_ref),
                )
            )
        ]
        for copy in small:
            copy.start()
        role = lax.axis_index("role")
        column = lax.axis_index("pairs")
        small[0].wait()
        of_role = pairs_of_roles(owner_ref)
        extra = of_role[0]
        mine = pick(of_role, role)
        large = [
            pltpu.make_async_copy(coeff_hbm.at[mine, :, pl.ds(0, part)], low_ref.at[pl.ds(0, pao)], sems.at[6]),
            pltpu.make_async_copy(coeff_hbm.at[mine, :, pl.ds(part, part)], high_ref, sems.at[7]),
        ]
        for copy in large:
            copy.start()
        for copy in small[1:]:
            copy.wait()
        nums[MINE] = mine.astype(F32)
        nums[EXTRA] = extra.astype(F32)
        nums[OWNER] = owner_ref[extra].astype(F32)
        for s in range(roles):
            nums[ROLE_PAIR + s] = of_role[s].astype(F32)
        nums[NV_MINE] = nvirt_ref[mine].astype(F32)
        nums[NV_EXTRA] = nvirt_ref[extra].astype(F32)
        nums[FIRST] = (occ_ref[0, mine] - column * occ_block).astype(F32)
        odd = lax.rem(column, 2) == 1
        inner_at = jnp.where(odd, 0, 2)
        outer_at = 2 - inner_at
        occ_all = occ_block * columns
        second = lax.rem(occ_ref[1, mine] - (column - 1) * occ_block + occ_all, occ_all)
        block = (second >= occ_block).astype(I32) + (second >= 2 * occ_block).astype(I32)
        place = (second - block * occ_block).astype(F32)
        nums[SECOND] = place
        lane = lax.broadcasted_iota(I32, (riders, part), 1)
        row = lax.broadcasted_iota(I32, (riders, part), 0)
        told = jnp.where(lane == place_at, place, 0.0)
        told = jnp.where(lane == mine_at, mine.astype(F32), told)
        told = jnp.where(lane == extra_at, extra.astype(F32), told)
        nums[WHOSE] = jnp.where(block == 1, 0, jnp.where(block == inner_at, 1, 2)).astype(F32)
        nums[OCC_MINE] = eps_ref[occ_ref[0, mine]] + eps_ref[occ_ref[1, mine]]
        nums[OCC_EXTRA] = eps_ref[occ_ref[0, extra]] + eps_ref[occ_ref[1, extra]]
        pair_all = pairs * columns
        for which, pair in enumerate((mine, extra)):
            for q in range(3 * pairs):
                near_w[q] = jnp.float32(0)
            for k in range(partner_count):
                at = lax.rem(partner_ref[pair, k] - (column - 1) * pairs + pair_all, pair_all)
                near_w[at] += coupling_ref[pair, k]
            for q in range(pairs):
                to = which * pairs + q
                nums[own_weights + to] = near_w[pairs + q]
                nums[own_weights + weights + to] = near_w[inner_at * pairs + q]
                told = jnp.where(lane == to, near_w[outer_at * pairs + q], told)
                told = jnp.where(lane == weights + to, near_w[inner_at * pairs + q], told)
        coarse = told.astype(BF16).astype(F32)
        middle = (told - coarse).astype(BF16).astype(F32)
        fine = told - coarse - middle
        told = jnp.where(row == 0, coarse, jnp.where(row == 1, middle, jnp.where(row == 2, fine, 0.0)))
        low_ref[pao:, :] = told.astype(BF16)
        for copy in large:
            copy.wait()

    rode = (VMEM, (pao + riders, part), BF16)
    x_low, x_high, nums = call(
        plan_body,
        [HBM] * 7,
        [rode, (VMEM, (pao, part), BF16), (SMEM, (own_weights + 2 * weights,), F32)],
        (pair_owner, pair_occ.T, partners, coupling, eps_occ, nvirt, coeff),
        scratch=[
            pltpu.SMEM(pair_owner.shape, I32),
            pltpu.SMEM(pair_occ.shape[::-1], I32),
            pltpu.SMEM(partners.shape, I32),
            pltpu.SMEM(coupling.shape, F32),
            pltpu.SMEM(eps_occ.shape, F32),
            pltpu.SMEM(nvirt.shape, I32),
            pltpu.SMEM((3 * pairs,), F32),
            pltpu.SemaphoreType.DMA((8,)),
        ],
        vmem=60,
    )
    low_out, high_out, low_in = outer(x_low), outer(x_high), inner(x_low)

    def told_of(low_ref):
        rows = low_ref[pao:, :].astype(F32)
        return rows[0:1] + rows[1:2] + rows[2:3]

    def overlaps(x, coeff_ref, out_ref):
        turned = x.T
        for q in range(pairs):
            s = mxu(turned, coeff_ref[q], NN) * (1.0 / pao)
            out_ref[q] = s.astype(BF16)

    def coupled(s_ref, parts):
        total = None
        for at, weight, amp in parts:
            s = s_ref[at]
            u = mxu(s, amp, NN).astype(BF16)
            term = weight * mxu(u, s, NT)
            total = term if total is None else total + term
        return total

    tiles = [pl.ds(at, tile) for at in range(0, aux, tile)]

    def half_into(y_ref, three_ref, at_occ, x):
        for rows in tiles:
            y_ref[rows, :] = (mxu(three_ref[at_occ, rows, :], x, NN) * pao_scale).astype(BF16)

    def fetch_body(three_ref, after_ref, held_ref, sem):
        copy = pltpu.make_async_copy(three_ref, held_ref, sem)
        copy.start()
        copy.wait()

    (blocks,) = call(
        fetch_body,
        [ANY, ANY],
        [(VMEM, three_index.shape, BF16)],
        (three_index, nums),
        scratch=[pltpu.SemaphoreType.DMA],
        vmem=50,
    )

    def outer_low_body(three_ref, x_ref, y_ref):
        half_into(y_ref, three_ref, whole(told_of(x_ref)[0, place_at]), x_ref[:pao, :])
        y_ref[aux:, :] = jnp.zeros((riders, part), BF16)

    (y_low,) = call(
        outer_low_body,
        [VMEM, VMEM],
        [(VMEM, (aux + riders, part), BF16)],
        (blocks, low_out),
    )
    y_low_from_out = outer(y_low)

    def outer_high_body(three_ref, low_ref, x_ref, after_ref, y_ref):
        half_into(y_ref, three_ref, whole(told_of(low_ref)[0, place_at]), x_ref[...])

    (y_high,) = call(
        outer_high_body,
        [VMEM, VMEM, VMEM, ANY],
        [(VMEM, (aux, part), BF16)],
        (blocks, low_out, high_out, y_low),
    )
    y_high_from_out = outer(y_high)

    def outer_body(coeff_ref, amps_ref, low_ref, high_ref, after_ref, s_ref, c_ref, x_ref):
        x_ref[:, :part] = low_ref[:pao, :]
        x_ref[:, part:] = high_ref[...]
        overlaps(x_ref[...], coeff_ref, s_ref)
        told = told_of(low_ref)
        c = coupled(s_ref, [(q, told[0, q], amps_ref[q]) for q in range(pairs)])
        c_ref[:virt, :] = c.astype(BF16)
        c_ref[virt:, :] = jnp.zeros((riders, virt), BF16)

    s_out, c_out = call(
        outer_body,
        [VMEM, VMEM, VMEM, VMEM, ANY],
        [all_s, longer],
        (coeff, amps, low_out, high_out, y_high),
        scratch=[pltpu.VMEM((pao, virt), BF16)],
    )
    c_from_out = outer(c_out)

    def own_half_body(
        nums, three_ref, three_in_ref, coeff_ref, after_ref, first_ref, second_ref, extra_ref, block_ref, sem
    ):
        x = coeff_ref[whole(nums[MINE])]
        extra_ref[...] = coeff_ref[whole(nums[EXTRA])]
        whose, second = whole(nums[WHOSE]), whole(nums[SECOND])
        copy = pltpu.make_async_copy(three_in_ref.at[second], block_ref.at[0], sem)

        @pl.when(whose == 1)
        def _():
            copy.start()

        turned = x.T
        first = whole(nums[FIRST])
        for rows in tiles:
            first_ref[:, rows] = (mxu(turned, three_ref[first, rows, :], NT) * pao_scale).astype(BF16)

        @pl.when(whose == 0)
        def _():
            half_into(second_ref, three_ref, second, x)

        @pl.when(whose == 1)
        def _():
            copy.wait()
            half_into(second_ref, block_ref, 0, x)

    first_t, second, x_extra = call(
        own_half_body,
        [SMEM, VMEM, ANY, VMEM, ANY],
        [
            (VMEM, (virt, aux), BF16),
            (VMEM, (aux, virt), BF16),
            (VMEM, (pao, virt), BF16),
        ],
        (nums, blocks, three_in, coeff, c_out),
        scratch=[pltpu.VMEM((1, aux, pao), BF16), pltpu.SemaphoreType.DMA],
    )
    x_extra_out = outer(x_extra)

    def own_body(
        nums, coeff_ref, coeff_in_ref, amps_ref, amps_in_ref, eps_ref, after_ref,
        s_ref, c_ref, gain_ref, gain_extra_ref, s_in_ref,
    ):
        mine, extra = whole(nums[MINE]), whole(nums[EXTRA])
        x = coeff_ref[mine]
        total = None
        for at, of_s, of_coeff, of_amps in (
            (own_weights, s_ref, coeff_ref, amps_ref),
            (own_weights + weights, s_in_ref, coeff_in_ref, amps_in_ref),
        ):
            overlaps(x, of_coeff, of_s)
            c = coupled(of_s, [(q, nums[at + q], of_amps[q]) for q in range(pairs)])
            total = c if total is None else total + c
        c_ref[...] = total

        def gain(pair, count, occupied):
            row = jnp.broadcast_to(eps_ref[pl.ds(pair, 1), :], square)
            energy = row + row.T - occupied
            inside = (lax.broadcasted_iota(I32, square, 0) < count) & (
                lax.broadcasted_iota(I32, square, 1) < count
            )
            return jnp.where(inside, 1.0 / (energy + 1.0), 0.0)

        gain_ref[...] = gain(mine, whole(nums[NV_MINE]), nums[OCC_MINE])
        gain_extra_ref[...] = gain(extra, whole(nums[NV_EXTRA]), nums[OCC_EXTRA])

    s_own, c_own, gain, gain_extra = call(
        own_body,
        [SMEM] + [VMEM] * 5 + [ANY],
        [all_s, sq_f, sq_f, sq_f],
        (nums, coeff, coeff_in, amps, amps_in, eps_virt, c_out),
        scratch=[pltpu.VMEM((pairs, virt, virt), BF16)],
    )

    def more_body(nums, coeff_ref, in_ref, low_ref, after_ref, se_ref, s_in_ref, se_in_ref):
        @pl.when(lax.axis_index("role") > 0)
        def _():
            told = told_of(low_ref)
            overlaps(coeff_ref[whole(nums[EXTRA])], coeff_ref, se_ref)
            overlaps(in_ref[whole(told[0, mine_at])], coeff_ref, s_in_ref)
            overlaps(in_ref[whole(told[0, extra_at])], coeff_ref, se_in_ref)

    se_own, s_in, se_in = call(
        more_body,
        [SMEM, VMEM, VMEM, VMEM, ANY],
        [all_s, all_s, all_s],
        (nums, coeff, coeff_in, low_in, c_own),
    )

    def first_body(
        nums, first_ref, second_ref, low_ref, high_ref, amps_ref, c_ref, co_ref, gain_ref, after_ref,
        amp_ref, k_ref,
    ):
        first = first_ref[...]
        outside = whole(nums[WHOSE]) == 2

        @pl.when(outside)
        def _():
            k_ref[:, :part] = mxu(first, low_ref[:aux, :], NN) * aux_scale
            k_ref[:, part:] = mxu(first, high_ref[...], NN) * aux_scale

        @pl.when(jnp.logical_not(outside))
        def _():
            k_ref[...] = mxu(first, second_ref[...], NN) * aux_scale

        old = amps_ref[whole(nums[MINE])].astype(F32)
        c = c_ref[...] + co_ref[:virt, :].astype(F32)
        amp_ref[...] = (gain_ref[...] * (old - k_ref[...] - c)).astype(BF16)

    amp, k_first = call(
        first_body,
        [SMEM] + [VMEM] * 8 + [ANY],
        [sq_b, sq_f],
        (
            nums, first_t, second, y_low_from_out, y_high_from_out,
            amps, c_own, c_from_out, gain, se_own,
        ),
    )
    amp_roles = [amp] + [swap(amp, m) for m in range(1, roles)]

    def rest_body(amp_ref, k_ref, out_ref, out_b_ref):
        amp = amp_ref[...]
        k = k_ref[...]
        right = k + mxu(k.astype(BF16), amp, NN) * virt_scale
        both = right + mxu(amp.T, right.astype(BF16), NN) * virt_scale
        rest = amp.astype(F32) - both
        out_ref[...] = rest
        out_b_ref[:virt, :] = rest.astype(BF16)
        out_b_ref[virt:, :] = jnp.zeros((2 * riders, virt), BF16)

    longest = (VMEM, (virt + 2 * riders, virt), BF16)
    rest, rest_b = call(rest_body, [VMEM, VMEM], [sq_f, longest], (amp, k_first))
    rests = [lax.ppermute(rest_b, "role", [(0, s)]) for s in range(1, roles)]

    def extra_out_body(coeff_ref, x_ref, after_ref, s_ref):
        @pl.when(lax.axis_index("role") > 0)
        def _():
            overlaps(x_ref[...], coeff_ref, s_ref)

    (se_out,) = call(
        extra_out_body,
        [VMEM, VMEM, ANY],
        [all_s],
        (coeff, x_extra_out, amp),
    )

    def parts_of(nums, weight_of, amp_refs):
        role = lax.axis_index("role")
        parts = []
        for m in range(roles):
            at = whole(nums[ROLE_PAIR + (role ^ m)])
            parts.append((at, weight_of(at), amp_refs[m][...]))
        return parts

    def told_weight(told, first):
        return lambda at: pick([told[:, first + q : first + q + 1] for q in range(pairs)], at)

    def outer_again_body(nums, low_ref, s_ref, se_ref, *refs):
        amp_refs, c_ref = refs[:roles], refs[-1]

        @pl.when(lax.axis_index("role") > 0)
        def _():
            told = told_of(low_ref)
            for slot, of_s in enumerate((s_ref, se_ref)):
                parts = parts_of(nums, told_weight(told, slot * pairs), amp_refs)
                c_ref[slot] = coupled(of_s, parts).astype(BF16)

    (cc_out,) = call(
        outer_again_body,
        [SMEM] + [VMEM] * (3 + roles),
        [two_b],
        (nums, low_out, s_out, se_out, *amp_roles),
    )
    cc_from_out = outer(cc_out)

    def inner_again_body(nums, low_ref, s_ref, se_ref, *refs):
        amp_refs, c_refs = refs[:roles], refs[-2:]

        @pl.when(lax.axis_index("role") > 0)
        def _():
            told = told_of(low_ref)
            for slot, of_s, c_ref in zip(range(2), (s_ref, se_ref), c_refs):
                parts = parts_of(nums, told_weight(told, weights + slot * pairs), amp_refs)
                c_ref[:virt, :] = coupled(of_s, parts).astype(BF16)
                c_ref[virt:, :] = jnp.zeros((riders, virt), BF16)

    c_in, ce_in = call(
        inner_again_body,
        [SMEM] + [VMEM] * (3 + roles) + [ANY],
        [longer, longer],
        (nums, low_in, s_in, se_in, *amp_roles, cc_out),
    )
    c_from_in, ce_from_in = inner(c_in), inner(ce_in)

    def own_again_body(nums, rest_ref, s_ref, se_ref, *refs):
        amp_refs, (after_ref, out_ref, out_extra_ref) = refs[:roles], refs[-3:]

        @pl.when(lax.axis_index("role") > 0)
        def _():
            parts = parts_of(nums, lambda at: nums[own_weights + at], amp_refs)
            out_ref[...] = rest_ref[...] - coupled(s_ref, parts)
            parts = parts_of(nums, lambda at: nums[own_weights + pairs + at], amp_refs)
            out_extra_ref[...] = -coupled(se_ref, parts)

    rest, rest_extra = call(
        own_again_body,
        [SMEM] + [VMEM] * (3 + roles) + [ANY],
        [sq_f, sq_f],
        (nums, rest, s_own, se_own, *amp_roles, c_in),
    )

    def last_body(
        nums, coeff_ref, gain_ref, gain_extra_ref, rest_ref, rest_extra_ref, co_ref, ci_ref, cei_ref, *refs
    ):
        rest_refs, (amp_out, orb_out, amp_ref, orb_ref, sems) = refs[: roles - 1], refs[roles - 1 :]
        role = lax.axis_index("role")
        copies = []

        def send(source, target):
            copies.append(pltpu.make_async_copy(source, target, sems.at[len(copies)]))
            copies[-1].start()

        def store(slot, here, gain, rest, c_in, pair):
            @pl.when(here)
            def _():
                total = rest[...] - co_ref[slot].astype(F32) - c_in[:virt, :].astype(F32)
                for s in range(1, roles):
                    if slot:
                        come = rest_refs[s - 1][:virt, :].astype(F32)
                        total += jnp.where(role == s, come, 0.0)
                amp_ref[slot] = (gain[...] * total).astype(BF16)

            @pl.when(jnp.logical_not(here))
            def _():
                amp_ref[slot] = jnp.zeros(square, BF16)

            send(amp_ref.at[slot], amp_out.at[slot])
            for at in range(0, pao, virt):
                rows = pl.ds(at, virt)

                @pl.when(here)
                def _():
                    x = coeff_ref[pair, rows, :]
                    dressed = x.astype(F32) + mxu(x, amp_ref[slot], NN) * virt_scale
                    orb_ref[slot, rows, :] = dressed.astype(BF16)

                @pl.when(jnp.logical_not(here))
                def _():
                    orb_ref[slot, rows, :] = jnp.zeros((virt, virt), BF16)

                send(orb_ref.at[slot, rows], orb_out.at[slot, rows])

        store(0, role > 0, gain_ref, rest_ref, ci_ref, whole(nums[MINE]))
        has_extra = role == whole(nums[OWNER])
        store(1, has_extra, gain_extra_ref, rest_extra_ref, cei_ref, whole(nums[EXTRA]))
        for copy in copies:
            copy.wait()

    amps_out, dressed_out = call(
        last_body,
        [SMEM] + [VMEM] * (8 + roles - 1),
        [(ANY, (slots, virt, virt), BF16), (ANY, (slots, pao, virt), BF16)],
        (
            nums, coeff, gain, gain_extra, rest, rest_extra,
            cc_from_out, c_from_in, ce_from_in, *rests,
        ),
        scratch=[
            pltpu.VMEM((slots, virt, virt), BF16),
            pltpu.VMEM((slots, pao, virt), BF16),
            pltpu.SemaphoreType.DMA((slots * (1 + pao // virt),)),
        ],
    )
    return amps_out, dressed_out


def solution(mesh):
    in_specs = (
        P("pairs", None, None),
        P("pairs", None, None),
        P("pairs", None, None),
        P("pairs", None),
        P(),
        P("pairs"),
        P("pairs", None),
        P("pairs", None),
        P("pairs", None),
        P("pairs"),
    )
    out_specs = (P(("role", "pairs"), None, None), P(("role", "pairs"), None, None))
    return jax.shard_map(local, mesh=mesh, in_specs=in_specs, out_specs=out_specs, check_vma=False)
```

```python
import math

import jax
import jax.numpy as jnp
from jax import lax
from jax.experimental import pallas as pl
from jax.experimental.pallas import tpu as pltpu
from jax.sharding import PartitionSpec as P

F32 = jnp.float32
BF16 = jnp.bfloat16
I32 = jnp.int32
NN = ((1,), (0,))
NT = ((1,), (1,))

VMEM = pl.BlockSpec(memory_space=pltpu.VMEM)
SMEM = pl.BlockSpec(memory_space=pltpu.SMEM)
ANY = pl.BlockSpec(memory_space=pl.ANY)
HBM = pl.BlockSpec(memory_space=pltpu.HBM)

MINE, EXTRA, OWNER, FIRST, SECOND, WHOSE, NV_MINE, NV_EXTRA, OCC_MINE, OCC_EXTRA, ROLE_PAIR = range(11)


def whole(number):
    return number.astype(jnp.int32)


def mxu(a, b, dims):
    return lax.dot_general(a, b, (dims, ((), ())), preferred_element_type=F32)


def call(body, ins, outs, args, scratch=(), vmem=48):
    return pl.pallas_call(
        body,
        in_specs=ins,
        out_specs=[spec for spec, _, _ in outs],
        out_shape=[jax.ShapeDtypeStruct(shape, dtype) for _, shape, dtype in outs],
        scratch_shapes=list(scratch),
        cost_estimate=pl.CostEstimate(flops=1, bytes_accessed=1, transcendentals=0),
        compiler_params=pltpu.CompilerParams(vmem_limit_bytes=vmem * 1024 * 1024),
    )(*args)


def local(
    three_index, coeff, amps, eps_virt, eps_occ, nvirt, pair_occ, partners, coupling, pair_owner
):
    columns = lax.axis_size("pairs")
    roles = lax.axis_size("role")
    occ_block, aux, pao = three_index.shape
    pairs, _, virt = coeff.shape
    partner_count = partners.shape[1]
    slots = 2
    assert roles == pairs and pairs % 2 == 0 and columns % 2 == 0 and virt % 2 == 0
    tile = min(256, aux)
    pao_scale = 1.0 / math.sqrt(pao)
    aux_scale = 1.0 / math.sqrt(aux)
    virt_scale = 1.0 / math.sqrt(virt)
    square = (virt, virt)
    part = virt // 2
    sq_b = (VMEM, square, BF16)
    sq_f = (VMEM, square, F32)
    two_b = (VMEM, (2, virt, virt), BF16)
    all_s = (VMEM, (pairs, virt, virt), BF16)
    half = (VMEM, (aux, virt), BF16)

    inner_of = [i ^ 1 for i in range(columns)]
    outer_of = [(i + (1 if i % 2 else -1)) % columns for i in range(columns)]

    def inner(x):
        return lax.ppermute(x, "pairs", list(enumerate(inner_of)))

    def outer(x):
        return lax.ppermute(x, "pairs", list(enumerate(outer_of)))

    def swap(x, by):
        return lax.ppermute(x, "role", [(i, i ^ by) for i in range(roles)])

    three_in, coeff_in, amps_in = inner(three_index), inner(coeff), inner(amps)

    def pairs_of_roles(owner_ref):
        of_role = [jnp.int32(0)] * roles
        for p in range(pairs):
            earlier = jnp.int32(0)
            for o in range(p):
                earlier += (owner_ref[o] == owner_ref[p]).astype(I32)
            for s in range(roles):
                hit = (earlier == 0) & (owner_ref[p] == s) if s else earlier == 1
                of_role[s] = jnp.where(hit, p, of_role[s])
        return of_role

    def pick(numbers, at):
        chosen = numbers[0]
        for s in range(1, len(numbers)):
            chosen = jnp.where(at == s, numbers[s], chosen)
        return chosen

    weights = 2 * pairs
    place_at, mine_at, extra_at = 2 * weights, 2 * weights + 1, 2 * weights + 2
    riders = 16
    longer = (VMEM, (virt + riders, virt), BF16)
    own_weights = ROLE_PAIR + roles

    def plan_body(
        owner_hbm, occ_hbm, partner_hbm, coupling_hbm, eps_hbm, nvirt_hbm, coeff_hbm,
        low_ref, high_ref, nums,
        owner_ref, occ_ref, partner_ref, coupling_ref, eps_ref, nvirt_ref, near_w, sems,
    ):
        small = [
            pltpu.make_async_copy(source, target, sems.at[at])
            for at, (source, target) in enumerate(
                (
                    (owner_hbm, owner_ref),
                    (occ_hbm, occ_ref),
                    (partner_hbm, partner_ref),
                    (coupling_hbm, coupling_ref),
                    (eps_hbm, eps_ref),
                    (nvirt_hbm, nvirt_ref),
                )
            )
        ]
        for copy in small:
            copy.start()
        role = lax.axis_index("role")
        column = lax.axis_index("pairs")
        small[0].wait()
        of_role = pairs_of_roles(owner_ref)
        extra = of_role[0]
        mine = pick(of_role, role)
        large = [
            pltpu.make_async_copy(coeff_hbm.at[mine, :, pl.ds(0, part)], low_ref.at[pl.ds(0, pao)], sems.at[6]),
            pltpu.make_async_copy(coeff_hbm.at[mine, :, pl.ds(part, part)], high_ref, sems.at[7]),
        ]
        for copy in large:
            copy.start()
        for copy in small[1:]:
            copy.wait()
        nums[MINE] = mine.astype(F32)
        nums[EXTRA] = extra.astype(F32)
        nums[OWNER] = owner_ref[extra].astype(F32)
        for s in range(roles):
            nums[ROLE_PAIR + s] = of_role[s].astype(F32)
        nums[NV_MINE] = nvirt_ref[mine].astype(F32)
        nums[NV_EXTRA] = nvirt_ref[extra].astype(F32)
        nums[FIRST] = (occ_ref[0, mine] - column * occ_block).astype(F32)
        odd = lax.rem(column, 2) == 1
        inner_at = jnp.where(odd, 0, 2)
        outer_at = 2 - inner_at
        occ_all = occ_block * columns
        second = lax.rem(occ_ref[1, mine] - (column - 1) * occ_block + occ_all, occ_all)
        block = (second >= occ_block).astype(I32) + (second >= 2 * occ_block).astype(I32)
        place = (second - block * occ_block).astype(F32)
        nums[SECOND] = place
        lane = lax.broadcasted_iota(I32, (riders, part), 1)
        row = lax.broadcasted_iota(I32, (riders, part), 0)
        told = jnp.where(lane == place_at, place, 0.0)
        told = jnp.where(lane == mine_at, mine.astype(F32), told)
        told = jnp.where(lane == extra_at, extra.astype(F32), told)
        nums[WHOSE] = jnp.where(block == 1, 0, jnp.where(block == inner_at, 1, 2)).astype(F32)
        nums[OCC_MINE] = eps_ref[occ_ref[0, mine]] + eps_ref[occ_ref[1, mine]]
        nums[OCC_EXTRA] = eps_ref[occ_ref[0, extra]] + eps_ref[occ_ref[1, extra]]
        pair_all = pairs * columns
        for which, pair in enumerate((mine, extra)):
            for q in range(3 * pairs):
                near_w[q] = jnp.float32(0)
            for k in range(partner_count):
                at = lax.rem(partner_ref[pair, k] - (column - 1) * pairs + pair_all, pair_all)
                near_w[at] += coupling_ref[pair, k]
            for q in range(pairs):
                to = which * pairs + q
                nums[own_weights + to] = near_w[pairs + q]
                nums[own_weights + weights + to] = near_w[inner_at * pairs + q]
                told = jnp.where(lane == to, near_w[outer_at * pairs + q], told)
                told = jnp.where(lane == weights + to, near_w[inner_at * pairs + q], told)
        coarse = told.astype(BF16).astype(F32)
        middle = (told - coarse).astype(BF16).astype(F32)
        fine = told - coarse - middle
        told = jnp.where(row == 0, coarse, jnp.where(row == 1, middle, jnp.where(row == 2, fine, 0.0)))
        low_ref[pao:, :] = told.astype(BF16)
        for copy in large:
            copy.wait()

    rode = (VMEM, (pao + riders, part), BF16)
    x_low, x_high, nums = call(
        plan_body,
        [HBM] * 7,
        [rode, (VMEM, (pao, part), BF16), (SMEM, (own_weights + 2 * weights,), F32)],
        (pair_owner, pair_occ.T, partners, coupling, eps_occ, nvirt, coeff),
        scratch=[
            pltpu.SMEM(pair_owner.shape, I32),
            pltpu.SMEM(pair_occ.shape[::-1], I32),
            pltpu.SMEM(partners.shape, I32),
            pltpu.SMEM(coupling.shape, F32),
            pltpu.SMEM(eps_occ.shape, F32),
            pltpu.SMEM(nvirt.shape, I32),
            pltpu.SMEM((3 * pairs,), F32),
            pltpu.SemaphoreType.DMA((8,)),
        ],
        vmem=60,
    )
    low_out, high_out, low_in = outer(x_low), outer(x_high), inner(x_low)

    def told_of(low_ref):
        rows = low_ref[pao:, :].astype(F32)
        return rows[0:1] + rows[1:2] + rows[2:3]

    def overlaps(x, coeff_ref, out_ref):
        turned = x.T
        for q in range(pairs):
            s = mxu(turned, coeff_ref[q], NN) * (1.0 / pao)
            out_ref[q] = s.astype(BF16)

    def coupled(s_ref, parts):
        total = None
        for at, weight, amp in parts:
            s = s_ref[at]
            u = mxu(s, amp, NN).astype(BF16)
            term = weight * mxu(u, s, NT)
            total = term if total is None else total + term
        return total

    tiles = [pl.ds(at, tile) for at in range(0, aux, tile)]

    def half_into(y_ref, three_ref, at_occ, x):
        for rows in tiles:
            y_ref[rows, :] = (mxu(three_ref[at_occ, rows, :], x, NN) * pao_scale).astype(BF16)

    def fetch_body(three_ref, after_ref, held_ref, sem):
        copy = pltpu.make_async_copy(three_ref, held_ref, sem)
        copy.start()
        copy.wait()

    (blocks,) = call(
        fetch_body,
        [ANY, ANY],
        [(VMEM, three_index.shape, BF16)],
        (three_index, nums),
        scratch=[pltpu.SemaphoreType.DMA],
        vmem=50,
    )

    def outer_low_body(three_ref, x_ref, y_ref):
        half_into(y_ref, three_ref, whole(told_of(x_ref)[0, place_at]), x_ref[:pao, :])
        y_ref[aux:, :] = jnp.zeros((riders, part), BF16)

    (y_low,) = call(
        outer_low_body,
        [VMEM, VMEM],
        [(VMEM, (aux + riders, part), BF16)],
        (blocks, low_out),
    )
    y_low_from_out = outer(y_low)

    def outer_high_body(three_ref, low_ref, x_ref, after_ref, y_ref):
        half_into(y_ref, three_ref, whole(told_of(low_ref)[0, place_at]), x_ref[...])

    (y_high,) = call(
        outer_high_body,
        [VMEM, VMEM, VMEM, ANY],
        [(VMEM, (aux, part), BF16)],
        (blocks, low_out, high_out, y_low),
    )
    y_high_from_out = outer(y_high)

    def outer_body(coeff_ref, amps_ref, low_ref, high_ref, after_ref, s_ref, c_ref, x_ref):
        x_ref[:, :part] = low_ref[:pao, :]
        x_ref[:, part:] = high_ref[...]
        overlaps(x_ref[...], coeff_ref, s_ref)
        told = told_of(low_ref)
        c = coupled(s_ref, [(q, told[0, q], amps_ref[q]) for q in range(pairs)])
        c_ref[:virt, :] = c.astype(BF16)
        c_ref[virt:, :] = jnp.zeros((riders, virt), BF16)

    s_out, c_out = call(
        outer_body,
        [VMEM, VMEM, VMEM, VMEM, ANY],
        [all_s, longer],
        (coeff, amps, low_out, high_out, y_high),
        scratch=[pltpu.VMEM((pao, virt), BF16)],
    )
    c_from_out = outer(c_out)

    def own_half_body(
        nums, three_ref, three_in_ref, coeff_ref, after_ref, first_ref, second_ref, extra_ref, block_ref, sem
    ):
        x = coeff_ref[whole(nums[MINE])]
        extra_ref[...] = coeff_ref[whole(nums[EXTRA])]
        whose, second = whole(nums[WHOSE]), whole(nums[SECOND])
        copy = pltpu.make_async_copy(three_in_ref.at[second], block_ref.at[0], sem)

        @pl.when(whose == 1)
        def _():
            copy.start()

        turned = x.T
        first = whole(nums[FIRST])
        for rows in tiles:
            first_ref[:, rows] = (mxu(turned, three_ref[first, rows, :], NT) * pao_scale).astype(BF16)

        @pl.when(whose == 0)
        def _():
            half_into(second_ref, three_ref, second, x)

        @pl.when(whose == 1)
        def _():
            copy.wait()
            half_into(second_ref, block_ref, 0, x)

    first_t, second, x_extra = call(
        own_half_body,
        [SMEM, VMEM, ANY, VMEM, ANY],
        [
            (VMEM, (virt, aux), BF16),
            (VMEM, (aux, virt), BF16),
            (VMEM, (pao, virt), BF16),
        ],
        (nums, blocks, three_in, coeff, c_out),
        scratch=[pltpu.VMEM((1, aux, pao), BF16), pltpu.SemaphoreType.DMA],
    )
    x_extra_out = outer(x_extra)

    def own_body(
        nums, coeff_ref, coeff_in_ref, amps_ref, amps_in_ref, eps_ref, after_ref,
        s_ref, c_ref, gain_ref, gain_extra_ref, s_in_ref,
    ):
        mine, extra = whole(nums[MINE]), whole(nums[EXTRA])
        x = coeff_ref[mine]
        total = None
        for at, of_s, of_coeff, of_amps in (
            (own_weights, s_ref, coeff_ref, amps_ref),
            (own_weights + weights, s_in_ref, coeff_in_ref, amps_in_ref),
        ):
            overlaps(x, of_coeff, of_s)
            c = coupled(of_s, [(q, nums[at + q], of_amps[q]) for q in range(pairs)])
            total = c if total is None else total + c
        c_ref[...] = total

        def gain(pair, count, occupied):
            row = jnp.broadcast_to(eps_ref[pl.ds(pair, 1), :], square)
            energy = row + row.T - occupied
            inside = (lax.broadcasted_iota(I32, square, 0) < count) & (
                lax.broadcasted_iota(I32, square, 1) < count
            )
            return jnp.where(inside, 1.0 / (energy + 1.0), 0.0)

        gain_ref[...] = gain(mine, whole(nums[NV_MINE]), nums[OCC_MINE])
        gain_extra_ref[...] = gain(extra, whole(nums[NV_EXTRA]), nums[OCC_EXTRA])

    s_own, c_own, gain, gain_extra = call(
        own_body,
        [SMEM] + [VMEM] * 5 + [ANY],
        [all_s, sq_f, sq_f, sq_f],
        (nums, coeff, coeff_in, amps, amps_in, eps_virt, c_out),
        scratch=[pltpu.VMEM((pairs, virt, virt), BF16)],
    )

    def more_body(nums, coeff_ref, in_ref, low_ref, after_ref, se_ref, s_in_ref, se_in_ref):
        @pl.when(lax.axis_index("role") > 0)
        def _():
            told = told_of(low_ref)
            overlaps(coeff_ref[whole(nums[EXTRA])], coeff_ref, se_ref)
            overlaps(in_ref[whole(told[0, mine_at])], coeff_ref, s_in_ref)
            overlaps(in_ref[whole(told[0, extra_at])], coeff_ref, se_in_ref)

    se_own, s_in, se_in = call(
        more_body,
        [SMEM, VMEM, VMEM, VMEM, ANY],
        [all_s, all_s, all_s],
        (nums, coeff, coeff_in, low_in, c_own),
    )

    def first_body(
        nums, first_ref, second_ref, low_ref, high_ref, amps_ref, c_ref, co_ref, gain_ref, after_ref,
        amp_ref, amp_long_ref, k_ref,
    ):
        first = first_ref[...]
        outside = whole(nums[WHOSE]) == 2

        @pl.when(outside)
        def _():
            k_ref[:, :part] = mxu(first, low_ref[:aux, :], NN) * aux_scale
            k_ref[:, part:] = mxu(first, high_ref[...], NN) * aux_scale

        @pl.when(jnp.logical_not(outside))
        def _():
            k_ref[...] = mxu(first, second_ref[...], NN) * aux_scale

        old = amps_ref[whole(nums[MINE])].astype(F32)
        c = c_ref[...] + co_ref[:virt, :].astype(F32)
        amp = (gain_ref[...] * (old - k_ref[...] - c)).astype(BF16)
        amp_ref[...] = amp
        amp_long_ref[:virt, :] = amp
        amp_long_ref[virt:, :] = jnp.zeros((riders, virt), BF16)

    amp, amp_long, k_first = call(
        first_body,
        [SMEM] + [VMEM] * 8 + [ANY],
        [sq_b, longer, sq_f],
        (
            nums, first_t, second, y_low_from_out, y_high_from_out,
            amps, c_own, c_from_out, gain, se_own,
        ),
    )
    amp_roles = [amp] + [swap(amp, m) for m in range(1, roles - 1)] + [swap(amp_long, roles - 1)]

    def rest_body(amp_ref, k_ref, out_ref, out_b_ref):
        amp = amp_ref[...]
        k = k_ref[...]
        right = k + mxu(k.astype(BF16), amp, NN) * virt_scale
        both = right + mxu(amp.T, right.astype(BF16), NN) * virt_scale
        rest = amp.astype(F32) - both
        out_ref[...] = rest
        out_b_ref[:virt, :] = rest.astype(BF16)
        out_b_ref[virt:, :] = jnp.zeros((2 * riders, virt), BF16)

    longest = (VMEM, (virt + 2 * riders, virt), BF16)
    rest, rest_b = call(rest_body, [VMEM, VMEM], [sq_f, longest], (amp, k_first))
    rests = [lax.ppermute(rest_b, "role", [(0, s)]) for s in range(roles - 1, 0, -1)]

    def extra_out_body(coeff_ref, x_ref, after_ref, s_ref):
        @pl.when(lax.axis_index("role") > 0)
        def _():
            overlaps(x_ref[...], coeff_ref, s_ref)

    (se_out,) = call(
        extra_out_body,
        [VMEM, VMEM, ANY],
        [all_s],
        (coeff, x_extra_out, amp),
    )

    def parts_of(nums, weight_of, amp_refs):
        role = lax.axis_index("role")
        parts = []
        for m in range(roles):
            at = whole(nums[ROLE_PAIR + (role ^ m)])
            parts.append((at, weight_of(at), amp_refs[m][:virt, :]))
        return parts

    def told_weight(told, first):
        return lambda at: pick([told[:, first + q : first + q + 1] for q in range(pairs)], at)

    def outer_again_body(nums, low_ref, s_ref, se_ref, *refs):
        amp_refs, c_ref = refs[:roles], refs[-1]

        @pl.when(lax.axis_index("role") > 0)
        def _():
            told = told_of(low_ref)
            for slot, of_s in enumerate((s_ref, se_ref)):
                parts = parts_of(nums, told_weight(told, slot * pairs), amp_refs)
                c_ref[slot] = coupled(of_s, parts).astype(BF16)

    (cc_out,) = call(
        outer_again_body,
        [SMEM] + [VMEM] * (3 + roles),
        [two_b],
        (nums, low_out, s_out, se_out, *amp_roles),
    )
    cc_from_out = outer(cc_out)

    def inner_again_body(nums, low_ref, s_ref, se_ref, *refs):
        amp_refs, c_refs = refs[:roles], refs[-2:]

        @pl.when(lax.axis_index("role") > 0)
        def _():
            told = told_of(low_ref)
            for slot, of_s, c_ref in zip(range(2), (s_ref, se_ref), c_refs):
                parts = parts_of(nums, told_weight(told, weights + slot * pairs), amp_refs)
                c_ref[:virt, :] = coupled(of_s, parts).astype(BF16)
                c_ref[virt:, :] = jnp.zeros((riders, virt), BF16)

    c_in, ce_in = call(
        inner_again_body,
        [SMEM] + [VMEM] * (3 + roles) + [ANY],
        [longer, longer],
        (nums, low_in, s_in, se_in, *amp_roles, cc_out),
    )
    c_from_in, ce_from_in = inner(c_in), inner(ce_in)

    def own_again_body(nums, rest_ref, s_ref, se_ref, *refs):
        amp_refs, (after_ref, out_ref, out_extra_ref) = refs[:roles], refs[-3:]

        @pl.when(lax.axis_index("role") > 0)
        def _():
            parts = parts_of(nums, lambda at: nums[own_weights + at], amp_refs)
            out_ref[...] = rest_ref[...] - coupled(s_ref, parts)
            parts = parts_of(nums, lambda at: nums[own_weights + pairs + at], amp_refs)
            out_extra_ref[...] = -coupled(se_ref, parts)

    rest, rest_extra = call(
        own_again_body,
        [SMEM] + [VMEM] * (3 + roles) + [ANY],
        [sq_f, sq_f],
        (nums, rest, s_own, se_own, *amp_roles, c_in),
    )

    def last_body(
        nums, coeff_ref, gain_ref, gain_extra_ref, rest_ref, rest_extra_ref, co_ref, ci_ref, cei_ref, *refs
    ):
        rest_refs, (amp_out, orb_out, amp_ref, orb_ref, sems) = refs[: roles - 1], refs[roles - 1 :]
        role = lax.axis_index("role")
        copies = []

        def send(source, target):
            copies.append(pltpu.make_async_copy(source, target, sems.at[len(copies)]))
            copies[-1].start()

        def store(slot, here, gain, rest, c_in, pair):
            @pl.when(here)
            def _():
                total = rest[...] - co_ref[slot].astype(F32) - c_in[:virt, :].astype(F32)
                for s in range(1, roles):
                    if slot:
                        come = rest_refs[roles - 1 - s][:virt, :].astype(F32)
                        total += jnp.where(role == s, come, 0.0)
                amp_ref[slot] = (gain[...] * total).astype(BF16)

            @pl.when(jnp.logical_not(here))
            def _():
                amp_ref[slot] = jnp.zeros(square, BF16)

            send(amp_ref.at[slot], amp_out.at[slot])
            for at in range(0, pao, virt):
                rows = pl.ds(at, virt)

                @pl.when(here)
                def _():
                    x = coeff_ref[pair, rows, :]
                    dressed = x.astype(F32) + mxu(x, amp_ref[slot], NN) * virt_scale
                    orb_ref[slot, rows, :] = dressed.astype(BF16)

                @pl.when(jnp.logical_not(here))
                def _():
                    orb_ref[slot, rows, :] = jnp.zeros((virt, virt), BF16)

                send(orb_ref.at[slot, rows], orb_out.at[slot, rows])

        store(0, role > 0, gain_ref, rest_ref, ci_ref, whole(nums[MINE]))
        has_extra = role == whole(nums[OWNER])
        store(1, has_extra, gain_extra_ref, rest_extra_ref, cei_ref, whole(nums[EXTRA]))
        for copy in copies:
            copy.wait()

    amps_out, dressed_out = call(
        last_body,
        [SMEM] + [VMEM] * (8 + roles - 1),
        [(ANY, (slots, virt, virt), BF16), (ANY, (slots, pao, virt), BF16)],
        (
            nums, coeff, gain, gain_extra, rest, rest_extra,
            cc_from_out, c_from_in, ce_from_in, *rests,
        ),
        scratch=[
            pltpu.VMEM((slots, virt, virt), BF16),
            pltpu.VMEM((slots, pao, virt), BF16),
            pltpu.SemaphoreType.DMA((slots * (1 + pao // virt),)),
        ],
    )
    return amps_out, dressed_out


def solution(mesh):
    in_specs = (
        P("pairs", None, None),
        P("pairs", None, None),
        P("pairs", None, None),
        P("pairs", None),
        P(),
        P("pairs"),
        P("pairs", None),
        P("pairs", None),
        P("pairs", None),
        P("pairs"),
    )
    out_specs = (P(("role", "pairs"), None, None), P(("role", "pairs"), None, None))
    return jax.shard_map(local, mesh=mesh, in_specs=in_specs, out_specs=out_specs, check_vma=False)
```

```python
import functools
import math

import jax
import jax.numpy as jnp
from jax import lax
from jax.experimental import pallas as pl
from jax.experimental.pallas import tpu as pltpu
from jax.sharding import PartitionSpec as P

F32 = jnp.float32
BF16 = jnp.bfloat16
I32 = jnp.int32
NN = ((1,), (0,))
NT = ((1,), (1,))

VMEM = pl.BlockSpec(memory_space=pltpu.VMEM)
SMEM = pl.BlockSpec(memory_space=pltpu.SMEM)
ANY = pl.BlockSpec(memory_space=pl.ANY)
HBM = pl.BlockSpec(memory_space=pltpu.HBM)

MINE, EXTRA, OWNER, FIRST, SECOND, WHOSE, NV_MINE, NV_EXTRA, OCC_MINE, OCC_EXTRA, ROLE_PAIR = range(11)


def whole(number):
    return number.astype(jnp.int32)


def mxu(a, b, dims):
    return lax.dot_general(a, b, (dims, ((), ())), preferred_element_type=F32)


def call(body, ins, outs, args, scratch=(), vmem=48):
    return pl.pallas_call(
        body,
        in_specs=ins,
        out_specs=[spec for spec, _, _ in outs],
        out_shape=[jax.ShapeDtypeStruct(shape, dtype) for _, shape, dtype in outs],
        scratch_shapes=list(scratch),
        cost_estimate=pl.CostEstimate(flops=1, bytes_accessed=1, transcendentals=0),
        compiler_params=pltpu.CompilerParams(vmem_limit_bytes=vmem * 1024 * 1024),
    )(*args)


def local(
    three_index, coeff, amps, eps_virt, eps_occ, nvirt, pair_occ, partners, coupling, pair_owner
):
    columns = lax.axis_size("pairs")
    roles = lax.axis_size("role")
    occ_block, aux, pao = three_index.shape
    pairs, _, virt = coeff.shape
    partner_count = partners.shape[1]
    slots = 2
    assert roles == pairs and pairs % 2 == 0 and columns % 2 == 0 and virt % 2 == 0
    tile = min(256, aux)
    pao_scale = 1.0 / math.sqrt(pao)
    aux_scale = 1.0 / math.sqrt(aux)
    virt_scale = 1.0 / math.sqrt(virt)
    square = (virt, virt)
    part = virt // 2
    sq_b = (VMEM, square, BF16)
    sq_f = (VMEM, square, F32)
    two_b = (VMEM, (2, virt, virt), BF16)
    all_s = (VMEM, (pairs, virt, virt), BF16)
    half = (VMEM, (aux, virt), BF16)

    inner_of = [i ^ 1 for i in range(columns)]
    outer_of = [(i + (1 if i % 2 else -1)) % columns for i in range(columns)]

    def inner(x):
        return lax.ppermute(x, "pairs", list(enumerate(inner_of)))

    def outer(x):
        return lax.ppermute(x, "pairs", list(enumerate(outer_of)))

    def swap(x, by):
        return lax.ppermute(x, "role", [(i, i ^ by) for i in range(roles)])

    three_in, coeff_in, amps_in = inner(three_index), inner(coeff), inner(amps)

    def pairs_of_roles(owner_ref):
        of_role = [jnp.int32(0)] * roles
        for p in range(pairs):
            earlier = jnp.int32(0)
            for o in range(p):
                earlier += (owner_ref[o] == owner_ref[p]).astype(I32)
            for s in range(roles):
                hit = (earlier == 0) & (owner_ref[p] == s) if s else earlier == 1
                of_role[s] = jnp.where(hit, p, of_role[s])
        return of_role

    def pick(numbers, at):
        chosen = numbers[0]
        for s in range(1, len(numbers)):
            chosen = jnp.where(at == s, numbers[s], chosen)
        return chosen

    weights = 2 * pairs
    place_at, mine_at, extra_at = 2 * weights, 2 * weights + 1, 2 * weights + 2
    riders = 16
    longer = (VMEM, (virt + riders, virt), BF16)
    longest = (VMEM, (virt + 2 * riders, virt), BF16)
    own_weights = ROLE_PAIR + roles

    def plan_body(
        owner_hbm, occ_hbm, partner_hbm, coupling_hbm, eps_hbm, nvirt_hbm, coeff_hbm,
        low_ref, high_ref, nums,
        owner_ref, occ_ref, partner_ref, coupling_ref, eps_ref, nvirt_ref, near_w, sems,
    ):
        small = [
            pltpu.make_async_copy(source, target, sems.at[at])
            for at, (source, target) in enumerate(
                (
                    (owner_hbm, owner_ref),
                    (occ_hbm, occ_ref),
                    (partner_hbm, partner_ref),
                    (coupling_hbm, coupling_ref),
                    (eps_hbm, eps_ref),
                    (nvirt_hbm, nvirt_ref),
                )
            )
        ]
        for copy in small:
            copy.start()
        role = lax.axis_index("role")
        column = lax.axis_index("pairs")
        small[0].wait()
        of_role = pairs_of_roles(owner_ref)
        extra = of_role[0]
        mine = pick(of_role, role)
        large = [
            pltpu.make_async_copy(coeff_hbm.at[mine, :, pl.ds(0, part)], low_ref.at[pl.ds(0, pao)], sems.at[6]),
            pltpu.make_async_copy(coeff_hbm.at[mine, :, pl.ds(part, part)], high_ref, sems.at[7]),
        ]
        for copy in large:
            copy.start()
        for copy in small[1:]:
            copy.wait()
        nums[MINE] = mine.astype(F32)
        nums[EXTRA] = extra.astype(F32)
        nums[OWNER] = owner_ref[extra].astype(F32)
        for s in range(roles):
            nums[ROLE_PAIR + s] = of_role[s].astype(F32)
        nums[NV_MINE] = nvirt_ref[mine].astype(F32)
        nums[NV_EXTRA] = nvirt_ref[extra].astype(F32)
        nums[FIRST] = (occ_ref[0, mine] - column * occ_block).astype(F32)
        odd = lax.rem(column, 2) == 1
        inner_at = jnp.where(odd, 0, 2)
        outer_at = 2 - inner_at
        occ_all = occ_block * columns
        second = lax.rem(occ_ref[1, mine] - (column - 1) * occ_block + occ_all, occ_all)
        block = (second >= occ_block).astype(I32) + (second >= 2 * occ_block).astype(I32)
        place = (second - block * occ_block).astype(F32)
        nums[SECOND] = place
        lane = lax.broadcasted_iota(I32, (riders, part), 1)
        row = lax.broadcasted_iota(I32, (riders, part), 0)
        told = jnp.where(lane == place_at, place, 0.0)
        told = jnp.where(lane == mine_at, mine.astype(F32), told)
        told = jnp.where(lane == extra_at, extra.astype(F32), told)
        nums[WHOSE] = jnp.where(block == 1, 0, jnp.where(block == inner_at, 1, 2)).astype(F32)
        nums[OCC_MINE] = eps_ref[occ_ref[0, mine]] + eps_ref[occ_ref[1, mine]]
        nums[OCC_EXTRA] = eps_ref[occ_ref[0, extra]] + eps_ref[occ_ref[1, extra]]
        pair_all = pairs * columns
        for which, pair in enumerate((mine, extra)):
            for q in range(3 * pairs):
                near_w[q] = jnp.float32(0)
            for k in range(partner_count):
                at = lax.rem(partner_ref[pair, k] - (column - 1) * pairs + pair_all, pair_all)
                near_w[at] += coupling_ref[pair, k]
            for q in range(pairs):
                to = which * pairs + q
                nums[own_weights + to] = near_w[pairs + q]
                nums[own_weights + weights + to] = near_w[inner_at * pairs + q]
                told = jnp.where(lane == to, near_w[outer_at * pairs + q], told)
                told = jnp.where(lane == weights + to, near_w[inner_at * pairs + q], told)
        coarse = told.astype(BF16).astype(F32)
        middle = (told - coarse).astype(BF16).astype(F32)
        fine = told - coarse - middle
        told = jnp.where(row == 0, coarse, jnp.where(row == 1, middle, jnp.where(row == 2, fine, 0.0)))
        low_ref[pao:, :] = told.astype(BF16)
        for copy in large:
            copy.wait()

    rode = (VMEM, (pao + riders, part), BF16)
    x_low, x_high, nums = call(
        plan_body,
        [HBM] * 7,
        [rode, (VMEM, (pao, part), BF16), (SMEM, (own_weights + 2 * weights,), F32)],
        (pair_owner, pair_occ.T, partners, coupling, eps_occ, nvirt, coeff),
        scratch=[
            pltpu.SMEM(pair_owner.shape, I32),
            pltpu.SMEM(pair_occ.shape[::-1], I32),
            pltpu.SMEM(partners.shape, I32),
            pltpu.SMEM(coupling.shape, F32),
            pltpu.SMEM(eps_occ.shape, F32),
            pltpu.SMEM(nvirt.shape, I32),
            pltpu.SMEM((3 * pairs,), F32),
            pltpu.SemaphoreType.DMA((8,)),
        ],
        vmem=60,
    )
    low_out, high_out, low_in = outer(x_low), outer(x_high), inner(x_low)

    def told_of(low_ref):
        rows = low_ref[pao:, :].astype(F32)
        return rows[0:1] + rows[1:2] + rows[2:3]

    def overlaps(x, coeff_ref, out_ref):
        turned = x.T
        for q in range(pairs):
            s = mxu(turned, coeff_ref[q], NN) * (1.0 / pao)
            out_ref[q] = s.astype(BF16)

    def coupled(s_ref, parts):
        total = None
        for at, weight, amp in parts:
            s = s_ref[at]
            u = mxu(s, amp, NN).astype(BF16)
            term = weight * mxu(u, s, NT)
            total = term if total is None else total + term
        return total

    tiles = [pl.ds(at, tile) for at in range(0, aux, tile)]

    def half_into(y_ref, three_ref, at_occ, x):
        for rows in tiles:
            y_ref[rows, :] = (mxu(three_ref[at_occ, rows, :], x, NN) * pao_scale).astype(BF16)

    def fetch_body(three_ref, after_ref, held_ref, sem):
        copy = pltpu.make_async_copy(three_ref, held_ref, sem)
        copy.start()
        copy.wait()

    (blocks,) = call(
        fetch_body,
        [ANY, ANY],
        [(VMEM, three_index.shape, BF16)],
        (three_index, nums),
        scratch=[pltpu.SemaphoreType.DMA],
        vmem=50,
    )

    def outer_low_body(three_ref, x_ref, y_ref):
        half_into(y_ref, three_ref, whole(told_of(x_ref)[0, place_at]), x_ref[:pao, :])
        y_ref[aux:, :] = jnp.zeros((riders, part), BF16)

    (y_low,) = call(
        outer_low_body,
        [VMEM, VMEM],
        [(VMEM, (aux + riders, part), BF16)],
        (blocks, low_out),
    )
    y_low_from_out = outer(y_low)

    def outer_high_body(three_ref, low_ref, x_ref, after_ref, y_ref):
        half_into(y_ref, three_ref, whole(told_of(low_ref)[0, place_at]), x_ref[...])

    (y_high,) = call(
        outer_high_body,
        [VMEM, VMEM, VMEM, ANY],
        [(VMEM, (aux, part), BF16)],
        (blocks, low_out, high_out, y_low),
    )
    y_high_from_out = outer(y_high)

    def outer_body(coeff_ref, amps_ref, low_ref, high_ref, after_ref, s_ref, c_ref, x_ref):
        x_ref[:, :part] = low_ref[:pao, :]
        x_ref[:, part:] = high_ref[...]
        overlaps(x_ref[...], coeff_ref, s_ref)
        told = told_of(low_ref)
        c = coupled(s_ref, [(q, told[0, q], amps_ref[q]) for q in range(pairs)])
        c_ref[:virt, :] = c.astype(BF16)
        c_ref[virt:, :] = jnp.zeros((riders, virt), BF16)

    s_out, c_out = call(
        outer_body,
        [VMEM, VMEM, VMEM, VMEM, ANY],
        [all_s, longer],
        (coeff, amps, low_out, high_out, y_high),
        scratch=[pltpu.VMEM((pao, virt), BF16)],
    )
    c_from_out = outer(c_out)

    def own_half_body(
        nums, three_ref, three_in_ref, coeff_ref, after_ref,
        first_ref, second_ref, extra_0_ref, extra_1_ref, block_ref, sem,
    ):
        x = coeff_ref[whole(nums[MINE])]
        extra_0_ref[...] = coeff_ref[whole(nums[EXTRA]), : pao // 2, :]
        extra_1_ref[...] = coeff_ref[whole(nums[EXTRA]), pao // 2 :, :]
        whose, second = whole(nums[WHOSE]), whole(nums[SECOND])
        copy = pltpu.make_async_copy(three_in_ref.at[second], block_ref.at[0], sem)

        @pl.when(whose == 1)
        def _():
            copy.start()

        turned = x.T
        first = whole(nums[FIRST])
        for rows in tiles:
            first_ref[:, rows] = (mxu(turned, three_ref[first, rows, :], NT) * pao_scale).astype(BF16)

        @pl.when(whose == 0)
        def _():
            half_into(second_ref, three_ref, second, x)

        @pl.when(whose == 1)
        def _():
            copy.wait()
            half_into(second_ref, block_ref, 0, x)

    first_t, second, *x_extra = call(
        own_half_body,
        [SMEM, VMEM, ANY, VMEM, ANY],
        [
            (VMEM, (virt, aux), BF16),
            (VMEM, (aux, virt), BF16),
            (VMEM, (pao // 2, virt), BF16),
            (VMEM, (pao // 2, virt), BF16),
        ],
        (nums, blocks, three_in, coeff, c_out),
        scratch=[pltpu.VMEM((1, aux, pao), BF16), pltpu.SemaphoreType.DMA],
    )
    x_extra_out = [outer(x) for x in x_extra]

    def own_body(
        nums, coeff_ref, coeff_in_ref, amps_ref, amps_in_ref, eps_ref, after_ref,
        s_ref, c_ref, gain_ref, gain_extra_ref, s_in_ref,
    ):
        mine, extra = whole(nums[MINE]), whole(nums[EXTRA])
        x = coeff_ref[mine]
        total = None
        for at, of_s, of_coeff, of_amps in (
            (own_weights, s_ref, coeff_ref, amps_ref),
            (own_weights + weights, s_in_ref, coeff_in_ref, amps_in_ref),
        ):
            overlaps(x, of_coeff, of_s)
            c = coupled(of_s, [(q, nums[at + q], of_amps[q]) for q in range(pairs)])
            total = c if total is None else total + c
        c_ref[...] = total

        def gain(pair, count, occupied):
            row = jnp.broadcast_to(eps_ref[pl.ds(pair, 1), :], square)
            energy = row + row.T - occupied
            inside = (lax.broadcasted_iota(I32, square, 0) < count) & (
                lax.broadcasted_iota(I32, square, 1) < count
            )
            return jnp.where(inside, 1.0 / (energy + 1.0), 0.0)

        gain_ref[...] = gain(mine, whole(nums[NV_MINE]), nums[OCC_MINE])
        gain_extra_ref[...] = gain(extra, whole(nums[NV_EXTRA]), nums[OCC_EXTRA])

    s_own, c_own, gain, gain_extra = call(
        own_body,
        [SMEM] + [VMEM] * 5 + [ANY],
        [all_s, sq_f, sq_f, sq_f],
        (nums, coeff, coeff_in, amps, amps_in, eps_virt, c_out),
        scratch=[pltpu.VMEM((pairs, virt, virt), BF16)],
    )

    def more_body(nums, coeff_ref, in_ref, low_ref, after_ref, se_ref, s_in_ref, se_in_ref):
        @pl.when(lax.axis_index("role") > 0)
        def _():
            told = told_of(low_ref)
            overlaps(coeff_ref[whole(nums[EXTRA])], coeff_ref, se_ref)
            overlaps(in_ref[whole(told[0, mine_at])], coeff_ref, s_in_ref)
            overlaps(in_ref[whole(told[0, extra_at])], coeff_ref, se_in_ref)

    se_own, s_in, se_in = call(
        more_body,
        [SMEM, VMEM, VMEM, VMEM, ANY],
        [all_s, all_s, all_s],
        (nums, coeff, coeff_in, low_in, c_own),
    )

    def first_body(
        nums, first_ref, second_ref, low_ref, high_ref, amps_ref, c_ref, co_ref, gain_ref, after_ref,
        amp_ref, amp_long_ref, k_ref,
    ):
        first = first_ref[...]
        outside = whole(nums[WHOSE]) == 2

        @pl.when(outside)
        def _():
            k_ref[:, :part] = mxu(first, low_ref[:aux, :], NN) * aux_scale
            k_ref[:, part:] = mxu(first, high_ref[...], NN) * aux_scale

        @pl.when(jnp.logical_not(outside))
        def _():
            k_ref[...] = mxu(first, second_ref[...], NN) * aux_scale

        old = amps_ref[whole(nums[MINE])].astype(F32)
        c = c_ref[...] + co_ref[:virt, :].astype(F32)
        amp = (gain_ref[...] * (old - k_ref[...] - c)).astype(BF16)
        for ref in (amp_ref, amp_long_ref):
            ref[:virt, :] = amp
            ref[virt:, :] = jnp.zeros((ref.shape[0] - virt, virt), BF16)

    amp, amp_long, k_first = call(
        first_body,
        [SMEM] + [VMEM] * 8 + [ANY],
        [longer, longest, sq_f],
        (
            nums, first_t, second, y_low_from_out, y_high_from_out,
            amps, c_own, c_from_out, gain, se_own,
        ),
    )
    amp_roles = [amp] + [swap(amp, m) for m in range(1, roles - 1)] + [swap(amp_long, roles - 1)]

    def rest_body(amp_ref, k_ref, out_ref, out_b_ref):
        amp = amp_ref[:virt, :]
        k = k_ref[...]
        right = k + mxu(k.astype(BF16), amp, NN) * virt_scale
        both = right + mxu(amp.T, right.astype(BF16), NN) * virt_scale
        rest = amp.astype(F32) - both
        out_ref[...] = rest
        out_b_ref[:virt, :] = rest.astype(BF16)
        out_b_ref[virt:, :] = jnp.zeros((2 * riders, virt), BF16)

    rest, rest_b = call(rest_body, [VMEM, VMEM], [sq_f, longest], (amp, k_first))
    rests = [lax.ppermute(rest_b, "role", [(0, s)]) for s in range(roles - 1, 0, -1)]

    def parts_of(nums, weight_of, amp_refs):
        role = lax.axis_index("role")
        parts = []
        for m in range(roles):
            at = whole(nums[ROLE_PAIR + (role ^ m)])
            parts.append((at, weight_of(at), amp_refs[m][:virt, :]))
        return parts

    def told_weight(told, first):
        return lambda at: pick([told[:, first + q : first + q + 1] for q in range(pairs)], at)

    def outer_again_body(slot, nums, low_ref, s_ref, *refs):
        amp_refs, c_ref = refs[:roles], refs[-1]

        @pl.when(lax.axis_index("role") > 0)
        def _():
            parts = parts_of(nums, told_weight(told_of(low_ref), slot * pairs), amp_refs)
            c = coupled(s_ref, parts).astype(BF16)
            if slot:
                c_ref[0] = refs[roles][...]
                c_ref[1] = c
            else:
                c_ref[...] = c

    def outer_again(slot, s, out, *before):
        (c,) = call(
            functools.partial(outer_again_body, slot),
            [SMEM] + [VMEM] * (2 + roles + len(before)),
            [out],
            (nums, low_out, s, *amp_roles, *before),
        )
        return c

    c_mine = outer_again(0, s_out, sq_b)

    def extra_out_body(coeff_ref, x_0_ref, x_1_ref, after_ref, s_ref, x_ref):
        @pl.when(lax.axis_index("role") > 0)
        def _():
            x_ref[: pao // 2, :] = x_0_ref[...]
            x_ref[pao // 2 :, :] = x_1_ref[...]
            overlaps(x_ref[...], coeff_ref, s_ref)

    (se_out,) = call(
        extra_out_body,
        [VMEM, VMEM, VMEM, ANY],
        [all_s],
        (coeff, *x_extra_out, c_mine),
        scratch=[pltpu.VMEM((pao, virt), BF16)],
    )

    cc_out = outer_again(1, se_out, two_b, c_mine)
    cc_from_out = outer(cc_out)

    def inner_again_body(nums, low_ref, s_ref, se_ref, *refs):
        amp_refs, c_refs = refs[:roles], refs[-2:]

        @pl.when(lax.axis_index("role") > 0)
        def _():
            told = told_of(low_ref)
            for slot, of_s, c_ref in zip(range(2), (s_ref, se_ref), c_refs):
                parts = parts_of(nums, told_weight(told, weights + slot * pairs), amp_refs)
                c_ref[:virt, :] = coupled(of_s, parts).astype(BF16)
                c_ref[virt:, :] = jnp.zeros((riders, virt), BF16)

    c_in, ce_in = call(
        inner_again_body,
        [SMEM] + [VMEM] * (3 + roles) + [ANY],
        [longer, longer],
        (nums, low_in, s_in, se_in, *amp_roles, cc_out),
    )
    c_from_in, ce_from_in = inner(c_in), inner(ce_in)

    def own_again_body(nums, rest_ref, s_ref, se_ref, *refs):
        amp_refs, (after_ref, out_ref, out_extra_ref) = refs[:roles], refs[-3:]

        @pl.when(lax.axis_index("role") > 0)
        def _():
            parts = parts_of(nums, lambda at: nums[own_weights + at], amp_refs)
            out_ref[...] = rest_ref[...] - coupled(s_ref, parts)
            parts = parts_of(nums, lambda at: nums[own_weights + pairs + at], amp_refs)
            out_extra_ref[...] = -coupled(se_ref, parts)

    rest, rest_extra = call(
        own_again_body,
        [SMEM] + [VMEM] * (3 + roles) + [ANY],
        [sq_f, sq_f],
        (nums, rest, s_own, se_own, *amp_roles, c_in),
    )

    def last_body(
        nums, coeff_ref, gain_ref, gain_extra_ref, rest_ref, rest_extra_ref, co_ref, ci_ref, cei_ref, *refs
    ):
        rest_refs, (amp_out, orb_out, amp_ref, orb_ref, sems) = refs[: roles - 1], refs[roles - 1 :]
        role = lax.axis_index("role")
        copies = []

        def send(source, target):
            copies.append(pltpu.make_async_copy(source, target, sems.at[len(copies)]))
            copies[-1].start()

        def store(slot, here, gain, rest, c_in, pair):
            @pl.when(here)
            def _():
                total = rest[...] - co_ref[slot].astype(F32) - c_in[:virt, :].astype(F32)
                for s in range(1, roles):
                    if slot:
                        come = rest_refs[roles - 1 - s][:virt, :].astype(F32)
                        total += jnp.where(role == s, come, 0.0)
                amp_ref[slot] = (gain[...] * total).astype(BF16)

            @pl.when(jnp.logical_not(here))
            def _():
                amp_ref[slot] = jnp.zeros(square, BF16)

            send(amp_ref.at[slot], amp_out.at[slot])
            for at in range(0, pao, virt):
                rows = pl.ds(at, virt)

                @pl.when(here)
                def _():
                    x = coeff_ref[pair, rows, :]
                    dressed = x.astype(F32) + mxu(x, amp_ref[slot], NN) * virt_scale
                    orb_ref[slot, rows, :] = dressed.astype(BF16)

                @pl.when(jnp.logical_not(here))
                def _():
                    orb_ref[slot, rows, :] = jnp.zeros((virt, virt), BF16)

                send(orb_ref.at[slot, rows], orb_out.at[slot, rows])

        store(0, role > 0, gain_ref, rest_ref, ci_ref, whole(nums[MINE]))
        has_extra = role == whole(nums[OWNER])
        store(1, has_extra, gain_extra_ref, rest_extra_ref, cei_ref, whole(nums[EXTRA]))
        for copy in copies:
            copy.wait()

    amps_out, dressed_out = call(
        last_body,
        [SMEM] + [VMEM] * (8 + roles - 1),
        [(ANY, (slots, virt, virt), BF16), (ANY, (slots, pao, virt), BF16)],
        (
            nums, coeff, gain, gain_extra, rest, rest_extra,
            cc_from_out, c_from_in, ce_from_in, *rests,
        ),
        scratch=[
            pltpu.VMEM((slots, virt, virt), BF16),
            pltpu.VMEM((slots, pao, virt), BF16),
            pltpu.SemaphoreType.DMA((slots * (1 + pao // virt),)),
        ],
    )
    return amps_out, dressed_out


def solution(mesh):
    in_specs = (
        P("pairs", None, None),
        P("pairs", None, None),
        P("pairs", None, None),
        P("pairs", None),
        P(),
        P("pairs"),
        P("pairs", None),
        P("pairs", None),
        P("pairs", None),
        P("pairs"),
    )
    out_specs = (P(("role", "pairs"), None, None), P(("role", "pairs"), None, None))
    return jax.shard_map(local, mesh=mesh, in_specs=in_specs, out_specs=out_specs, check_vma=False)
```

```python
import math

import jax
import jax.numpy as jnp
from jax import lax
from jax.experimental import pallas as pl
from jax.experimental.pallas import tpu as pltpu
from jax.sharding import PartitionSpec as P

F32 = jnp.float32
BF16 = jnp.bfloat16
I32 = jnp.int32
NN = ((1,), (0,))
NT = ((1,), (1,))

VMEM = pl.BlockSpec(memory_space=pltpu.VMEM)
ANY = pl.BlockSpec(memory_space=pl.ANY)
HBM = pl.BlockSpec(memory_space=pltpu.HBM)

MINE, EXTRA, OWNER, FIRST, SECOND, WHOSE, NV_MINE, NV_EXTRA, OCC_MINE, OCC_EXTRA, ROLE_PAIR = range(11)


def whole(number):
    return number.astype(jnp.int32)


def read(nums_ref):
    row = nums_ref[0:1, :]
    return lambda at: row[0, at], lambda at: row[:, at : at + 1]


def mxu(a, b, dims):
    return lax.dot_general(a, b, (dims, ((), ())), preferred_element_type=F32)


def call(body, ins, outs, args, scratch=(), vmem=48):
    return pl.pallas_call(
        body,
        in_specs=ins,
        out_specs=[spec for spec, _, _ in outs],
        out_shape=[jax.ShapeDtypeStruct(shape, dtype) for _, shape, dtype in outs],
        scratch_shapes=list(scratch),
        cost_estimate=pl.CostEstimate(flops=1, bytes_accessed=1, transcendentals=0),
        compiler_params=pltpu.CompilerParams(vmem_limit_bytes=vmem * 1024 * 1024),
    )(*args)


def local(
    three_index, coeff, amps, eps_virt, eps_occ, nvirt, pair_occ, partners, coupling, pair_owner
):
    columns = lax.axis_size("pairs")
    roles = lax.axis_size("role")
    occ_block, aux, pao = three_index.shape
    pairs, _, virt = coeff.shape
    partner_count = partners.shape[1]
    slots = 2
    assert roles == pairs and pairs % 2 == 0 and columns % 2 == 0 and virt % 2 == 0
    tile = min(256, aux)
    pao_scale = 1.0 / math.sqrt(pao)
    aux_scale = 1.0 / math.sqrt(aux)
    virt_scale = 1.0 / math.sqrt(virt)
    square = (virt, virt)
    part = virt // 2
    sq_b = (VMEM, square, BF16)
    sq_f = (VMEM, square, F32)
    two_b = (VMEM, (2, virt, virt), BF16)
    all_s = (VMEM, (pairs, virt, virt), BF16)
    half = (VMEM, (aux, virt), BF16)

    inner_of = [i ^ 1 for i in range(columns)]
    outer_of = [(i + (1 if i % 2 else -1)) % columns for i in range(columns)]

    def inner(x):
        return lax.ppermute(x, "pairs", list(enumerate(inner_of)))

    def outer(x):
        return lax.ppermute(x, "pairs", list(enumerate(outer_of)))

    def swap(x, by):
        return lax.ppermute(x, "role", [(i, i ^ by) for i in range(roles)])

    three_in, coeff_in, amps_in = inner(three_index), inner(coeff), inner(amps)

    def pairs_of_roles(owner_ref):
        of_role = [jnp.int32(0)] * roles
        for p in range(pairs):
            earlier = jnp.int32(0)
            for o in range(p):
                earlier += (owner_ref[o] == owner_ref[p]).astype(I32)
            for s in range(roles):
                hit = (earlier == 0) & (owner_ref[p] == s) if s else earlier == 1
                of_role[s] = jnp.where(hit, p, of_role[s])
        return of_role

    def pick(numbers, at):
        chosen = numbers[0]
        for s in range(1, len(numbers)):
            chosen = jnp.where(at == s, numbers[s], chosen)
        return chosen

    weights = 2 * pairs
    place_at, mine_at, extra_at = 2 * weights, 2 * weights + 1, 2 * weights + 2
    riders = 16
    longer = (VMEM, (virt + riders, virt), BF16)
    own_weights = ROLE_PAIR + roles

    def plan_body(
        owner_hbm, occ_hbm, partner_hbm, coupling_hbm, eps_hbm, nvirt_hbm, coeff_hbm,
        low_ref, high_ref, nums_ref,
        owner_ref, occ_ref, partner_ref, coupling_ref, eps_ref, nvirt_ref, near_w, sems,
    ):
        small = [
            pltpu.make_async_copy(source, target, sems.at[at])
            for at, (source, target) in enumerate(
                (
                    (owner_hbm, owner_ref),
                    (occ_hbm, occ_ref),
                    (partner_hbm, partner_ref),
                    (coupling_hbm, coupling_ref),
                    (eps_hbm, eps_ref),
                    (nvirt_hbm, nvirt_ref),
                )
            )
        ]
        for copy in small:
            copy.start()
        role = lax.axis_index("role")
        column = lax.axis_index("pairs")
        small[0].wait()
        of_role = pairs_of_roles(owner_ref)
        extra = of_role[0]
        mine = pick(of_role, role)
        large = [
            pltpu.make_async_copy(coeff_hbm.at[mine, :, pl.ds(0, part)], low_ref.at[pl.ds(0, pao)], sems.at[6]),
            pltpu.make_async_copy(coeff_hbm.at[mine, :, pl.ds(part, part)], high_ref, sems.at[7]),
        ]
        for copy in large:
            copy.start()
        for copy in small[1:]:
            copy.wait()
        nums = {}
        nums[MINE] = mine.astype(F32)
        nums[EXTRA] = extra.astype(F32)
        nums[OWNER] = owner_ref[extra].astype(F32)
        for m in range(roles):
            nums[ROLE_PAIR + m] = pick(of_role, role ^ m).astype(F32)
        nums[NV_MINE] = nvirt_ref[mine].astype(F32)
        nums[NV_EXTRA] = nvirt_ref[extra].astype(F32)
        nums[FIRST] = (occ_ref[0, mine] - column * occ_block).astype(F32)
        odd = lax.rem(column, 2) == 1
        inner_at = jnp.where(odd, 0, 2)
        outer_at = 2 - inner_at
        occ_all = occ_block * columns
        second = lax.rem(occ_ref[1, mine] - (column - 1) * occ_block + occ_all, occ_all)
        block = (second >= occ_block).astype(I32) + (second >= 2 * occ_block).astype(I32)
        place = (second - block * occ_block).astype(F32)
        nums[SECOND] = place
        lane = lax.broadcasted_iota(I32, (riders, part), 1)
        row = lax.broadcasted_iota(I32, (riders, part), 0)
        told = jnp.where(lane == place_at, place, 0.0)
        told = jnp.where(lane == mine_at, mine.astype(F32), told)
        told = jnp.where(lane == extra_at, extra.astype(F32), told)
        nums[WHOSE] = jnp.where(block == 1, 0, jnp.where(block == inner_at, 1, 2)).astype(F32)
        nums[OCC_MINE] = eps_ref[occ_ref[0, mine]] + eps_ref[occ_ref[1, mine]]
        nums[OCC_EXTRA] = eps_ref[occ_ref[0, extra]] + eps_ref[occ_ref[1, extra]]
        pair_all = pairs * columns
        for which, pair in enumerate((mine, extra)):
            for q in range(3 * pairs):
                near_w[q] = jnp.float32(0)
            for k in range(partner_count):
                at = lax.rem(partner_ref[pair, k] - (column - 1) * pairs + pair_all, pair_all)
                near_w[at] += coupling_ref[pair, k]
            for q in range(pairs):
                to = which * pairs + q
                nums[own_weights + to] = near_w[pairs + q]
                nums[own_weights + weights + to] = near_w[inner_at * pairs + q]
                told = jnp.where(lane == to, near_w[outer_at * pairs + q], told)
                told = jnp.where(lane == weights + to, near_w[inner_at * pairs + q], told)
        row_of_nums = jnp.zeros(nums_ref.shape, F32)
        lane_of_nums = lax.broadcasted_iota(I32, nums_ref.shape, 1)
        for at, number in nums.items():
            row_of_nums = jnp.where(lane_of_nums == at, number, row_of_nums)
        nums_ref[...] = row_of_nums
        coarse = told.astype(BF16).astype(F32)
        middle = (told - coarse).astype(BF16).astype(F32)
        fine = told - coarse - middle
        told = jnp.where(row == 0, coarse, jnp.where(row == 1, middle, jnp.where(row == 2, fine, 0.0)))
        low_ref[pao:, :] = told.astype(BF16)
        for copy in large:
            copy.wait()

    rode = (VMEM, (pao + riders, part), BF16)
    x_low, x_high, nums = call(
        plan_body,
        [HBM] * 7,
        [rode, (VMEM, (pao, part), BF16), (VMEM, (8, part), F32)],
        (pair_owner, pair_occ.T, partners, coupling, eps_occ, nvirt, coeff),
        scratch=[
            pltpu.SMEM(pair_owner.shape, I32),
            pltpu.SMEM(pair_occ.shape[::-1], I32),
            pltpu.SMEM(partners.shape, I32),
            pltpu.SMEM(coupling.shape, F32),
            pltpu.SMEM(eps_occ.shape, F32),
            pltpu.SMEM(nvirt.shape, I32),
            pltpu.SMEM((3 * pairs,), F32),
            pltpu.SemaphoreType.DMA((8,)),
        ],
        vmem=60,
    )
    low_out, high_out, low_in = outer(x_low), outer(x_high), inner(x_low)

    def told_of(low_ref):
        rows = low_ref[pao:, :].astype(F32)
        return rows[0:1] + rows[1:2] + rows[2:3]

    def overlaps(x, coeff_ref, out_ref):
        turned = x.T
        for q in range(pairs):
            s = mxu(turned, coeff_ref[q], NN) * (1.0 / pao)
            out_ref[q] = s.astype(BF16)

    def coupled(s_ref, parts):
        total = None
        for at, weight, amp in parts:
            s = s_ref[at]
            u = mxu(s, amp, NN).astype(BF16)
            term = weight * mxu(u, s, NT)
            total = term if total is None else total + term
        return total

    tiles = [pl.ds(at, tile) for at in range(0, aux, tile)]

    def half_into(y_ref, three_ref, at_occ, x):
        for rows in tiles:
            y_ref[rows, :] = (mxu(three_ref[at_occ, rows, :], x, NN) * pao_scale).astype(BF16)

    def fetch_body(three_ref, after_ref, held_ref, sem):
        copy = pltpu.make_async_copy(three_ref, held_ref, sem)
        copy.start()
        copy.wait()

    (blocks,) = call(
        fetch_body,
        [ANY, ANY],
        [(VMEM, three_index.shape, BF16)],
        (three_index, nums),
        scratch=[pltpu.SemaphoreType.DMA],
        vmem=50,
    )

    def outer_low_body(three_ref, x_ref, y_ref):
        half_into(y_ref, three_ref, whole(told_of(x_ref)[0, place_at]), x_ref[:pao, :])
        y_ref[aux:, :] = jnp.zeros((riders, part), BF16)

    (y_low,) = call(
        outer_low_body,
        [VMEM, VMEM],
        [(VMEM, (aux + riders, part), BF16)],
        (blocks, low_out),
    )
    y_low_from_out = outer(y_low)

    def outer_high_body(three_ref, low_ref, x_ref, after_ref, y_ref):
        half_into(y_ref, three_ref, whole(told_of(low_ref)[0, place_at]), x_ref[...])

    (y_high,) = call(
        outer_high_body,
        [VMEM, VMEM, VMEM, ANY],
        [(VMEM, (aux, part), BF16)],
        (blocks, low_out, high_out, y_low),
    )
    y_high_from_out = outer(y_high)

    def outer_body(coeff_ref, amps_ref, low_ref, high_ref, after_ref, s_ref, c_ref, x_ref):
        x_ref[:, :part] = low_ref[:pao, :]
        x_ref[:, part:] = high_ref[...]
        overlaps(x_ref[...], coeff_ref, s_ref)
        told = told_of(low_ref)
        c = coupled(s_ref, [(q, told[0, q], amps_ref[q]) for q in range(pairs)])
        c_ref[:virt, :] = c.astype(BF16)
        c_ref[virt:, :] = jnp.zeros((riders, virt), BF16)

    s_out, c_out = call(
        outer_body,
        [VMEM, VMEM, VMEM, VMEM, ANY],
        [all_s, longer],
        (coeff, amps, low_out, high_out, y_high),
        scratch=[pltpu.VMEM((pao, virt), BF16)],
    )
    c_from_out = outer(c_out)

    def own_half_body(
        nums, three_ref, three_in_ref, coeff_ref, after_ref, first_ref, second_ref, extra_ref, block_ref, sem
    ):
        num, _ = read(nums)
        x = coeff_ref[whole(num(MINE))]
        extra_ref[...] = coeff_ref[whole(num(EXTRA))]
        whose, second = whole(num(WHOSE)), whole(num(SECOND))
        copy = pltpu.make_async_copy(three_in_ref.at[second], block_ref.at[0], sem)

        @pl.when(whose == 1)
        def _():
            copy.start()

        turned = x.T
        first = whole(num(FIRST))
        for rows in tiles:
            first_ref[:, rows] = (mxu(turned, three_ref[first, rows, :], NT) * pao_scale).astype(BF16)

        @pl.when(whose == 0)
        def _():
            half_into(second_ref, three_ref, second, x)

        @pl.when(whose == 1)
        def _():
            copy.wait()
            half_into(second_ref, block_ref, 0, x)

    first_t, second, x_extra = call(
        own_half_body,
        [VMEM, VMEM, ANY, VMEM, ANY],
        [
            (VMEM, (virt, aux), BF16),
            (VMEM, (aux, virt), BF16),
            (VMEM, (pao, virt), BF16),
        ],
        (nums, blocks, three_in, coeff, c_out),
        scratch=[pltpu.VMEM((1, aux, pao), BF16), pltpu.SemaphoreType.DMA],
    )
    x_extra_out = outer(x_extra)

    def own_body(
        nums, coeff_ref, coeff_in_ref, amps_ref, amps_in_ref, eps_ref, after_ref,
        s_ref, c_ref, gain_ref, gain_extra_ref, s_in_ref,
    ):
        num, weight = read(nums)
        mine, extra = whole(num(MINE)), whole(num(EXTRA))
        x = coeff_ref[mine]
        total = None
        for at, of_s, of_coeff, of_amps in (
            (own_weights, s_ref, coeff_ref, amps_ref),
            (own_weights + weights, s_in_ref, coeff_in_ref, amps_in_ref),
        ):
            overlaps(x, of_coeff, of_s)
            c = coupled(of_s, [(q, weight(at + q), of_amps[q]) for q in range(pairs)])
            total = c if total is None else total + c
        c_ref[...] = total

        def gain(pair, count, occupied):
            row = jnp.broadcast_to(eps_ref[pl.ds(pair, 1), :], square)
            energy = row + row.T - occupied
            inside = (lax.broadcasted_iota(I32, square, 0) < count) & (
                lax.broadcasted_iota(I32, square, 1) < count
            )
            return jnp.where(inside, 1.0 / (energy + 1.0), 0.0)

        gain_ref[...] = gain(mine, whole(num(NV_MINE)), num(OCC_MINE))
        gain_extra_ref[...] = gain(extra, whole(num(NV_EXTRA)), num(OCC_EXTRA))

    s_own, c_own, gain, gain_extra = call(
        own_body,
        [VMEM] + [VMEM] * 5 + [ANY],
        [all_s, sq_f, sq_f, sq_f],
        (nums, coeff, coeff_in, amps, amps_in, eps_virt, c_out),
        scratch=[pltpu.VMEM((pairs, virt, virt), BF16)],
    )

    def more_body(nums, coeff_ref, in_ref, low_ref, after_ref, se_ref, s_in_ref, se_in_ref):
        @pl.when(lax.axis_index("role") > 0)
        def _():
            told = told_of(low_ref)
            num, _ = read(nums)
            overlaps(coeff_ref[whole(num(EXTRA))], coeff_ref, se_ref)
            overlaps(in_ref[whole(told[0, mine_at])], coeff_ref, s_in_ref)
            overlaps(in_ref[whole(told[0, extra_at])], coeff_ref, se_in_ref)

    se_own, s_in, se_in = call(
        more_body,
        [VMEM, VMEM, VMEM, VMEM, ANY],
        [all_s, all_s, all_s],
        (nums, coeff, coeff_in, low_in, c_own),
    )

    def first_body(
        nums, first_ref, second_ref, low_ref, high_ref, amps_ref, c_ref, co_ref, gain_ref, after_ref,
        amp_ref, amp_long_ref, k_ref,
    ):
        first = first_ref[...]
        num, _ = read(nums)
        outside = whole(num(WHOSE)) == 2

        @pl.when(outside)
        def _():
            k_ref[:, :part] = mxu(first, low_ref[:aux, :], NN) * aux_scale
            k_ref[:, part:] = mxu(first, high_ref[...], NN) * aux_scale

        @pl.when(jnp.logical_not(outside))
        def _():
            k_ref[...] = mxu(first, second_ref[...], NN) * aux_scale

        old = amps_ref[whole(num(MINE))].astype(F32)
        c = c_ref[...] + co_ref[:virt, :].astype(F32)
        amp = (gain_ref[...] * (old - k_ref[...] - c)).astype(BF16)
        amp_ref[...] = amp
        amp_long_ref[:virt, :] = amp
        amp_long_ref[virt:, :] = jnp.zeros((riders, virt), BF16)

    amp, amp_long, k_first = call(
        first_body,
        [VMEM] + [VMEM] * 8 + [ANY],
        [sq_b, longer, sq_f],
        (
            nums, first_t, second, y_low_from_out, y_high_from_out,
            amps, c_own, c_from_out, gain, se_own,
        ),
    )
    amp_roles = [amp] + [swap(amp, m) for m in range(1, roles - 1)] + [swap(amp_long, roles - 1)]

    def rest_body(amp_ref, k_ref, out_ref, out_b_ref):
        amp = amp_ref[...]
        k = k_ref[...]
        right = k + mxu(k.astype(BF16), amp, NN) * virt_scale
        both = right + mxu(amp.T, right.astype(BF16), NN) * virt_scale
        rest = amp.astype(F32) - both
        out_ref[...] = rest
        out_b_ref[:virt, :] = rest.astype(BF16)
        out_b_ref[virt:, :] = jnp.zeros((2 * riders, virt), BF16)

    longest = (VMEM, (virt + 2 * riders, virt), BF16)
    rest, rest_b = call(rest_body, [VMEM, VMEM], [sq_f, longest], (amp, k_first))
    rests = [lax.ppermute(rest_b, "role", [(0, s)]) for s in range(roles - 1, 0, -1)]

    def extra_out_body(coeff_ref, x_ref, after_ref, s_ref):
        @pl.when(lax.axis_index("role") > 0)
        def _():
            overlaps(x_ref[...], coeff_ref, s_ref)

    (se_out,) = call(
        extra_out_body,
        [VMEM, VMEM, ANY],
        [all_s],
        (coeff, x_extra_out, amp),
    )

    def parts_of(nums, weight_of, amp_refs):
        num, _ = read(nums)
        parts = []
        for m in range(roles):
            at = whole(num(ROLE_PAIR + m))
            parts.append((at, weight_of(at), amp_refs[m][:virt, :]))
        return parts

    def told_weight(told, first):
        return lambda at: pick([told[:, first + q : first + q + 1] for q in range(pairs)], at)

    def outer_again_body(nums, low_ref, s_ref, se_ref, *refs):
        amp_refs, c_ref = refs[:roles], refs[-1]

        @pl.when(lax.axis_index("role") > 0)
        def _():
            told = told_of(low_ref)
            for slot, of_s in enumerate((s_ref, se_ref)):
                parts = parts_of(nums, told_weight(told, slot * pairs), amp_refs)
                c_ref[slot] = coupled(of_s, parts).astype(BF16)

    (cc_out,) = call(
        outer_again_body,
        [VMEM] + [VMEM] * (3 + roles),
        [two_b],
        (nums, low_out, s_out, se_out, *amp_roles),
    )
    cc_from_out = outer(cc_out)

    def inner_again_body(nums, low_ref, s_ref, se_ref, *refs):
        amp_refs, c_refs = refs[:roles], refs[-2:]

        @pl.when(lax.axis_index("role") > 0)
        def _():
            told = told_of(low_ref)
            for slot, of_s, c_ref in zip(range(2), (s_ref, se_ref), c_refs):
                parts = parts_of(nums, told_weight(told, weights + slot * pairs), amp_refs)
                c_ref[:virt, :] = coupled(of_s, parts).astype(BF16)
                c_ref[virt:, :] = jnp.zeros((riders, virt), BF16)

    c_in, ce_in = call(
        inner_again_body,
        [VMEM] + [VMEM] * (3 + roles) + [ANY],
        [longer, longer],
        (nums, low_in, s_in, se_in, *amp_roles, cc_out),
    )
    c_from_in, ce_from_in = inner(c_in), inner(ce_in)

    def own_again_body(nums, rest_ref, s_ref, se_ref, *refs):
        amp_refs, (after_ref, out_ref, out_extra_ref) = refs[:roles], refs[-3:]

        @pl.when(lax.axis_index("role") > 0)
        def _():
            row = nums[0:1, :]
            parts = parts_of(nums, told_weight(row, own_weights), amp_refs)
            out_ref[...] = rest_ref[...] - coupled(s_ref, parts)
            parts = parts_of(nums, told_weight(row, own_weights + pairs), amp_refs)
            out_extra_ref[...] = -coupled(se_ref, parts)

    rest, rest_extra = call(
        own_again_body,
        [VMEM] + [VMEM] * (3 + roles) + [ANY],
        [sq_f, sq_f],
        (nums, rest, s_own, se_own, *amp_roles, c_in),
    )

    def last_body(
        nums, coeff_ref, gain_ref, gain_extra_ref, rest_ref, rest_extra_ref, co_ref, ci_ref, cei_ref, *refs
    ):
        rest_refs, (amp_out, orb_out, amp_ref, orb_ref, sems) = refs[: roles - 1], refs[roles - 1 :]
        num, _ = read(nums)
        role = lax.axis_index("role")
        copies = []

        def send(source, target):
            copies.append(pltpu.make_async_copy(source, target, sems.at[len(copies)]))
            copies[-1].start()

        def store(slot, here, gain, rest, c_in, pair):
            @pl.when(here)
            def _():
                total = rest[...] - co_ref[slot].astype(F32) - c_in[:virt, :].astype(F32)
                for s in range(1, roles):
                    if slot:
                        come = rest_refs[roles - 1 - s][:virt, :].astype(F32)
                        total += jnp.where(role == s, come, 0.0)
                amp_ref[slot] = (gain[...] * total).astype(BF16)

            @pl.when(jnp.logical_not(here))
            def _():
                amp_ref[slot] = jnp.zeros(square, BF16)

            send(amp_ref.at[slot], amp_out.at[slot])
            for at in range(0, pao, virt):
                rows = pl.ds(at, virt)

                @pl.when(here)
                def _():
                    x = coeff_ref[pair, rows, :]
                    dressed = x.astype(F32) + mxu(x, amp_ref[slot], NN) * virt_scale
                    orb_ref[slot, rows, :] = dressed.astype(BF16)

                @pl.when(jnp.logical_not(here))
                def _():
                    orb_ref[slot, rows, :] = jnp.zeros((virt, virt), BF16)

                send(orb_ref.at[slot, rows], orb_out.at[slot, rows])

        store(0, role > 0, gain_ref, rest_ref, ci_ref, whole(num(MINE)))
        has_extra = role == whole(num(OWNER))
        store(1, has_extra, gain_extra_ref, rest_extra_ref, cei_ref, whole(num(EXTRA)))
        for copy in copies:
            copy.wait()

    amps_out, dressed_out = call(
        last_body,
        [VMEM] + [VMEM] * (8 + roles - 1),
        [(ANY, (slots, virt, virt), BF16), (ANY, (slots, pao, virt), BF16)],
        (
            nums, coeff, gain, gain_extra, rest, rest_extra,
            cc_from_out, c_from_in, ce_from_in, *rests,
        ),
        scratch=[
            pltpu.VMEM((slots, virt, virt), BF16),
            pltpu.VMEM((slots, pao, virt), BF16),
            pltpu.SemaphoreType.DMA((slots * (1 + pao // virt),)),
        ],
    )
    return amps_out, dressed_out


def solution(mesh):
    in_specs = (
        P("pairs", None, None),
        P("pairs", None, None),
        P("pairs", None, None),
        P("pairs", None),
        P(),
        P("pairs"),
        P("pairs", None),
        P("pairs", None),
        P("pairs", None),
        P("pairs"),
    )
    out_specs = (P(("role", "pairs"), None, None), P(("role", "pairs"), None, None))
    return jax.shard_map(local, mesh=mesh, in_specs=in_specs, out_specs=out_specs, check_vma=False)
```

```python
import math

import jax
import jax.numpy as jnp
from jax import lax
from jax.experimental import pallas as pl
from jax.experimental.pallas import tpu as pltpu
from jax.sharding import PartitionSpec as P

F32 = jnp.float32
BF16 = jnp.bfloat16
I32 = jnp.int32
NN = ((1,), (0,))
NT = ((1,), (1,))

VMEM = pl.BlockSpec(memory_space=pltpu.VMEM)
ANY = pl.BlockSpec(memory_space=pl.ANY)
HBM = pl.BlockSpec(memory_space=pltpu.HBM)

MINE, EXTRA, OWNER, FIRST, SECOND, WHOSE, NV_MINE, NV_EXTRA, OCC_MINE, OCC_EXTRA, ROLE_PAIR = range(11)


def whole(number):
    return number.astype(jnp.int32)


def read(nums_ref):
    row = nums_ref[0:1, :]
    return lambda at: row[0, at], lambda at: row[:, at : at + 1]


def mxu(a, b, dims):
    return lax.dot_general(a, b, (dims, ((), ())), preferred_element_type=F32)


def call(body, ins, outs, args, scratch=(), vmem=48):
    return pl.pallas_call(
        body,
        in_specs=ins,
        out_specs=[spec for spec, _, _ in outs],
        out_shape=[jax.ShapeDtypeStruct(shape, dtype) for _, shape, dtype in outs],
        scratch_shapes=list(scratch),
        cost_estimate=pl.CostEstimate(flops=1, bytes_accessed=1, transcendentals=0),
        compiler_params=pltpu.CompilerParams(vmem_limit_bytes=vmem * 1024 * 1024),
    )(*args)


def local(
    three_index, coeff, amps, eps_virt, eps_occ, nvirt, pair_occ, partners, coupling, pair_owner
):
    columns = lax.axis_size("pairs")
    roles = lax.axis_size("role")
    occ_block, aux, pao = three_index.shape
    pairs, _, virt = coeff.shape
    partner_count = partners.shape[1]
    slots = 2
    assert roles == pairs and pairs % 2 == 0 and columns % 2 == 0 and virt % 2 == 0
    tile = min(256, aux)
    pao_scale = 1.0 / math.sqrt(pao)
    aux_scale = 1.0 / math.sqrt(aux)
    virt_scale = 1.0 / math.sqrt(virt)
    square = (virt, virt)
    part = virt // 2
    sq_b = (VMEM, square, BF16)
    sq_f = (VMEM, square, F32)
    two_b = (VMEM, (2, virt, virt), BF16)
    all_s = (VMEM, (pairs, virt, virt), BF16)
    half = (VMEM, (aux, virt), BF16)

    inner_of = [i ^ 1 for i in range(columns)]
    outer_of = [(i + (1 if i % 2 else -1)) % columns for i in range(columns)]

    def inner(x):
        return lax.ppermute(x, "pairs", list(enumerate(inner_of)))

    def outer(x):
        return lax.ppermute(x, "pairs", list(enumerate(outer_of)))

    def swap(x, by):
        return lax.ppermute(x, "role", [(i, i ^ by) for i in range(roles)])

    three_in, coeff_in, amps_in = inner(three_index), inner(coeff), inner(amps)

    def pairs_of_roles(owner_ref):
        of_role = [jnp.int32(0)] * roles
        for p in range(pairs):
            earlier = jnp.int32(0)
            for o in range(p):
                earlier += (owner_ref[o] == owner_ref[p]).astype(I32)
            for s in range(roles):
                hit = (earlier == 0) & (owner_ref[p] == s) if s else earlier == 1
                of_role[s] = jnp.where(hit, p, of_role[s])
        return of_role

    def pick(numbers, at):
        chosen = numbers[0]
        for s in range(1, len(numbers)):
            chosen = jnp.where(at == s, numbers[s], chosen)
        return chosen

    weights = 2 * pairs
    place_at, mine_at, extra_at = 2 * weights, 2 * weights + 1, 2 * weights + 2
    riders = 16
    longer = (VMEM, (virt + riders, virt), BF16)
    own_weights = ROLE_PAIR + roles

    def plan_body(
        owner_hbm, occ_hbm, partner_hbm, coupling_hbm, eps_hbm, nvirt_hbm, coeff_hbm,
        low_ref, high_ref, nums_ref,
        owner_ref, occ_ref, partner_ref, coupling_ref, eps_ref, nvirt_ref, near_w, sems,
    ):
        small = [
            pltpu.make_async_copy(source, target, sems.at[at])
            for at, (source, target) in enumerate(
                (
                    (owner_hbm, owner_ref),
                    (occ_hbm, occ_ref),
                    (partner_hbm, partner_ref),
                    (coupling_hbm, coupling_ref),
                    (eps_hbm, eps_ref),
                    (nvirt_hbm, nvirt_ref),
                )
            )
        ]
        for copy in small:
            copy.start()
        role = lax.axis_index("role")
        column = lax.axis_index("pairs")
        small[0].wait()
        of_role = pairs_of_roles(owner_ref)
        extra = of_role[0]
        mine = pick(of_role, role)
        large = [
            pltpu.make_async_copy(coeff_hbm.at[mine, :, pl.ds(0, part)], low_ref.at[pl.ds(0, pao)], sems.at[6]),
            pltpu.make_async_copy(coeff_hbm.at[mine, :, pl.ds(part, part)], high_ref, sems.at[7]),
        ]
        for copy in large:
            copy.start()
        for copy in small[1:]:
            copy.wait()
        nums = {}
        nums[MINE] = mine.astype(F32)
        nums[EXTRA] = extra.astype(F32)
        nums[OWNER] = owner_ref[extra].astype(F32)
        for m in range(roles):
            nums[ROLE_PAIR + m] = pick(of_role, role ^ m).astype(F32)
        nums[NV_MINE] = nvirt_ref[mine].astype(F32)
        nums[NV_EXTRA] = nvirt_ref[extra].astype(F32)
        nums[FIRST] = (occ_ref[0, mine] - column * occ_block).astype(F32)
        odd = lax.rem(column, 2) == 1
        inner_at = jnp.where(odd, 0, 2)
        outer_at = 2 - inner_at
        occ_all = occ_block * columns
        second = lax.rem(occ_ref[1, mine] - (column - 1) * occ_block + occ_all, occ_all)
        block = (second >= occ_block).astype(I32) + (second >= 2 * occ_block).astype(I32)
        place = (second - block * occ_block).astype(F32)
        nums[SECOND] = place
        lane = lax.broadcasted_iota(I32, (riders, part), 1)
        row = lax.broadcasted_iota(I32, (riders, part), 0)
        told = jnp.where(lane == place_at, place, 0.0)
        told = jnp.where(lane == mine_at, mine.astype(F32), told)
        told = jnp.where(lane == extra_at, extra.astype(F32), told)
        nums[WHOSE] = jnp.where(block == 1, 0, jnp.where(block == inner_at, 1, 2)).astype(F32)
        nums[OCC_MINE] = eps_ref[occ_ref[0, mine]] + eps_ref[occ_ref[1, mine]]
        nums[OCC_EXTRA] = eps_ref[occ_ref[0, extra]] + eps_ref[occ_ref[1, extra]]
        pair_all = pairs * columns
        for which, pair in enumerate((mine, extra)):
            for q in range(3 * pairs):
                near_w[q] = jnp.float32(0)
            for k in range(partner_count):
                at = lax.rem(partner_ref[pair, k] - (column - 1) * pairs + pair_all, pair_all)
                near_w[at] += coupling_ref[pair, k]
            for q in range(pairs):
                to = which * pairs + q
                nums[own_weights + to] = near_w[pairs + q]
                nums[own_weights + weights + to] = near_w[inner_at * pairs + q]
                told = jnp.where(lane == to, near_w[outer_at * pairs + q], told)
                told = jnp.where(lane == weights + to, near_w[inner_at * pairs + q], told)
        row_of_nums = jnp.zeros(nums_ref.shape, F32)
        lane_of_nums = lax.broadcasted_iota(I32, nums_ref.shape, 1)
        for at, number in nums.items():
            row_of_nums = jnp.where(lane_of_nums == at, number, row_of_nums)
        nums_ref[...] = row_of_nums
        coarse = told.astype(BF16).astype(F32)
        middle = (told - coarse).astype(BF16).astype(F32)
        fine = told - coarse - middle
        told = jnp.where(row == 0, coarse, jnp.where(row == 1, middle, jnp.where(row == 2, fine, 0.0)))
        low_ref[pao:, :] = told.astype(BF16)
        for copy in large:
            copy.wait()

    rode = (VMEM, (pao + riders, part), BF16)
    x_low, x_high, nums = call(
        plan_body,
        [HBM] * 7,
        [rode, (VMEM, (pao, part), BF16), (VMEM, (8, part), F32)],
        (pair_owner, pair_occ.T, partners, coupling, eps_occ, nvirt, coeff),
        scratch=[
            pltpu.SMEM(pair_owner.shape, I32),
            pltpu.SMEM(pair_occ.shape[::-1], I32),
            pltpu.SMEM(partners.shape, I32),
            pltpu.SMEM(coupling.shape, F32),
            pltpu.SMEM(eps_occ.shape, F32),
            pltpu.SMEM(nvirt.shape, I32),
            pltpu.SMEM((3 * pairs,), F32),
            pltpu.SemaphoreType.DMA((8,)),
        ],
        vmem=60,
    )
    low_out, high_out, low_in = outer(x_low), outer(x_high), inner(x_low)

    def told_of(low_ref):
        rows = low_ref[pao:, :].astype(F32)
        return rows[0:1] + rows[1:2] + rows[2:3]

    def overlaps(x, coeff_ref, out_ref):
        turned = x.T
        for q in range(pairs):
            s = mxu(turned, coeff_ref[q], NN) * (1.0 / pao)
            out_ref[q] = s.astype(BF16)

    def coupled(s_ref, parts):
        total = None
        for at, weight, amp in parts:
            s = s_ref[at]
            u = mxu(s, amp, NN).astype(BF16)
            term = weight * mxu(u, s, NT)
            total = term if total is None else total + term
        return total

    tiles = [pl.ds(at, tile) for at in range(0, aux, tile)]

    def half_into(y_ref, three_ref, at_occ, x):
        for rows in tiles:
            y_ref[rows, :] = (mxu(three_ref[at_occ, rows, :], x, NN) * pao_scale).astype(BF16)

    def fetch_body(three_ref, after_ref, held_ref, sem):
        copy = pltpu.make_async_copy(three_ref, held_ref, sem)
        copy.start()
        copy.wait()

    (blocks,) = call(
        fetch_body,
        [ANY, ANY],
        [(VMEM, three_index.shape, BF16)],
        (three_index, nums),
        scratch=[pltpu.SemaphoreType.DMA],
        vmem=50,
    )

    def outer_low_body(three_ref, x_ref, y_ref):
        half_into(y_ref, three_ref, whole(told_of(x_ref)[0, place_at]), x_ref[:pao, :])
        y_ref[aux:, :] = jnp.zeros((riders, part), BF16)

    (y_low,) = call(
        outer_low_body,
        [VMEM, VMEM],
        [(VMEM, (aux + riders, part), BF16)],
        (blocks, low_out),
    )
    y_low_from_out = outer(y_low)

    def outer_high_body(three_ref, low_ref, x_ref, after_ref, y_ref):
        half_into(y_ref, three_ref, whole(told_of(low_ref)[0, place_at]), x_ref[...])

    (y_high,) = call(
        outer_high_body,
        [VMEM, VMEM, VMEM, ANY],
        [(VMEM, (aux, part), BF16)],
        (blocks, low_out, high_out, y_low),
    )
    y_high_from_out = outer(y_high)

    def outer_body(coeff_ref, amps_ref, low_ref, high_ref, after_ref, s_ref, c_ref, x_ref):
        x_ref[:, :part] = low_ref[:pao, :]
        x_ref[:, part:] = high_ref[...]
        overlaps(x_ref[...], coeff_ref, s_ref)
        told = told_of(low_ref)
        c = coupled(s_ref, [(q, told[0, q], amps_ref[q]) for q in range(pairs)])
        c_ref[:virt, :] = c.astype(BF16)
        c_ref[virt:, :] = jnp.zeros((riders, virt), BF16)

    s_out, c_out = call(
        outer_body,
        [VMEM, VMEM, VMEM, VMEM, ANY],
        [all_s, longer],
        (coeff, amps, low_out, high_out, y_high),
        scratch=[pltpu.VMEM((pao, virt), BF16)],
    )
    c_from_out = outer(c_out)

    def own_half_body(
        nums, three_ref, three_in_ref, coeff_ref, after_ref, first_ref, second_ref, extra_ref, block_ref, sem
    ):
        num, _ = read(nums)
        x = coeff_ref[whole(num(MINE))]
        extra_ref[...] = coeff_ref[whole(num(EXTRA))]
        whose, second = whole(num(WHOSE)), whole(num(SECOND))
        copy = pltpu.make_async_copy(three_in_ref.at[second], block_ref.at[0], sem)

        @pl.when(whose == 1)
        def _():
            copy.start()

        turned = x.T
        first = whole(num(FIRST))
        for rows in tiles:
            first_ref[:, rows] = (mxu(turned, three_ref[first, rows, :], NT) * pao_scale).astype(BF16)

        @pl.when(whose == 0)
        def _():
            half_into(second_ref, three_ref, second, x)

        @pl.when(whose == 1)
        def _():
            copy.wait()
            half_into(second_ref, block_ref, 0, x)

    first_t, second, x_extra = call(
        own_half_body,
        [VMEM, VMEM, ANY, VMEM, ANY],
        [
            (VMEM, (virt, aux), BF16),
            (VMEM, (aux, virt), BF16),
            (VMEM, (pao, virt), BF16),
        ],
        (nums, blocks, three_in, coeff, c_out),
        scratch=[pltpu.VMEM((1, aux, pao), BF16), pltpu.SemaphoreType.DMA],
    )
    x_extra_out = outer(x_extra)

    def own_body(
        nums, coeff_ref, coeff_in_ref, amps_ref, amps_in_ref, eps_ref, after_ref,
        s_ref, c_ref, gain_ref, gain_extra_ref, s_in_ref,
    ):
        num, weight = read(nums)
        mine, extra = whole(num(MINE)), whole(num(EXTRA))
        x = coeff_ref[mine]
        total = None
        for at, of_s, of_coeff, of_amps in (
            (own_weights, s_ref, coeff_ref, amps_ref),
            (own_weights + weights, s_in_ref, coeff_in_ref, amps_in_ref),
        ):
            overlaps(x, of_coeff, of_s)
            c = coupled(of_s, [(q, weight(at + q), of_amps[q]) for q in range(pairs)])
            total = c if total is None else total + c
        c_ref[...] = total

        def gain(pair, count, occupied):
            row = jnp.broadcast_to(eps_ref[pl.ds(pair, 1), :], square)
            energy = row + row.T - occupied
            inside = (lax.broadcasted_iota(I32, square, 0) < count) & (
                lax.broadcasted_iota(I32, square, 1) < count
            )
            return jnp.where(inside, 1.0 / (energy + 1.0), 0.0)

        gain_ref[...] = gain(mine, whole(num(NV_MINE)), num(OCC_MINE))
        gain_extra_ref[...] = gain(extra, whole(num(NV_EXTRA)), num(OCC_EXTRA))

    s_own, c_own, gain, gain_extra = call(
        own_body,
        [VMEM] + [VMEM] * 5 + [ANY],
        [all_s, sq_f, sq_f, sq_f],
        (nums, coeff, coeff_in, amps, amps_in, eps_virt, c_out),
        scratch=[pltpu.VMEM((pairs, virt, virt), BF16)],
    )

    def more_body(nums, coeff_ref, in_ref, low_ref, after_ref, se_ref, s_in_ref, se_in_ref):
        @pl.when(lax.axis_index("role") > 0)
        def _():
            told = told_of(low_ref)
            num, _ = read(nums)
            overlaps(coeff_ref[whole(num(EXTRA))], coeff_ref, se_ref)
            overlaps(in_ref[whole(told[0, mine_at])], coeff_ref, s_in_ref)
            overlaps(in_ref[whole(told[0, extra_at])], coeff_ref, se_in_ref)

    se_own, s_in, se_in = call(
        more_body,
        [VMEM, VMEM, VMEM, VMEM, ANY],
        [all_s, all_s, all_s],
        (nums, coeff, coeff_in, low_in, c_own),
    )

    def first_body(
        nums, first_ref, second_ref, low_ref, high_ref, amps_ref, c_ref, co_ref, gain_ref, after_ref,
        amp_ref, k_ref,
    ):
        first = first_ref[...]
        num, _ = read(nums)
        outside = whole(num(WHOSE)) == 2

        @pl.when(outside)
        def _():
            k_ref[:, :part] = mxu(first, low_ref[:aux, :], NN) * aux_scale
            k_ref[:, part:] = mxu(first, high_ref[...], NN) * aux_scale

        @pl.when(jnp.logical_not(outside))
        def _():
            k_ref[...] = mxu(first, second_ref[...], NN) * aux_scale

        old = amps_ref[whole(num(MINE))].astype(F32)
        c = c_ref[...] + co_ref[:virt, :].astype(F32)
        amp_ref[...] = (gain_ref[...] * (old - k_ref[...] - c)).astype(BF16)

    amp, k_first = call(
        first_body,
        [VMEM] + [VMEM] * 8 + [ANY],
        [sq_b, sq_f],
        (
            nums, first_t, second, y_low_from_out, y_high_from_out,
            amps, c_own, c_from_out, gain, se_own,
        ),
    )
    amp_roles = [amp] + [swap(amp, m) for m in range(1, roles)]

    def rest_body(amp_ref, k_ref, out_ref, out_b_ref):
        amp = amp_ref[...]
        k = k_ref[...]
        right = k + mxu(k.astype(BF16), amp, NN) * virt_scale
        both = right + mxu(amp.T, right.astype(BF16), NN) * virt_scale
        rest = amp.astype(F32) - both
        out_ref[...] = rest
        out_b_ref[:virt, :] = rest.astype(BF16)
        out_b_ref[virt:, :] = jnp.zeros((2 * riders, virt), BF16)

    longest = (VMEM, (virt + 2 * riders, virt), BF16)
    rest, rest_b = call(rest_body, [VMEM, VMEM], [sq_f, longest], (amp, k_first))
    sends = [1, *range(roles - 1, 1, -1)]
    rests = [lax.ppermute(rest_b, "role", [(0, s)]) for s in sends]

    def extra_out_body(coeff_ref, x_ref, after_ref, s_ref):
        @pl.when(lax.axis_index("role") > 0)
        def _():
            overlaps(x_ref[...], coeff_ref, s_ref)

    (se_out,) = call(
        extra_out_body,
        [VMEM, VMEM, ANY],
        [all_s],
        (coeff, x_extra_out, amp),
    )

    def parts_of(nums, weight_of, amp_refs):
        num, _ = read(nums)
        parts = []
        for m in range(roles):
            at = whole(num(ROLE_PAIR + m))
            parts.append((at, weight_of(at), amp_refs[m][...]))
        return parts

    def told_weight(told, first):
        return lambda at: pick([told[:, first + q : first + q + 1] for q in range(pairs)], at)

    def outer_again_body(nums, low_ref, s_ref, se_ref, *refs):
        amp_refs, c_ref = refs[:roles], refs[-1]

        @pl.when(lax.axis_index("role") > 0)
        def _():
            told = told_of(low_ref)
            for slot, of_s in enumerate((s_ref, se_ref)):
                parts = parts_of(nums, told_weight(told, slot * pairs), amp_refs)
                c_ref[slot] = coupled(of_s, parts).astype(BF16)

    (cc_out,) = call(
        outer_again_body,
        [VMEM] + [VMEM] * (3 + roles),
        [two_b],
        (nums, low_out, s_out, se_out, *amp_roles),
    )
    cc_from_out = outer(cc_out)

    def inner_again_body(nums, low_ref, s_ref, se_ref, *refs):
        amp_refs, c_refs = refs[:roles], refs[-2:]

        @pl.when(lax.axis_index("role") > 0)
        def _():
            told = told_of(low_ref)
            for slot, of_s, c_ref in zip(range(2), (s_ref, se_ref), c_refs):
                parts = parts_of(nums, told_weight(told, weights + slot * pairs), amp_refs)
                c_ref[:virt, :] = coupled(of_s, parts).astype(BF16)
                c_ref[virt:, :] = jnp.zeros((riders, virt), BF16)

    c_in, ce_in = call(
        inner_again_body,
        [VMEM] + [VMEM] * (3 + roles) + [ANY],
        [longer, longer],
        (nums, low_in, s_in, se_in, *amp_roles, cc_out),
    )
    c_from_in, ce_from_in = inner(c_in), inner(ce_in)

    def own_again_body(nums, rest_ref, s_ref, se_ref, *refs):
        amp_refs, (after_ref, out_ref, out_extra_ref) = refs[:roles], refs[-3:]

        @pl.when(lax.axis_index("role") > 0)
        def _():
            row = nums[0:1, :]
            parts = parts_of(nums, told_weight(row, own_weights), amp_refs)
            out_ref[...] = rest_ref[...] - coupled(s_ref, parts)
            parts = parts_of(nums, told_weight(row, own_weights + pairs), amp_refs)
            out_extra_ref[...] = -coupled(se_ref, parts)

    rest, rest_extra = call(
        own_again_body,
        [VMEM] + [VMEM] * (3 + roles) + [ANY],
        [sq_f, sq_f],
        (nums, rest, s_own, se_own, *amp_roles, c_in),
    )

    def last_body(
        nums, coeff_ref, gain_ref, gain_extra_ref, rest_ref, rest_extra_ref, co_ref, ci_ref, cei_ref, *refs
    ):
        rest_refs, (amp_out, orb_out, amp_ref, orb_ref, sems) = refs[: roles - 1], refs[roles - 1 :]
        num, _ = read(nums)
        role = lax.axis_index("role")
        copies = []

        def send(source, target):
            copies.append(pltpu.make_async_copy(source, target, sems.at[len(copies)]))
            copies[-1].start()

        def store(slot, here, gain, rest, c_in, pair):
            @pl.when(here)
            def _():
                total = rest[...] - co_ref[slot].astype(F32) - c_in[:virt, :].astype(F32)
                for s in range(1, roles):
                    if slot:
                        come = rest_refs[sends.index(s)][:virt, :].astype(F32)
                        total += jnp.where(role == s, come, 0.0)
                amp_ref[slot] = (gain[...] * total).astype(BF16)

            @pl.when(jnp.logical_not(here))
            def _():
                amp_ref[slot] = jnp.zeros(square, BF16)

            send(amp_ref.at[slot], amp_out.at[slot])
            for at in range(0, pao, virt):
                rows = pl.ds(at, virt)

                @pl.when(here)
                def _():
                    x = coeff_ref[pair, rows, :]
                    dressed = x.astype(F32) + mxu(x, amp_ref[slot], NN) * virt_scale
                    orb_ref[slot, rows, :] = dressed.astype(BF16)

                @pl.when(jnp.logical_not(here))
                def _():
                    orb_ref[slot, rows, :] = jnp.zeros((virt, virt), BF16)

                send(orb_ref.at[slot, rows], orb_out.at[slot, rows])

        store(0, role > 0, gain_ref, rest_ref, ci_ref, whole(num(MINE)))
        has_extra = role == whole(num(OWNER))
        store(1, has_extra, gain_extra_ref, rest_extra_ref, cei_ref, whole(num(EXTRA)))
        for copy in copies:
            copy.wait()

    amps_out, dressed_out = call(
        last_body,
        [VMEM] + [VMEM] * (8 + roles - 1),
        [(ANY, (slots, virt, virt), BF16), (ANY, (slots, pao, virt), BF16)],
        (
            nums, coeff, gain, gain_extra, rest, rest_extra,
            cc_from_out, c_from_in, ce_from_in, *rests,
        ),
        scratch=[
            pltpu.VMEM((slots, virt, virt), BF16),
            pltpu.VMEM((slots, pao, virt), BF16),
            pltpu.SemaphoreType.DMA((slots * (1 + pao // virt),)),
        ],
    )
    return amps_out, dressed_out


def solution(mesh):
    in_specs = (
        P("pairs", None, None),
        P("pairs", None, None),
        P("pairs", None, None),
        P("pairs", None),
        P(),
        P("pairs"),
        P("pairs", None),
        P("pairs", None),
        P("pairs", None),
        P("pairs"),
    )
    out_specs = (P(("role", "pairs"), None, None), P(("role", "pairs"), None, None))
    return jax.shard_map(local, mesh=mesh, in_specs=in_specs, out_specs=out_specs, check_vma=False)
```

```python
import math

import jax
import jax.numpy as jnp
from jax import lax
from jax.experimental import pallas as pl
from jax.experimental.pallas import tpu as pltpu
from jax.sharding import PartitionSpec as P

F32 = jnp.float32
BF16 = jnp.bfloat16
I32 = jnp.int32
NN = ((1,), (0,))
NT = ((1,), (1,))

VMEM = pl.BlockSpec(memory_space=pltpu.VMEM)
ANY = pl.BlockSpec(memory_space=pl.ANY)
HBM = pl.BlockSpec(memory_space=pltpu.HBM)

MINE, EXTRA, OWNER, FIRST, SECOND, WHOSE, NV_MINE, NV_EXTRA, OCC_MINE, OCC_EXTRA, ROLE_PAIR = range(11)


def whole(number):
    return number.astype(jnp.int32)


def read(nums_ref):
    row = nums_ref[0:1, :]
    return lambda at: row[0, at], lambda at: row[:, at : at + 1]


def mxu(a, b, dims):
    return lax.dot_general(a, b, (dims, ((), ())), preferred_element_type=F32)


def call(body, ins, outs, args, scratch=(), vmem=48):
    return pl.pallas_call(
        body,
        in_specs=ins,
        out_specs=[spec for spec, _, _ in outs],
        out_shape=[jax.ShapeDtypeStruct(shape, dtype) for _, shape, dtype in outs],
        scratch_shapes=list(scratch),
        cost_estimate=pl.CostEstimate(flops=1, bytes_accessed=1, transcendentals=0),
        compiler_params=pltpu.CompilerParams(vmem_limit_bytes=vmem * 1024 * 1024),
    )(*args)


def local(
    three_index, coeff, amps, eps_virt, eps_occ, nvirt, pair_occ, partners, coupling, pair_owner
):
    columns = lax.axis_size("pairs")
    roles = lax.axis_size("role")
    occ_block, aux, pao = three_index.shape
    pairs, _, virt = coeff.shape
    partner_count = partners.shape[1]
    slots = 2
    assert roles == pairs and pairs % 2 == 0 and columns % 2 == 0 and virt % 2 == 0
    assert roles & (roles - 1) == 0
    tile = min(256, aux)
    pao_scale = 1.0 / math.sqrt(pao)
    aux_scale = 1.0 / math.sqrt(aux)
    virt_scale = 1.0 / math.sqrt(virt)
    square = (virt, virt)
    part = virt // 2
    sq_b = (VMEM, square, BF16)
    sq_f = (VMEM, square, F32)
    two_b = (VMEM, (2, virt, virt), BF16)
    all_s = (VMEM, (pairs, virt, virt), BF16)
    half = (VMEM, (aux, virt), BF16)

    inner_of = [i ^ 1 for i in range(columns)]
    outer_of = [(i + (1 if i % 2 else -1)) % columns for i in range(columns)]

    def inner(x):
        return lax.ppermute(x, "pairs", list(enumerate(inner_of)))

    def outer(x):
        return lax.ppermute(x, "pairs", list(enumerate(outer_of)))

    def swap(x, by):
        return lax.ppermute(x, "role", [(i, i ^ by) for i in range(roles)])

    three_in, coeff_in, amps_in = inner(three_index), inner(coeff), inner(amps)

    def pairs_of_roles(owner_ref):
        of_role = [jnp.int32(0)] * roles
        for p in range(pairs):
            earlier = jnp.int32(0)
            for o in range(p):
                earlier += (owner_ref[o] == owner_ref[p]).astype(I32)
            for s in range(roles):
                hit = (earlier == 0) & (owner_ref[p] == s) if s else earlier == 1
                of_role[s] = jnp.where(hit, p, of_role[s])
        return of_role

    def pick(numbers, at):
        chosen = numbers[0]
        for s in range(1, len(numbers)):
            chosen = jnp.where(at == s, numbers[s], chosen)
        return chosen

    weights = 2 * pairs
    place_at, mine_at, extra_at = 2 * weights, 2 * weights + 1, 2 * weights + 2
    riders = 16
    longer = (VMEM, (virt + riders, virt), BF16)
    own_weights = ROLE_PAIR + roles

    def plan_body(
        owner_hbm, occ_hbm, partner_hbm, coupling_hbm, eps_hbm, nvirt_hbm, coeff_hbm,
        low_ref, high_ref, nums_ref,
        owner_ref, occ_ref, partner_ref, coupling_ref, eps_ref, nvirt_ref, near_w, sems,
    ):
        small = [
            pltpu.make_async_copy(source, target, sems.at[at])
            for at, (source, target) in enumerate(
                (
                    (owner_hbm, owner_ref),
                    (occ_hbm, occ_ref),
                    (partner_hbm, partner_ref),
                    (coupling_hbm, coupling_ref),
                    (eps_hbm, eps_ref),
                    (nvirt_hbm, nvirt_ref),
                )
            )
        ]
        for copy in small:
            copy.start()
        role = lax.axis_index("role")
        column = lax.axis_index("pairs")
        small[0].wait()
        of_role = pairs_of_roles(owner_ref)
        extra = of_role[0]
        mine = pick(of_role, role)
        large = [
            pltpu.make_async_copy(coeff_hbm.at[mine, :, pl.ds(0, part)], low_ref.at[pl.ds(0, pao)], sems.at[6]),
            pltpu.make_async_copy(coeff_hbm.at[mine, :, pl.ds(part, part)], high_ref, sems.at[7]),
        ]
        for copy in large:
            copy.start()
        for copy in small[1:]:
            copy.wait()
        nums = {}
        nums[MINE] = mine.astype(F32)
        nums[EXTRA] = extra.astype(F32)
        nums[OWNER] = owner_ref[extra].astype(F32)
        for m in range(roles):
            nums[ROLE_PAIR + m] = pick(of_role, role ^ m).astype(F32)
        nums[NV_MINE] = nvirt_ref[mine].astype(F32)
        nums[NV_EXTRA] = nvirt_ref[extra].astype(F32)
        nums[FIRST] = (occ_ref[0, mine] - column * occ_block).astype(F32)
        odd = lax.rem(column, 2) == 1
        inner_at = jnp.where(odd, 0, 2)
        outer_at = 2 - inner_at
        occ_all = occ_block * columns
        second = lax.rem(occ_ref[1, mine] - (column - 1) * occ_block + occ_all, occ_all)
        block = (second >= occ_block).astype(I32) + (second >= 2 * occ_block).astype(I32)
        place = (second - block * occ_block).astype(F32)
        nums[SECOND] = place
        lane = lax.broadcasted_iota(I32, (riders, part), 1)
        row = lax.broadcasted_iota(I32, (riders, part), 0)
        told = jnp.where(lane == place_at, place, 0.0)
        told = jnp.where(lane == mine_at, mine.astype(F32), told)
        told = jnp.where(lane == extra_at, extra.astype(F32), told)
        nums[WHOSE] = jnp.where(block == 1, 0, jnp.where(block == inner_at, 1, 2)).astype(F32)
        nums[OCC_MINE] = eps_ref[occ_ref[0, mine]] + eps_ref[occ_ref[1, mine]]
        nums[OCC_EXTRA] = eps_ref[occ_ref[0, extra]] + eps_ref[occ_ref[1, extra]]
        pair_all = pairs * columns
        for which, pair in enumerate((mine, extra)):
            for q in range(3 * pairs):
                near_w[q] = jnp.float32(0)
            for k in range(partner_count):
                at = lax.rem(partner_ref[pair, k] - (column - 1) * pairs + pair_all, pair_all)
                near_w[at] += coupling_ref[pair, k]
            for q in range(pairs):
                to = which * pairs + q
                nums[own_weights + to] = near_w[pairs + q]
                nums[own_weights + weights + to] = near_w[inner_at * pairs + q]
                told = jnp.where(lane == to, near_w[outer_at * pairs + q], told)
                told = jnp.where(lane == weights + to, near_w[inner_at * pairs + q], told)
        row_of_nums = jnp.zeros(nums_ref.shape, F32)
        lane_of_nums = lax.broadcasted_iota(I32, nums_ref.shape, 1)
        for at, number in nums.items():
            row_of_nums = jnp.where(lane_of_nums == at, number, row_of_nums)
        nums_ref[...] = row_of_nums
        coarse = told.astype(BF16).astype(F32)
        middle = (told - coarse).astype(BF16).astype(F32)
        fine = told - coarse - middle
        told = jnp.where(row == 0, coarse, jnp.where(row == 1, middle, jnp.where(row == 2, fine, 0.0)))
        low_ref[pao:, :] = told.astype(BF16)
        for copy in large:
            copy.wait()

    rode = (VMEM, (pao + riders, part), BF16)
    x_low, x_high, nums = call(
        plan_body,
        [HBM] * 7,
        [rode, (VMEM, (pao, part), BF16), (VMEM, (8, part), F32)],
        (pair_owner, pair_occ.T, partners, coupling, eps_occ, nvirt, coeff),
        scratch=[
            pltpu.SMEM(pair_owner.shape, I32),
            pltpu.SMEM(pair_occ.shape[::-1], I32),
            pltpu.SMEM(partners.shape, I32),
            pltpu.SMEM(coupling.shape, F32),
            pltpu.SMEM(eps_occ.shape, F32),
            pltpu.SMEM(nvirt.shape, I32),
            pltpu.SMEM((3 * pairs,), F32),
            pltpu.SemaphoreType.DMA((8,)),
        ],
        vmem=60,
    )
    low_out, high_out, low_in = outer(x_low), outer(x_high), inner(x_low)

    def told_of(low_ref):
        rows = low_ref[pao:, :].astype(F32)
        return rows[0:1] + rows[1:2] + rows[2:3]

    def overlaps(x, coeff_ref, out_ref):
        turned = x.T
        for q in range(pairs):
            s = mxu(turned, coeff_ref[q], NN) * (1.0 / pao)
            out_ref[q] = s.astype(BF16)

    def coupled(s_ref, parts):
        total = None
        for at, weight, amp in parts:
            s = s_ref[at]
            u = mxu(s, amp, NN).astype(BF16)
            term = weight * mxu(u, s, NT)
            total = term if total is None else total + term
        return total

    tiles = [pl.ds(at, tile) for at in range(0, aux, tile)]

    def half_into(y_ref, three_ref, at_occ, x):
        for rows in tiles:
            y_ref[rows, :] = (mxu(three_ref[at_occ, rows, :], x, NN) * pao_scale).astype(BF16)

    def fetch_body(three_ref, after_ref, held_ref, sem):
        copy = pltpu.make_async_copy(three_ref, held_ref, sem)
        copy.start()
        copy.wait()

    (blocks,) = call(
        fetch_body,
        [ANY, ANY],
        [(VMEM, three_index.shape, BF16)],
        (three_index, nums),
        scratch=[pltpu.SemaphoreType.DMA],
        vmem=50,
    )

    def outer_low_body(three_ref, x_ref, y_ref):
        half_into(y_ref, three_ref, whole(told_of(x_ref)[0, place_at]), x_ref[:pao, :])
        y_ref[aux:, :] = jnp.zeros((riders, part), BF16)

    (y_low,) = call(
        outer_low_body,
        [VMEM, VMEM],
        [(VMEM, (aux + riders, part), BF16)],
        (blocks, low_out),
    )
    y_low_from_out = outer(y_low)

    def outer_high_body(three_ref, low_ref, x_ref, after_ref, y_ref):
        half_into(y_ref, three_ref, whole(told_of(low_ref)[0, place_at]), x_ref[...])

    (y_high,) = call(
        outer_high_body,
        [VMEM, VMEM, VMEM, ANY],
        [(VMEM, (aux, part), BF16)],
        (blocks, low_out, high_out, y_low),
    )
    y_high_from_out = outer(y_high)

    def outer_body(coeff_ref, amps_ref, low_ref, high_ref, after_ref, s_ref, c_ref, x_ref):
        x_ref[:, :part] = low_ref[:pao, :]
        x_ref[:, part:] = high_ref[...]
        overlaps(x_ref[...], coeff_ref, s_ref)
        told = told_of(low_ref)
        c = coupled(s_ref, [(q, told[0, q], amps_ref[q]) for q in range(pairs)])
        c_ref[:virt, :] = c.astype(BF16)
        c_ref[virt:, :] = jnp.zeros((riders, virt), BF16)

    s_out, c_out = call(
        outer_body,
        [VMEM, VMEM, VMEM, VMEM, ANY],
        [all_s, longer],
        (coeff, amps, low_out, high_out, y_high),
        scratch=[pltpu.VMEM((pao, virt), BF16)],
    )
    c_from_out = outer(c_out)

    def own_half_body(
        nums, three_ref, three_in_ref, coeff_ref, after_ref, first_ref, second_ref, extra_ref, block_ref, sem
    ):
        num, _ = read(nums)
        x = coeff_ref[whole(num(MINE))]
        extra_ref[...] = coeff_ref[whole(num(EXTRA))]
        whose, second = whole(num(WHOSE)), whole(num(SECOND))
        copy = pltpu.make_async_copy(three_in_ref.at[second], block_ref.at[0], sem)

        @pl.when(whose == 1)
        def _():
            copy.start()

        turned = x.T
        first = whole(num(FIRST))
        for rows in tiles:
            first_ref[:, rows] = (mxu(turned, three_ref[first, rows, :], NT) * pao_scale).astype(BF16)

        @pl.when(whose == 0)
        def _():
            half_into(second_ref, three_ref, second, x)

        @pl.when(whose == 1)
        def _():
            copy.wait()
            half_into(second_ref, block_ref, 0, x)

    first_t, second, x_extra = call(
        own_half_body,
        [VMEM, VMEM, ANY, VMEM, ANY],
        [
            (VMEM, (virt, aux), BF16),
            (VMEM, (aux, virt), BF16),
            (VMEM, (pao, virt), BF16),
        ],
        (nums, blocks, three_in, coeff, c_out),
        scratch=[pltpu.VMEM((1, aux, pao), BF16), pltpu.SemaphoreType.DMA],
    )
    x_extra_out = outer(x_extra)

    def own_body(
        nums, coeff_ref, coeff_in_ref, amps_ref, amps_in_ref, eps_ref, after_ref,
        s_ref, c_ref, gain_ref, gain_extra_ref, s_in_ref,
    ):
        num, weight = read(nums)
        mine, extra = whole(num(MINE)), whole(num(EXTRA))
        x = coeff_ref[mine]
        total = None
        for at, of_s, of_coeff, of_amps in (
            (own_weights, s_ref, coeff_ref, amps_ref),
            (own_weights + weights, s_in_ref, coeff_in_ref, amps_in_ref),
        ):
            overlaps(x, of_coeff, of_s)
            c = coupled(of_s, [(q, weight(at + q), of_amps[q]) for q in range(pairs)])
            total = c if total is None else total + c
        c_ref[...] = total

        def gain(pair, count, occupied):
            row = jnp.broadcast_to(eps_ref[pl.ds(pair, 1), :], square)
            energy = row + row.T - occupied
            inside = (lax.broadcasted_iota(I32, square, 0) < count) & (
                lax.broadcasted_iota(I32, square, 1) < count
            )
            return jnp.where(inside, 1.0 / (energy + 1.0), 0.0)

        gain_ref[...] = gain(mine, whole(num(NV_MINE)), num(OCC_MINE))
        gain_extra_ref[...] = gain(extra, whole(num(NV_EXTRA)), num(OCC_EXTRA))

    s_own, c_own, gain, gain_extra = call(
        own_body,
        [VMEM] + [VMEM] * 5 + [ANY],
        [all_s, sq_f, sq_f, sq_f],
        (nums, coeff, coeff_in, amps, amps_in, eps_virt, c_out),
        scratch=[pltpu.VMEM((pairs, virt, virt), BF16)],
    )

    def more_body(nums, coeff_ref, in_ref, low_ref, after_ref, se_ref, s_in_ref, se_in_ref):
        @pl.when(lax.axis_index("role") > 0)
        def _():
            told = told_of(low_ref)
            num, _ = read(nums)
            overlaps(coeff_ref[whole(num(EXTRA))], coeff_ref, se_ref)
            overlaps(in_ref[whole(told[0, mine_at])], coeff_ref, s_in_ref)
            overlaps(in_ref[whole(told[0, extra_at])], coeff_ref, se_in_ref)

    se_own, s_in, se_in = call(
        more_body,
        [VMEM, VMEM, VMEM, VMEM, ANY],
        [all_s, all_s, all_s],
        (nums, coeff, coeff_in, low_in, c_own),
    )

    def first_body(
        nums, first_ref, second_ref, low_ref, high_ref, amps_ref, c_ref, co_ref, gain_ref, after_ref,
        amp_ref, k_ref,
    ):
        first = first_ref[...]
        num, _ = read(nums)
        outside = whole(num(WHOSE)) == 2

        @pl.when(outside)
        def _():
            k_ref[:, :part] = mxu(first, low_ref[:aux, :], NN) * aux_scale
            k_ref[:, part:] = mxu(first, high_ref[...], NN) * aux_scale

        @pl.when(jnp.logical_not(outside))
        def _():
            k_ref[...] = mxu(first, second_ref[...], NN) * aux_scale

        old = amps_ref[whole(num(MINE))].astype(F32)
        c = c_ref[...] + co_ref[:virt, :].astype(F32)
        amp_ref[...] = (gain_ref[...] * (old - k_ref[...] - c)).astype(BF16)

    amp, k_first = call(
        first_body,
        [VMEM] + [VMEM] * 8 + [ANY],
        [sq_b, sq_f],
        (
            nums, first_t, second, y_low_from_out, y_high_from_out,
            amps, c_own, c_from_out, gain, se_own,
        ),
    )
    amp_roles = [amp] + [swap(amp, m) for m in range(1, roles)]

    def rest_body(amp_ref, k_ref, out_ref, out_b_ref):
        amp = amp_ref[...]
        k = k_ref[...]
        right = k + mxu(k.astype(BF16), amp, NN) * virt_scale
        both = right + mxu(amp.T, right.astype(BF16), NN) * virt_scale
        rest = amp.astype(F32) - both
        out_ref[...] = rest
        out_b_ref[:virt, :] = rest.astype(BF16)
        out_b_ref[virt:, :] = jnp.zeros((2 * riders, virt), BF16)

    longest = (VMEM, (virt + 2 * riders, virt), BF16)
    rest, rest_b = call(rest_body, [VMEM, VMEM], [sq_f, longest], (amp, k_first))

    def relay_body(held_ref, come_ref, out_ref):
        role = lax.axis_index("role")

        @pl.when(role == 0)
        def _():
            out_ref[...] = held_ref[...]

        @pl.when(role > 0)
        def _():
            out_ref[...] = come_ref[...]

    rests, held, step = [], rest_b, 1
    while step < roles:
        rests.append(lax.ppermute(held, "role", [(i, i + step) for i in range(step)]))
        step *= 2
        if step < roles:
            (held,) = call(relay_body, [VMEM, VMEM], [longest], (held, rests[-1]))

    def extra_out_body(coeff_ref, x_ref, after_ref, s_ref):
        @pl.when(lax.axis_index("role") > 0)
        def _():
            overlaps(x_ref[...], coeff_ref, s_ref)

    (se_out,) = call(
        extra_out_body,
        [VMEM, VMEM, ANY],
        [all_s],
        (coeff, x_extra_out, amp),
    )

    def parts_of(nums, weight_of, amp_refs):
        num, _ = read(nums)
        parts = []
        for m in range(roles):
            at = whole(num(ROLE_PAIR + m))
            parts.append((at, weight_of(at), amp_refs[m][...]))
        return parts

    def told_weight(told, first):
        return lambda at: pick([told[:, first + q : first + q + 1] for q in range(pairs)], at)

    def outer_again_body(nums, low_ref, s_ref, se_ref, *refs):
        amp_refs, c_ref = refs[:roles], refs[-1]

        @pl.when(lax.axis_index("role") > 0)
        def _():
            told = told_of(low_ref)
            for slot, of_s in enumerate((s_ref, se_ref)):
                parts = parts_of(nums, told_weight(told, slot * pairs), amp_refs)
                c_ref[slot] = coupled(of_s, parts).astype(BF16)

    (cc_out,) = call(
        outer_again_body,
        [VMEM] + [VMEM] * (3 + roles),
        [two_b],
        (nums, low_out, s_out, se_out, *amp_roles),
    )
    cc_from_out = outer(cc_out)

    def inner_again_body(nums, low_ref, s_ref, se_ref, *refs):
        amp_refs, c_refs = refs[:roles], refs[-2:]

        @pl.when(lax.axis_index("role") > 0)
        def _():
            told = told_of(low_ref)
            for slot, of_s, c_ref in zip(range(2), (s_ref, se_ref), c_refs):
                parts = parts_of(nums, told_weight(told, weights + slot * pairs), amp_refs)
                c_ref[:virt, :] = coupled(of_s, parts).astype(BF16)
                c_ref[virt:, :] = jnp.zeros((riders, virt), BF16)

    c_in, ce_in = call(
        inner_again_body,
        [VMEM] + [VMEM] * (3 + roles) + [ANY],
        [longer, longer],
        (nums, low_in, s_in, se_in, *amp_roles, cc_out),
    )
    c_from_in, ce_from_in = inner(c_in), inner(ce_in)

    def own_again_body(nums, rest_ref, s_ref, se_ref, *refs):
        amp_refs, (after_ref, out_ref, out_extra_ref) = refs[:roles], refs[-3:]

        @pl.when(lax.axis_index("role") > 0)
        def _():
            row = nums[0:1, :]
            parts = parts_of(nums, told_weight(row, own_weights), amp_refs)
            out_ref[...] = rest_ref[...] - coupled(s_ref, parts)
            parts = parts_of(nums, told_weight(row, own_weights + pairs), amp_refs)
            out_extra_ref[...] = -coupled(se_ref, parts)

    rest, rest_extra = call(
        own_again_body,
        [VMEM] + [VMEM] * (3 + roles) + [ANY],
        [sq_f, sq_f],
        (nums, rest, s_own, se_own, *amp_roles, c_in),
    )

    def last_body(
        nums, coeff_ref, gain_ref, gain_extra_ref, rest_ref, rest_extra_ref, co_ref, ci_ref, cei_ref, *refs
    ):
        rest_refs, (amp_out, orb_out, amp_ref, orb_ref, sems) = refs[:-5], refs[-5:]
        num, _ = read(nums)
        role = lax.axis_index("role")
        copies = []

        def send(source, target):
            copies.append(pltpu.make_async_copy(source, target, sems.at[len(copies)]))
            copies[-1].start()

        def store(slot, here, gain, rest, c_in, pair):
            @pl.when(here)
            def _():
                total = rest[...] - co_ref[slot].astype(F32) - c_in[:virt, :].astype(F32)
                if slot:
                    come = rest_refs[0][:virt, :]
                    for at, ref in enumerate(rest_refs[1:], 1):
                        come = jnp.where(role >= 1 << at, ref[:virt, :], come)
                    total += come.astype(F32)
                amp_ref[slot] = (gain[...] * total).astype(BF16)

            @pl.when(jnp.logical_not(here))
            def _():
                amp_ref[slot] = jnp.zeros(square, BF16)

            send(amp_ref.at[slot], amp_out.at[slot])
            for at in range(0, pao, virt):
                rows = pl.ds(at, virt)

                @pl.when(here)
                def _():
                    x = coeff_ref[pair, rows, :]
                    dressed = x.astype(F32) + mxu(x, amp_ref[slot], NN) * virt_scale
                    orb_ref[slot, rows, :] = dressed.astype(BF16)

                @pl.when(jnp.logical_not(here))
                def _():
                    orb_ref[slot, rows, :] = jnp.zeros((virt, virt), BF16)

                send(orb_ref.at[slot, rows], orb_out.at[slot, rows])

        store(0, role > 0, gain_ref, rest_ref, ci_ref, whole(num(MINE)))
        has_extra = role == whole(num(OWNER))
        store(1, has_extra, gain_extra_ref, rest_extra_ref, cei_ref, whole(num(EXTRA)))
        for copy in copies:
            copy.wait()

    amps_out, dressed_out = call(
        last_body,
        [VMEM] * (9 + len(rests)),
        [(ANY, (slots, virt, virt), BF16), (ANY, (slots, pao, virt), BF16)],
        (
            nums, coeff, gain, gain_extra, rest, rest_extra,
            cc_from_out, c_from_in, ce_from_in, *rests,
        ),
        scratch=[
            pltpu.VMEM((slots, virt, virt), BF16),
            pltpu.VMEM((slots, pao, virt), BF16),
            pltpu.SemaphoreType.DMA((slots * (1 + pao // virt),)),
        ],
    )
    return amps_out, dressed_out


def solution(mesh):
    in_specs = (
        P("pairs", None, None),
        P("pairs", None, None),
        P("pairs", None, None),
        P("pairs", None),
        P(),
        P("pairs"),
        P("pairs", None),
        P("pairs", None),
        P("pairs", None),
        P("pairs"),
    )
    out_specs = (P(("role", "pairs"), None, None), P(("role", "pairs"), None, None))
    return jax.shard_map(local, mesh=mesh, in_specs=in_specs, out_specs=out_specs, check_vma=False)
```

```python
import math

import jax
import jax.numpy as jnp
from jax import lax
from jax.experimental import pallas as pl
from jax.experimental.pallas import tpu as pltpu
from jax.sharding import PartitionSpec as P

F32 = jnp.float32
BF16 = jnp.bfloat16
I32 = jnp.int32
NN = ((1,), (0,))
NT = ((1,), (1,))

VMEM = pl.BlockSpec(memory_space=pltpu.VMEM)
ANY = pl.BlockSpec(memory_space=pl.ANY)
HBM = pl.BlockSpec(memory_space=pltpu.HBM)

MINE, EXTRA, OWNER, FIRST, SECOND, WHOSE, NV_MINE, NV_EXTRA, OCC_MINE, OCC_EXTRA, ROLE_PAIR = range(11)


def whole(number):
    return number.astype(jnp.int32)


def read(nums_ref):
    row = nums_ref[0:1, :]
    return lambda at: row[0, at], lambda at: row[:, at : at + 1]


def mxu(a, b, dims):
    return lax.dot_general(a, b, (dims, ((), ())), preferred_element_type=F32)


def call(body, ins, outs, args, scratch=(), vmem=48, in_place=None):
    return pl.pallas_call(
        body,
        in_specs=ins,
        out_specs=[spec for spec, _, _ in outs],
        out_shape=[jax.ShapeDtypeStruct(shape, dtype) for _, shape, dtype in outs],
        scratch_shapes=list(scratch),
        input_output_aliases=in_place or {},
        cost_estimate=pl.CostEstimate(flops=1, bytes_accessed=1, transcendentals=0),
        compiler_params=pltpu.CompilerParams(vmem_limit_bytes=vmem * 1024 * 1024),
    )(*args)


def local(
    three_index, coeff, amps, eps_virt, eps_occ, nvirt, pair_occ, partners, coupling, pair_owner
):
    columns = lax.axis_size("pairs")
    roles = lax.axis_size("role")
    occ_block, aux, pao = three_index.shape
    pairs, _, virt = coeff.shape
    partner_count = partners.shape[1]
    slots = 2
    assert roles == pairs and pairs % 2 == 0 and columns % 2 == 0 and virt % 2 == 0
    assert roles & (roles - 1) == 0
    tile = min(256, aux)
    pao_scale = 1.0 / math.sqrt(pao)
    aux_scale = 1.0 / math.sqrt(aux)
    virt_scale = 1.0 / math.sqrt(virt)
    square = (virt, virt)
    part = virt // 2
    sq_b = (VMEM, square, BF16)
    sq_f = (VMEM, square, F32)
    two_b = (VMEM, (2, virt, virt), BF16)
    all_s = (VMEM, (pairs, virt, virt), BF16)
    half = (VMEM, (aux, virt), BF16)

    inner_of = [i ^ 1 for i in range(columns)]
    outer_of = [(i + (1 if i % 2 else -1)) % columns for i in range(columns)]

    def inner(x):
        return lax.ppermute(x, "pairs", list(enumerate(inner_of)))

    def outer(x):
        return lax.ppermute(x, "pairs", list(enumerate(outer_of)))

    def swap(x, by):
        return lax.ppermute(x, "role", [(i, i ^ by) for i in range(roles)])

    three_in, coeff_in, amps_in = inner(three_index), inner(coeff), inner(amps)

    def pairs_of_roles(owner_ref):
        of_role = [jnp.int32(0)] * roles
        for p in range(pairs):
            earlier = jnp.int32(0)
            for o in range(p):
                earlier += (owner_ref[o] == owner_ref[p]).astype(I32)
            for s in range(roles):
                hit = (earlier == 0) & (owner_ref[p] == s) if s else earlier == 1
                of_role[s] = jnp.where(hit, p, of_role[s])
        return of_role

    def pick(numbers, at):
        chosen = numbers[0]
        for s in range(1, len(numbers)):
            chosen = jnp.where(at == s, numbers[s], chosen)
        return chosen

    weights = 2 * pairs
    place_at, mine_at, extra_at = 2 * weights, 2 * weights + 1, 2 * weights + 2
    riders = 16
    longer = (VMEM, (virt + riders, virt), BF16)
    own_weights = ROLE_PAIR + roles

    def plan_body(
        owner_hbm, occ_hbm, partner_hbm, coupling_hbm, eps_hbm, nvirt_hbm, coeff_hbm,
        low_ref, high_ref, nums_ref,
        owner_ref, occ_ref, partner_ref, coupling_ref, eps_ref, nvirt_ref, near_w, sems,
    ):
        small = [
            pltpu.make_async_copy(source, target, sems.at[at])
            for at, (source, target) in enumerate(
                (
                    (owner_hbm, owner_ref),
                    (occ_hbm, occ_ref),
                    (partner_hbm, partner_ref),
                    (coupling_hbm, coupling_ref),
                    (eps_hbm, eps_ref),
                    (nvirt_hbm, nvirt_ref),
                )
            )
        ]
        for copy in small:
            copy.start()
        role = lax.axis_index("role")
        column = lax.axis_index("pairs")
        small[0].wait()
        of_role = pairs_of_roles(owner_ref)
        extra = of_role[0]
        mine = pick(of_role, role)
        large = [
            pltpu.make_async_copy(coeff_hbm.at[mine, :, pl.ds(0, part)], low_ref.at[pl.ds(0, pao)], sems.at[6]),
            pltpu.make_async_copy(coeff_hbm.at[mine, :, pl.ds(part, part)], high_ref, sems.at[7]),
        ]
        for copy in large:
            copy.start()
        for copy in small[1:]:
            copy.wait()
        nums = {}
        nums[MINE] = mine.astype(F32)
        nums[EXTRA] = extra.astype(F32)
        nums[OWNER] = owner_ref[extra].astype(F32)
        for m in range(roles):
            nums[ROLE_PAIR + m] = pick(of_role, role ^ m).astype(F32)
        nums[NV_MINE] = nvirt_ref[mine].astype(F32)
        nums[NV_EXTRA] = nvirt_ref[extra].astype(F32)
        nums[FIRST] = (occ_ref[0, mine] - column * occ_block).astype(F32)
        odd = lax.rem(column, 2) == 1
        inner_at = jnp.where(odd, 0, 2)
        outer_at = 2 - inner_at
        occ_all = occ_block * columns
        second = lax.rem(occ_ref[1, mine] - (column - 1) * occ_block + occ_all, occ_all)
        block = (second >= occ_block).astype(I32) + (second >= 2 * occ_block).astype(I32)
        place = (second - block * occ_block).astype(F32)
        nums[SECOND] = place
        lane = lax.broadcasted_iota(I32, (riders, part), 1)
        row = lax.broadcasted_iota(I32, (riders, part), 0)
        told = jnp.where(lane == place_at, place, 0.0)
        told = jnp.where(lane == mine_at, mine.astype(F32), told)
        told = jnp.where(lane == extra_at, extra.astype(F32), told)
        nums[WHOSE] = jnp.where(block == 1, 0, jnp.where(block == inner_at, 1, 2)).astype(F32)
        nums[OCC_MINE] = eps_ref[occ_ref[0, mine]] + eps_ref[occ_ref[1, mine]]
        nums[OCC_EXTRA] = eps_ref[occ_ref[0, extra]] + eps_ref[occ_ref[1, extra]]
        pair_all = pairs * columns
        for which, pair in enumerate((mine, extra)):
            for q in range(3 * pairs):
                near_w[q] = jnp.float32(0)
            for k in range(partner_count):
                at = lax.rem(partner_ref[pair, k] - (column - 1) * pairs + pair_all, pair_all)
                near_w[at] += coupling_ref[pair, k]
            for q in range(pairs):
                to = which * pairs + q
                nums[own_weights + to] = near_w[pairs + q]
                nums[own_weights + weights + to] = near_w[inner_at * pairs + q]
                told = jnp.where(lane == to, near_w[outer_at * pairs + q], told)
                told = jnp.where(lane == weights + to, near_w[inner_at * pairs + q], told)
        row_of_nums = jnp.zeros(nums_ref.shape, F32)
        lane_of_nums = lax.broadcasted_iota(I32, nums_ref.shape, 1)
        for at, number in nums.items():
            row_of_nums = jnp.where(lane_of_nums == at, number, row_of_nums)
        nums_ref[...] = row_of_nums
        coarse = told.astype(BF16).astype(F32)
        middle = (told - coarse).astype(BF16).astype(F32)
        fine = told - coarse - middle
        told = jnp.where(row == 0, coarse, jnp.where(row == 1, middle, jnp.where(row == 2, fine, 0.0)))
        low_ref[pao:, :] = told.astype(BF16)
        for copy in large:
            copy.wait()

    rode = (VMEM, (pao + riders, part), BF16)
    x_low, x_high, nums = call(
        plan_body,
        [HBM] * 7,
        [rode, (VMEM, (pao, part), BF16), (VMEM, (8, part), F32)],
        (pair_owner, pair_occ.T, partners, coupling, eps_occ, nvirt, coeff),
        scratch=[
            pltpu.SMEM(pair_owner.shape, I32),
            pltpu.SMEM(pair_occ.shape[::-1], I32),
            pltpu.SMEM(partners.shape, I32),
            pltpu.SMEM(coupling.shape, F32),
            pltpu.SMEM(eps_occ.shape, F32),
            pltpu.SMEM(nvirt.shape, I32),
            pltpu.SMEM((3 * pairs,), F32),
            pltpu.SemaphoreType.DMA((8,)),
        ],
        vmem=60,
    )
    low_out, high_out, low_in = outer(x_low), outer(x_high), inner(x_low)

    def told_of(low_ref):
        rows = low_ref[pao:, :].astype(F32)
        return rows[0:1] + rows[1:2] + rows[2:3]

    def overlaps(x, coeff_ref, out_ref):
        turned = x.T
        for q in range(pairs):
            s = mxu(turned, coeff_ref[q], NN) * (1.0 / pao)
            out_ref[q] = s.astype(BF16)

    def coupled(s_ref, parts):
        total = None
        for at, weight, amp in parts:
            s = s_ref[at]
            u = mxu(s, amp, NN).astype(BF16)
            term = weight * mxu(u, s, NT)
            total = term if total is None else total + term
        return total

    tiles = [pl.ds(at, tile) for at in range(0, aux, tile)]

    def half_into(y_ref, three_ref, at_occ, x):
        for rows in tiles:
            y_ref[rows, :] = (mxu(three_ref[at_occ, rows, :], x, NN) * pao_scale).astype(BF16)

    def fetch_body(three_ref, after_ref, held_ref, sem):
        copy = pltpu.make_async_copy(three_ref, held_ref, sem)
        copy.start()
        copy.wait()

    (blocks,) = call(
        fetch_body,
        [ANY, ANY],
        [(VMEM, three_index.shape, BF16)],
        (three_index, nums),
        scratch=[pltpu.SemaphoreType.DMA],
        vmem=50,
    )

    def outer_low_body(three_ref, x_ref, y_ref):
        half_into(y_ref, three_ref, whole(told_of(x_ref)[0, place_at]), x_ref[:pao, :])
        y_ref[aux:, :] = jnp.zeros((riders, part), BF16)

    (y_low,) = call(
        outer_low_body,
        [VMEM, VMEM],
        [(VMEM, (aux + riders, part), BF16)],
        (blocks, low_out),
    )
    y_low_from_out = outer(y_low)

    def outer_high_body(three_ref, low_ref, x_ref, after_ref, y_ref):
        half_into(y_ref, three_ref, whole(told_of(low_ref)[0, place_at]), x_ref[...])

    (y_high,) = call(
        outer_high_body,
        [VMEM, VMEM, VMEM, ANY],
        [(VMEM, (aux, part), BF16)],
        (blocks, low_out, high_out, y_low),
    )
    y_high_from_out = outer(y_high)

    def outer_body(coeff_ref, amps_ref, low_ref, high_ref, after_ref, s_ref, c_ref, x_ref):
        x_ref[:, :part] = low_ref[:pao, :]
        x_ref[:, part:] = high_ref[...]
        overlaps(x_ref[...], coeff_ref, s_ref)
        told = told_of(low_ref)
        c = coupled(s_ref, [(q, told[0, q], amps_ref[q]) for q in range(pairs)])
        c_ref[:virt, :] = c.astype(BF16)
        c_ref[virt:, :] = jnp.zeros((riders, virt), BF16)

    s_out, c_out = call(
        outer_body,
        [VMEM, VMEM, VMEM, VMEM, ANY],
        [all_s, longer],
        (coeff, amps, low_out, high_out, y_high),
        scratch=[pltpu.VMEM((pao, virt), BF16)],
    )
    c_from_out = outer(c_out)

    def own_half_body(
        nums, three_ref, three_in_ref, coeff_ref, after_ref, first_ref, second_ref, extra_ref, block_ref, sem
    ):
        num, _ = read(nums)
        x = coeff_ref[whole(num(MINE))]
        extra_ref[...] = coeff_ref[whole(num(EXTRA))]
        whose, second = whole(num(WHOSE)), whole(num(SECOND))
        copy = pltpu.make_async_copy(three_in_ref.at[second], block_ref.at[0], sem)

        @pl.when(whose == 1)
        def _():
            copy.start()

        turned = x.T
        first = whole(num(FIRST))
        for rows in tiles:
            first_ref[:, rows] = (mxu(turned, three_ref[first, rows, :], NT) * pao_scale).astype(BF16)

        @pl.when(whose == 0)
        def _():
            half_into(second_ref, three_ref, second, x)

        @pl.when(whose == 1)
        def _():
            copy.wait()
            half_into(second_ref, block_ref, 0, x)

    first_t, second, x_extra = call(
        own_half_body,
        [VMEM, VMEM, ANY, VMEM, ANY],
        [
            (VMEM, (virt, aux), BF16),
            (VMEM, (aux, virt), BF16),
            (VMEM, (pao, virt), BF16),
        ],
        (nums, blocks, three_in, coeff, c_out),
        scratch=[pltpu.VMEM((1, aux, pao), BF16), pltpu.SemaphoreType.DMA],
    )
    x_extra_out = outer(x_extra)

    def own_body(
        nums, coeff_ref, coeff_in_ref, amps_ref, amps_in_ref, eps_ref, after_ref,
        s_ref, c_ref, gain_ref, gain_extra_ref, s_in_ref,
    ):
        num, weight = read(nums)
        mine, extra = whole(num(MINE)), whole(num(EXTRA))
        x = coeff_ref[mine]
        total = None
        for at, of_s, of_coeff, of_amps in (
            (own_weights, s_ref, coeff_ref, amps_ref),
            (own_weights + weights, s_in_ref, coeff_in_ref, amps_in_ref),
        ):
            overlaps(x, of_coeff, of_s)
            c = coupled(of_s, [(q, weight(at + q), of_amps[q]) for q in range(pairs)])
            total = c if total is None else total + c
        c_ref[...] = total

        def gain(pair, count, occupied):
            row = jnp.broadcast_to(eps_ref[pl.ds(pair, 1), :], square)
            energy = row + row.T - occupied
            inside = (lax.broadcasted_iota(I32, square, 0) < count) & (
                lax.broadcasted_iota(I32, square, 1) < count
            )
            return jnp.where(inside, 1.0 / (energy + 1.0), 0.0)

        gain_ref[...] = gain(mine, whole(num(NV_MINE)), num(OCC_MINE))
        gain_extra_ref[...] = gain(extra, whole(num(NV_EXTRA)), num(OCC_EXTRA))

    s_own, c_own, gain, gain_extra = call(
        own_body,
        [VMEM] + [VMEM] * 5 + [ANY],
        [all_s, sq_f, sq_f, sq_f],
        (nums, coeff, coeff_in, amps, amps_in, eps_virt, c_out),
        scratch=[pltpu.VMEM((pairs, virt, virt), BF16)],
    )

    def more_body(nums, coeff_ref, in_ref, low_ref, after_ref, se_ref, s_in_ref, se_in_ref):
        @pl.when(lax.axis_index("role") > 0)
        def _():
            told = told_of(low_ref)
            num, _ = read(nums)
            overlaps(coeff_ref[whole(num(EXTRA))], coeff_ref, se_ref)
            overlaps(in_ref[whole(told[0, mine_at])], coeff_ref, s_in_ref)
            overlaps(in_ref[whole(told[0, extra_at])], coeff_ref, se_in_ref)

    se_own, s_in, se_in = call(
        more_body,
        [VMEM, VMEM, VMEM, VMEM, ANY],
        [all_s, all_s, all_s],
        (nums, coeff, coeff_in, low_in, c_own),
    )

    def first_body(
        nums, first_ref, second_ref, low_ref, high_ref, amps_ref, c_ref, co_ref, gain_ref, after_ref,
        amp_ref, k_ref,
    ):
        first = first_ref[...]
        num, _ = read(nums)
        outside = whole(num(WHOSE)) == 2

        @pl.when(outside)
        def _():
            k_ref[:, :part] = mxu(first, low_ref[:aux, :], NN) * aux_scale
            k_ref[:, part:] = mxu(first, high_ref[...], NN) * aux_scale

        @pl.when(jnp.logical_not(outside))
        def _():
            k_ref[...] = mxu(first, second_ref[...], NN) * aux_scale

        old = amps_ref[whole(num(MINE))].astype(F32)
        c = c_ref[...] + co_ref[:virt, :].astype(F32)
        amp_ref[...] = (gain_ref[...] * (old - k_ref[...] - c)).astype(BF16)

    amp, k_first = call(
        first_body,
        [VMEM] + [VMEM] * 8 + [ANY],
        [sq_b, sq_f],
        (
            nums, first_t, second, y_low_from_out, y_high_from_out,
            amps, c_own, c_from_out, gain, se_own,
        ),
    )
    amp_roles = [amp] + [swap(amp, m) for m in range(1, roles)]

    def rest_body(amp_ref, k_ref, out_ref, out_b_ref):
        amp = amp_ref[...]
        k = k_ref[...]
        right = k + mxu(k.astype(BF16), amp, NN) * virt_scale
        both = right + mxu(amp.T, right.astype(BF16), NN) * virt_scale
        rest = amp.astype(F32) - both
        out_ref[...] = rest
        out_b_ref[:virt, :] = rest.astype(BF16)
        out_b_ref[virt:, :] = jnp.zeros((2 * riders, virt), BF16)

    longest = (VMEM, (virt + 2 * riders, virt), BF16)
    rest, rest_b = call(rest_body, [VMEM, VMEM], [sq_f, longest], (amp, k_first))

    def relay_body(held_ref, come_ref, out_ref):
        role = lax.axis_index("role")

        @pl.when(role == 0)
        def _():
            out_ref[...] = held_ref[...]

        @pl.when(role > 0)
        def _():
            out_ref[...] = come_ref[...]

    rests, held, step = [], rest_b, 1
    while step < roles:
        rests.append(lax.ppermute(held, "role", [(i, i + step) for i in range(step)]))
        step *= 2
        if step < roles:
            (held,) = call(relay_body, [VMEM, VMEM], [longest], (held, rests[-1]))

    def extra_out_body(coeff_ref, x_ref, after_ref, s_ref):
        @pl.when(lax.axis_index("role") > 0)
        def _():
            overlaps(x_ref[...], coeff_ref, s_ref)

    (se_out,) = call(
        extra_out_body,
        [VMEM, VMEM, ANY],
        [all_s],
        (coeff, x_extra_out, amp),
    )

    def parts_of(nums, weight_of, amp_refs):
        num, _ = read(nums)
        parts = []
        for m in range(roles):
            at = whole(num(ROLE_PAIR + m))
            parts.append((at, weight_of(at), amp_refs[m][...]))
        return parts

    def told_weight(told, first):
        return lambda at: pick([told[:, first + q : first + q + 1] for q in range(pairs)], at)

    def outer_again_body(nums, low_ref, s_ref, se_ref, *refs):
        amp_refs, c_ref = refs[:roles], refs[-1]

        @pl.when(lax.axis_index("role") > 0)
        def _():
            told = told_of(low_ref)
            for slot, of_s in enumerate((s_ref, se_ref)):
                parts = parts_of(nums, told_weight(told, slot * pairs), amp_refs)
                c_ref[slot] = coupled(of_s, parts).astype(BF16)

    (cc_out,) = call(
        outer_again_body,
        [VMEM] + [VMEM] * (3 + roles),
        [two_b],
        (nums, low_out, s_out, se_out, *amp_roles),
    )
    cc_from_out = outer(cc_out)

    def inner_again_body(nums, low_ref, s_ref, se_ref, *refs):
        amp_refs, c_refs = refs[:roles], refs[-2:]

        @pl.when(lax.axis_index("role") > 0)
        def _():
            told = told_of(low_ref)
            for slot, of_s, c_ref in zip(range(2), (s_ref, se_ref), c_refs):
                parts = parts_of(nums, told_weight(told, weights + slot * pairs), amp_refs)
                c_ref[:virt, :] = coupled(of_s, parts).astype(BF16)
                c_ref[virt:, :] = jnp.zeros((riders, virt), BF16)

    c_in, ce_in = call(
        inner_again_body,
        [VMEM] + [VMEM] * (3 + roles) + [ANY],
        [longer, longer],
        (nums, low_in, s_in, se_in, *amp_roles, cc_out),
    )
    c_from_in, ce_from_in = inner(c_in), inner(ce_in)

    def own_again_body(nums, rest_ref, s_ref, se_ref, *refs):
        amp_refs, (after_ref, out_ref, out_extra_ref) = refs[:roles], refs[-3:]

        @pl.when(lax.axis_index("role") > 0)
        def _():
            row = nums[0:1, :]
            parts = parts_of(nums, told_weight(row, own_weights), amp_refs)
            out_ref[...] = rest_ref[...] - coupled(s_ref, parts)
            parts = parts_of(nums, told_weight(row, own_weights + pairs), amp_refs)
            out_extra_ref[...] = -coupled(se_ref, parts)

    rest, rest_extra = call(
        own_again_body,
        [VMEM] + [VMEM] * (3 + roles) + [ANY],
        [sq_f, sq_f],
        (nums, rest, s_own, se_own, *amp_roles, c_in),
    )

    def taken(num):
        role = lax.axis_index("role")
        return role > 0, role == whole(num(OWNER))

    def clear_body(nums, after_ref, amp_out, orb_out, zero_ref, sems):
        num, _ = read(nums)
        zero_ref[...] = jnp.zeros((pao, virt), BF16)
        for slot, here in enumerate(taken(num)):

            @pl.when(jnp.logical_not(here))
            def _():
                copies = [
                    pltpu.make_async_copy(zero_ref.at[pl.ds(0, virt)], amp_out.at[slot], sems.at[0]),
                    pltpu.make_async_copy(zero_ref, orb_out.at[slot], sems.at[1]),
                ]
                for copy in copies:
                    copy.start()
                for copy in copies:
                    copy.wait()

    outs = [(ANY, (slots, virt, virt), BF16), (ANY, (slots, pao, virt), BF16)]
    cleared = call(
        clear_body,
        [VMEM, ANY],
        outs,
        (nums, c_in),
        scratch=[pltpu.VMEM((pao, virt), BF16), pltpu.SemaphoreType.DMA((2,))],
    )

    def last_body(
        nums, coeff_ref, gain_ref, gain_extra_ref, rest_ref, rest_extra_ref, co_ref, ci_ref, cei_ref, *refs
    ):
        rest_refs, (amp_out, orb_out, amp_ref, orb_ref, sems) = refs[: len(rests)], refs[-5:]
        num, _ = read(nums)
        role = lax.axis_index("role")
        halves = [pl.ds(at, virt) for at in range(0, pao, virt)]

        def copies_of(slot):
            copies = [(amp_ref.at[slot], amp_out.at[slot])]
            copies += [(orb_ref.at[slot, rows], orb_out.at[slot, rows]) for rows in halves]
            first = slot * len(copies)
            return [
                pltpu.make_async_copy(source, target, sems.at[first + at])
                for at, (source, target) in enumerate(copies)
            ]

        here = taken(num)
        gains, kept = (gain_ref, gain_extra_ref), (rest_ref, rest_extra_ref)
        for slot, pair in ((0, MINE), (1, EXTRA)):

            @pl.when(here[slot])
            def _():
                copies = copies_of(slot)
                c_in = (ci_ref, cei_ref)[slot][:virt, :]
                total = kept[slot][...] - co_ref[slot].astype(F32) - c_in.astype(F32)
                if slot:
                    come = rest_refs[0][:virt, :]
                    for at, ref in enumerate(rest_refs[1:], 1):
                        come = jnp.where(role >= 1 << at, ref[:virt, :], come)
                    total += come.astype(F32)
                amp_ref[slot] = (gains[slot][...] * total).astype(BF16)
                copies[0].start()
                for rows, copy in zip(halves, copies[1:]):
                    x = coeff_ref[whole(num(pair)), rows, :]
                    dressed = x.astype(F32) + mxu(x, amp_ref[slot], NN) * virt_scale
                    orb_ref[slot, rows, :] = dressed.astype(BF16)
                    copy.start()

        for slot in range(slots):

            @pl.when(here[slot])
            def _():
                for copy in copies_of(slot):
                    copy.wait()

    ins = (
        nums, coeff, gain, gain_extra, rest, rest_extra, cc_from_out, c_from_in, ce_from_in, *rests, *cleared
    )
    amps_out, dressed_out = call(
        last_body,
        [VMEM] * (len(ins) - 2) + [ANY] * 2,
        outs,
        ins,
        scratch=[
            pltpu.VMEM((slots, virt, virt), BF16),
            pltpu.VMEM((slots, pao, virt), BF16),
            pltpu.SemaphoreType.DMA((slots * (1 + pao // virt),)),
        ],
        in_place={len(ins) - 2: 0, len(ins) - 1: 1},
    )
    return amps_out, dressed_out


def solution(mesh):
    in_specs = (
        P("pairs", None, None),
        P("pairs", None, None),
        P("pairs", None, None),
        P("pairs", None),
        P(),
        P("pairs"),
        P("pairs", None),
        P("pairs", None),
        P("pairs", None),
        P("pairs"),
    )
    out_specs = (P(("role", "pairs"), None, None), P(("role", "pairs"), None, None))
    return jax.shard_map(local, mesh=mesh, in_specs=in_specs, out_specs=out_specs, check_vma=False)
```

```python
import math

import jax
import jax.numpy as jnp
from jax import lax
from jax.experimental import pallas as pl
from jax.experimental.pallas import tpu as pltpu
from jax.sharding import PartitionSpec as P

F32 = jnp.float32
BF16 = jnp.bfloat16
I32 = jnp.int32
NN = ((1,), (0,))
NT = ((1,), (1,))

VMEM = pl.BlockSpec(memory_space=pltpu.VMEM)
ANY = pl.BlockSpec(memory_space=pl.ANY)
HBM = pl.BlockSpec(memory_space=pltpu.HBM)

MINE, EXTRA, OWNER, FIRST, SECOND, WHOSE, NV_MINE, NV_EXTRA, OCC_MINE, OCC_EXTRA, ROLE_PAIR = range(11)


def whole(number):
    return number.astype(jnp.int32)


def read(nums_ref):
    row = nums_ref[0:1, :]
    return lambda at: row[0, at], lambda at: row[:, at : at + 1]


def mxu(a, b, dims):
    return lax.dot_general(a, b, (dims, ((), ())), preferred_element_type=F32)


def call(body, ins, outs, args, scratch=(), vmem=48, in_place=None):
    return pl.pallas_call(
        body,
        in_specs=ins,
        out_specs=[spec for spec, _, _ in outs],
        out_shape=[jax.ShapeDtypeStruct(shape, dtype) for _, shape, dtype in outs],
        scratch_shapes=list(scratch),
        input_output_aliases=in_place or {},
        cost_estimate=pl.CostEstimate(flops=1, bytes_accessed=1, transcendentals=0),
        compiler_params=pltpu.CompilerParams(vmem_limit_bytes=vmem * 1024 * 1024),
    )(*args)


def local(
    three_index, coeff, amps, eps_virt, eps_occ, nvirt, pair_occ, partners, coupling, pair_owner
):
    columns = lax.axis_size("pairs")
    roles = lax.axis_size("role")
    occ_block, aux, pao = three_index.shape
    pairs, _, virt = coeff.shape
    partner_count = partners.shape[1]
    slots = 2
    assert roles == pairs and pairs % 2 == 0 and columns % 2 == 0 and virt % 2 == 0
    assert roles & (roles - 1) == 0
    tile = min(256, aux)
    pao_scale = 1.0 / math.sqrt(pao)
    aux_scale = 1.0 / math.sqrt(aux)
    virt_scale = 1.0 / math.sqrt(virt)
    square = (virt, virt)
    part = virt // 2
    sq_b = (VMEM, square, BF16)
    sq_f = (VMEM, square, F32)
    two_b = (VMEM, (2, virt, virt), BF16)
    all_s = (VMEM, (pairs, virt, virt), BF16)
    half = (VMEM, (aux, virt), BF16)

    inner_of = [i ^ 1 for i in range(columns)]
    outer_of = [(i + (1 if i % 2 else -1)) % columns for i in range(columns)]

    def inner(x):
        return lax.ppermute(x, "pairs", list(enumerate(inner_of)))

    def outer(x):
        return lax.ppermute(x, "pairs", list(enumerate(outer_of)))

    def swap(x, by):
        return lax.ppermute(x, "role", [(i, i ^ by) for i in range(roles)])

    three_in, coeff_in, amps_in = inner(three_index), inner(coeff), inner(amps)

    def pairs_of_roles(owner_ref):
        of_role = [jnp.int32(0)] * roles
        for p in range(pairs):
            earlier = jnp.int32(0)
            for o in range(p):
                earlier += (owner_ref[o] == owner_ref[p]).astype(I32)
            for s in range(roles):
                hit = (earlier == 0) & (owner_ref[p] == s) if s else earlier == 1
                of_role[s] = jnp.where(hit, p, of_role[s])
        return of_role

    def pick(numbers, at):
        chosen = numbers[0]
        for s in range(1, len(numbers)):
            chosen = jnp.where(at == s, numbers[s], chosen)
        return chosen

    weights = 2 * pairs
    place_at, mine_at, extra_at = 2 * weights, 2 * weights + 1, 2 * weights + 2
    riders = 16
    longer = (VMEM, (virt + riders, virt), BF16)
    own_weights = ROLE_PAIR + roles

    def plan_body(
        owner_hbm, occ_hbm, partner_hbm, coupling_hbm, eps_hbm, nvirt_hbm, coeff_hbm,
        low_ref, high_ref, nums_ref,
        owner_ref, occ_ref, partner_ref, coupling_ref, eps_ref, nvirt_ref, near_w, coeff_ref, sems,
    ):
        small = [
            pltpu.make_async_copy(source, target, sems.at[at])
            for at, (source, target) in enumerate(
                (
                    (owner_hbm, owner_ref),
                    (occ_hbm, occ_ref),
                    (partner_hbm, partner_ref),
                    (coupling_hbm, coupling_ref),
                    (eps_hbm, eps_ref),
                    (nvirt_hbm, nvirt_ref),
                )
            )
        ]
        large = pltpu.make_async_copy(coeff_hbm, coeff_ref, sems.at[6])
        for copy in (*small, large):
            copy.start()
        role = lax.axis_index("role")
        column = lax.axis_index("pairs")
        small[0].wait()
        of_role = pairs_of_roles(owner_ref)
        extra = of_role[0]
        mine = pick(of_role, role)
        for copy in small[1:]:
            copy.wait()
        nums = {}
        nums[MINE] = mine.astype(F32)
        nums[EXTRA] = extra.astype(F32)
        nums[OWNER] = owner_ref[extra].astype(F32)
        for m in range(roles):
            nums[ROLE_PAIR + m] = pick(of_role, role ^ m).astype(F32)
        nums[NV_MINE] = nvirt_ref[mine].astype(F32)
        nums[NV_EXTRA] = nvirt_ref[extra].astype(F32)
        nums[FIRST] = (occ_ref[0, mine] - column * occ_block).astype(F32)
        odd = lax.rem(column, 2) == 1
        inner_at = jnp.where(odd, 0, 2)
        outer_at = 2 - inner_at
        occ_all = occ_block * columns
        second = lax.rem(occ_ref[1, mine] - (column - 1) * occ_block + occ_all, occ_all)
        block = (second >= occ_block).astype(I32) + (second >= 2 * occ_block).astype(I32)
        place = (second - block * occ_block).astype(F32)
        nums[SECOND] = place
        lane = lax.broadcasted_iota(I32, (riders, part), 1)
        row = lax.broadcasted_iota(I32, (riders, part), 0)
        told = jnp.where(lane == place_at, place, 0.0)
        told = jnp.where(lane == mine_at, mine.astype(F32), told)
        told = jnp.where(lane == extra_at, extra.astype(F32), told)
        nums[WHOSE] = jnp.where(block == 1, 0, jnp.where(block == inner_at, 1, 2)).astype(F32)
        nums[OCC_MINE] = eps_ref[occ_ref[0, mine]] + eps_ref[occ_ref[1, mine]]
        nums[OCC_EXTRA] = eps_ref[occ_ref[0, extra]] + eps_ref[occ_ref[1, extra]]
        pair_all = pairs * columns
        for which, pair in enumerate((mine, extra)):
            for q in range(3 * pairs):
                near_w[q] = jnp.float32(0)
            for k in range(partner_count):
                at = lax.rem(partner_ref[pair, k] - (column - 1) * pairs + pair_all, pair_all)
                near_w[at] += coupling_ref[pair, k]
            for q in range(pairs):
                to = which * pairs + q
                nums[own_weights + to] = near_w[pairs + q]
                nums[own_weights + weights + to] = near_w[inner_at * pairs + q]
                told = jnp.where(lane == to, near_w[outer_at * pairs + q], told)
                told = jnp.where(lane == weights + to, near_w[inner_at * pairs + q], told)
        row_of_nums = jnp.zeros(nums_ref.shape, F32)
        lane_of_nums = lax.broadcasted_iota(I32, nums_ref.shape, 1)
        for at, number in nums.items():
            row_of_nums = jnp.where(lane_of_nums == at, number, row_of_nums)
        nums_ref[...] = row_of_nums
        coarse = told.astype(BF16).astype(F32)
        middle = (told - coarse).astype(BF16).astype(F32)
        fine = told - coarse - middle
        told = jnp.where(row == 0, coarse, jnp.where(row == 1, middle, jnp.where(row == 2, fine, 0.0)))
        low_ref[pao:, :] = told.astype(BF16)
        large.wait()
        low_ref[:pao, :] = coeff_ref[mine, :, :part]
        high_ref[...] = coeff_ref[mine, :, part:]

    rode = (VMEM, (pao + riders, part), BF16)
    x_low, x_high, nums = call(
        plan_body,
        [HBM] * 7,
        [rode, (VMEM, (pao, part), BF16), (VMEM, (8, part), F32)],
        (pair_owner, pair_occ.T, partners, coupling, eps_occ, nvirt, coeff),
        scratch=[
            pltpu.SMEM(pair_owner.shape, I32),
            pltpu.SMEM(pair_occ.shape[::-1], I32),
            pltpu.SMEM(partners.shape, I32),
            pltpu.SMEM(coupling.shape, F32),
            pltpu.SMEM(eps_occ.shape, F32),
            pltpu.SMEM(nvirt.shape, I32),
            pltpu.SMEM((3 * pairs,), F32),
            pltpu.VMEM(coeff.shape, BF16),
            pltpu.SemaphoreType.DMA((7,)),
        ],
        vmem=60,
    )
    low_out, high_out, low_in = outer(x_low), outer(x_high), inner(x_low)

    def told_of(low_ref):
        rows = low_ref[pao:, :].astype(F32)
        return rows[0:1] + rows[1:2] + rows[2:3]

    def overlaps(x, coeff_ref, out_ref):
        turned = x.T
        for q in range(pairs):
            s = mxu(turned, coeff_ref[q], NN) * (1.0 / pao)
            out_ref[q] = s.astype(BF16)

    def coupled(s_ref, parts):
        total = None
        for at, weight, amp in parts:
            s = s_ref[at]
            u = mxu(s, amp, NN).astype(BF16)
            term = weight * mxu(u, s, NT)
            total = term if total is None else total + term
        return total

    tiles = [pl.ds(at, tile) for at in range(0, aux, tile)]

    def half_into(y_ref, three_ref, at_occ, x):
        for rows in tiles:
            y_ref[rows, :] = (mxu(three_ref[at_occ, rows, :], x, NN) * pao_scale).astype(BF16)

    def fetch_body(three_ref, after_ref, held_ref, sem):
        copy = pltpu.make_async_copy(three_ref, held_ref, sem)
        copy.start()
        copy.wait()

    (blocks,) = call(
        fetch_body,
        [ANY, ANY],
        [(VMEM, three_index.shape, BF16)],
        (three_index, nums),
        scratch=[pltpu.SemaphoreType.DMA],
        vmem=50,
    )

    def outer_low_body(three_ref, x_ref, y_ref):
        half_into(y_ref, three_ref, whole(told_of(x_ref)[0, place_at]), x_ref[:pao, :])
        y_ref[aux:, :] = jnp.zeros((riders, part), BF16)

    (y_low,) = call(
        outer_low_body,
        [VMEM, VMEM],
        [(VMEM, (aux + riders, part), BF16)],
        (blocks, low_out),
    )
    y_low_from_out = outer(y_low)

    def outer_high_body(three_ref, low_ref, x_ref, after_ref, y_ref):
        half_into(y_ref, three_ref, whole(told_of(low_ref)[0, place_at]), x_ref[...])

    (y_high,) = call(
        outer_high_body,
        [VMEM, VMEM, VMEM, ANY],
        [(VMEM, (aux, part), BF16)],
        (blocks, low_out, high_out, y_low),
    )
    y_high_from_out = outer(y_high)

    def outer_body(coeff_ref, amps_ref, low_ref, high_ref, after_ref, s_ref, c_ref, x_ref):
        x_ref[:, :part] = low_ref[:pao, :]
        x_ref[:, part:] = high_ref[...]
        overlaps(x_ref[...], coeff_ref, s_ref)
        told = told_of(low_ref)
        c = coupled(s_ref, [(q, told[0, q], amps_ref[q]) for q in range(pairs)])
        c_ref[:virt, :] = c.astype(BF16)
        c_ref[virt:, :] = jnp.zeros((riders, virt), BF16)

    s_out, c_out = call(
        outer_body,
        [VMEM, VMEM, VMEM, VMEM, ANY],
        [all_s, longer],
        (coeff, amps, low_out, high_out, y_high),
        scratch=[pltpu.VMEM((pao, virt), BF16)],
    )
    c_from_out = outer(c_out)

    def own_half_body(
        nums, three_ref, three_in_ref, coeff_ref, after_ref, first_ref, second_ref, extra_ref, block_ref, sem
    ):
        num, _ = read(nums)
        x = coeff_ref[whole(num(MINE))]
        extra_ref[...] = coeff_ref[whole(num(EXTRA))]
        whose, second = whole(num(WHOSE)), whole(num(SECOND))
        copy = pltpu.make_async_copy(three_in_ref.at[second], block_ref.at[0], sem)

        @pl.when(whose == 1)
        def _():
            copy.start()

        turned = x.T
        first = whole(num(FIRST))
        for rows in tiles:
            first_ref[:, rows] = (mxu(turned, three_ref[first, rows, :], NT) * pao_scale).astype(BF16)

        @pl.when(whose == 0)
        def _():
            half_into(second_ref, three_ref, second, x)

        @pl.when(whose == 1)
        def _():
            copy.wait()
            half_into(second_ref, block_ref, 0, x)

    first_t, second, x_extra = call(
        own_half_body,
        [VMEM, VMEM, ANY, VMEM, ANY],
        [
            (VMEM, (virt, aux), BF16),
            (VMEM, (aux, virt), BF16),
            (VMEM, (pao, virt), BF16),
        ],
        (nums, blocks, three_in, coeff, c_out),
        scratch=[pltpu.VMEM((1, aux, pao), BF16), pltpu.SemaphoreType.DMA],
    )
    x_extra_out = outer(x_extra)

    def own_body(
        nums, coeff_ref, coeff_in_ref, amps_ref, amps_in_ref, eps_ref, after_ref,
        s_ref, c_ref, gain_ref, gain_extra_ref, s_in_ref,
    ):
        num, weight = read(nums)
        mine, extra = whole(num(MINE)), whole(num(EXTRA))
        x = coeff_ref[mine]
        total = None
        for at, of_s, of_coeff, of_amps in (
            (own_weights, s_ref, coeff_ref, amps_ref),
            (own_weights + weights, s_in_ref, coeff_in_ref, amps_in_ref),
        ):
            overlaps(x, of_coeff, of_s)
            c = coupled(of_s, [(q, weight(at + q), of_amps[q]) for q in range(pairs)])
            total = c if total is None else total + c
        c_ref[...] = total

        def gain(pair, count, occupied):
            row = jnp.broadcast_to(eps_ref[pl.ds(pair, 1), :], square)
            energy = row + row.T - occupied
            inside = (lax.broadcasted_iota(I32, square, 0) < count) & (
                lax.broadcasted_iota(I32, square, 1) < count
            )
            return jnp.where(inside, 1.0 / (energy + 1.0), 0.0)

        gain_ref[...] = gain(mine, whole(num(NV_MINE)), num(OCC_MINE))
        gain_extra_ref[...] = gain(extra, whole(num(NV_EXTRA)), num(OCC_EXTRA))

    s_own, c_own, gain, gain_extra = call(
        own_body,
        [VMEM] + [VMEM] * 5 + [ANY],
        [all_s, sq_f, sq_f, sq_f],
        (nums, coeff, coeff_in, amps, amps_in, eps_virt, c_out),
        scratch=[pltpu.VMEM((pairs, virt, virt), BF16)],
    )

    def more_body(nums, coeff_ref, in_ref, low_ref, after_ref, se_ref, s_in_ref, se_in_ref):
        @pl.when(lax.axis_index("role") > 0)
        def _():
            told = told_of(low_ref)
            num, _ = read(nums)
            overlaps(coeff_ref[whole(num(EXTRA))], coeff_ref, se_ref)
            overlaps(in_ref[whole(told[0, mine_at])], coeff_ref, s_in_ref)
            overlaps(in_ref[whole(told[0, extra_at])], coeff_ref, se_in_ref)

    se_own, s_in, se_in = call(
        more_body,
        [VMEM, VMEM, VMEM, VMEM, ANY],
        [all_s, all_s, all_s],
        (nums, coeff, coeff_in, low_in, c_own),
    )

    def first_body(
        nums, first_ref, second_ref, low_ref, high_ref, amps_ref, c_ref, co_ref, gain_ref, after_ref,
        amp_ref, k_ref,
    ):
        first = first_ref[...]
        num, _ = read(nums)
        outside = whole(num(WHOSE)) == 2

        @pl.when(outside)
        def _():
            k_ref[:, :part] = mxu(first, low_ref[:aux, :], NN) * aux_scale
            k_ref[:, part:] = mxu(first, high_ref[...], NN) * aux_scale

        @pl.when(jnp.logical_not(outside))
        def _():
            k_ref[...] = mxu(first, second_ref[...], NN) * aux_scale

        old = amps_ref[whole(num(MINE))].astype(F32)
        c = c_ref[...] + co_ref[:virt, :].astype(F32)
        amp_ref[...] = (gain_ref[...] * (old - k_ref[...] - c)).astype(BF16)

    amp, k_first = call(
        first_body,
        [VMEM] + [VMEM] * 8 + [ANY],
        [sq_b, sq_f],
        (
            nums, first_t, second, y_low_from_out, y_high_from_out,
            amps, c_own, c_from_out, gain, se_own,
        ),
    )
    amp_roles = [amp] + [swap(amp, m) for m in range(1, roles)]

    def rest_body(amp_ref, k_ref, out_ref, out_b_ref):
        amp = amp_ref[...]
        k = k_ref[...]
        right = k + mxu(k.astype(BF16), amp, NN) * virt_scale
        both = right + mxu(amp.T, right.astype(BF16), NN) * virt_scale
        rest = amp.astype(F32) - both
        out_ref[...] = rest
        out_b_ref[:virt, :] = rest.astype(BF16)
        out_b_ref[virt:, :] = jnp.zeros((riders, virt), BF16)

    rest, rest_b = call(rest_body, [VMEM, VMEM], [sq_f, longer], (amp, k_first))

    def relay_body(held_ref, come_ref, out_ref):
        role = lax.axis_index("role")

        @pl.when(role == 0)
        def _():
            out_ref[...] = held_ref[...]

        @pl.when(role > 0)
        def _():
            out_ref[...] = come_ref[...]

    rests, held, step = [], rest_b, 1
    while step < roles:
        rests.append(lax.ppermute(held, "role", [(i, i + step) for i in range(step)]))
        step *= 2
        if step < roles:
            (held,) = call(relay_body, [VMEM, VMEM], [longer], (held, rests[-1]))

    def extra_out_body(coeff_ref, x_ref, after_ref, s_ref):
        @pl.when(lax.axis_index("role") > 0)
        def _():
            overlaps(x_ref[...], coeff_ref, s_ref)

    (se_out,) = call(
        extra_out_body,
        [VMEM, VMEM, ANY],
        [all_s],
        (coeff, x_extra_out, amp),
    )

    def parts_of(nums, weight_of, amp_refs):
        num, _ = read(nums)
        parts = []
        for m in range(roles):
            at = whole(num(ROLE_PAIR + m))
            parts.append((at, weight_of(at), amp_refs[m][...]))
        return parts

    def told_weight(told, first):
        return lambda at: pick([told[:, first + q : first + q + 1] for q in range(pairs)], at)

    def outer_again_body(nums, low_ref, s_ref, se_ref, *refs):
        amp_refs, c_ref = refs[:roles], refs[-1]

        @pl.when(lax.axis_index("role") > 0)
        def _():
            told = told_of(low_ref)
            for slot, of_s in enumerate((s_ref, se_ref)):
                parts = parts_of(nums, told_weight(told, slot * pairs), amp_refs)
                c_ref[slot] = coupled(of_s, parts).astype(BF16)

    (cc_out,) = call(
        outer_again_body,
        [VMEM] + [VMEM] * (3 + roles),
        [two_b],
        (nums, low_out, s_out, se_out, *amp_roles),
    )
    cc_from_out = outer(cc_out)

    def inner_again_body(nums, low_ref, s_ref, se_ref, *refs):
        amp_refs, c_refs = refs[:roles], refs[-2:]

        @pl.when(lax.axis_index("role") > 0)
        def _():
            told = told_of(low_ref)
            for slot, of_s, c_ref in zip(range(2), (s_ref, se_ref), c_refs):
                parts = parts_of(nums, told_weight(told, weights + slot * pairs), amp_refs)
                c_ref[...] = coupled(of_s, parts).astype(BF16)

    c_in, ce_in = call(
        inner_again_body,
        [VMEM] + [VMEM] * (3 + roles) + [ANY],
        [sq_b, sq_b],
        (nums, low_in, s_in, se_in, *amp_roles, cc_out),
    )
    c_from_in, ce_from_in = inner(c_in), inner(ce_in)

    def own_again_body(nums, rest_ref, s_ref, se_ref, *refs):
        amp_refs, (after_ref, out_ref, out_extra_ref) = refs[:roles], refs[-3:]

        @pl.when(lax.axis_index("role") > 0)
        def _():
            row = nums[0:1, :]
            parts = parts_of(nums, told_weight(row, own_weights), amp_refs)
            out_ref[...] = rest_ref[...] - coupled(s_ref, parts)
            parts = parts_of(nums, told_weight(row, own_weights + pairs), amp_refs)
            out_extra_ref[...] = -coupled(se_ref, parts)

    rest, rest_extra = call(
        own_again_body,
        [VMEM] + [VMEM] * (3 + roles) + [ANY],
        [sq_f, sq_f],
        (nums, rest, s_own, se_own, *amp_roles, c_in),
    )

    def taken(num):
        role = lax.axis_index("role")
        return role > 0, role == whole(num(OWNER))

    def clear_body(nums, after_ref, amp_out, orb_out, zero_ref, sems):
        num, _ = read(nums)
        zero_ref[...] = jnp.zeros((pao, virt), BF16)
        for slot, here in enumerate(taken(num)):

            @pl.when(jnp.logical_not(here))
            def _():
                copies = [
                    pltpu.make_async_copy(zero_ref.at[pl.ds(0, virt)], amp_out.at[slot], sems.at[0]),
                    pltpu.make_async_copy(zero_ref, orb_out.at[slot], sems.at[1]),
                ]
                for copy in copies:
                    copy.start()
                for copy in copies:
                    copy.wait()

    outs = [(ANY, (slots, virt, virt), BF16), (ANY, (slots, pao, virt), BF16)]
    cleared = call(
        clear_body,
        [VMEM, ANY],
        outs,
        (nums, c_in),
        scratch=[pltpu.VMEM((pao, virt), BF16), pltpu.SemaphoreType.DMA((2,))],
    )

    def last_body(
        nums, coeff_ref, gain_ref, gain_extra_ref, rest_ref, rest_extra_ref, co_ref, ci_ref, cei_ref, *refs
    ):
        rest_refs, (amp_out, orb_out, amp_ref, orb_ref, sems) = refs[: len(rests)], refs[-5:]
        num, _ = read(nums)
        role = lax.axis_index("role")
        halves = [pl.ds(at, virt) for at in range(0, pao, virt)]

        def copies_of(slot):
            copies = [(amp_ref.at[slot], amp_out.at[slot])]
            copies += [(orb_ref.at[slot, rows], orb_out.at[slot, rows]) for rows in halves]
            first = slot * len(copies)
            return [
                pltpu.make_async_copy(source, target, sems.at[first + at])
                for at, (source, target) in enumerate(copies)
            ]

        here = taken(num)
        gains, kept = (gain_ref, gain_extra_ref), (rest_ref, rest_extra_ref)
        for slot, pair in ((0, MINE), (1, EXTRA)):

            @pl.when(here[slot])
            def _():
                copies = copies_of(slot)
                c_in = (ci_ref, cei_ref)[slot][...]
                total = kept[slot][...] - co_ref[slot].astype(F32) - c_in.astype(F32)
                if slot:
                    come = rest_refs[0][:virt, :]
                    for at, ref in enumerate(rest_refs[1:], 1):
                        come = jnp.where(role >= 1 << at, ref[:virt, :], come)
                    total += come.astype(F32)
                amp_ref[slot] = (gains[slot][...] * total).astype(BF16)
                copies[0].start()
                for rows, copy in zip(halves, copies[1:]):
                    x = coeff_ref[whole(num(pair)), rows, :]
                    dressed = x.astype(F32) + mxu(x, amp_ref[slot], NN) * virt_scale
                    orb_ref[slot, rows, :] = dressed.astype(BF16)
                    copy.start()

        for slot in range(slots):

            @pl.when(here[slot])
            def _():
                for copy in copies_of(slot):
                    copy.wait()

    ins = (
        nums, coeff, gain, gain_extra, rest, rest_extra, cc_from_out, c_from_in, ce_from_in, *rests, *cleared
    )
    amps_out, dressed_out = call(
        last_body,
        [VMEM] * (len(ins) - 2) + [ANY] * 2,
        outs,
        ins,
        scratch=[
            pltpu.VMEM((slots, virt, virt), BF16),
            pltpu.VMEM((slots, pao, virt), BF16),
            pltpu.SemaphoreType.DMA((slots * (1 + pao // virt),)),
        ],
        in_place={len(ins) - 2: 0, len(ins) - 1: 1},
    )
    return amps_out, dressed_out


def solution(mesh):
    in_specs = (
        P("pairs", None, None),
        P("pairs", None, None),
        P("pairs", None, None),
        P("pairs", None),
        P(),
        P("pairs"),
        P("pairs", None),
        P("pairs", None),
        P("pairs", None),
        P("pairs"),
    )
    out_specs = (P(("role", "pairs"), None, None), P(("role", "pairs"), None, None))
    return jax.shard_map(local, mesh=mesh, in_specs=in_specs, out_specs=out_specs, check_vma=False)
```

```python
import math

import jax
import jax.numpy as jnp
from jax import lax
from jax.experimental import pallas as pl
from jax.experimental.pallas import tpu as pltpu
from jax.sharding import PartitionSpec as P

F32 = jnp.float32
BF16 = jnp.bfloat16
I32 = jnp.int32
NN = ((1,), (0,))
NT = ((1,), (1,))

VMEM = pl.BlockSpec(memory_space=pltpu.VMEM)
ANY = pl.BlockSpec(memory_space=pl.ANY)
HBM = pl.BlockSpec(memory_space=pltpu.HBM)

MINE, EXTRA, OWNER, FIRST, SECOND, WHOSE, NV_MINE, NV_EXTRA, OCC_MINE, OCC_EXTRA, ROLE_PAIR = range(11)


def whole(number):
    return number.astype(jnp.int32)


def read(nums_ref):
    row = nums_ref[0:1, :]
    return lambda at: row[0, at], lambda at: row[:, at : at + 1]


def mxu(a, b, dims):
    return lax.dot_general(a, b, (dims, ((), ())), preferred_element_type=F32)


def call(body, ins, outs, args, scratch=(), vmem=48, in_place=None):
    return pl.pallas_call(
        body,
        in_specs=ins,
        out_specs=[spec for spec, _, _ in outs],
        out_shape=[jax.ShapeDtypeStruct(shape, dtype) for _, shape, dtype in outs],
        scratch_shapes=list(scratch),
        input_output_aliases=in_place or {},
        cost_estimate=pl.CostEstimate(flops=1, bytes_accessed=1, transcendentals=0),
        compiler_params=pltpu.CompilerParams(vmem_limit_bytes=vmem * 1024 * 1024),
    )(*args)


def local(
    three_index, coeff, amps, eps_virt, eps_occ, nvirt, pair_occ, partners, coupling, pair_owner
):
    columns = lax.axis_size("pairs")
    roles = lax.axis_size("role")
    occ_block, aux, pao = three_index.shape
    pairs, _, virt = coeff.shape
    partner_count = partners.shape[1]
    slots = 2
    assert roles == pairs and pairs % 2 == 0 and columns % 2 == 0 and virt % 2 == 0
    assert roles & (roles - 1) == 0
    tile = min(256, aux)
    pao_scale = 1.0 / math.sqrt(pao)
    aux_scale = 1.0 / math.sqrt(aux)
    virt_scale = 1.0 / math.sqrt(virt)
    square = (virt, virt)
    part = virt // 2
    sq_b = (VMEM, square, BF16)
    sq_f = (VMEM, square, F32)
    two_b = (VMEM, (2, virt, virt), BF16)
    all_s = (VMEM, (pairs, virt, virt), BF16)
    half = (VMEM, (aux, virt), BF16)

    inner_of = [i ^ 1 for i in range(columns)]
    outer_of = [(i + (1 if i % 2 else -1)) % columns for i in range(columns)]

    def inner(x):
        return lax.ppermute(x, "pairs", list(enumerate(inner_of)))

    def outer(x):
        return lax.ppermute(x, "pairs", list(enumerate(outer_of)))

    def swap(x, by):
        return lax.ppermute(x, "role", [(i, i ^ by) for i in range(roles)])

    three_in, coeff_in, amps_in = inner(three_index), inner(coeff), inner(amps)

    def pairs_of_roles(owner_ref):
        of_role = [jnp.int32(0)] * roles
        for p in range(pairs):
            earlier = jnp.int32(0)
            for o in range(p):
                earlier += (owner_ref[o] == owner_ref[p]).astype(I32)
            for s in range(roles):
                hit = (earlier == 0) & (owner_ref[p] == s) if s else earlier == 1
                of_role[s] = jnp.where(hit, p, of_role[s])
        return of_role

    def pick(numbers, at):
        chosen = numbers[0]
        for s in range(1, len(numbers)):
            chosen = jnp.where(at == s, numbers[s], chosen)
        return chosen

    weights = 2 * pairs
    place_at, mine_at, extra_at = 2 * weights, 2 * weights + 1, 2 * weights + 2
    riders = 16
    longer = (VMEM, (virt + riders, virt), BF16)
    own_weights = ROLE_PAIR + roles

    def plan_body(
        owner_hbm, occ_hbm, partner_hbm, coupling_hbm, eps_hbm, nvirt_hbm, coeff_hbm,
        low_ref, high_ref, nums_ref,
        owner_ref, occ_ref, partner_ref, coupling_ref, eps_ref, nvirt_ref, near_w, coeff_ref, sems,
    ):
        small = [
            pltpu.make_async_copy(source, target, sems.at[at])
            for at, (source, target) in enumerate(
                (
                    (owner_hbm, owner_ref),
                    (occ_hbm, occ_ref),
                    (partner_hbm, partner_ref),
                    (coupling_hbm, coupling_ref),
                    (eps_hbm, eps_ref),
                    (nvirt_hbm, nvirt_ref),
                )
            )
        ]
        large = pltpu.make_async_copy(coeff_hbm, coeff_ref, sems.at[6])
        for copy in (*small, large):
            copy.start()
        role = lax.axis_index("role")
        column = lax.axis_index("pairs")
        small[0].wait()
        of_role = pairs_of_roles(owner_ref)
        extra = of_role[0]
        mine = pick(of_role, role)
        for copy in small[1:]:
            copy.wait()
        nums = {}
        nums[MINE] = mine.astype(F32)
        nums[EXTRA] = extra.astype(F32)
        nums[OWNER] = owner_ref[extra].astype(F32)
        for m in range(roles):
            nums[ROLE_PAIR + m] = pick(of_role, role ^ m).astype(F32)
        nums[NV_MINE] = nvirt_ref[mine].astype(F32)
        nums[NV_EXTRA] = nvirt_ref[extra].astype(F32)
        nums[FIRST] = (occ_ref[0, mine] - column * occ_block).astype(F32)
        odd = lax.rem(column, 2) == 1
        inner_at = jnp.where(odd, 0, 2)
        outer_at = 2 - inner_at
        occ_all = occ_block * columns
        second = lax.rem(occ_ref[1, mine] - (column - 1) * occ_block + occ_all, occ_all)
        block = (second >= occ_block).astype(I32) + (second >= 2 * occ_block).astype(I32)
        place = (second - block * occ_block).astype(F32)
        nums[SECOND] = place
        lane = lax.broadcasted_iota(I32, (riders, part), 1)
        row = lax.broadcasted_iota(I32, (riders, part), 0)
        told = jnp.where(lane == place_at, place, 0.0)
        told = jnp.where(lane == mine_at, mine.astype(F32), told)
        told = jnp.where(lane == extra_at, extra.astype(F32), told)
        nums[WHOSE] = jnp.where(block == 1, 0, jnp.where(block == inner_at, 1, 2)).astype(F32)
        nums[OCC_MINE] = eps_ref[occ_ref[0, mine]] + eps_ref[occ_ref[1, mine]]
        nums[OCC_EXTRA] = eps_ref[occ_ref[0, extra]] + eps_ref[occ_ref[1, extra]]
        pair_all = pairs * columns
        for which, pair in enumerate((mine, extra)):
            for q in range(3 * pairs):
                near_w[q] = jnp.float32(0)
            for k in range(partner_count):
                at = lax.rem(partner_ref[pair, k] - (column - 1) * pairs + pair_all, pair_all)
                near_w[at] += coupling_ref[pair, k]
            for q in range(pairs):
                to = which * pairs + q
                nums[own_weights + to] = near_w[pairs + q]
                nums[own_weights + weights + to] = near_w[inner_at * pairs + q]
                told = jnp.where(lane == to, near_w[outer_at * pairs + q], told)
                told = jnp.where(lane == weights + to, near_w[inner_at * pairs + q], told)
        row_of_nums = jnp.zeros(nums_ref.shape, F32)
        lane_of_nums = lax.broadcasted_iota(I32, nums_ref.shape, 1)
        for at, number in nums.items():
            row_of_nums = jnp.where(lane_of_nums == at, number, row_of_nums)
        nums_ref[...] = row_of_nums
        coarse = told.astype(BF16).astype(F32)
        middle = (told - coarse).astype(BF16).astype(F32)
        fine = told - coarse - middle
        told = jnp.where(row == 0, coarse, jnp.where(row == 1, middle, jnp.where(row == 2, fine, 0.0)))
        low_ref[pao:, :] = told.astype(BF16)
        large.wait()
        low_ref[:pao, :] = coeff_ref[mine, :, :part]
        high_ref[...] = coeff_ref[mine, :, part:]

    rode = (VMEM, (pao + riders, part), BF16)
    x_low, x_high, nums = call(
        plan_body,
        [HBM] * 7,
        [rode, (VMEM, (pao, part), BF16), (VMEM, (8, part), F32)],
        (pair_owner, pair_occ.T, partners, coupling, eps_occ, nvirt, coeff),
        scratch=[
            pltpu.SMEM(pair_owner.shape, I32),
            pltpu.SMEM(pair_occ.shape[::-1], I32),
            pltpu.SMEM(partners.shape, I32),
            pltpu.SMEM(coupling.shape, F32),
            pltpu.SMEM(eps_occ.shape, F32),
            pltpu.SMEM(nvirt.shape, I32),
            pltpu.SMEM((3 * pairs,), F32),
            pltpu.VMEM(coeff.shape, BF16),
            pltpu.SemaphoreType.DMA((7,)),
        ],
        vmem=60,
    )
    low_out, low_in = outer(x_low), inner(x_low)

    def told_of(low_ref):
        rows = low_ref[pao:, :].astype(F32)
        return rows[0:1] + rows[1:2] + rows[2:3]

    def overlaps(x, coeff_ref, out_ref):
        turned = x.T
        for q in range(pairs):
            s = mxu(turned, coeff_ref[q], NN) * (1.0 / pao)
            out_ref[q] = s.astype(BF16)

    def coupled(s_ref, parts):
        total = None
        for at, weight, amp in parts:
            s = s_ref[at]
            u = mxu(s, amp, NN).astype(BF16)
            term = weight * mxu(u, s, NT)
            total = term if total is None else total + term
        return total

    tiles = [pl.ds(at, tile) for at in range(0, aux, tile)]

    def half_into(y_ref, three_ref, at_occ, x):
        for rows in tiles:
            y_ref[rows, :] = (mxu(three_ref[at_occ, rows, :], x, NN) * pao_scale).astype(BF16)

    def fetch_body(three_ref, after_ref, held_ref, sem):
        copy = pltpu.make_async_copy(three_ref, held_ref, sem)
        copy.start()
        copy.wait()

    (blocks,) = call(
        fetch_body,
        [ANY, ANY],
        [(VMEM, three_index.shape, BF16)],
        (three_index, nums),
        scratch=[pltpu.SemaphoreType.DMA],
        vmem=50,
    )

    x_high, _ = lax.optimization_barrier((x_high, blocks))
    high_out = outer(x_high)

    def outer_low_body(three_ref, x_ref, y_ref):
        half_into(y_ref, three_ref, whole(told_of(x_ref)[0, place_at]), x_ref[:pao, :])
        y_ref[aux:, :] = jnp.zeros((riders, part), BF16)

    (y_low,) = call(
        outer_low_body,
        [VMEM, VMEM],
        [(VMEM, (aux + riders, part), BF16)],
        (blocks, low_out),
    )
    y_low_from_out = outer(y_low)

    def outer_high_body(three_ref, low_ref, x_ref, after_ref, y_ref):
        half_into(y_ref, three_ref, whole(told_of(low_ref)[0, place_at]), x_ref[...])

    (y_high,) = call(
        outer_high_body,
        [VMEM, VMEM, VMEM, ANY],
        [(VMEM, (aux, part), BF16)],
        (blocks, low_out, high_out, y_low),
    )
    y_high_from_out = outer(y_high)

    def outer_body(coeff_ref, amps_ref, low_ref, high_ref, after_ref, s_ref, c_ref, x_ref):
        x_ref[:, :part] = low_ref[:pao, :]
        x_ref[:, part:] = high_ref[...]
        overlaps(x_ref[...], coeff_ref, s_ref)
        told = told_of(low_ref)
        c = coupled(s_ref, [(q, told[0, q], amps_ref[q]) for q in range(pairs)])
        c_ref[:virt, :] = c.astype(BF16)
        c_ref[virt:, :] = jnp.zeros((riders, virt), BF16)

    s_out, c_out = call(
        outer_body,
        [VMEM, VMEM, VMEM, VMEM, ANY],
        [all_s, longer],
        (coeff, amps, low_out, high_out, y_high),
        scratch=[pltpu.VMEM((pao, virt), BF16)],
    )
    c_from_out = outer(c_out)

    def own_half_body(
        nums, three_ref, three_in_ref, coeff_ref, after_ref, first_ref, second_ref, extra_ref, block_ref, sem
    ):
        num, _ = read(nums)
        x = coeff_ref[whole(num(MINE))]
        extra_ref[...] = coeff_ref[whole(num(EXTRA))]
        whose, second = whole(num(WHOSE)), whole(num(SECOND))
        copy = pltpu.make_async_copy(three_in_ref.at[second], block_ref.at[0], sem)

        @pl.when(whose == 1)
        def _():
            copy.start()

        turned = x.T
        first = whole(num(FIRST))
        for rows in tiles:
            first_ref[:, rows] = (mxu(turned, three_ref[first, rows, :], NT) * pao_scale).astype(BF16)

        @pl.when(whose == 0)
        def _():
            half_into(second_ref, three_ref, second, x)

        @pl.when(whose == 1)
        def _():
            copy.wait()
            half_into(second_ref, block_ref, 0, x)

    first_t, second, x_extra = call(
        own_half_body,
        [VMEM, VMEM, ANY, VMEM, ANY],
        [
            (VMEM, (virt, aux), BF16),
            (VMEM, (aux, virt), BF16),
            (VMEM, (pao, virt), BF16),
        ],
        (nums, blocks, three_in, coeff, c_out),
        scratch=[pltpu.VMEM((1, aux, pao), BF16), pltpu.SemaphoreType.DMA],
    )
    x_extra_out = outer(x_extra)

    def own_body(
        nums, coeff_ref, coeff_in_ref, amps_ref, amps_in_ref, eps_ref, after_ref,
        s_ref, c_ref, gain_ref, gain_extra_ref, s_in_ref,
    ):
        num, weight = read(nums)
        mine, extra = whole(num(MINE)), whole(num(EXTRA))
        x = coeff_ref[mine]
        total = None
        for at, of_s, of_coeff, of_amps in (
            (own_weights, s_ref, coeff_ref, amps_ref),
            (own_weights + weights, s_in_ref, coeff_in_ref, amps_in_ref),
        ):
            overlaps(x, of_coeff, of_s)
            c = coupled(of_s, [(q, weight(at + q), of_amps[q]) for q in range(pairs)])
            total = c if total is None else total + c
        c_ref[...] = total

        def gain(pair, count, occupied):
            row = jnp.broadcast_to(eps_ref[pl.ds(pair, 1), :], square)
            energy = row + row.T - occupied
            inside = (lax.broadcasted_iota(I32, square, 0) < count) & (
                lax.broadcasted_iota(I32, square, 1) < count
            )
            return jnp.where(inside, 1.0 / (energy + 1.0), 0.0)

        gain_ref[...] = gain(mine, whole(num(NV_MINE)), num(OCC_MINE))
        gain_extra_ref[...] = gain(extra, whole(num(NV_EXTRA)), num(OCC_EXTRA))

    s_own, c_own, gain, gain_extra = call(
        own_body,
        [VMEM] + [VMEM] * 5 + [ANY],
        [all_s, sq_f, sq_f, sq_f],
        (nums, coeff, coeff_in, amps, amps_in, eps_virt, c_out),
        scratch=[pltpu.VMEM((pairs, virt, virt), BF16)],
    )

    def more_body(nums, coeff_ref, in_ref, low_ref, after_ref, se_ref, s_in_ref, se_in_ref):
        @pl.when(lax.axis_index("role") > 0)
        def _():
            told = told_of(low_ref)
            num, _ = read(nums)
            overlaps(coeff_ref[whole(num(EXTRA))], coeff_ref, se_ref)
            overlaps(in_ref[whole(told[0, mine_at])], coeff_ref, s_in_ref)
            overlaps(in_ref[whole(told[0, extra_at])], coeff_ref, se_in_ref)

    se_own, s_in, se_in = call(
        more_body,
        [VMEM, VMEM, VMEM, VMEM, ANY],
        [all_s, all_s, all_s],
        (nums, coeff, coeff_in, low_in, c_own),
    )

    def first_body(
        nums, first_ref, second_ref, low_ref, high_ref, amps_ref, c_ref, co_ref, gain_ref, after_ref,
        amp_ref, k_ref,
    ):
        first = first_ref[...]
        num, _ = read(nums)
        outside = whole(num(WHOSE)) == 2

        @pl.when(outside)
        def _():
            k_ref[:, :part] = mxu(first, low_ref[:aux, :], NN) * aux_scale
            k_ref[:, part:] = mxu(first, high_ref[...], NN) * aux_scale

        @pl.when(jnp.logical_not(outside))
        def _():
            k_ref[...] = mxu(first, second_ref[...], NN) * aux_scale

        old = amps_ref[whole(num(MINE))].astype(F32)
        c = c_ref[...] + co_ref[:virt, :].astype(F32)
        amp_ref[...] = (gain_ref[...] * (old - k_ref[...] - c)).astype(BF16)

    amp, k_first = call(
        first_body,
        [VMEM] + [VMEM] * 8 + [ANY],
        [sq_b, sq_f],
        (
            nums, first_t, second, y_low_from_out, y_high_from_out,
            amps, c_own, c_from_out, gain, se_own,
        ),
    )
    amp_roles = [amp] + [swap(amp, m) for m in range(1, roles)]

    def rest_body(amp_ref, k_ref, out_ref, out_b_ref):
        amp = amp_ref[...]
        k = k_ref[...]
        right = k + mxu(k.astype(BF16), amp, NN) * virt_scale
        both = right + mxu(amp.T, right.astype(BF16), NN) * virt_scale
        rest = amp.astype(F32) - both
        out_ref[...] = rest
        out_b_ref[:virt, :] = rest.astype(BF16)
        out_b_ref[virt:, :] = jnp.zeros((riders, virt), BF16)

    rest, rest_b = call(rest_body, [VMEM, VMEM], [sq_f, longer], (amp, k_first))

    def relay_body(held_ref, come_ref, out_ref):
        role = lax.axis_index("role")

        @pl.when(role == 0)
        def _():
            out_ref[...] = held_ref[...]

        @pl.when(role > 0)
        def _():
            out_ref[...] = come_ref[...]

    rests, held, step = [], rest_b, 1
    while step < roles:
        rests.append(lax.ppermute(held, "role", [(i, i + step) for i in range(step)]))
        step *= 2
        if step < roles:
            (held,) = call(relay_body, [VMEM, VMEM], [longer], (held, rests[-1]))

    def extra_out_body(coeff_ref, x_ref, after_ref, s_ref):
        @pl.when(lax.axis_index("role") > 0)
        def _():
            overlaps(x_ref[...], coeff_ref, s_ref)

    (se_out,) = call(
        extra_out_body,
        [VMEM, VMEM, ANY],
        [all_s],
        (coeff, x_extra_out, amp),
    )

    def parts_of(nums, weight_of, amp_refs):
        num, _ = read(nums)
        parts = []
        for m in range(roles):
            at = whole(num(ROLE_PAIR + m))
            parts.append((at, weight_of(at), amp_refs[m][...]))
        return parts

    def told_weight(told, first):
        return lambda at: pick([told[:, first + q : first + q + 1] for q in range(pairs)], at)

    def outer_again_body(nums, low_ref, s_ref, se_ref, *refs):
        amp_refs, c_ref = refs[:roles], refs[-1]

        @pl.when(lax.axis_index("role") > 0)
        def _():
            told = told_of(low_ref)
            for slot, of_s in enumerate((s_ref, se_ref)):
                parts = parts_of(nums, told_weight(told, slot * pairs), amp_refs)
                c_ref[slot] = coupled(of_s, parts).astype(BF16)

    (cc_out,) = call(
        outer_again_body,
        [VMEM] + [VMEM] * (3 + roles),
        [two_b],
        (nums, low_out, s_out, se_out, *amp_roles),
    )
    cc_from_out = outer(cc_out)

    def inner_again_body(nums, low_ref, s_ref, se_ref, *refs):
        amp_refs, c_refs = refs[:roles], refs[-2:]

        @pl.when(lax.axis_index("role") > 0)
        def _():
            told = told_of(low_ref)
            for slot, of_s, c_ref in zip(range(2), (s_ref, se_ref), c_refs):
                parts = parts_of(nums, told_weight(told, weights + slot * pairs), amp_refs)
                c_ref[...] = coupled(of_s, parts).astype(BF16)

    c_in, ce_in = call(
        inner_again_body,
        [VMEM] + [VMEM] * (3 + roles) + [ANY],
        [sq_b, sq_b],
        (nums, low_in, s_in, se_in, *amp_roles, cc_out),
    )
    c_from_in, ce_from_in = inner(c_in), inner(ce_in)

    def own_again_body(nums, rest_ref, s_ref, se_ref, *refs):
        amp_refs, (after_ref, out_ref, out_extra_ref) = refs[:roles], refs[-3:]

        @pl.when(lax.axis_index("role") > 0)
        def _():
            row = nums[0:1, :]
            parts = parts_of(nums, told_weight(row, own_weights), amp_refs)
            out_ref[...] = rest_ref[...] - coupled(s_ref, parts)
            parts = parts_of(nums, told_weight(row, own_weights + pairs), amp_refs)
            out_extra_ref[...] = -coupled(se_ref, parts)

    rest, rest_extra = call(
        own_again_body,
        [VMEM] + [VMEM] * (3 + roles) + [ANY],
        [sq_f, sq_f],
        (nums, rest, s_own, se_own, *amp_roles, c_in),
    )

    def taken(num):
        role = lax.axis_index("role")
        return role > 0, role == whole(num(OWNER))

    def clear_body(nums, after_ref, amp_out, orb_out, zero_ref, sems):
        num, _ = read(nums)
        zero_ref[...] = jnp.zeros((pao, virt), BF16)
        for slot, here in enumerate(taken(num)):

            @pl.when(jnp.logical_not(here))
            def _():
                copies = [
                    pltpu.make_async_copy(zero_ref.at[pl.ds(0, virt)], amp_out.at[slot], sems.at[0]),
                    pltpu.make_async_copy(zero_ref, orb_out.at[slot], sems.at[1]),
                ]
                for copy in copies:
                    copy.start()
                for copy in copies:
                    copy.wait()

    outs = [(ANY, (slots, virt, virt), BF16), (ANY, (slots, pao, virt), BF16)]
    cleared = call(
        clear_body,
        [VMEM, ANY],
        outs,
        (nums, c_in),
        scratch=[pltpu.VMEM((pao, virt), BF16), pltpu.SemaphoreType.DMA((2,))],
    )

    def last_body(
        nums, coeff_ref, gain_ref, gain_extra_ref, rest_ref, rest_extra_ref, co_ref, ci_ref, cei_ref, *refs
    ):
        rest_refs, (amp_out, orb_out, amp_ref, orb_ref, sems) = refs[: len(rests)], refs[-5:]
        num, _ = read(nums)
        role = lax.axis_index("role")
        halves = [pl.ds(at, virt) for at in range(0, pao, virt)]

        def copies_of(slot):
            copies = [(amp_ref.at[slot], amp_out.at[slot])]
            copies += [(orb_ref.at[slot, rows], orb_out.at[slot, rows]) for rows in halves]
            first = slot * len(copies)
            return [
                pltpu.make_async_copy(source, target, sems.at[first + at])
                for at, (source, target) in enumerate(copies)
            ]

        here = taken(num)
        gains, kept = (gain_ref, gain_extra_ref), (rest_ref, rest_extra_ref)
        for slot, pair in ((0, MINE), (1, EXTRA)):

            @pl.when(here[slot])
            def _():
                copies = copies_of(slot)
                c_in = (ci_ref, cei_ref)[slot][...]
                total = kept[slot][...] - co_ref[slot].astype(F32) - c_in.astype(F32)
                if slot:
                    come = rest_refs[0][:virt, :]
                    for at, ref in enumerate(rest_refs[1:], 1):
                        come = jnp.where(role >= 1 << at, ref[:virt, :], come)
                    total += come.astype(F32)
                amp_ref[slot] = (gains[slot][...] * total).astype(BF16)
                copies[0].start()
                for rows, copy in zip(halves, copies[1:]):
                    x = coeff_ref[whole(num(pair)), rows, :]
                    dressed = x.astype(F32) + mxu(x, amp_ref[slot], NN) * virt_scale
                    orb_ref[slot, rows, :] = dressed.astype(BF16)
                    copy.start()

        for slot in range(slots):

            @pl.when(here[slot])
            def _():
                for copy in copies_of(slot):
                    copy.wait()

    ins = (
        nums, coeff, gain, gain_extra, rest, rest_extra, cc_from_out, c_from_in, ce_from_in, *rests, *cleared
    )
    amps_out, dressed_out = call(
        last_body,
        [VMEM] * (len(ins) - 2) + [ANY] * 2,
        outs,
        ins,
        scratch=[
            pltpu.VMEM((slots, virt, virt), BF16),
            pltpu.VMEM((slots, pao, virt), BF16),
            pltpu.SemaphoreType.DMA((slots * (1 + pao // virt),)),
        ],
        in_place={len(ins) - 2: 0, len(ins) - 1: 1},
    )
    return amps_out, dressed_out


def solution(mesh):
    in_specs = (
        P("pairs", None, None),
        P("pairs", None, None),
        P("pairs", None, None),
        P("pairs", None),
        P(),
        P("pairs"),
        P("pairs", None),
        P("pairs", None),
        P("pairs", None),
        P("pairs"),
    )
    out_specs = (P(("role", "pairs"), None, None), P(("role", "pairs"), None, None))
    return jax.shard_map(local, mesh=mesh, in_specs=in_specs, out_specs=out_specs, check_vma=False)
```

```python
import math

import jax
import jax.numpy as jnp
from jax import lax
from jax.experimental import pallas as pl
from jax.experimental.pallas import tpu as pltpu
from jax.sharding import PartitionSpec as P

F32 = jnp.float32
BF16 = jnp.bfloat16
I32 = jnp.int32
NN = ((1,), (0,))
NT = ((1,), (1,))

VMEM = pl.BlockSpec(memory_space=pltpu.VMEM)
ANY = pl.BlockSpec(memory_space=pl.ANY)
HBM = pl.BlockSpec(memory_space=pltpu.HBM)

MINE, EXTRA, OWNER, FIRST, SECOND, WHOSE, NV_MINE, NV_EXTRA, OCC_MINE, OCC_EXTRA, ROLE_PAIR = range(11)


def whole(number):
    return number.astype(jnp.int32)


def read(nums_ref):
    row = nums_ref[0:1, :]
    return lambda at: row[0, at], lambda at: row[:, at : at + 1]


def mxu(a, b, dims):
    return lax.dot_general(a, b, (dims, ((), ())), preferred_element_type=F32)


def call(body, ins, outs, args, scratch=(), vmem=48, in_place=None):
    return pl.pallas_call(
        body,
        in_specs=ins,
        out_specs=[spec for spec, _, _ in outs],
        out_shape=[jax.ShapeDtypeStruct(shape, dtype) for _, shape, dtype in outs],
        scratch_shapes=list(scratch),
        input_output_aliases=in_place or {},
        cost_estimate=pl.CostEstimate(flops=1, bytes_accessed=1, transcendentals=0),
        compiler_params=pltpu.CompilerParams(vmem_limit_bytes=vmem * 1024 * 1024),
    )(*args)


def local(
    three_index, coeff, amps, eps_virt, eps_occ, nvirt, pair_occ, partners, coupling, pair_owner
):
    columns = lax.axis_size("pairs")
    roles = lax.axis_size("role")
    occ_block, aux, pao = three_index.shape
    pairs, _, virt = coeff.shape
    partner_count = partners.shape[1]
    slots = 2
    assert roles == pairs and pairs % 2 == 0 and columns % 2 == 0 and virt % 2 == 0
    assert roles & (roles - 1) == 0
    tile = min(256, aux)
    pao_scale = 1.0 / math.sqrt(pao)
    aux_scale = 1.0 / math.sqrt(aux)
    virt_scale = 1.0 / math.sqrt(virt)
    square = (virt, virt)
    part = virt // 2
    sq_b = (VMEM, square, BF16)
    sq_f = (VMEM, square, F32)
    two_b = (VMEM, (2, virt, virt), BF16)
    all_s = (VMEM, (pairs, virt, virt), BF16)
    half = (VMEM, (aux, virt), BF16)

    inner_of = [i ^ 1 for i in range(columns)]
    outer_of = [(i + (1 if i % 2 else -1)) % columns for i in range(columns)]

    def inner(x):
        return lax.ppermute(x, "pairs", list(enumerate(inner_of)))

    def outer(x):
        return lax.ppermute(x, "pairs", list(enumerate(outer_of)))

    def outer_for_owners(x):
        pairings = [
            (s * columns + i, s * columns + j)
            for s in range(roles)
            for i, j in enumerate(outer_of if s else inner_of)
        ]
        return lax.ppermute(x, ("role", "pairs"), pairings)

    def swap(x, by):
        return lax.ppermute(x, "role", [(i, i ^ by) for i in range(roles)])

    three_in, coeff_in, amps_in = inner(three_index), inner(coeff), inner(amps)

    def pairs_of_roles(owner_ref):
        of_role = [jnp.int32(0)] * roles
        for p in range(pairs):
            earlier = jnp.int32(0)
            for o in range(p):
                earlier += (owner_ref[o] == owner_ref[p]).astype(I32)
            for s in range(roles):
                hit = (earlier == 0) & (owner_ref[p] == s) if s else earlier == 1
                of_role[s] = jnp.where(hit, p, of_role[s])
        return of_role

    def pick(numbers, at):
        chosen = numbers[0]
        for s in range(1, len(numbers)):
            chosen = jnp.where(at == s, numbers[s], chosen)
        return chosen

    weights = 2 * pairs
    place_at, mine_at, extra_at = 2 * weights, 2 * weights + 1, 2 * weights + 2
    riders = 16
    longer = (VMEM, (virt + riders, virt), BF16)
    own_weights = ROLE_PAIR + roles

    def plan_body(
        owner_hbm, occ_hbm, partner_hbm, coupling_hbm, eps_hbm, nvirt_hbm, coeff_hbm,
        low_ref, high_ref, nums_ref,
        owner_ref, occ_ref, partner_ref, coupling_ref, eps_ref, nvirt_ref, near_w, coeff_ref, sems,
    ):
        small = [
            pltpu.make_async_copy(source, target, sems.at[at])
            for at, (source, target) in enumerate(
                (
                    (owner_hbm, owner_ref),
                    (occ_hbm, occ_ref),
                    (partner_hbm, partner_ref),
                    (coupling_hbm, coupling_ref),
                    (eps_hbm, eps_ref),
                    (nvirt_hbm, nvirt_ref),
                )
            )
        ]
        large = pltpu.make_async_copy(coeff_hbm, coeff_ref, sems.at[6])
        for copy in (*small, large):
            copy.start()
        role = lax.axis_index("role")
        column = lax.axis_index("pairs")
        small[0].wait()
        of_role = pairs_of_roles(owner_ref)
        extra = of_role[0]
        mine = pick(of_role, role)
        for copy in small[1:]:
            copy.wait()
        nums = {}
        nums[MINE] = mine.astype(F32)
        nums[EXTRA] = extra.astype(F32)
        nums[OWNER] = owner_ref[extra].astype(F32)
        for m in range(roles):
            nums[ROLE_PAIR + m] = pick(of_role, role ^ m).astype(F32)
        nums[NV_MINE] = nvirt_ref[mine].astype(F32)
        nums[NV_EXTRA] = nvirt_ref[extra].astype(F32)
        nums[FIRST] = (occ_ref[0, mine] - column * occ_block).astype(F32)
        odd = lax.rem(column, 2) == 1
        inner_at = jnp.where(odd, 0, 2)
        outer_at = 2 - inner_at
        occ_all = occ_block * columns
        second = lax.rem(occ_ref[1, mine] - (column - 1) * occ_block + occ_all, occ_all)
        block = (second >= occ_block).astype(I32) + (second >= 2 * occ_block).astype(I32)
        place = (second - block * occ_block).astype(F32)
        nums[SECOND] = place
        lane = lax.broadcasted_iota(I32, (riders, part), 1)
        row = lax.broadcasted_iota(I32, (riders, part), 0)
        told = jnp.where(lane == place_at, place, 0.0)
        told = jnp.where(lane == mine_at, mine.astype(F32), told)
        told = jnp.where(lane == extra_at, extra.astype(F32), told)
        nums[WHOSE] = jnp.where(block == 1, 0, jnp.where(block == inner_at, 1, 2)).astype(F32)
        nums[OCC_MINE] = eps_ref[occ_ref[0, mine]] + eps_ref[occ_ref[1, mine]]
        nums[OCC_EXTRA] = eps_ref[occ_ref[0, extra]] + eps_ref[occ_ref[1, extra]]
        pair_all = pairs * columns
        for which, pair in enumerate((mine, extra)):
            for q in range(3 * pairs):
                near_w[q] = jnp.float32(0)
            for k in range(partner_count):
                at = lax.rem(partner_ref[pair, k] - (column - 1) * pairs + pair_all, pair_all)
                near_w[at] += coupling_ref[pair, k]
            for q in range(pairs):
                to = which * pairs + q
                nums[own_weights + to] = near_w[pairs + q]
                nums[own_weights + weights + to] = near_w[inner_at * pairs + q]
                told = jnp.where(lane == to, near_w[outer_at * pairs + q], told)
                told = jnp.where(lane == weights + to, near_w[inner_at * pairs + q], told)
        row_of_nums = jnp.zeros(nums_ref.shape, F32)
        lane_of_nums = lax.broadcasted_iota(I32, nums_ref.shape, 1)
        for at, number in nums.items():
            row_of_nums = jnp.where(lane_of_nums == at, number, row_of_nums)
        nums_ref[...] = row_of_nums
        coarse = told.astype(BF16).astype(F32)
        middle = (told - coarse).astype(BF16).astype(F32)
        fine = told - coarse - middle
        told = jnp.where(row == 0, coarse, jnp.where(row == 1, middle, jnp.where(row == 2, fine, 0.0)))
        low_ref[pao:, :] = told.astype(BF16)
        large.wait()
        low_ref[:pao, :] = coeff_ref[mine, :, :part]
        high_ref[...] = coeff_ref[mine, :, part:]

    rode = (VMEM, (pao + riders, part), BF16)
    x_low, x_high, nums = call(
        plan_body,
        [HBM] * 7,
        [rode, (VMEM, (pao, part), BF16), (VMEM, (8, part), F32)],
        (pair_owner, pair_occ.T, partners, coupling, eps_occ, nvirt, coeff),
        scratch=[
            pltpu.SMEM(pair_owner.shape, I32),
            pltpu.SMEM(pair_occ.shape[::-1], I32),
            pltpu.SMEM(partners.shape, I32),
            pltpu.SMEM(coupling.shape, F32),
            pltpu.SMEM(eps_occ.shape, F32),
            pltpu.SMEM(nvirt.shape, I32),
            pltpu.SMEM((3 * pairs,), F32),
            pltpu.VMEM(coeff.shape, BF16),
            pltpu.SemaphoreType.DMA((7,)),
        ],
        vmem=60,
    )
    low_out, high_out, low_in = outer(x_low), outer(x_high), inner(x_low)

    def told_of(low_ref):
        rows = low_ref[pao:, :].astype(F32)
        return rows[0:1] + rows[1:2] + rows[2:3]

    def overlaps(x, coeff_ref, out_ref):
        turned = x.T
        for q in range(pairs):
            s = mxu(turned, coeff_ref[q], NN) * (1.0 / pao)
            out_ref[q] = s.astype(BF16)

    def coupled(s_ref, parts):
        total = None
        for at, weight, amp in parts:
            s = s_ref[at]
            u = mxu(s, amp, NN).astype(BF16)
            term = weight * mxu(u, s, NT)
            total = term if total is None else total + term
        return total

    tiles = [pl.ds(at, tile) for at in range(0, aux, tile)]

    def half_into(y_ref, three_ref, at_occ, x):
        for rows in tiles:
            y_ref[rows, :] = (mxu(three_ref[at_occ, rows, :], x, NN) * pao_scale).astype(BF16)

    def fetch_body(three_ref, after_ref, held_ref, sem):
        copy = pltpu.make_async_copy(three_ref, held_ref, sem)
        copy.start()
        copy.wait()

    (blocks,) = call(
        fetch_body,
        [ANY, ANY],
        [(VMEM, three_index.shape, BF16)],
        (three_index, nums),
        scratch=[pltpu.SemaphoreType.DMA],
        vmem=50,
    )

    def outer_low_body(three_ref, x_ref, y_ref):
        half_into(y_ref, three_ref, whole(told_of(x_ref)[0, place_at]), x_ref[:pao, :])
        y_ref[aux:, :] = jnp.zeros((riders, part), BF16)

    (y_low,) = call(
        outer_low_body,
        [VMEM, VMEM],
        [(VMEM, (aux + riders, part), BF16)],
        (blocks, low_out),
    )
    y_low_from_out = outer(y_low)

    def outer_high_body(three_ref, low_ref, x_ref, after_ref, y_ref):
        half_into(y_ref, three_ref, whole(told_of(low_ref)[0, place_at]), x_ref[...])

    (y_high,) = call(
        outer_high_body,
        [VMEM, VMEM, VMEM, ANY],
        [(VMEM, (aux, part), BF16)],
        (blocks, low_out, high_out, y_low),
    )
    y_high_from_out = outer(y_high)

    def outer_body(coeff_ref, amps_ref, low_ref, high_ref, after_ref, s_ref, c_ref, x_ref):
        x_ref[:, :part] = low_ref[:pao, :]
        x_ref[:, part:] = high_ref[...]
        overlaps(x_ref[...], coeff_ref, s_ref)
        told = told_of(low_ref)
        c = coupled(s_ref, [(q, told[0, q], amps_ref[q]) for q in range(pairs)])
        c_ref[:virt, :] = c.astype(BF16)
        c_ref[virt:, :] = jnp.zeros((riders, virt), BF16)

    s_out, c_out = call(
        outer_body,
        [VMEM, VMEM, VMEM, VMEM, ANY],
        [all_s, longer],
        (coeff, amps, low_out, high_out, y_high),
        scratch=[pltpu.VMEM((pao, virt), BF16)],
    )
    c_from_out = outer(c_out)

    def own_half_body(
        nums, three_ref, three_in_ref, coeff_ref, after_ref, first_ref, second_ref, extra_ref, block_ref, sem
    ):
        num, _ = read(nums)
        x = coeff_ref[whole(num(MINE))]
        extra_ref[...] = coeff_ref[whole(num(EXTRA))]
        whose, second = whole(num(WHOSE)), whole(num(SECOND))
        copy = pltpu.make_async_copy(three_in_ref.at[second], block_ref.at[0], sem)

        @pl.when(whose == 1)
        def _():
            copy.start()

        turned = x.T
        first = whole(num(FIRST))
        for rows in tiles:
            first_ref[:, rows] = (mxu(turned, three_ref[first, rows, :], NT) * pao_scale).astype(BF16)

        @pl.when(whose == 0)
        def _():
            half_into(second_ref, three_ref, second, x)

        @pl.when(whose == 1)
        def _():
            copy.wait()
            half_into(second_ref, block_ref, 0, x)

    first_t, second, x_extra = call(
        own_half_body,
        [VMEM, VMEM, ANY, VMEM, ANY],
        [
            (VMEM, (virt, aux), BF16),
            (VMEM, (aux, virt), BF16),
            (VMEM, (pao, virt), BF16),
        ],
        (nums, blocks, three_in, coeff, c_out),
        scratch=[pltpu.VMEM((1, aux, pao), BF16), pltpu.SemaphoreType.DMA],
    )
    x_extra_out = outer_for_owners(x_extra)

    def own_body(
        nums, coeff_ref, coeff_in_ref, amps_ref, amps_in_ref, eps_ref, after_ref,
        s_ref, c_ref, gain_ref, gain_extra_ref, s_in_ref,
    ):
        num, weight = read(nums)
        mine, extra = whole(num(MINE)), whole(num(EXTRA))
        x = coeff_ref[mine]
        total = None
        for at, of_s, of_coeff, of_amps in (
            (own_weights, s_ref, coeff_ref, amps_ref),
            (own_weights + weights, s_in_ref, coeff_in_ref, amps_in_ref),
        ):
            overlaps(x, of_coeff, of_s)
            c = coupled(of_s, [(q, weight(at + q), of_amps[q]) for q in range(pairs)])
            total = c if total is None else total + c
        c_ref[...] = total

        def gain(pair, count, occupied):
            row = jnp.broadcast_to(eps_ref[pl.ds(pair, 1), :], square)
            energy = row + row.T - occupied
            inside = (lax.broadcasted_iota(I32, square, 0) < count) & (
                lax.broadcasted_iota(I32, square, 1) < count
            )
            return jnp.where(inside, 1.0 / (energy + 1.0), 0.0)

        gain_ref[...] = gain(mine, whole(num(NV_MINE)), num(OCC_MINE))
        gain_extra_ref[...] = gain(extra, whole(num(NV_EXTRA)), num(OCC_EXTRA))

    s_own, c_own, gain, gain_extra = call(
        own_body,
        [VMEM] + [VMEM] * 5 + [ANY],
        [all_s, sq_f, sq_f, sq_f],
        (nums, coeff, coeff_in, amps, amps_in, eps_virt, c_out),
        scratch=[pltpu.VMEM((pairs, virt, virt), BF16)],
    )

    def more_body(nums, coeff_ref, in_ref, low_ref, after_ref, se_ref, s_in_ref, se_in_ref):
        @pl.when(lax.axis_index("role") > 0)
        def _():
            told = told_of(low_ref)
            num, _ = read(nums)
            overlaps(coeff_ref[whole(num(EXTRA))], coeff_ref, se_ref)
            overlaps(in_ref[whole(told[0, mine_at])], coeff_ref, s_in_ref)
            overlaps(in_ref[whole(told[0, extra_at])], coeff_ref, se_in_ref)

    se_own, s_in, se_in = call(
        more_body,
        [VMEM, VMEM, VMEM, VMEM, ANY],
        [all_s, all_s, all_s],
        (nums, coeff, coeff_in, low_in, c_own),
    )

    def first_body(
        nums, first_ref, second_ref, low_ref, high_ref, amps_ref, c_ref, co_ref, gain_ref, after_ref,
        amp_ref, k_ref,
    ):
        first = first_ref[...]
        num, _ = read(nums)
        outside = whole(num(WHOSE)) == 2

        @pl.when(outside)
        def _():
            k_ref[:, :part] = mxu(first, low_ref[:aux, :], NN) * aux_scale
            k_ref[:, part:] = mxu(first, high_ref[...], NN) * aux_scale

        @pl.when(jnp.logical_not(outside))
        def _():
            k_ref[...] = mxu(first, second_ref[...], NN) * aux_scale

        old = amps_ref[whole(num(MINE))].astype(F32)
        c = c_ref[...] + co_ref[:virt, :].astype(F32)
        amp_ref[...] = (gain_ref[...] * (old - k_ref[...] - c)).astype(BF16)

    amp, k_first = call(
        first_body,
        [VMEM] + [VMEM] * 8 + [ANY],
        [sq_b, sq_f],
        (
            nums, first_t, second, y_low_from_out, y_high_from_out,
            amps, c_own, c_from_out, gain, se_own,
        ),
    )
    amp_roles = [amp] + [swap(amp, m) for m in range(1, roles)]

    def rest_body(amp_ref, k_ref, out_ref, out_b_ref):
        amp = amp_ref[...]
        k = k_ref[...]
        right = k + mxu(k.astype(BF16), amp, NN) * virt_scale
        both = right + mxu(amp.T, right.astype(BF16), NN) * virt_scale
        rest = amp.astype(F32) - both
        out_ref[...] = rest
        out_b_ref[:virt, :] = rest.astype(BF16)
        out_b_ref[virt:, :] = jnp.zeros((riders, virt), BF16)

    rest, rest_b = call(rest_body, [VMEM, VMEM], [sq_f, longer], (amp, k_first))

    def relay_body(held_ref, come_ref, out_ref):
        role = lax.axis_index("role")

        @pl.when(role == 0)
        def _():
            out_ref[...] = held_ref[...]

        @pl.when(role > 0)
        def _():
            out_ref[...] = come_ref[...]

    rests, held, step = [], rest_b, 1
    while step < roles:
        rests.append(lax.ppermute(held, "role", [(i, i + step) for i in range(step)]))
        step *= 2
        if step < roles:
            (held,) = call(relay_body, [VMEM, VMEM], [longer], (held, rests[-1]))

    def extra_out_body(coeff_ref, x_ref, after_ref, s_ref):
        @pl.when(lax.axis_index("role") > 0)
        def _():
            overlaps(x_ref[...], coeff_ref, s_ref)

    (se_out,) = call(
        extra_out_body,
        [VMEM, VMEM, ANY],
        [all_s],
        (coeff, x_extra_out, amp),
    )

    def parts_of(nums, weight_of, amp_refs):
        num, _ = read(nums)
        parts = []
        for m in range(roles):
            at = whole(num(ROLE_PAIR + m))
            parts.append((at, weight_of(at), amp_refs[m][...]))
        return parts

    def told_weight(told, first):
        return lambda at: pick([told[:, first + q : first + q + 1] for q in range(pairs)], at)

    def outer_again_body(nums, low_ref, s_ref, se_ref, *refs):
        amp_refs, c_ref = refs[:roles], refs[-1]

        @pl.when(lax.axis_index("role") > 0)
        def _():
            told = told_of(low_ref)
            for slot, of_s in enumerate((s_ref, se_ref)):
                parts = parts_of(nums, told_weight(told, slot * pairs), amp_refs)
                c_ref[slot] = coupled(of_s, parts).astype(BF16)

    (cc_out,) = call(
        outer_again_body,
        [VMEM] + [VMEM] * (3 + roles),
        [two_b],
        (nums, low_out, s_out, se_out, *amp_roles),
    )
    cc_from_out = outer_for_owners(cc_out)

    def inner_again_body(nums, low_ref, s_ref, se_ref, *refs):
        amp_refs, c_refs = refs[:roles], refs[-2:]

        @pl.when(lax.axis_index("role") > 0)
        def _():
            told = told_of(low_ref)
            for slot, of_s, c_ref in zip(range(2), (s_ref, se_ref), c_refs):
                parts = parts_of(nums, told_weight(told, weights + slot * pairs), amp_refs)
                c_ref[...] = coupled(of_s, parts).astype(BF16)

    c_in, ce_in = call(
        inner_again_body,
        [VMEM] + [VMEM] * (3 + roles) + [ANY],
        [sq_b, sq_b],
        (nums, low_in, s_in, se_in, *amp_roles, cc_out),
    )
    c_from_in, ce_from_in = inner(c_in), inner(ce_in)

    def own_again_body(nums, rest_ref, s_ref, se_ref, *refs):
        amp_refs, (after_ref, out_ref, out_extra_ref) = refs[:roles], refs[-3:]

        @pl.when(lax.axis_index("role") > 0)
        def _():
            row = nums[0:1, :]
            parts = parts_of(nums, told_weight(row, own_weights), amp_refs)
            out_ref[...] = rest_ref[...] - coupled(s_ref, parts)
            parts = parts_of(nums, told_weight(row, own_weights + pairs), amp_refs)
            out_extra_ref[...] = -coupled(se_ref, parts)

    rest, rest_extra = call(
        own_again_body,
        [VMEM] + [VMEM] * (3 + roles) + [ANY],
        [sq_f, sq_f],
        (nums, rest, s_own, se_own, *amp_roles, c_in),
    )

    def taken(num):
        role = lax.axis_index("role")
        return role > 0, role == whole(num(OWNER))

    def clear_body(nums, after_ref, amp_out, orb_out, zero_ref, sems):
        num, _ = read(nums)
        zero_ref[...] = jnp.zeros((pao, virt), BF16)
        for slot, here in enumerate(taken(num)):

            @pl.when(jnp.logical_not(here))
            def _():
                copies = [
                    pltpu.make_async_copy(zero_ref.at[pl.ds(0, virt)], amp_out.at[slot], sems.at[0]),
                    pltpu.make_async_copy(zero_ref, orb_out.at[slot], sems.at[1]),
                ]
                for copy in copies:
                    copy.start()
                for copy in copies:
                    copy.wait()

    outs = [(ANY, (slots, virt, virt), BF16), (ANY, (slots, pao, virt), BF16)]
    cleared = call(
        clear_body,
        [VMEM, ANY],
        outs,
        (nums, c_in),
        scratch=[pltpu.VMEM((pao, virt), BF16), pltpu.SemaphoreType.DMA((2,))],
    )

    def last_body(
        nums, coeff_ref, gain_ref, gain_extra_ref, rest_ref, rest_extra_ref, co_ref, ci_ref, cei_ref, *refs
    ):
        rest_refs, (amp_out, orb_out, amp_ref, orb_ref, sems) = refs[: len(rests)], refs[-5:]
        num, _ = read(nums)
        role = lax.axis_index("role")
        halves = [pl.ds(at, virt) for at in range(0, pao, virt)]

        def copies_of(slot):
            copies = [(amp_ref.at[slot], amp_out.at[slot])]
            copies += [(orb_ref.at[slot, rows], orb_out.at[slot, rows]) for rows in halves]
            first = slot * len(copies)
            return [
                pltpu.make_async_copy(source, target, sems.at[first + at])
                for at, (source, target) in enumerate(copies)
            ]

        here = taken(num)
        gains, kept = (gain_ref, gain_extra_ref), (rest_ref, rest_extra_ref)
        for slot, pair in ((0, MINE), (1, EXTRA)):

            @pl.when(here[slot])
            def _():
                copies = copies_of(slot)
                c_in = (ci_ref, cei_ref)[slot][...]
                total = kept[slot][...] - co_ref[slot].astype(F32) - c_in.astype(F32)
                if slot:
                    come = rest_refs[0][:virt, :]
                    for at, ref in enumerate(rest_refs[1:], 1):
                        come = jnp.where(role >= 1 << at, ref[:virt, :], come)
                    total += come.astype(F32)
                amp_ref[slot] = (gains[slot][...] * total).astype(BF16)
                copies[0].start()
                for rows, copy in zip(halves, copies[1:]):
                    x = coeff_ref[whole(num(pair)), rows, :]
                    dressed = x.astype(F32) + mxu(x, amp_ref[slot], NN) * virt_scale
                    orb_ref[slot, rows, :] = dressed.astype(BF16)
                    copy.start()

        for slot in range(slots):

            @pl.when(here[slot])
            def _():
                for copy in copies_of(slot):
                    copy.wait()

    ins = (
        nums, coeff, gain, gain_extra, rest, rest_extra, cc_from_out, c_from_in, ce_from_in, *rests, *cleared
    )
    amps_out, dressed_out = call(
        last_body,
        [VMEM] * (len(ins) - 2) + [ANY] * 2,
        outs,
        ins,
        scratch=[
            pltpu.VMEM((slots, virt, virt), BF16),
            pltpu.VMEM((slots, pao, virt), BF16),
            pltpu.SemaphoreType.DMA((slots * (1 + pao // virt),)),
        ],
        in_place={len(ins) - 2: 0, len(ins) - 1: 1},
    )
    return amps_out, dressed_out


def solution(mesh):
    in_specs = (
        P("pairs", None, None),
        P("pairs", None, None),
        P("pairs", None, None),
        P("pairs", None),
        P(),
        P("pairs"),
        P("pairs", None),
        P("pairs", None),
        P("pairs", None),
        P("pairs"),
    )
    out_specs = (P(("role", "pairs"), None, None), P(("role", "pairs"), None, None))
    return jax.shard_map(local, mesh=mesh, in_specs=in_specs, out_specs=out_specs, check_vma=False)
```

```python
import math

import jax
import jax.numpy as jnp
from jax import lax
from jax.experimental import pallas as pl
from jax.experimental.pallas import tpu as pltpu
from jax.sharding import PartitionSpec as P

F32 = jnp.float32
BF16 = jnp.bfloat16
I32 = jnp.int32
NN = ((1,), (0,))
NT = ((1,), (1,))

VMEM = pl.BlockSpec(memory_space=pltpu.VMEM)
ANY = pl.BlockSpec(memory_space=pl.ANY)
HBM = pl.BlockSpec(memory_space=pltpu.HBM)

MINE, EXTRA, OWNER, FIRST, SECOND, WHOSE, NV_MINE, NV_EXTRA, OCC_MINE, OCC_EXTRA, ROLE_PAIR = range(11)


def whole(number):
    return number.astype(jnp.int32)


def read(nums_ref):
    row = nums_ref[0:1, :]
    return lambda at: row[0, at], lambda at: row[:, at : at + 1]


def mxu(a, b, dims):
    return lax.dot_general(a, b, (dims, ((), ())), preferred_element_type=F32)


def call(body, ins, outs, args, scratch=(), vmem=48, in_place=None):
    return pl.pallas_call(
        body,
        in_specs=ins,
        out_specs=[spec for spec, _, _ in outs],
        out_shape=[jax.ShapeDtypeStruct(shape, dtype) for _, shape, dtype in outs],
        scratch_shapes=list(scratch),
        input_output_aliases=in_place or {},
        cost_estimate=pl.CostEstimate(flops=1, bytes_accessed=1, transcendentals=0),
        compiler_params=pltpu.CompilerParams(vmem_limit_bytes=vmem * 1024 * 1024),
    )(*args)


def local(
    three_index, coeff, amps, eps_virt, eps_occ, nvirt, pair_occ, partners, coupling, pair_owner
):
    columns = lax.axis_size("pairs")
    roles = lax.axis_size("role")
    occ_block, aux, pao = three_index.shape
    pairs, _, virt = coeff.shape
    partner_count = partners.shape[1]
    slots = 2
    assert roles == pairs and pairs % 2 == 0 and columns % 2 == 0 and virt % 2 == 0
    assert roles & (roles - 1) == 0
    tile = min(256, aux)
    pao_scale = 1.0 / math.sqrt(pao)
    aux_scale = 1.0 / math.sqrt(aux)
    virt_scale = 1.0 / math.sqrt(virt)
    square = (virt, virt)
    part = virt // 2
    sq_b = (VMEM, square, BF16)
    sq_f = (VMEM, square, F32)
    two_b = (VMEM, (2, virt, virt), BF16)
    all_s = (VMEM, (pairs, virt, virt), BF16)
    half = (VMEM, (aux, virt), BF16)

    inner_of = [i ^ 1 for i in range(columns)]
    outer_of = [(i + (1 if i % 2 else -1)) % columns for i in range(columns)]

    def inner(x):
        return lax.ppermute(x, "pairs", list(enumerate(inner_of)))

    def outer(x):
        return lax.ppermute(x, "pairs", list(enumerate(outer_of)))

    def outer_for_owners(x):
        pairings = [
            (s * columns + i, s * columns + j)
            for s in range(roles)
            for i, j in enumerate(outer_of if s else inner_of)
        ]
        return lax.ppermute(x, ("role", "pairs"), pairings)

    def swap(x, by):
        return lax.ppermute(x, "role", [(i, i ^ by) for i in range(roles)])

    three_in, coeff_in, amps_in = inner(three_index), inner(coeff), inner(amps)

    def pairs_of_roles(owner_ref):
        of_role = [jnp.int32(0)] * roles
        for p in range(pairs):
            earlier = jnp.int32(0)
            for o in range(p):
                earlier += (owner_ref[o] == owner_ref[p]).astype(I32)
            for s in range(roles):
                hit = (earlier == 0) & (owner_ref[p] == s) if s else earlier == 1
                of_role[s] = jnp.where(hit, p, of_role[s])
        return of_role

    def pick(numbers, at):
        chosen = numbers[0]
        for s in range(1, len(numbers)):
            chosen = jnp.where(at == s, numbers[s], chosen)
        return chosen

    weights = 2 * pairs
    place_at, mine_at, extra_at = 2 * weights, 2 * weights + 1, 2 * weights + 2
    riders = 16
    longer = (VMEM, (virt + riders, virt), BF16)
    own_weights = ROLE_PAIR + roles

    def plan_body(
        owner_hbm, occ_hbm, partner_hbm, coupling_hbm, eps_hbm, nvirt_hbm, coeff_hbm,
        low_ref, high_ref, nums_ref,
        owner_ref, occ_ref, partner_ref, coupling_ref, eps_ref, nvirt_ref, near_w, coeff_ref, sems,
    ):
        small = [
            pltpu.make_async_copy(source, target, sems.at[at])
            for at, (source, target) in enumerate(
                (
                    (owner_hbm, owner_ref),
                    (occ_hbm, occ_ref),
                    (partner_hbm, partner_ref),
                    (coupling_hbm, coupling_ref),
                    (eps_hbm, eps_ref),
                    (nvirt_hbm, nvirt_ref),
                )
            )
        ]
        large = pltpu.make_async_copy(coeff_hbm, coeff_ref, sems.at[6])
        for copy in (*small, large):
            copy.start()
        role = lax.axis_index("role")
        column = lax.axis_index("pairs")
        small[0].wait()
        of_role = pairs_of_roles(owner_ref)
        extra = of_role[0]
        mine = pick(of_role, role)
        for copy in small[1:]:
            copy.wait()
        nums = {}
        nums[MINE] = mine.astype(F32)
        nums[EXTRA] = extra.astype(F32)
        nums[OWNER] = owner_ref[extra].astype(F32)
        for m in range(roles):
            nums[ROLE_PAIR + m] = pick(of_role, role ^ m).astype(F32)
        nums[NV_MINE] = nvirt_ref[mine].astype(F32)
        nums[NV_EXTRA] = nvirt_ref[extra].astype(F32)
        nums[FIRST] = (occ_ref[0, mine] - column * occ_block).astype(F32)
        odd = lax.rem(column, 2) == 1
        inner_at = jnp.where(odd, 0, 2)
        outer_at = 2 - inner_at
        occ_all = occ_block * columns
        second = lax.rem(occ_ref[1, mine] - (column - 1) * occ_block + occ_all, occ_all)
        block = (second >= occ_block).astype(I32) + (second >= 2 * occ_block).astype(I32)
        place = (second - block * occ_block).astype(F32)
        nums[SECOND] = place
        lane = lax.broadcasted_iota(I32, (riders, part), 1)
        row = lax.broadcasted_iota(I32, (riders, part), 0)
        told = jnp.where(lane == place_at, place, 0.0)
        told = jnp.where(lane == mine_at, mine.astype(F32), told)
        told = jnp.where(lane == extra_at, extra.astype(F32), told)
        nums[WHOSE] = jnp.where(block == 1, 0, jnp.where(block == inner_at, 1, 2)).astype(F32)
        nums[OCC_MINE] = eps_ref[occ_ref[0, mine]] + eps_ref[occ_ref[1, mine]]
        nums[OCC_EXTRA] = eps_ref[occ_ref[0, extra]] + eps_ref[occ_ref[1, extra]]
        pair_all = pairs * columns
        for which, pair in enumerate((mine, extra)):
            for q in range(3 * pairs):
                near_w[q] = jnp.float32(0)
            for k in range(partner_count):
                at = lax.rem(partner_ref[pair, k] - (column - 1) * pairs + pair_all, pair_all)
                near_w[at] += coupling_ref[pair, k]
            for q in range(pairs):
                to = which * pairs + q
                nums[own_weights + to] = near_w[pairs + q]
                nums[own_weights + weights + to] = near_w[inner_at * pairs + q]
                told = jnp.where(lane == to, near_w[outer_at * pairs + q], told)
                told = jnp.where(lane == weights + to, near_w[inner_at * pairs + q], told)
        row_of_nums = jnp.zeros(nums_ref.shape, F32)
        lane_of_nums = lax.broadcasted_iota(I32, nums_ref.shape, 1)
        for at, number in nums.items():
            row_of_nums = jnp.where(lane_of_nums == at, number, row_of_nums)
        nums_ref[...] = row_of_nums
        coarse = told.astype(BF16).astype(F32)
        middle = (told - coarse).astype(BF16).astype(F32)
        fine = told - coarse - middle
        told = jnp.where(row == 0, coarse, jnp.where(row == 1, middle, jnp.where(row == 2, fine, 0.0)))
        low_ref[pao:, :] = told.astype(BF16)
        large.wait()
        low_ref[:pao, :] = coeff_ref[mine, :, :part]
        high_ref[...] = coeff_ref[mine, :, part:]

    rode = (VMEM, (pao + riders, part), BF16)
    x_low, x_high, nums = call(
        plan_body,
        [HBM] * 7,
        [rode, (VMEM, (pao, part), BF16), (VMEM, (8, part), F32)],
        (pair_owner, pair_occ.T, partners, coupling, eps_occ, nvirt, coeff),
        scratch=[
            pltpu.SMEM(pair_owner.shape, I32),
            pltpu.SMEM(pair_occ.shape[::-1], I32),
            pltpu.SMEM(partners.shape, I32),
            pltpu.SMEM(coupling.shape, F32),
            pltpu.SMEM(eps_occ.shape, F32),
            pltpu.SMEM(nvirt.shape, I32),
            pltpu.SMEM((3 * pairs,), F32),
            pltpu.VMEM(coeff.shape, BF16),
            pltpu.SemaphoreType.DMA((7,)),
        ],
        vmem=60,
    )
    low_out, high_out, low_in = outer(x_low), outer(x_high), inner(x_low)

    def told_of(low_ref):
        rows = low_ref[pao:, :].astype(F32)
        return rows[0:1] + rows[1:2] + rows[2:3]

    def overlaps(x, coeff_ref, out_ref):
        turned = x.T
        for q in range(pairs):
            s = mxu(turned, coeff_ref[q], NN) * (1.0 / pao)
            out_ref[q] = s.astype(BF16)

    def coupled(s_ref, parts):
        total = None
        for at, weight, amp in parts:
            s = s_ref[at]
            u = mxu(s, amp, NN).astype(BF16)
            term = weight * mxu(u, s, NT)
            total = term if total is None else total + term
        return total

    tiles = [pl.ds(at, tile) for at in range(0, aux, tile)]

    def half_into(y_ref, three_ref, at_occ, x):
        for rows in tiles:
            y_ref[rows, :] = (mxu(three_ref[at_occ, rows, :], x, NN) * pao_scale).astype(BF16)

    def fetch_body(three_ref, after_ref, held_ref, sem):
        copy = pltpu.make_async_copy(three_ref, held_ref, sem)
        copy.start()
        copy.wait()

    (blocks,) = call(
        fetch_body,
        [ANY, ANY],
        [(VMEM, three_index.shape, BF16)],
        (three_index, nums),
        scratch=[pltpu.SemaphoreType.DMA],
        vmem=50,
    )

    def outer_low_body(three_ref, x_ref, y_ref):
        half_into(y_ref, three_ref, whole(told_of(x_ref)[0, place_at]), x_ref[:pao, :])
        y_ref[aux:, :] = jnp.zeros((riders, part), BF16)

    (y_low,) = call(
        outer_low_body,
        [VMEM, VMEM],
        [(VMEM, (aux + riders, part), BF16)],
        (blocks, low_out),
    )
    y_low_from_out = outer(y_low)

    def outer_high_body(three_ref, low_ref, x_ref, after_ref, y_ref):
        half_into(y_ref, three_ref, whole(told_of(low_ref)[0, place_at]), x_ref[...])

    (y_high,) = call(
        outer_high_body,
        [VMEM, VMEM, VMEM, ANY],
        [(VMEM, (aux, part), BF16)],
        (blocks, low_out, high_out, y_low),
    )
    y_high_from_out = outer(y_high)

    def outer_body(coeff_ref, amps_ref, low_ref, high_ref, after_ref, s_ref, c_ref, x_ref):
        x_ref[:, :part] = low_ref[:pao, :]
        x_ref[:, part:] = high_ref[...]
        overlaps(x_ref[...], coeff_ref, s_ref)
        told = told_of(low_ref)
        c = coupled(s_ref, [(q, told[0, q], amps_ref[q]) for q in range(pairs)])
        c_ref[:virt, :] = c.astype(BF16)
        c_ref[virt:, :] = jnp.zeros((riders, virt), BF16)

    s_out, c_out = call(
        outer_body,
        [VMEM, VMEM, VMEM, VMEM, ANY],
        [all_s, longer],
        (coeff, amps, low_out, high_out, y_high),
        scratch=[pltpu.VMEM((pao, virt), BF16)],
    )
    c_from_out = outer(c_out)

    def own_half_body(
        nums, three_ref, three_in_ref, coeff_ref, after_ref, first_ref, second_ref, extra_ref, block_ref, sem
    ):
        num, _ = read(nums)
        x = coeff_ref[whole(num(MINE))]
        extra_ref[...] = coeff_ref[whole(num(EXTRA))]
        whose, second = whole(num(WHOSE)), whole(num(SECOND))
        copy = pltpu.make_async_copy(three_in_ref.at[second], block_ref.at[0], sem)

        @pl.when(whose == 1)
        def _():
            copy.start()

        turned = x.T
        first = whole(num(FIRST))
        for rows in tiles:
            first_ref[:, rows] = (mxu(turned, three_ref[first, rows, :], NT) * pao_scale).astype(BF16)

        @pl.when(whose == 0)
        def _():
            half_into(second_ref, three_ref, second, x)

        @pl.when(whose == 1)
        def _():
            copy.wait()
            half_into(second_ref, block_ref, 0, x)

    first_t, second, x_extra = call(
        own_half_body,
        [VMEM, VMEM, ANY, VMEM, ANY],
        [
            (VMEM, (virt, aux), BF16),
            (VMEM, (aux, virt), BF16),
            (VMEM, (pao, virt), BF16),
        ],
        (nums, blocks, three_in, coeff, c_out),
        scratch=[pltpu.VMEM((1, aux, pao), BF16), pltpu.SemaphoreType.DMA],
    )
    x_extra_out = outer_for_owners(x_extra)

    def own_body(
        nums, coeff_ref, coeff_in_ref, amps_ref, amps_in_ref, eps_ref, after_ref,
        s_ref, c_ref, gain_ref, gain_extra_ref, s_in_ref,
    ):
        num, weight = read(nums)
        mine, extra = whole(num(MINE)), whole(num(EXTRA))
        x = coeff_ref[mine]
        total = None
        for at, of_s, of_coeff, of_amps in (
            (own_weights, s_ref, coeff_ref, amps_ref),
            (own_weights + weights, s_in_ref, coeff_in_ref, amps_in_ref),
        ):
            overlaps(x, of_coeff, of_s)
            c = coupled(of_s, [(q, weight(at + q), of_amps[q]) for q in range(pairs)])
            total = c if total is None else total + c
        c_ref[...] = total

        def gain(pair, count, occupied):
            row = jnp.broadcast_to(eps_ref[pl.ds(pair, 1), :], square)
            energy = row + row.T - occupied
            inside = (lax.broadcasted_iota(I32, square, 0) < count) & (
                lax.broadcasted_iota(I32, square, 1) < count
            )
            return jnp.where(inside, 1.0 / (energy + 1.0), 0.0)

        gain_ref[...] = gain(mine, whole(num(NV_MINE)), num(OCC_MINE))
        gain_extra_ref[...] = gain(extra, whole(num(NV_EXTRA)), num(OCC_EXTRA))

    s_own, c_own, gain, gain_extra = call(
        own_body,
        [VMEM] + [VMEM] * 5 + [ANY],
        [all_s, sq_f, sq_f, sq_f],
        (nums, coeff, coeff_in, amps, amps_in, eps_virt, c_out),
        scratch=[pltpu.VMEM((pairs, virt, virt), BF16)],
    )

    def more_body(nums, coeff_ref, in_ref, low_ref, after_ref, se_ref, s_in_ref, se_in_ref):
        @pl.when(lax.axis_index("role") > 0)
        def _():
            told = told_of(low_ref)
            num, _ = read(nums)
            overlaps(coeff_ref[whole(num(EXTRA))], coeff_ref, se_ref)
            overlaps(in_ref[whole(told[0, mine_at])], coeff_ref, s_in_ref)
            overlaps(in_ref[whole(told[0, extra_at])], coeff_ref, se_in_ref)

    se_own, s_in, se_in = call(
        more_body,
        [VMEM, VMEM, VMEM, VMEM, ANY],
        [all_s, all_s, all_s],
        (nums, coeff, coeff_in, low_in, c_own),
    )

    def first_body(
        nums, first_ref, second_ref, low_ref, high_ref, amps_ref, c_ref, co_ref, gain_ref, after_ref,
        amp_ref, k_ref,
    ):
        first = first_ref[...]
        num, _ = read(nums)
        outside = whole(num(WHOSE)) == 2

        @pl.when(outside)
        def _():
            k_ref[:, :part] = mxu(first, low_ref[:aux, :], NN) * aux_scale
            k_ref[:, part:] = mxu(first, high_ref[...], NN) * aux_scale

        @pl.when(jnp.logical_not(outside))
        def _():
            k_ref[...] = mxu(first, second_ref[...], NN) * aux_scale

        old = amps_ref[whole(num(MINE))].astype(F32)
        c = c_ref[...] + co_ref[:virt, :].astype(F32)
        amp_ref[...] = (gain_ref[...] * (old - k_ref[...] - c)).astype(BF16)

    amp, k_first = call(
        first_body,
        [VMEM] + [VMEM] * 8 + [ANY],
        [sq_b, sq_f],
        (
            nums, first_t, second, y_low_from_out, y_high_from_out,
            amps, c_own, c_from_out, gain, se_own,
        ),
    )
    amp_roles = [amp] + [swap(amp, m) for m in range(1, roles)]

    def rest_body(amp_ref, k_ref, out_ref, out_b_ref):
        amp = amp_ref[...]
        k = k_ref[...]
        right = k + mxu(k.astype(BF16), amp, NN) * virt_scale
        both = right + mxu(amp.T, right.astype(BF16), NN) * virt_scale
        rest = amp.astype(F32) - both
        out_ref[...] = rest
        out_b_ref[:virt, :] = rest.astype(BF16)
        out_b_ref[virt:, :] = jnp.zeros((riders, virt), BF16)

    rest, rest_b = call(rest_body, [VMEM, VMEM], [sq_f, longer], (amp, k_first))

    def relay_body(held_ref, come_ref, out_ref):
        role = lax.axis_index("role")

        @pl.when(role == 0)
        def _():
            out_ref[...] = held_ref[...]

        @pl.when(role > 0)
        def _():
            out_ref[...] = come_ref[...]

    rests, held, step = [], rest_b, 1
    while step < roles:
        rests.append(lax.ppermute(held, "role", [(i, i + step) for i in range(step)]))
        step *= 2
        if step < roles:
            (held,) = call(relay_body, [VMEM, VMEM], [longer], (held, rests[-1]))

    def extra_out_body(coeff_ref, x_ref, after_ref, s_ref):
        @pl.when(lax.axis_index("role") > 0)
        def _():
            overlaps(x_ref[...], coeff_ref, s_ref)

    (se_out,) = call(
        extra_out_body,
        [VMEM, VMEM, ANY],
        [all_s],
        (coeff, x_extra_out, amp),
    )

    def parts_of(nums, weight_of, amp_refs):
        num, _ = read(nums)
        parts = []
        for m in range(roles):
            at = whole(num(ROLE_PAIR + m))
            parts.append((at, weight_of(at), amp_refs[m][...]))
        return parts

    def told_weight(told, first):
        return lambda at: pick([told[:, first + q : first + q + 1] for q in range(pairs)], at)

    def outer_again_body(nums, low_ref, s_ref, se_ref, *refs):
        amp_refs, c_ref = refs[:roles], refs[-1]

        @pl.when(lax.axis_index("role") > 0)
        def _():
            told = told_of(low_ref)
            for slot, of_s in enumerate((s_ref, se_ref)):
                parts = parts_of(nums, told_weight(told, slot * pairs), amp_refs)
                c_ref[slot] = coupled(of_s, parts).astype(BF16)

    (cc_out,) = call(
        outer_again_body,
        [VMEM] + [VMEM] * (3 + roles),
        [two_b],
        (nums, low_out, s_out, se_out, *amp_roles),
    )
    cc_from_out = outer(cc_out)

    def inner_again_body(nums, low_ref, s_ref, se_ref, *refs):
        amp_refs, c_refs = refs[:roles], refs[-2:]

        @pl.when(lax.axis_index("role") > 0)
        def _():
            told = told_of(low_ref)
            for slot, of_s, c_ref in zip(range(2), (s_ref, se_ref), c_refs):
                parts = parts_of(nums, told_weight(told, weights + slot * pairs), amp_refs)
                c_ref[...] = coupled(of_s, parts).astype(BF16)

    c_in, ce_in = call(
        inner_again_body,
        [VMEM] + [VMEM] * (3 + roles) + [ANY],
        [sq_b, sq_b],
        (nums, low_in, s_in, se_in, *amp_roles, cc_out),
    )
    c_from_in, ce_from_in = inner(c_in), inner(ce_in)

    def own_again_body(nums, rest_ref, s_ref, se_ref, *refs):
        amp_refs, (after_ref, out_ref, out_extra_ref) = refs[:roles], refs[-3:]

        @pl.when(lax.axis_index("role") > 0)
        def _():
            row = nums[0:1, :]
            parts = parts_of(nums, told_weight(row, own_weights), amp_refs)
            out_ref[...] = rest_ref[...] - coupled(s_ref, parts)
            parts = parts_of(nums, told_weight(row, own_weights + pairs), amp_refs)
            out_extra_ref[...] = -coupled(se_ref, parts)

    rest, rest_extra = call(
        own_again_body,
        [VMEM] + [VMEM] * (3 + roles) + [ANY],
        [sq_f, sq_f],
        (nums, rest, s_own, se_own, *amp_roles, c_in),
    )

    def taken(num):
        role = lax.axis_index("role")
        return role > 0, role == whole(num(OWNER))

    def clear_body(nums, after_ref, amp_out, orb_out, zero_ref, sems):
        num, _ = read(nums)
        zero_ref[...] = jnp.zeros((pao, virt), BF16)
        for slot, here in enumerate(taken(num)):

            @pl.when(jnp.logical_not(here))
            def _():
                copies = [
                    pltpu.make_async_copy(zero_ref.at[pl.ds(0, virt)], amp_out.at[slot], sems.at[0]),
                    pltpu.make_async_copy(zero_ref, orb_out.at[slot], sems.at[1]),
                ]
                for copy in copies:
                    copy.start()
                for copy in copies:
                    copy.wait()

    outs = [(ANY, (slots, virt, virt), BF16), (ANY, (slots, pao, virt), BF16)]
    cleared = call(
        clear_body,
        [VMEM, ANY],
        outs,
        (nums, c_in),
        scratch=[pltpu.VMEM((pao, virt), BF16), pltpu.SemaphoreType.DMA((2,))],
    )

    def last_body(
        nums, coeff_ref, gain_ref, gain_extra_ref, rest_ref, rest_extra_ref, co_ref, ci_ref, cei_ref, *refs
    ):
        rest_refs, (amp_out, orb_out, amp_ref, orb_ref, sems) = refs[: len(rests)], refs[-5:]
        num, _ = read(nums)
        role = lax.axis_index("role")
        halves = [pl.ds(at, virt) for at in range(0, pao, virt)]

        def copies_of(slot):
            copies = [(amp_ref.at[slot], amp_out.at[slot])]
            copies += [(orb_ref.at[slot, rows], orb_out.at[slot, rows]) for rows in halves]
            first = slot * len(copies)
            return [
                pltpu.make_async_copy(source, target, sems.at[first + at])
                for at, (source, target) in enumerate(copies)
            ]

        here = taken(num)
        gains, kept = (gain_ref, gain_extra_ref), (rest_ref, rest_extra_ref)
        for slot, pair in ((0, MINE), (1, EXTRA)):

            @pl.when(here[slot])
            def _():
                copies = copies_of(slot)
                c_in = (ci_ref, cei_ref)[slot][...]
                total = kept[slot][...] - co_ref[slot].astype(F32) - c_in.astype(F32)
                if slot:
                    come = rest_refs[0][:virt, :]
                    for at, ref in enumerate(rest_refs[1:], 1):
                        come = jnp.where(role >= 1 << at, ref[:virt, :], come)
                    total += come.astype(F32)
                amp_ref[slot] = (gains[slot][...] * total).astype(BF16)
                copies[0].start()
                for rows, copy in zip(halves, copies[1:]):
                    x = coeff_ref[whole(num(pair)), rows, :]
                    dressed = x.astype(F32) + mxu(x, amp_ref[slot], NN) * virt_scale
                    orb_ref[slot, rows, :] = dressed.astype(BF16)
                    copy.start()

        for slot in range(slots):

            @pl.when(here[slot])
            def _():
                for copy in copies_of(slot):
                    copy.wait()

    ins = (
        nums, coeff, gain, gain_extra, rest, rest_extra, cc_from_out, c_from_in, ce_from_in, *rests, *cleared
    )
    amps_out, dressed_out = call(
        last_body,
        [VMEM] * (len(ins) - 2) + [ANY] * 2,
        outs,
        ins,
        scratch=[
            pltpu.VMEM((slots, virt, virt), BF16),
            pltpu.VMEM((slots, pao, virt), BF16),
            pltpu.SemaphoreType.DMA((slots * (1 + pao // virt),)),
        ],
        in_place={len(ins) - 2: 0, len(ins) - 1: 1},
    )
    return amps_out, dressed_out


def solution(mesh):
    in_specs = (
        P("pairs", None, None),
        P("pairs", None, None),
        P("pairs", None, None),
        P("pairs", None),
        P(),
        P("pairs"),
        P("pairs", None),
        P("pairs", None),
        P("pairs", None),
        P("pairs"),
    )
    out_specs = (P(("role", "pairs"), None, None), P(("role", "pairs"), None, None))
    return jax.shard_map(local, mesh=mesh, in_specs=in_specs, out_specs=out_specs, check_vma=False)
```

```python
import functools
import math

import jax
import jax.numpy as jnp
from jax import lax
from jax.experimental import pallas as pl
from jax.experimental.pallas import tpu as pltpu
from jax.sharding import PartitionSpec as P

F32 = jnp.float32
BF16 = jnp.bfloat16
I32 = jnp.int32
NN = ((1,), (0,))
NT = ((1,), (1,))

VMEM = pl.BlockSpec(memory_space=pltpu.VMEM)
ANY = pl.BlockSpec(memory_space=pl.ANY)
HBM = pl.BlockSpec(memory_space=pltpu.HBM)

MINE, EXTRA, OWNER, FIRST, SECOND, WHOSE, NV_MINE, NV_EXTRA, OCC_MINE, OCC_EXTRA, ROLE_PAIR = range(11)


def whole(number):
    return number.astype(jnp.int32)


def read(nums_ref):
    row = nums_ref[0:1, :]
    return lambda at: row[0, at], lambda at: row[:, at : at + 1]


def mxu(a, b, dims):
    return lax.dot_general(a, b, (dims, ((), ())), preferred_element_type=F32)


def call(body, ins, outs, args, scratch=(), vmem=48, in_place=None):
    return pl.pallas_call(
        body,
        in_specs=ins,
        out_specs=[spec for spec, _, _ in outs],
        out_shape=[jax.ShapeDtypeStruct(shape, dtype) for _, shape, dtype in outs],
        scratch_shapes=list(scratch),
        input_output_aliases=in_place or {},
        cost_estimate=pl.CostEstimate(flops=1, bytes_accessed=1, transcendentals=0),
        compiler_params=pltpu.CompilerParams(vmem_limit_bytes=vmem * 1024 * 1024),
    )(*args)


def local(
    three_index, coeff, amps, eps_virt, eps_occ, nvirt, pair_occ, partners, coupling, pair_owner
):
    columns = lax.axis_size("pairs")
    roles = lax.axis_size("role")
    occ_block, aux, pao = three_index.shape
    pairs, _, virt = coeff.shape
    partner_count = partners.shape[1]
    slots = 2
    assert roles == pairs and pairs % 2 == 0 and columns % 2 == 0 and virt % 2 == 0
    assert roles & (roles - 1) == 0
    tile = min(256, aux)
    pao_scale = 1.0 / math.sqrt(pao)
    aux_scale = 1.0 / math.sqrt(aux)
    virt_scale = 1.0 / math.sqrt(virt)
    square = (virt, virt)
    part = virt // 2
    sq_b = (VMEM, square, BF16)
    sq_f = (VMEM, square, F32)
    all_s = (VMEM, (pairs, virt, virt), BF16)
    half = (VMEM, (aux, virt), BF16)

    inner_of = [i ^ 1 for i in range(columns)]
    outer_of = [(i + (1 if i % 2 else -1)) % columns for i in range(columns)]

    def inner(x):
        return lax.ppermute(x, "pairs", list(enumerate(inner_of)))

    def outer(x):
        return lax.ppermute(x, "pairs", list(enumerate(outer_of)))

    def swap(x, by):
        return lax.ppermute(x, "role", [(i, i ^ by) for i in range(roles)])

    three_in, coeff_in, amps_in = inner(three_index), inner(coeff), inner(amps)

    def pairs_of_roles(owner_ref):
        of_role = [jnp.int32(0)] * roles
        for p in range(pairs):
            earlier = jnp.int32(0)
            for o in range(p):
                earlier += (owner_ref[o] == owner_ref[p]).astype(I32)
            for s in range(roles):
                hit = (earlier == 0) & (owner_ref[p] == s) if s else earlier == 1
                of_role[s] = jnp.where(hit, p, of_role[s])
        return of_role

    def pick(numbers, at):
        chosen = numbers[0]
        for s in range(1, len(numbers)):
            chosen = jnp.where(at == s, numbers[s], chosen)
        return chosen

    weights = 2 * pairs
    place_at, mine_at, extra_at = 2 * weights, 2 * weights + 1, 2 * weights + 2
    riders = 16
    longer = (VMEM, (virt + riders, virt), BF16)
    own_weights = ROLE_PAIR + roles

    def plan_body(
        owner_hbm, occ_hbm, partner_hbm, coupling_hbm, eps_hbm, nvirt_hbm, coeff_hbm,
        low_ref, high_ref, nums_ref,
        owner_ref, occ_ref, partner_ref, coupling_ref, eps_ref, nvirt_ref, near_w, coeff_ref, sems,
    ):
        small = [
            pltpu.make_async_copy(source, target, sems.at[at])
            for at, (source, target) in enumerate(
                (
                    (owner_hbm, owner_ref),
                    (occ_hbm, occ_ref),
                    (partner_hbm, partner_ref),
                    (coupling_hbm, coupling_ref),
                    (eps_hbm, eps_ref),
                    (nvirt_hbm, nvirt_ref),
                )
            )
        ]
        large = pltpu.make_async_copy(coeff_hbm, coeff_ref, sems.at[6])
        for copy in (*small, large):
            copy.start()
        role = lax.axis_index("role")
        column = lax.axis_index("pairs")
        small[0].wait()
        of_role = pairs_of_roles(owner_ref)
        extra = of_role[0]
        mine = pick(of_role, role)
        for copy in small[1:]:
            copy.wait()
        nums = {}
        nums[MINE] = mine.astype(F32)
        nums[EXTRA] = extra.astype(F32)
        nums[OWNER] = owner_ref[extra].astype(F32)
        for m in range(roles):
            nums[ROLE_PAIR + m] = pick(of_role, role ^ m).astype(F32)
        nums[NV_MINE] = nvirt_ref[mine].astype(F32)
        nums[NV_EXTRA] = nvirt_ref[extra].astype(F32)
        nums[FIRST] = (occ_ref[0, mine] - column * occ_block).astype(F32)
        odd = lax.rem(column, 2) == 1
        inner_at = jnp.where(odd, 0, 2)
        outer_at = 2 - inner_at
        occ_all = occ_block * columns
        second = lax.rem(occ_ref[1, mine] - (column - 1) * occ_block + occ_all, occ_all)
        block = (second >= occ_block).astype(I32) + (second >= 2 * occ_block).astype(I32)
        place = (second - block * occ_block).astype(F32)
        nums[SECOND] = place
        lane = lax.broadcasted_iota(I32, (riders, part), 1)
        row = lax.broadcasted_iota(I32, (riders, part), 0)
        told = jnp.where(lane == place_at, place, 0.0)
        told = jnp.where(lane == mine_at, mine.astype(F32), told)
        told = jnp.where(lane == extra_at, extra.astype(F32), told)
        nums[WHOSE] = jnp.where(block == 1, 0, jnp.where(block == inner_at, 1, 2)).astype(F32)
        nums[OCC_MINE] = eps_ref[occ_ref[0, mine]] + eps_ref[occ_ref[1, mine]]
        nums[OCC_EXTRA] = eps_ref[occ_ref[0, extra]] + eps_ref[occ_ref[1, extra]]
        pair_all = pairs * columns
        for which, pair in enumerate((mine, extra)):
            for q in range(3 * pairs):
                near_w[q] = jnp.float32(0)
            for k in range(partner_count):
                at = lax.rem(partner_ref[pair, k] - (column - 1) * pairs + pair_all, pair_all)
                near_w[at] += coupling_ref[pair, k]
            for q in range(pairs):
                to = which * pairs + q
                nums[own_weights + to] = near_w[pairs + q]
                nums[own_weights + weights + to] = near_w[inner_at * pairs + q]
                told = jnp.where(lane == to, near_w[outer_at * pairs + q], told)
                told = jnp.where(lane == weights + to, near_w[inner_at * pairs + q], told)
        row_of_nums = jnp.zeros(nums_ref.shape, F32)
        lane_of_nums = lax.broadcasted_iota(I32, nums_ref.shape, 1)
        for at, number in nums.items():
            row_of_nums = jnp.where(lane_of_nums == at, number, row_of_nums)
        nums_ref[...] = row_of_nums
        coarse = told.astype(BF16).astype(F32)
        middle = (told - coarse).astype(BF16).astype(F32)
        fine = told - coarse - middle
        told = jnp.where(row == 0, coarse, jnp.where(row == 1, middle, jnp.where(row == 2, fine, 0.0)))
        low_ref[pao:, :] = told.astype(BF16)
        large.wait()
        low_ref[:pao, :] = coeff_ref[mine, :, :part]
        high_ref[...] = coeff_ref[mine, :, part:]

    rode = (VMEM, (pao + riders, part), BF16)
    x_low, x_high, nums = call(
        plan_body,
        [HBM] * 7,
        [rode, (VMEM, (pao, part), BF16), (VMEM, (8, part), F32)],
        (pair_owner, pair_occ.T, partners, coupling, eps_occ, nvirt, coeff),
        scratch=[
            pltpu.SMEM(pair_owner.shape, I32),
            pltpu.SMEM(pair_occ.shape[::-1], I32),
            pltpu.SMEM(partners.shape, I32),
            pltpu.SMEM(coupling.shape, F32),
            pltpu.SMEM(eps_occ.shape, F32),
            pltpu.SMEM(nvirt.shape, I32),
            pltpu.SMEM((3 * pairs,), F32),
            pltpu.VMEM(coeff.shape, BF16),
            pltpu.SemaphoreType.DMA((7,)),
        ],
        vmem=60,
    )
    low_out, high_out, low_in = outer(x_low), outer(x_high), inner(x_low)

    def told_of(low_ref):
        rows = low_ref[pao:, :].astype(F32)
        return rows[0:1] + rows[1:2] + rows[2:3]

    def overlaps(x, coeff_ref, out_ref):
        turned = x.T
        for q in range(pairs):
            s = mxu(turned, coeff_ref[q], NN) * (1.0 / pao)
            out_ref[q] = s.astype(BF16)

    def coupled(s_ref, parts):
        total = None
        for at, weight, amp in parts:
            s = s_ref[at]
            u = mxu(s, amp, NN).astype(BF16)
            term = weight * mxu(u, s, NT)
            total = term if total is None else total + term
        return total

    tiles = [pl.ds(at, tile) for at in range(0, aux, tile)]

    def half_into(y_ref, three_ref, at_occ, x):
        for rows in tiles:
            y_ref[rows, :] = (mxu(three_ref[at_occ, rows, :], x, NN) * pao_scale).astype(BF16)

    def fetch_body(three_ref, after_ref, held_ref, sem):
        copy = pltpu.make_async_copy(three_ref, held_ref, sem)
        copy.start()
        copy.wait()

    (blocks,) = call(
        fetch_body,
        [ANY, ANY],
        [(VMEM, three_index.shape, BF16)],
        (three_index, nums),
        scratch=[pltpu.SemaphoreType.DMA],
        vmem=50,
    )

    def outer_low_body(three_ref, x_ref, y_ref):
        half_into(y_ref, three_ref, whole(told_of(x_ref)[0, place_at]), x_ref[:pao, :])
        y_ref[aux:, :] = jnp.zeros((riders, part), BF16)

    (y_low,) = call(
        outer_low_body,
        [VMEM, VMEM],
        [(VMEM, (aux + riders, part), BF16)],
        (blocks, low_out),
    )
    y_low_from_out = outer(y_low)

    def outer_high_body(three_ref, low_ref, x_ref, after_ref, y_ref):
        half_into(y_ref, three_ref, whole(told_of(low_ref)[0, place_at]), x_ref[...])

    (y_high,) = call(
        outer_high_body,
        [VMEM, VMEM, VMEM, ANY],
        [(VMEM, (aux, part), BF16)],
        (blocks, low_out, high_out, y_low),
    )
    y_high_from_out = outer(y_high)

    def outer_body(coeff_ref, amps_ref, low_ref, high_ref, after_ref, s_ref, c_ref, x_ref):
        x_ref[:, :part] = low_ref[:pao, :]
        x_ref[:, part:] = high_ref[...]
        overlaps(x_ref[...], coeff_ref, s_ref)
        told = told_of(low_ref)
        c = coupled(s_ref, [(q, told[0, q], amps_ref[q]) for q in range(pairs)])
        c_ref[:virt, :] = c.astype(BF16)
        c_ref[virt:, :] = jnp.zeros((riders, virt), BF16)

    s_out, c_out = call(
        outer_body,
        [VMEM, VMEM, VMEM, VMEM, ANY],
        [all_s, longer],
        (coeff, amps, low_out, high_out, y_high),
        scratch=[pltpu.VMEM((pao, virt), BF16)],
    )
    c_from_out = outer(c_out)

    def own_half_body(
        nums, three_ref, three_in_ref, coeff_ref, after_ref, first_ref, second_ref, extra_ref, block_ref, sem
    ):
        num, _ = read(nums)
        x = coeff_ref[whole(num(MINE))]
        extra_ref[...] = coeff_ref[whole(num(EXTRA))]
        whose, second = whole(num(WHOSE)), whole(num(SECOND))
        copy = pltpu.make_async_copy(three_in_ref.at[second], block_ref.at[0], sem)

        @pl.when(whose == 1)
        def _():
            copy.start()

        turned = x.T
        first = whole(num(FIRST))
        for rows in tiles:
            first_ref[:, rows] = (mxu(turned, three_ref[first, rows, :], NT) * pao_scale).astype(BF16)

        @pl.when(whose == 0)
        def _():
            half_into(second_ref, three_ref, second, x)

        @pl.when(whose == 1)
        def _():
            copy.wait()
            half_into(second_ref, block_ref, 0, x)

    first_t, second, x_extra = call(
        own_half_body,
        [VMEM, VMEM, ANY, VMEM, ANY],
        [
            (VMEM, (virt, aux), BF16),
            (VMEM, (aux, virt), BF16),
            (VMEM, (pao, virt), BF16),
        ],
        (nums, blocks, three_in, coeff, c_out),
        scratch=[pltpu.VMEM((1, aux, pao), BF16), pltpu.SemaphoreType.DMA],
    )
    x_extra_out = outer(x_extra)

    def own_body(
        nums, coeff_ref, coeff_in_ref, amps_ref, amps_in_ref, eps_ref, after_ref,
        s_ref, c_ref, gain_ref, gain_extra_ref, s_in_ref,
    ):
        num, weight = read(nums)
        mine, extra = whole(num(MINE)), whole(num(EXTRA))
        x = coeff_ref[mine]
        total = None
        for at, of_s, of_coeff, of_amps in (
            (own_weights, s_ref, coeff_ref, amps_ref),
            (own_weights + weights, s_in_ref, coeff_in_ref, amps_in_ref),
        ):
            overlaps(x, of_coeff, of_s)
            c = coupled(of_s, [(q, weight(at + q), of_amps[q]) for q in range(pairs)])
            total = c if total is None else total + c
        c_ref[...] = total

        def gain(pair, count, occupied):
            row = jnp.broadcast_to(eps_ref[pl.ds(pair, 1), :], square)
            energy = row + row.T - occupied
            inside = (lax.broadcasted_iota(I32, square, 0) < count) & (
                lax.broadcasted_iota(I32, square, 1) < count
            )
            return jnp.where(inside, 1.0 / (energy + 1.0), 0.0)

        gain_ref[...] = gain(mine, whole(num(NV_MINE)), num(OCC_MINE))
        gain_extra_ref[...] = gain(extra, whole(num(NV_EXTRA)), num(OCC_EXTRA))

    s_own, c_own, gain, gain_extra = call(
        own_body,
        [VMEM] + [VMEM] * 5 + [ANY],
        [all_s, sq_f, sq_f, sq_f],
        (nums, coeff, coeff_in, amps, amps_in, eps_virt, c_out),
        scratch=[pltpu.VMEM((pairs, virt, virt), BF16)],
    )

    def more_body(nums, coeff_ref, in_ref, low_ref, after_ref, se_ref, s_in_ref, se_in_ref):
        @pl.when(lax.axis_index("role") > 0)
        def _():
            told = told_of(low_ref)
            num, _ = read(nums)
            overlaps(coeff_ref[whole(num(EXTRA))], coeff_ref, se_ref)
            overlaps(in_ref[whole(told[0, mine_at])], coeff_ref, s_in_ref)
            overlaps(in_ref[whole(told[0, extra_at])], coeff_ref, se_in_ref)

    se_own, s_in, se_in = call(
        more_body,
        [VMEM, VMEM, VMEM, VMEM, ANY],
        [all_s, all_s, all_s],
        (nums, coeff, coeff_in, low_in, c_own),
    )

    def first_body(
        nums, first_ref, second_ref, low_ref, high_ref, amps_ref, c_ref, co_ref, gain_ref, after_ref,
        amp_ref, k_ref,
    ):
        first = first_ref[...]
        num, _ = read(nums)
        outside = whole(num(WHOSE)) == 2

        @pl.when(outside)
        def _():
            k_ref[:, :part] = mxu(first, low_ref[:aux, :], NN) * aux_scale
            k_ref[:, part:] = mxu(first, high_ref[...], NN) * aux_scale

        @pl.when(jnp.logical_not(outside))
        def _():
            k_ref[...] = mxu(first, second_ref[...], NN) * aux_scale

        old = amps_ref[whole(num(MINE))].astype(F32)
        c = c_ref[...] + co_ref[:virt, :].astype(F32)
        amp_ref[...] = (gain_ref[...] * (old - k_ref[...] - c)).astype(BF16)

    amp, k_first = call(
        first_body,
        [VMEM] + [VMEM] * 8 + [ANY],
        [sq_b, sq_f],
        (
            nums, first_t, second, y_low_from_out, y_high_from_out,
            amps, c_own, c_from_out, gain, se_own,
        ),
    )
    amp_roles = [amp] + [swap(amp, m) for m in range(1, roles)]

    def rest_body(amp_ref, k_ref, out_ref, out_b_ref):
        amp = amp_ref[...]
        k = k_ref[...]
        right = k + mxu(k.astype(BF16), amp, NN) * virt_scale
        both = right + mxu(amp.T, right.astype(BF16), NN) * virt_scale
        rest = amp.astype(F32) - both
        out_ref[...] = rest
        out_b_ref[:virt, :] = rest.astype(BF16)
        out_b_ref[virt:, :] = jnp.zeros((riders, virt), BF16)

    rest, rest_b = call(rest_body, [VMEM, VMEM], [sq_f, longer], (amp, k_first))

    def relay_body(held_ref, come_ref, out_ref):
        role = lax.axis_index("role")

        @pl.when(role == 0)
        def _():
            out_ref[...] = held_ref[...]

        @pl.when(role > 0)
        def _():
            out_ref[...] = come_ref[...]

    rests, held, step = [], rest_b, 1
    while step < roles:
        rests.append(lax.ppermute(held, "role", [(i, i + step) for i in range(step)]))
        step *= 2
        if step < roles:
            (held,) = call(relay_body, [VMEM, VMEM], [longer], (held, rests[-1]))

    def extra_out_body(coeff_ref, x_ref, after_ref, s_ref):
        @pl.when(lax.axis_index("role") > 0)
        def _():
            overlaps(x_ref[...], coeff_ref, s_ref)

    (se_out,) = call(
        extra_out_body,
        [VMEM, VMEM, ANY],
        [all_s],
        (coeff, x_extra_out, amp),
    )

    def parts_of(nums, weight_of, amp_refs, first=0):
        num, _ = read(nums)
        parts = []
        for m, amp_ref in enumerate(amp_refs, first):
            at = whole(num(ROLE_PAIR + m))
            parts.append((at, weight_of(at), amp_ref[...]))
        return parts

    def told_weight(told, first):
        return lambda at: pick([told[:, first + q : first + q + 1] for q in range(pairs)], at)

    def outer_again_body(first, last, nums, low_ref, s_ref, se_ref, *refs):
        amp_refs, before, c_ref = refs[: last - first], refs[last - first : -1], refs[-1]

        @pl.when(lax.axis_index("role") > 0)
        def _():
            told = told_of(low_ref)
            for slot, of_s in enumerate((s_ref, se_ref)):
                parts = parts_of(nums, told_weight(told, slot * pairs), amp_refs, first)
                total = coupled(of_s, parts)
                for ref in before:
                    total += ref[slot]
                c_ref[slot] = total.astype(c_ref.dtype)

    def outer_again(first, last, dtype, *before):
        (c,) = call(
            functools.partial(outer_again_body, first, last),
            [VMEM] * (4 + last - first + len(before)),
            [(VMEM, (2, virt, virt), dtype)],
            (nums, low_out, s_out, se_out, *amp_roles[first:last], *before),
        )
        return c

    cc_out = outer_again(roles // 2, roles, BF16, outer_again(0, roles // 2, F32))
    cc_from_out = outer(cc_out)

    def inner_again_body(nums, low_ref, s_ref, se_ref, *refs):
        amp_refs, c_refs = refs[:roles], refs[-2:]

        @pl.when(lax.axis_index("role") > 0)
        def _():
            told = told_of(low_ref)
            for slot, of_s, c_ref in zip(range(2), (s_ref, se_ref), c_refs):
                parts = parts_of(nums, told_weight(told, weights + slot * pairs), amp_refs)
                c_ref[...] = coupled(of_s, parts).astype(BF16)

    c_in, ce_in = call(
        inner_again_body,
        [VMEM] + [VMEM] * (3 + roles) + [ANY],
        [sq_b, sq_b],
        (nums, low_in, s_in, se_in, *amp_roles, cc_out),
    )
    c_from_in, ce_from_in = inner(c_in), inner(ce_in)

    def own_again_body(nums, rest_ref, s_ref, se_ref, *refs):
        amp_refs, (after_ref, out_ref, out_extra_ref) = refs[:roles], refs[-3:]

        @pl.when(lax.axis_index("role") > 0)
        def _():
            row = nums[0:1, :]
            parts = parts_of(nums, told_weight(row, own_weights), amp_refs)
            out_ref[...] = rest_ref[...] - coupled(s_ref, parts)
            parts = parts_of(nums, told_weight(row, own_weights + pairs), amp_refs)
            out_extra_ref[...] = -coupled(se_ref, parts)

    rest, rest_extra = call(
        own_again_body,
        [VMEM] + [VMEM] * (3 + roles) + [ANY],
        [sq_f, sq_f],
        (nums, rest, s_own, se_own, *amp_roles, c_in),
    )

    def taken(num):
        role = lax.axis_index("role")
        return role > 0, role == whole(num(OWNER))

    def clear_body(nums, after_ref, amp_out, orb_out, zero_ref, sems):
        num, _ = read(nums)
        zero_ref[...] = jnp.zeros((pao, virt), BF16)
        for slot, here in enumerate(taken(num)):

            @pl.when(jnp.logical_not(here))
            def _():
                copies = [
                    pltpu.make_async_copy(zero_ref.at[pl.ds(0, virt)], amp_out.at[slot], sems.at[0]),
                    pltpu.make_async_copy(zero_ref, orb_out.at[slot], sems.at[1]),
                ]
                for copy in copies:
                    copy.start()
                for copy in copies:
                    copy.wait()

    outs = [(ANY, (slots, virt, virt), BF16), (ANY, (slots, pao, virt), BF16)]
    cleared = call(
        clear_body,
        [VMEM, ANY],
        outs,
        (nums, c_in),
        scratch=[pltpu.VMEM((pao, virt), BF16), pltpu.SemaphoreType.DMA((2,))],
    )

    def last_body(
        nums, coeff_ref, gain_ref, gain_extra_ref, rest_ref, rest_extra_ref, co_ref, ci_ref, cei_ref, *refs
    ):
        rest_refs, (amp_out, orb_out, amp_ref, orb_ref, sems) = refs[: len(rests)], refs[-5:]
        num, _ = read(nums)
        role = lax.axis_index("role")
        halves = [pl.ds(at, virt) for at in range(0, pao, virt)]

        def copies_of(slot):
            copies = [(amp_ref.at[slot], amp_out.at[slot])]
            copies += [(orb_ref.at[slot, rows], orb_out.at[slot, rows]) for rows in halves]
            first = slot * len(copies)
            return [
                pltpu.make_async_copy(source, target, sems.at[first + at])
                for at, (source, target) in enumerate(copies)
            ]

        here = taken(num)
        gains, kept = (gain_ref, gain_extra_ref), (rest_ref, rest_extra_ref)
        for slot, pair in ((0, MINE), (1, EXTRA)):

            @pl.when(here[slot])
            def _():
                copies = copies_of(slot)
                c_in = (ci_ref, cei_ref)[slot][...]
                total = kept[slot][...] - co_ref[slot].astype(F32) - c_in.astype(F32)
                if slot:
                    come = rest_refs[0][:virt, :]
                    for at, ref in enumerate(rest_refs[1:], 1):
                        come = jnp.where(role >= 1 << at, ref[:virt, :], come)
                    total += come.astype(F32)
                amp_ref[slot] = (gains[slot][...] * total).astype(BF16)
                copies[0].start()
                for rows, copy in zip(halves, copies[1:]):
                    x = coeff_ref[whole(num(pair)), rows, :]
                    dressed = x.astype(F32) + mxu(x, amp_ref[slot], NN) * virt_scale
                    orb_ref[slot, rows, :] = dressed.astype(BF16)
                    copy.start()

        for slot in range(slots):

            @pl.when(here[slot])
            def _():
                for copy in copies_of(slot):
                    copy.wait()

    ins = (
        nums, coeff, gain, gain_extra, rest, rest_extra, cc_from_out, c_from_in, ce_from_in, *rests, *cleared
    )
    amps_out, dressed_out = call(
        last_body,
        [VMEM] * (len(ins) - 2) + [ANY] * 2,
        outs,
        ins,
        scratch=[
            pltpu.VMEM((slots, virt, virt), BF16),
            pltpu.VMEM((slots, pao, virt), BF16),
            pltpu.SemaphoreType.DMA((slots * (1 + pao // virt),)),
        ],
        in_place={len(ins) - 2: 0, len(ins) - 1: 1},
    )
    return amps_out, dressed_out


def solution(mesh):
    in_specs = (
        P("pairs", None, None),
        P("pairs", None, None),
        P("pairs", None, None),
        P("pairs", None),
        P(),
        P("pairs"),
        P("pairs", None),
        P("pairs", None),
        P("pairs", None),
        P("pairs"),
    )
    out_specs = (P(("role", "pairs"), None, None), P(("role", "pairs"), None, None))
    return jax.shard_map(local, mesh=mesh, in_specs=in_specs, out_specs=out_specs, check_vma=False)
```

```python
import functools
import math

import jax
import jax.numpy as jnp
from jax import lax
from jax.experimental import pallas as pl
from jax.experimental.pallas import tpu as pltpu
from jax.sharding import PartitionSpec as P

F32 = jnp.float32
BF16 = jnp.bfloat16
I32 = jnp.int32
NN = ((1,), (0,))
NT = ((1,), (1,))

VMEM = pl.BlockSpec(memory_space=pltpu.VMEM)
ANY = pl.BlockSpec(memory_space=pl.ANY)
HBM = pl.BlockSpec(memory_space=pltpu.HBM)

MINE, EXTRA, OWNER, FIRST, SECOND, WHOSE, NV_MINE, NV_EXTRA, OCC_MINE, OCC_EXTRA, ROLE_PAIR = range(11)


def whole(number):
    return number.astype(jnp.int32)


def read(nums_ref):
    row = nums_ref[0:1, :]
    return lambda at: row[0, at], lambda at: row[:, at : at + 1]


def mxu(a, b, dims):
    return lax.dot_general(a, b, (dims, ((), ())), preferred_element_type=F32)


def call(body, ins, outs, args, scratch=(), vmem=48, in_place=None):
    return pl.pallas_call(
        body,
        in_specs=ins,
        out_specs=[spec for spec, _, _ in outs],
        out_shape=[jax.ShapeDtypeStruct(shape, dtype) for _, shape, dtype in outs],
        scratch_shapes=list(scratch),
        input_output_aliases=in_place or {},
        cost_estimate=pl.CostEstimate(flops=1, bytes_accessed=1, transcendentals=0),
        compiler_params=pltpu.CompilerParams(vmem_limit_bytes=vmem * 1024 * 1024),
    )(*args)


def local(
    three_index, coeff, amps, eps_virt, eps_occ, nvirt, pair_occ, partners, coupling, pair_owner
):
    columns = lax.axis_size("pairs")
    roles = lax.axis_size("role")
    occ_block, aux, pao = three_index.shape
    pairs, _, virt = coeff.shape
    partner_count = partners.shape[1]
    slots = 2
    assert roles == pairs and pairs % 2 == 0 and columns % 2 == 0 and virt % 2 == 0
    assert roles & (roles - 1) == 0
    tile = min(256, aux)
    pao_scale = 1.0 / math.sqrt(pao)
    aux_scale = 1.0 / math.sqrt(aux)
    virt_scale = 1.0 / math.sqrt(virt)
    square = (virt, virt)
    part = virt // 2
    sq_b = (VMEM, square, BF16)
    sq_f = (VMEM, square, F32)
    all_s = (VMEM, (pairs, virt, virt), BF16)
    half = (VMEM, (aux, virt), BF16)

    inner_of = [i ^ 1 for i in range(columns)]
    outer_of = [(i + (1 if i % 2 else -1)) % columns for i in range(columns)]

    def inner(x):
        return lax.ppermute(x, "pairs", list(enumerate(inner_of)))

    def outer(x):
        return lax.ppermute(x, "pairs", list(enumerate(outer_of)))

    def outer_for_owners(x):
        pairings = [
            (s * columns + i, s * columns + j)
            for s in range(roles)
            for i, j in enumerate(outer_of if s else inner_of)
        ]
        return lax.ppermute(x, ("role", "pairs"), pairings)

    def swap(x, by):
        return lax.ppermute(x, "role", [(i, i ^ by) for i in range(roles)])

    three_in, coeff_in, amps_in = inner(three_index), inner(coeff), inner(amps)

    def pairs_of_roles(owner_ref):
        of_role = [jnp.int32(0)] * roles
        for p in range(pairs):
            earlier = jnp.int32(0)
            for o in range(p):
                earlier += (owner_ref[o] == owner_ref[p]).astype(I32)
            for s in range(roles):
                hit = (earlier == 0) & (owner_ref[p] == s) if s else earlier == 1
                of_role[s] = jnp.where(hit, p, of_role[s])
        return of_role

    def pick(numbers, at):
        chosen = numbers[0]
        for s in range(1, len(numbers)):
            chosen = jnp.where(at == s, numbers[s], chosen)
        return chosen

    weights = 2 * pairs
    place_at, mine_at, extra_at = 2 * weights, 2 * weights + 1, 2 * weights + 2
    riders = 16
    longer = (VMEM, (virt + riders, virt), BF16)
    own_weights = ROLE_PAIR + roles

    def plan_body(
        owner_hbm, occ_hbm, partner_hbm, coupling_hbm, eps_hbm, nvirt_hbm, coeff_hbm,
        low_ref, high_ref, nums_ref,
        owner_ref, occ_ref, partner_ref, coupling_ref, eps_ref, nvirt_ref, near_w, coeff_ref, sems,
    ):
        small = [
            pltpu.make_async_copy(source, target, sems.at[at])
            for at, (source, target) in enumerate(
                (
                    (owner_hbm, owner_ref),
                    (occ_hbm, occ_ref),
                    (partner_hbm, partner_ref),
                    (coupling_hbm, coupling_ref),
                    (eps_hbm, eps_ref),
                    (nvirt_hbm, nvirt_ref),
                )
            )
        ]
        large = pltpu.make_async_copy(coeff_hbm, coeff_ref, sems.at[6])
        for copy in (*small, large):
            copy.start()
        role = lax.axis_index("role")
        column = lax.axis_index("pairs")
        small[0].wait()
        of_role = pairs_of_roles(owner_ref)
        extra = of_role[0]
        mine = pick(of_role, role)
        for copy in small[1:]:
            copy.wait()
        nums = {}
        nums[MINE] = mine.astype(F32)
        nums[EXTRA] = extra.astype(F32)
        nums[OWNER] = owner_ref[extra].astype(F32)
        for m in range(roles):
            nums[ROLE_PAIR + m] = pick(of_role, role ^ m).astype(F32)
        nums[NV_MINE] = nvirt_ref[mine].astype(F32)
        nums[NV_EXTRA] = nvirt_ref[extra].astype(F32)
        nums[FIRST] = (occ_ref[0, mine] - column * occ_block).astype(F32)
        odd = lax.rem(column, 2) == 1
        inner_at = jnp.where(odd, 0, 2)
        outer_at = 2 - inner_at
        occ_all = occ_block * columns
        second = lax.rem(occ_ref[1, mine] - (column - 1) * occ_block + occ_all, occ_all)
        block = (second >= occ_block).astype(I32) + (second >= 2 * occ_block).astype(I32)
        place = (second - block * occ_block).astype(F32)
        nums[SECOND] = place
        lane = lax.broadcasted_iota(I32, (riders, part), 1)
        row = lax.broadcasted_iota(I32, (riders, part), 0)
        told = jnp.where(lane == place_at, place, 0.0)
        told = jnp.where(lane == mine_at, mine.astype(F32), told)
        told = jnp.where(lane == extra_at, extra.astype(F32), told)
        nums[WHOSE] = jnp.where(block == 1, 0, jnp.where(block == inner_at, 1, 2)).astype(F32)
        nums[OCC_MINE] = eps_ref[occ_ref[0, mine]] + eps_ref[occ_ref[1, mine]]
        nums[OCC_EXTRA] = eps_ref[occ_ref[0, extra]] + eps_ref[occ_ref[1, extra]]
        pair_all = pairs * columns
        for which, pair in enumerate((mine, extra)):
            for q in range(3 * pairs):
                near_w[q] = jnp.float32(0)
            for k in range(partner_count):
                at = lax.rem(partner_ref[pair, k] - (column - 1) * pairs + pair_all, pair_all)
                near_w[at] += coupling_ref[pair, k]
            for q in range(pairs):
                to = which * pairs + q
                nums[own_weights + to] = near_w[pairs + q]
                nums[own_weights + weights + to] = near_w[inner_at * pairs + q]
                told = jnp.where(lane == to, near_w[outer_at * pairs + q], told)
                told = jnp.where(lane == weights + to, near_w[inner_at * pairs + q], told)
        row_of_nums = jnp.zeros(nums_ref.shape, F32)
        lane_of_nums = lax.broadcasted_iota(I32, nums_ref.shape, 1)
        for at, number in nums.items():
            row_of_nums = jnp.where(lane_of_nums == at, number, row_of_nums)
        nums_ref[...] = row_of_nums
        coarse = told.astype(BF16).astype(F32)
        middle = (told - coarse).astype(BF16).astype(F32)
        fine = told - coarse - middle
        told = jnp.where(row == 0, coarse, jnp.where(row == 1, middle, jnp.where(row == 2, fine, 0.0)))
        low_ref[pao:, :] = told.astype(BF16)
        large.wait()
        low_ref[:pao, :] = coeff_ref[mine, :, :part]
        high_ref[...] = coeff_ref[mine, :, part:]

    rode = (VMEM, (pao + riders, part), BF16)
    x_low, x_high, nums = call(
        plan_body,
        [HBM] * 7,
        [rode, (VMEM, (pao, part), BF16), (VMEM, (8, part), F32)],
        (pair_owner, pair_occ.T, partners, coupling, eps_occ, nvirt, coeff),
        scratch=[
            pltpu.SMEM(pair_owner.shape, I32),
            pltpu.SMEM(pair_occ.shape[::-1], I32),
            pltpu.SMEM(partners.shape, I32),
            pltpu.SMEM(coupling.shape, F32),
            pltpu.SMEM(eps_occ.shape, F32),
            pltpu.SMEM(nvirt.shape, I32),
            pltpu.SMEM((3 * pairs,), F32),
            pltpu.VMEM(coeff.shape, BF16),
            pltpu.SemaphoreType.DMA((7,)),
        ],
        vmem=60,
    )
    low_out, high_out, low_in = outer(x_low), outer(x_high), inner(x_low)

    def told_of(low_ref):
        rows = low_ref[pao:, :].astype(F32)
        return rows[0:1] + rows[1:2] + rows[2:3]

    def overlaps(x, coeff_ref, out_ref):
        turned = x.T
        for q in range(pairs):
            s = mxu(turned, coeff_ref[q], NN) * (1.0 / pao)
            out_ref[q] = s.astype(BF16)

    def coupled(s_ref, parts):
        total = None
        for at, weight, amp in parts:
            s = s_ref[at]
            u = mxu(s, amp, NN).astype(BF16)
            term = weight * mxu(u, s, NT)
            total = term if total is None else total + term
        return total

    tiles = [pl.ds(at, tile) for at in range(0, aux, tile)]

    def half_into(y_ref, three_ref, at_occ, x):
        for rows in tiles:
            y_ref[rows, :] = (mxu(three_ref[at_occ, rows, :], x, NN) * pao_scale).astype(BF16)

    def fetch_body(three_ref, after_ref, held_ref, sem):
        copy = pltpu.make_async_copy(three_ref, held_ref, sem)
        copy.start()
        copy.wait()

    (blocks,) = call(
        fetch_body,
        [ANY, ANY],
        [(VMEM, three_index.shape, BF16)],
        (three_index, nums),
        scratch=[pltpu.SemaphoreType.DMA],
        vmem=50,
    )

    def outer_low_body(three_ref, x_ref, y_ref):
        half_into(y_ref, three_ref, whole(told_of(x_ref)[0, place_at]), x_ref[:pao, :])
        y_ref[aux:, :] = jnp.zeros((riders, part), BF16)

    (y_low,) = call(
        outer_low_body,
        [VMEM, VMEM],
        [(VMEM, (aux + riders, part), BF16)],
        (blocks, low_out),
    )
    y_low_from_out = outer(y_low)

    def outer_high_body(three_ref, low_ref, x_ref, after_ref, y_ref):
        half_into(y_ref, three_ref, whole(told_of(low_ref)[0, place_at]), x_ref[...])

    (y_high,) = call(
        outer_high_body,
        [VMEM, VMEM, VMEM, ANY],
        [(VMEM, (aux, part), BF16)],
        (blocks, low_out, high_out, y_low),
    )
    y_high_from_out = outer(y_high)

    def outer_body(coeff_ref, amps_ref, low_ref, high_ref, after_ref, s_ref, c_ref, x_ref):
        x_ref[:, :part] = low_ref[:pao, :]
        x_ref[:, part:] = high_ref[...]
        overlaps(x_ref[...], coeff_ref, s_ref)
        told = told_of(low_ref)
        c = coupled(s_ref, [(q, told[0, q], amps_ref[q]) for q in range(pairs)])
        c_ref[:virt, :] = c.astype(BF16)
        c_ref[virt:, :] = jnp.zeros((riders, virt), BF16)

    s_out, c_out = call(
        outer_body,
        [VMEM, VMEM, VMEM, VMEM, ANY],
        [all_s, longer],
        (coeff, amps, low_out, high_out, y_high),
        scratch=[pltpu.VMEM((pao, virt), BF16)],
    )
    c_from_out = outer(c_out)

    def own_half_body(
        nums, three_ref, three_in_ref, coeff_ref, after_ref, first_ref, second_ref, extra_ref, block_ref, sem
    ):
        num, _ = read(nums)
        x = coeff_ref[whole(num(MINE))]
        extra_ref[...] = coeff_ref[whole(num(EXTRA))]
        whose, second = whole(num(WHOSE)), whole(num(SECOND))
        copy = pltpu.make_async_copy(three_in_ref.at[second], block_ref.at[0], sem)

        @pl.when(whose == 1)
        def _():
            copy.start()

        turned = x.T
        first = whole(num(FIRST))
        for rows in tiles:
            first_ref[:, rows] = (mxu(turned, three_ref[first, rows, :], NT) * pao_scale).astype(BF16)

        @pl.when(whose == 0)
        def _():
            half_into(second_ref, three_ref, second, x)

        @pl.when(whose == 1)
        def _():
            copy.wait()
            half_into(second_ref, block_ref, 0, x)

    first_t, second, x_extra = call(
        own_half_body,
        [VMEM, VMEM, ANY, VMEM, ANY],
        [
            (VMEM, (virt, aux), BF16),
            (VMEM, (aux, virt), BF16),
            (VMEM, (pao, virt), BF16),
        ],
        (nums, blocks, three_in, coeff, c_out),
        scratch=[pltpu.VMEM((1, aux, pao), BF16), pltpu.SemaphoreType.DMA],
    )
    x_extra_out = outer(x_extra)

    def own_body(
        nums, coeff_ref, coeff_in_ref, amps_ref, amps_in_ref, eps_ref, after_ref,
        s_ref, c_ref, gain_ref, gain_extra_ref, s_in_ref,
    ):
        num, weight = read(nums)
        mine, extra = whole(num(MINE)), whole(num(EXTRA))
        x = coeff_ref[mine]
        total = None
        for at, of_s, of_coeff, of_amps in (
            (own_weights, s_ref, coeff_ref, amps_ref),
            (own_weights + weights, s_in_ref, coeff_in_ref, amps_in_ref),
        ):
            overlaps(x, of_coeff, of_s)
            c = coupled(of_s, [(q, weight(at + q), of_amps[q]) for q in range(pairs)])
            total = c if total is None else total + c
        c_ref[...] = total

        def gain(pair, count, occupied):
            row = jnp.broadcast_to(eps_ref[pl.ds(pair, 1), :], square)
            energy = row + row.T - occupied
            inside = (lax.broadcasted_iota(I32, square, 0) < count) & (
                lax.broadcasted_iota(I32, square, 1) < count
            )
            return jnp.where(inside, 1.0 / (energy + 1.0), 0.0)

        gain_ref[...] = gain(mine, whole(num(NV_MINE)), num(OCC_MINE))
        gain_extra_ref[...] = gain(extra, whole(num(NV_EXTRA)), num(OCC_EXTRA))

    s_own, c_own, gain, gain_extra = call(
        own_body,
        [VMEM] + [VMEM] * 5 + [ANY],
        [all_s, sq_f, sq_f, sq_f],
        (nums, coeff, coeff_in, amps, amps_in, eps_virt, c_out),
        scratch=[pltpu.VMEM((pairs, virt, virt), BF16)],
    )

    def more_body(nums, coeff_ref, in_ref, low_ref, after_ref, se_ref, s_in_ref, se_in_ref):
        @pl.when(lax.axis_index("role") > 0)
        def _():
            told = told_of(low_ref)
            num, _ = read(nums)
            overlaps(coeff_ref[whole(num(EXTRA))], coeff_ref, se_ref)
            overlaps(in_ref[whole(told[0, mine_at])], coeff_ref, s_in_ref)
            overlaps(in_ref[whole(told[0, extra_at])], coeff_ref, se_in_ref)

    se_own, s_in, se_in = call(
        more_body,
        [VMEM, VMEM, VMEM, VMEM, ANY],
        [all_s, all_s, all_s],
        (nums, coeff, coeff_in, low_in, c_own),
    )

    def first_body(
        nums, first_ref, second_ref, low_ref, high_ref, amps_ref, c_ref, co_ref, gain_ref, after_ref,
        amp_ref, k_ref,
    ):
        first = first_ref[...]
        num, _ = read(nums)
        outside = whole(num(WHOSE)) == 2

        @pl.when(outside)
        def _():
            k_ref[:, :part] = mxu(first, low_ref[:aux, :], NN) * aux_scale
            k_ref[:, part:] = mxu(first, high_ref[...], NN) * aux_scale

        @pl.when(jnp.logical_not(outside))
        def _():
            k_ref[...] = mxu(first, second_ref[...], NN) * aux_scale

        old = amps_ref[whole(num(MINE))].astype(F32)
        c = c_ref[...] + co_ref[:virt, :].astype(F32)
        amp_ref[...] = (gain_ref[...] * (old - k_ref[...] - c)).astype(BF16)

    amp, k_first = call(
        first_body,
        [VMEM] + [VMEM] * 8 + [ANY],
        [sq_b, sq_f],
        (
            nums, first_t, second, y_low_from_out, y_high_from_out,
            amps, c_own, c_from_out, gain, se_own,
        ),
    )
    amp_roles = [amp] + [swap(amp, m) for m in range(1, roles)]

    def rest_body(amp_ref, k_ref, out_ref, out_b_ref):
        amp = amp_ref[...]
        k = k_ref[...]
        right = k + mxu(k.astype(BF16), amp, NN) * virt_scale
        both = right + mxu(amp.T, right.astype(BF16), NN) * virt_scale
        rest = amp.astype(F32) - both
        out_ref[...] = rest
        out_b_ref[:virt, :] = rest.astype(BF16)
        out_b_ref[virt:, :] = jnp.zeros((riders, virt), BF16)

    rest, rest_b = call(rest_body, [VMEM, VMEM], [sq_f, longer], (amp, k_first))

    def relay_body(held_ref, come_ref, out_ref):
        role = lax.axis_index("role")

        @pl.when(role == 0)
        def _():
            out_ref[...] = held_ref[...]

        @pl.when(role > 0)
        def _():
            out_ref[...] = come_ref[...]

    rests, held, step = [], rest_b, 1
    while step < roles:
        rests.append(lax.ppermute(held, "role", [(i, i + step) for i in range(step)]))
        step *= 2
        if step < roles:
            (held,) = call(relay_body, [VMEM, VMEM], [longer], (held, rests[-1]))

    def extra_out_body(coeff_ref, x_ref, after_ref, s_ref):
        @pl.when(lax.axis_index("role") > 0)
        def _():
            overlaps(x_ref[...], coeff_ref, s_ref)

    (se_out,) = call(
        extra_out_body,
        [VMEM, VMEM, ANY],
        [all_s],
        (coeff, x_extra_out, amp),
    )

    def parts_of(nums, weight_of, amp_refs, first=0):
        num, _ = read(nums)
        parts = []
        for m, amp_ref in enumerate(amp_refs, first):
            at = whole(num(ROLE_PAIR + m))
            parts.append((at, weight_of(at), amp_ref[...]))
        return parts

    def told_weight(told, first):
        return lambda at: pick([told[:, first + q : first + q + 1] for q in range(pairs)], at)

    def outer_again_body(first, last, nums, low_ref, s_ref, se_ref, *refs):
        amp_refs, before, c_ref = refs[: last - first], refs[last - first : -1], refs[-1]

        @pl.when(lax.axis_index("role") > 0)
        def _():
            told = told_of(low_ref)
            for slot, of_s in enumerate((s_ref, se_ref)):
                parts = parts_of(nums, told_weight(told, slot * pairs), amp_refs, first)
                total = coupled(of_s, parts)
                for ref in before:
                    total += ref[slot]
                c_ref[slot] = total.astype(c_ref.dtype)

    def outer_again(first, last, dtype, *before):
        (c,) = call(
            functools.partial(outer_again_body, first, last),
            [VMEM] * (4 + last - first + len(before)),
            [(VMEM, (2, virt, virt), dtype)],
            (nums, low_out, s_out, se_out, *amp_roles[first:last], *before),
        )
        return c

    cc_out = outer_again(roles // 2, roles, BF16, outer_again(0, roles // 2, F32))
    cc_from_out = outer_for_owners(cc_out)

    def inner_again_body(nums, low_ref, s_ref, se_ref, *refs):
        amp_refs, c_refs = refs[:roles], refs[-2:]

        @pl.when(lax.axis_index("role") > 0)
        def _():
            told = told_of(low_ref)
            for slot, of_s, c_ref in zip(range(2), (s_ref, se_ref), c_refs):
                parts = parts_of(nums, told_weight(told, weights + slot * pairs), amp_refs)
                c_ref[...] = coupled(of_s, parts).astype(BF16)

    c_in, ce_in = call(
        inner_again_body,
        [VMEM] + [VMEM] * (3 + roles) + [ANY],
        [sq_b, sq_b],
        (nums, low_in, s_in, se_in, *amp_roles, cc_out),
    )
    c_from_in, ce_from_in = inner(c_in), inner(ce_in)

    def own_again_body(nums, rest_ref, s_ref, se_ref, *refs):
        amp_refs, (after_ref, out_ref, out_extra_ref) = refs[:roles], refs[-3:]

        @pl.when(lax.axis_index("role") > 0)
        def _():
            row = nums[0:1, :]
            parts = parts_of(nums, told_weight(row, own_weights), amp_refs)
            out_ref[...] = rest_ref[...] - coupled(s_ref, parts)
            parts = parts_of(nums, told_weight(row, own_weights + pairs), amp_refs)
            out_extra_ref[...] = -coupled(se_ref, parts)

    rest, rest_extra = call(
        own_again_body,
        [VMEM] + [VMEM] * (3 + roles) + [ANY],
        [sq_f, sq_f],
        (nums, rest, s_own, se_own, *amp_roles, c_in),
    )

    def taken(num):
        role = lax.axis_index("role")
        return role > 0, role == whole(num(OWNER))

    def clear_body(nums, after_ref, amp_out, orb_out, zero_ref, sems):
        num, _ = read(nums)
        zero_ref[...] = jnp.zeros((pao, virt), BF16)
        for slot, here in enumerate(taken(num)):

            @pl.when(jnp.logical_not(here))
            def _():
                copies = [
                    pltpu.make_async_copy(zero_ref.at[pl.ds(0, virt)], amp_out.at[slot], sems.at[0]),
                    pltpu.make_async_copy(zero_ref, orb_out.at[slot], sems.at[1]),
                ]
                for copy in copies:
                    copy.start()
                for copy in copies:
                    copy.wait()

    outs = [(ANY, (slots, virt, virt), BF16), (ANY, (slots, pao, virt), BF16)]
    cleared = call(
        clear_body,
        [VMEM, ANY],
        outs,
        (nums, c_in),
        scratch=[pltpu.VMEM((pao, virt), BF16), pltpu.SemaphoreType.DMA((2,))],
    )

    def last_body(
        nums, coeff_ref, gain_ref, gain_extra_ref, rest_ref, rest_extra_ref, co_ref, ci_ref, cei_ref, *refs
    ):
        rest_refs, (amp_out, orb_out, amp_ref, orb_ref, sems) = refs[: len(rests)], refs[-5:]
        num, _ = read(nums)
        role = lax.axis_index("role")
        halves = [pl.ds(at, virt) for at in range(0, pao, virt)]

        def copies_of(slot):
            copies = [(amp_ref.at[slot], amp_out.at[slot])]
            copies += [(orb_ref.at[slot, rows], orb_out.at[slot, rows]) for rows in halves]
            first = slot * len(copies)
            return [
                pltpu.make_async_copy(source, target, sems.at[first + at])
                for at, (source, target) in enumerate(copies)
            ]

        here = taken(num)
        gains, kept = (gain_ref, gain_extra_ref), (rest_ref, rest_extra_ref)
        for slot, pair in ((0, MINE), (1, EXTRA)):

            @pl.when(here[slot])
            def _():
                copies = copies_of(slot)
                c_in = (ci_ref, cei_ref)[slot][...]
                total = kept[slot][...] - co_ref[slot].astype(F32) - c_in.astype(F32)
                if slot:
                    come = rest_refs[0][:virt, :]
                    for at, ref in enumerate(rest_refs[1:], 1):
                        come = jnp.where(role >= 1 << at, ref[:virt, :], come)
                    total += come.astype(F32)
                amp_ref[slot] = (gains[slot][...] * total).astype(BF16)
                copies[0].start()
                for rows, copy in zip(halves, copies[1:]):
                    x = coeff_ref[whole(num(pair)), rows, :]
                    dressed = x.astype(F32) + mxu(x, amp_ref[slot], NN) * virt_scale
                    orb_ref[slot, rows, :] = dressed.astype(BF16)
                    copy.start()

        for slot in range(slots):

            @pl.when(here[slot])
            def _():
                for copy in copies_of(slot):
                    copy.wait()

    ins = (
        nums, coeff, gain, gain_extra, rest, rest_extra, cc_from_out, c_from_in, ce_from_in, *rests, *cleared
    )
    amps_out, dressed_out = call(
        last_body,
        [VMEM] * (len(ins) - 2) + [ANY] * 2,
        outs,
        ins,
        scratch=[
            pltpu.VMEM((slots, virt, virt), BF16),
            pltpu.VMEM((slots, pao, virt), BF16),
            pltpu.SemaphoreType.DMA((slots * (1 + pao // virt),)),
        ],
        in_place={len(ins) - 2: 0, len(ins) - 1: 1},
    )
    return amps_out, dressed_out


def solution(mesh):
    in_specs = (
        P("pairs", None, None),
        P("pairs", None, None),
        P("pairs", None, None),
        P("pairs", None),
        P(),
        P("pairs"),
        P("pairs", None),
        P("pairs", None),
        P("pairs", None),
        P("pairs"),
    )
    out_specs = (P(("role", "pairs"), None, None), P(("role", "pairs"), None, None))
    return jax.shard_map(local, mesh=mesh, in_specs=in_specs, out_specs=out_specs, check_vma=False)
```
